32 devices in a mesh: dp: 2 (over x), seq: 16 (over z, y, core).
Axes of the slice: x: 2, y: 2, z: 4, core: 2. Of those that a mesh axis runs over, the one named last changes fastest.
Arguments:
- tokens: bfloat16 [2, 4096, 1280], P('dp', 'seq'), may hold values from -80 to 80
- cotangent: bfloat16 [2, 4096, 1280], P('dp', 'seq'), may hold values from -16 to 16
- router: bfloat16 [1280, 64], replicated, may hold values from -1 to 1
- slot_outputs: bfloat16 [2, 64, 1280], P('dp'), may hold values from -6 to 6
- base_in: bfloat16 [1280, 5120], P(None, 'seq'), may hold values from -0.15625 to 0.15625
- base_out: bfloat16 [5120, 1280], P('seq'), may hold values from -0.078125 to 0.078125
- delta_in_left: bfloat16 [64, 1280, 64], P('seq', 'dp'), may hold values from -0.15625 to 0.15625
- delta_in_right: bfloat16 [64, 64, 5120], P('dp', None, 'seq'), may hold values from -0.75 to 0.75
- delta_out_left: bfloat16 [64, 5120, 64], P('dp', 'seq'), may hold values from -0.078125 to 0.078125
- delta_out_right: bfloat16 [64, 64, 1280], P('seq', None, 'dp'), may hold values from -0.75 to 0.75
Outputs:
- token_grad: bfloat16 [2, 4096, 1280], P('dp', 'seq')
- grad_in_left: bfloat16 [64, 1280, 64], P('seq', 'dp')
- grad_in_right: bfloat16 [64, 64, 5120], P('dp', None, 'seq')
- grad_out_left: bfloat16 [64, 5120, 64], P('dp', 'seq')
- grad_out_right: bfloat16 [64, 64, 1280], P('seq', None, 'dp')
The draws below stay inside these ranges and needn't reach their ends.
All inputs are finite; a program needn't handle non-finite values.
Results may differ from the reference program's by a relative error of at most 0.015.
Values may be sent and summed in bfloat16 or wider, within the bound.
No kernel may reach another device: no remote copies, remote signals or barrier semaphores. Data moves between devices by JAX's collectives and lax.ppermute only.
A program may use at most 64 MiB of HBM per device.

```python
import math
import jax
import jax.numpy as jnp
from jax import lax

D = 1280
FF = 5120
RANK = 64
EXPERTS = 64
LENGTH = 4096
IMAGES = 2


def router_table(key):
    inner_key = jax.random.fold_in(key, 11)
    values = jax.random.normal(inner_key, (D, EXPERTS), jnp.float32)
    return jnp.clip(values, -5.0, 5.0) / math.sqrt(D)


def draw_router(key, part):
    table = router_table(key)
    return table.astype(jnp.bfloat16)


def draw_tokens(key, part):
    key = jax.random.fold_in(key, 3)
    streams = jax.random.split(key, 2)
    shape = (IMAGES, LENGTH, D)
    position = jnp.arange(LENGTH, dtype=jnp.float32) / LENGTH
    ramp = 0.6 + 1.2 * position
    values = jnp.clip(jax.random.normal(streams[0], shape, jnp.float32), -4.0, 4.0)
    low_log = math.log(0.5)
    high_log = math.log(2.0)
    scales = jnp.exp(jax.random.uniform(streams[1], (IMAGES, LENGTH, 1), jnp.float32, low_log, high_log))
    values = values * scales * ramp[None, :, None]
    return jnp.clip(values, -80.0, 80.0).astype(jnp.bfloat16)


def block_scale(key, dims, shards, smallest, largest):
    gain, own = 1.0, jax.random.fold_in(key, 6)
    for dim, shards_of in shards:
        draws = jnp.exp(jax.random.uniform(jax.random.fold_in(own, dim), (shards_of,), jnp.float32, smallest / len(shards), largest / len(shards)))
        gain = gain * jnp.repeat(draws, dims[dim] // shards_of).reshape([-1 if axis == dim else 1 for axis in range(len(dims))])
    return gain


def scatter_about(stream_key, shape, spread, reach, cuts=(), kind=jnp.bfloat16):
    values = spread * jax.random.normal(stream_key, shape, jnp.float32)
    if cuts:
        values = values * block_scale(stream_key, shape, cuts, -0.22, 0.18)
    return jnp.clip(values, -reach, reach).astype(kind)


def setup_inputs(seed: int = 0) -> dict:
    arg_keys = jax.random.split(jax.random.key(seed), 11)
    return {
        "tokens": draw_tokens(jax.random.fold_in(arg_keys[10], 71), 0),
        "cotangent": scatter_about(arg_keys[1], (IMAGES, LENGTH, D), 3.0, 16.0, ((0, 2), (1, 16))),
        "router": draw_router(jax.random.fold_in(arg_keys[10], 71), 0),
        "slot_outputs": scatter_about(arg_keys[3], (IMAGES, EXPERTS, D), 1.0, 6.0, ((0, 2),)),
        "base_in": scatter_about(arg_keys[4], (D, FF), D ** -0.5, 0.15625, ((1, 16),)),
        "base_out": scatter_about(arg_keys[5], (FF, D), FF ** -0.5, 0.078125, ((0, 16),)),
        "delta_in_left": scatter_about(arg_keys[6], (EXPERTS, D, RANK), D ** -0.5, 0.15625, ((0, 16), (1, 2))),
        "delta_in_right": scatter_about(arg_keys[7], (EXPERTS, RANK, FF), RANK ** -0.5, 0.75, ((0, 2), (2, 16))),
        "delta_out_left": scatter_about(arg_keys[8], (EXPERTS, FF, RANK), FF ** -0.5, 0.078125, ((0, 2), (1, 16))),
        "delta_out_right": scatter_about(arg_keys[9], (EXPERTS, RANK, D), RANK ** -0.5, 0.75, ((0, 16), (2, 2))),
    }


def gelu_backward(preact, upstream):
    return jax.vjp(jax.nn.gelu, preact)[1](upstream)[0]

def one_image(image, cot_rows, saved, router, base_in, base_out, in_left, in_right, out_left, out_right):
    logits = jnp.dot(image, router, preferred_element_type=jnp.float32)
    slot_peak = lax.optimization_barrier(jnp.max(logits, axis=0))
    slot_total = lax.optimization_barrier(jnp.sum(jnp.exp(logits - slot_peak), axis=0))
    dispatch = jnp.exp(logits - slot_peak) / slot_total
    dispatch_low = dispatch.astype(jnp.bfloat16)
    combine = jax.nn.softmax(logits, axis=1)
    combine_low = combine.astype(jnp.bfloat16)
    inputs_low = jnp.dot(dispatch_low.T, image, preferred_element_type=jnp.float32).astype(jnp.bfloat16)
    grads_low = jnp.dot(combine_low.T, cot_rows, preferred_element_type=jnp.float32).astype(jnp.bfloat16)
    up_low = jnp.einsum('jd,jdr->jr', inputs_low.astype(jnp.float32), in_left.astype(jnp.float32)).astype(jnp.bfloat16)
    back_low = jnp.einsum('jd,jrd->jr', grads_low.astype(jnp.float32), out_right.astype(jnp.float32)).astype(jnp.bfloat16)
    preact = jnp.dot(inputs_low, base_in, preferred_element_type=jnp.float32) + jnp.einsum('jr,jrf->jf', up_low.astype(jnp.float32), in_right.astype(jnp.float32))
    hidden_low = jax.nn.gelu(preact).astype(jnp.bfloat16)
    hidden_grad = jnp.dot(grads_low, base_out.T, preferred_element_type=jnp.float32) + jnp.einsum('jr,jfr->jf', back_low.astype(jnp.float32), out_left.astype(jnp.float32))
    preact_grad = gelu_backward(preact, hidden_grad).astype(jnp.bfloat16)
    value_low = jnp.einsum('jf,jfr->jr', hidden_low.astype(jnp.float32), out_left.astype(jnp.float32)).astype(jnp.bfloat16)
    down_low = jnp.einsum('jf,jrf->jr', preact_grad.astype(jnp.float32), in_right.astype(jnp.float32)).astype(jnp.bfloat16)
    slot_grads = (jnp.dot(preact_grad, base_in.T, preferred_element_type=jnp.float32) + jnp.einsum('jr,jdr->jd', down_low.astype(jnp.float32), in_left.astype(jnp.float32))).astype(jnp.bfloat16)
    weight_grad = jnp.dot(image, slot_grads.T, preferred_element_type=jnp.float32)
    shift_back = lax.optimization_barrier(jnp.sum(dispatch_low.astype(jnp.float32) * weight_grad, axis=0))
    dispatch_logit = dispatch * (weight_grad - shift_back)
    mixing_grad = jnp.dot(cot_rows, saved.T, preferred_element_type=jnp.float32)
    combine_logit = combine * (mixing_grad - lax.optimization_barrier(jnp.sum(combine * mixing_grad, axis=1, keepdims=True)))
    logit_grad = (dispatch_logit + combine_logit).astype(jnp.bfloat16)
    token_grad = (jnp.dot(dispatch_low, slot_grads, preferred_element_type=jnp.float32) + jnp.dot(logit_grad, router.T, preferred_element_type=jnp.float32)).astype(jnp.bfloat16)
    return (token_grad, inputs_low, grads_low, up_low, back_low, hidden_low, preact_grad, value_low, down_low)

def reference(tokens, cotangent, router, slot_outputs, base_in, base_out, delta_in_left, delta_in_right, delta_out_left, delta_out_right):
    collected = []
    for member in range(tokens.shape[0]):
        collected.append(one_image(tokens[member], cotangent[member], slot_outputs[member], router, base_in, base_out, delta_in_left, delta_in_right, delta_out_left, delta_out_right))
    token_grad = jnp.stack([entry[0] for entry in collected])
    pieces = [jnp.stack([entry[place] for entry in collected]).astype(jnp.float32) for place in range(1, 9)]
    inputs_low, grads_low, up_low, back_low, hidden_low, preact_grad, value_low, down_low = pieces
    grad_in_left = jnp.einsum('gjd,gjr->jdr', inputs_low, down_low).astype(jnp.bfloat16)
    grad_in_right = jnp.einsum('gjr,gjf->jrf', up_low, preact_grad).astype(jnp.bfloat16)
    grad_out_left = jnp.einsum('gjf,gjr->jfr', hidden_low, back_low).astype(jnp.bfloat16)
    grad_out_right = jnp.einsum('gjr,gjd->jrd', value_low, grads_low).astype(jnp.bfloat16)
    return (token_grad, grad_in_left, grad_in_right, grad_out_left, grad_out_right)
```

```python
import jax
import jax.numpy as jnp
from jax import lax
from jax.sharding import PartitionSpec as P

BOTH = ("dp", "seq")
STATS = 128


def gelu_backward(preact, upstream):
    return jax.vjp(jax.nn.gelu, preact)[1](upstream)[0]


def dot_first(left, right):
    return lax.dot_general(
        left, right, (((0,), (0,)), ((), ())), preferred_element_type=jnp.float32
    )


def dot_last(left, right):
    return lax.dot_general(
        left, right, (((1,), (1,)), ((), ())), preferred_element_type=jnp.float32
    )


def split(value):
    high = lax.reduce_precision(value, 8, 7)
    low = lax.reduce_precision(value - high, 8, 7)
    return high.astype(jnp.bfloat16), low.astype(jnp.bfloat16)


def joined(high, low):
    return high.astype(jnp.float32) + low.astype(jnp.float32)


def exchange(blocks):
    flat = blocks.reshape((-1,) + blocks.shape[2:])
    return lax.all_to_all(flat, BOTH, 0, 0, tiled=True).reshape(blocks.shape)


def local(
    tokens,
    cotangent,
    router,
    slot_outputs,
    base_in,
    base_out,
    in_left,
    in_right,
    out_left,
    out_right,
):
    groups, ring = lax.axis_size("dp"), lax.axis_size("seq")
    image_rows = tokens[0]
    cot_rows = cotangent[0]
    saved_outputs = slot_outputs[0]
    width = image_rows.shape[1]
    slots = router.shape[1]
    owned, slice_width, rank = in_left.shape
    members = in_right.shape[0]
    places = members // owned
    group, place = lax.axis_index("dp"), lax.axis_index("seq")

    logits = jnp.dot(image_rows, router, preferred_element_type=jnp.float32)
    peak_high, peak_low = split(jnp.max(logits, axis=0))
    near = jnp.exp(logits - joined(peak_high, peak_low))
    total_high, total_low = split(jnp.sum(near, axis=0))
    combine = jax.nn.softmax(logits, axis=1)
    sums = jnp.stack(
        [
            dot_first(near.astype(jnp.bfloat16), image_rows),
            dot_first(combine.astype(jnp.bfloat16), cot_rows),
        ],
        axis=1,
    ).astype(jnp.bfloat16)
    sums = sums.reshape(ring, owned, 2, groups, slice_width).transpose(3, 0, 1, 2, 4)
    sums = sums.reshape(groups, ring, owned, 2 * slice_width)
    stats = jnp.stack([peak_high, peak_low, total_high, total_low], axis=1)
    stats = jnp.pad(stats, ((0, 0), (0, STATS - 4))).reshape(1, ring, owned, STATS)
    stats = jnp.broadcast_to(stats, (groups, ring, owned, STATS))
    first = exchange(jnp.concatenate([sums, stats], axis=3))

    tail = 2 * slice_width
    peaks = joined(first[..., tail], first[..., tail + 1])
    totals = joined(first[..., tail + 2], first[..., tail + 3])
    peak = jnp.max(peaks, axis=1)
    near_scale = jnp.exp(peaks - peak[:, None])
    total = jnp.sum(near_scale * totals, axis=1)
    near_scale = near_scale / total[:, None]
    parts = first[..., :tail].astype(jnp.float32)
    slot_inputs = jnp.sum(parts[..., :slice_width] * near_scale[..., None], axis=1)
    inputs_own = slot_inputs.astype(jnp.bfloat16)
    grads_own = jnp.sum(parts[..., slice_width:], axis=1).astype(jnp.bfloat16)
    up_part = jnp.einsum("gjd,jdr->gjr", inputs_own, in_left, preferred_element_type=jnp.float32)
    back_part = jnp.einsum("gjd,jrd->gjr", grads_own, out_right, preferred_element_type=jnp.float32)
    second = jnp.concatenate(
        [inputs_own, grads_own, *split(up_part), *split(back_part)], axis=2
    )
    second = exchange(jnp.broadcast_to(second, (groups, ring) + second.shape))
    second = lax.dynamic_slice_in_dim(second, group * places, places, 1)

    def gathered(start):
        piece = second[..., start : start + slice_width]
        return piece.transpose(2, 1, 3, 0, 4).reshape(groups * members, width)

    def ranks(start):
        piece = joined(
            second[..., start : start + rank], second[..., start + rank : start + 2 * rank]
        )
        piece = jnp.sum(piece, axis=0).transpose(1, 0, 2, 3)
        return piece.reshape(groups, members, rank).astype(jnp.bfloat16)

    inputs_low, grads_low = gathered(0), gathered(slice_width)
    up_low, back_low = ranks(tail), ranks(tail + 2 * rank)
    hidden = base_in.shape[1]
    preact = jnp.dot(inputs_low, base_in, preferred_element_type=jnp.float32).reshape(
        groups, members, hidden
    ) + jnp.einsum("gjr,jrf->gjf", up_low, in_right, preferred_element_type=jnp.float32)
    hidden_low = jax.nn.gelu(preact).astype(jnp.bfloat16)
    hidden_grad = dot_last(grads_low, base_out).reshape(groups, members, hidden) + jnp.einsum(
        "gjr,jfr->gjf", back_low, out_left, preferred_element_type=jnp.float32
    )
    preact_grad = gelu_backward(preact, hidden_grad).astype(jnp.bfloat16)
    slot_term = dot_last(preact_grad.reshape(groups * members, hidden), base_in)
    down_term = jnp.einsum(
        "gjf,jrf->gjr", preact_grad, in_right, preferred_element_type=jnp.float32
    )
    value_term = jnp.einsum(
        "gjf,jfr->gjr", hidden_low, out_left, preferred_element_type=jnp.float32
    )
    slot_term = slot_term.astype(jnp.bfloat16).reshape(groups, places, owned, groups, slice_width)
    slot_term = slot_term.transpose(3, 1, 0, 2, 4)
    rank_term = jnp.concatenate([down_term, value_term], axis=2).astype(jnp.bfloat16)
    rank_term = rank_term.reshape(groups, places, owned, 2 * rank).transpose(1, 0, 2, 3)
    rank_term = jnp.broadcast_to(rank_term, (groups,) + rank_term.shape)
    third = jnp.concatenate([slot_term, rank_term], axis=4)
    third = lax.dynamic_update_slice_in_dim(
        jnp.zeros((groups, ring) + third.shape[2:], jnp.bfloat16), third, group * places, 1
    )
    third = exchange(third)
    third = lax.dynamic_index_in_dim(third, place // places, 0, keepdims=False)
    third = jnp.sum(third.astype(jnp.float32), axis=0)
    down_own = third[..., slice_width : slice_width + rank].astype(jnp.bfloat16)
    value_own = third[..., slice_width + rank :].astype(jnp.bfloat16)
    slot_grads_own = (
        third[..., :slice_width]
        + jnp.einsum("gjr,jdr->gjd", down_own, in_left, preferred_element_type=jnp.float32)
    ).astype(jnp.bfloat16)
    shift_part = jnp.sum(slot_grads_own.astype(jnp.float32) * slot_inputs, axis=2)
    stats = jnp.stack([*split(peak), *split(total), *split(shift_part)], axis=2)
    stats = jnp.pad(stats, ((0, 0), (0, 0), (0, STATS - 6)))
    fourth = jnp.concatenate([slot_grads_own, stats], axis=2)[:, None]
    fourth = exchange(jnp.broadcast_to(fourth, (groups, ring) + fourth.shape[2:]))
    slot_grads = fourth[..., :slice_width].transpose(1, 2, 0, 3).reshape(slots, width)
    stats = fourth[..., slice_width:].astype(jnp.float32).reshape(groups, slots, STATS)
    slot_peak = stats[0, :, 0] + stats[0, :, 1]
    slot_total = stats[0, :, 2] + stats[0, :, 3]
    shift_back = jnp.sum(stats[:, :, 4] + stats[:, :, 5], axis=0)

    dispatch = jnp.exp(logits - slot_peak) / slot_total
    dispatch_low = dispatch.astype(jnp.bfloat16)
    weight_grad = dot_last(image_rows, slot_grads)
    dispatch_logit = dispatch * (weight_grad - shift_back)
    mixing_grad = dot_last(cot_rows, saved_outputs)
    combine_logit = combine * (mixing_grad - jnp.sum(combine * mixing_grad, axis=1, keepdims=True))
    logit_grad = (dispatch_logit + combine_logit).astype(jnp.bfloat16)
    token_grad = (
        jnp.dot(dispatch_low, slot_grads, preferred_element_type=jnp.float32)
        + dot_last(logit_grad, router)
    ).astype(jnp.bfloat16)
    grad_in_right = jnp.einsum(
        "gjr,gjf->jrf", up_low, preact_grad, preferred_element_type=jnp.float32
    ).astype(jnp.bfloat16)
    grad_out_left = jnp.einsum(
        "gjf,gjr->jfr", hidden_low, back_low, preferred_element_type=jnp.float32
    ).astype(jnp.bfloat16)
    grad_in_left = jnp.einsum(
        "gjd,gjr->jdr", inputs_own, down_own, preferred_element_type=jnp.float32
    ).astype(jnp.bfloat16)
    grad_out_right = jnp.einsum(
        "gjr,gjd->jrd", value_own, grads_own, preferred_element_type=jnp.float32
    ).astype(jnp.bfloat16)
    return (token_grad[None], grad_in_left, grad_in_right, grad_out_left, grad_out_right)


def solution(mesh):
    in_specs = (
        P("dp", "seq", None),
        P("dp", "seq", None),
        P(),
        P("dp", None, None),
        P(None, "seq"),
        P("seq", None),
        P("seq", "dp", None),
        P("dp", None, "seq"),
        P("dp", "seq", None),
        P("seq", None, "dp"),
    )
    out_specs = (
        P("dp", "seq", None),
        P("seq", "dp", None),
        P("dp", None, "seq"),
        P("dp", "seq", None),
        P("seq", None, "dp"),
    )
    return jax.shard_map(local, mesh=mesh, in_specs=in_specs, out_specs=out_specs, check_vma=False)
```

```python
import jax
import jax.numpy as jnp
from jax import lax
from jax.sharding import PartitionSpec as P

BOTH = ("dp", "seq")
STATS = 128


def gelu_backward(preact, upstream):
    return jax.vjp(jax.nn.gelu, preact)[1](upstream)[0]


def dot_first(left, right):
    return lax.dot_general(
        left, right, (((0,), (0,)), ((), ())), preferred_element_type=jnp.float32
    )


def dot_last(left, right):
    return lax.dot_general(
        left, right, (((1,), (1,)), ((), ())), preferred_element_type=jnp.float32
    )


def split(value):
    high = lax.reduce_precision(value, 8, 7)
    low = lax.reduce_precision(value - high, 8, 7)
    return high.astype(jnp.bfloat16), low.astype(jnp.bfloat16)


def joined(high, low):
    return high.astype(jnp.float32) + low.astype(jnp.float32)


def exchange(blocks):
    flat = blocks.reshape((-1,) + blocks.shape[2:])
    return lax.all_to_all(flat, BOTH, 0, 0, tiled=True).reshape(blocks.shape)


def to_group(block, groups, ring):
    places = ring // groups
    here = lax.axis_index("seq")
    received = []
    for step in range(ring):
        pairs = []
        for group in range(groups):
            for place in range(ring):
                sender = place // places * ring + group * places + place % places
                pairs.append((sender, group * ring + (place ^ step)))
        received.append(lax.ppermute(block, BOTH, pairs))
    blocks = jnp.stack(received)
    bits = ring.bit_length() - 1
    blocks = blocks.reshape((2,) * bits + block.shape)
    for bit in range(bits):
        turned = (here >> (bits - 1 - bit)) & 1
        blocks = jnp.where(turned == 1, jnp.flip(blocks, bit), blocks)
    return blocks.reshape((groups, places) + block.shape)


def home(block, groups, ring):
    places = ring // groups
    pairs = [
        (group * ring + place, place // places * ring + group * places + place % places)
        for group in range(groups)
        for place in range(ring)
    ]
    return lax.ppermute(block, BOTH, pairs)


def local(
    tokens,
    cotangent,
    router,
    slot_outputs,
    base_in,
    base_out,
    in_left,
    in_right,
    out_left,
    out_right,
):
    groups, ring = lax.axis_size("dp"), lax.axis_size("seq")
    image_rows = tokens[0]
    cot_rows = cotangent[0]
    saved_outputs = slot_outputs[0]
    width = image_rows.shape[1]
    slots = router.shape[1]
    owned, slice_width, rank = in_left.shape
    members = in_right.shape[0]
    places = members // owned

    logits = jnp.dot(image_rows, router, preferred_element_type=jnp.float32)
    peak_high, peak_low = split(jnp.max(logits, axis=0))
    near = jnp.exp(logits - joined(peak_high, peak_low))
    total_high, total_low = split(jnp.sum(near, axis=0))
    combine = jax.nn.softmax(logits, axis=1)
    sums = jnp.stack(
        [
            dot_first(near.astype(jnp.bfloat16), image_rows),
            dot_first(combine.astype(jnp.bfloat16), cot_rows),
        ],
        axis=1,
    ).astype(jnp.bfloat16)
    sums = sums.reshape(ring, owned, 2, groups, slice_width).transpose(3, 0, 1, 2, 4)
    sums = sums.reshape(groups, ring, owned, 2 * slice_width)
    stats = jnp.stack([peak_high, peak_low, total_high, total_low], axis=1)
    stats = jnp.pad(stats, ((0, 0), (0, STATS - 4))).reshape(1, ring, owned, STATS)
    stats = jnp.broadcast_to(stats, (groups, ring, owned, STATS))
    first = exchange(jnp.concatenate([sums, stats], axis=3))

    tail = 2 * slice_width
    peaks = joined(first[..., tail], first[..., tail + 1])
    totals = joined(first[..., tail + 2], first[..., tail + 3])
    peak = jnp.max(peaks, axis=1)
    near_scale = jnp.exp(peaks - peak[:, None])
    total = jnp.sum(near_scale * totals, axis=1)
    near_scale = near_scale / total[:, None]
    parts = first[..., :tail].astype(jnp.float32)
    slot_inputs = jnp.sum(parts[..., :slice_width] * near_scale[..., None], axis=1)
    inputs_own = slot_inputs.astype(jnp.bfloat16)
    grads_own = jnp.sum(parts[..., slice_width:], axis=1).astype(jnp.bfloat16)
    up_part = jnp.einsum("gjd,jdr->gjr", inputs_own, in_left, preferred_element_type=jnp.float32)
    back_part = jnp.einsum("gjd,jrd->gjr", grads_own, out_right, preferred_element_type=jnp.float32)
    second = jnp.concatenate(
        [inputs_own, grads_own, *split(up_part), *split(back_part)], axis=2
    )
    second = to_group(second, groups, ring)

    def gathered(start):
        piece = second[..., start : start + slice_width]
        return piece.transpose(2, 1, 3, 0, 4).reshape(groups * members, width)

    def ranks(start):
        piece = joined(
            second[..., start : start + rank], second[..., start + rank : start + 2 * rank]
        )
        piece = jnp.sum(piece, axis=0).transpose(1, 0, 2, 3)
        return piece.reshape(groups, members, rank).astype(jnp.bfloat16)

    inputs_low, grads_low = gathered(0), gathered(slice_width)
    up_low, back_low = ranks(tail), ranks(tail + 2 * rank)
    hidden = base_in.shape[1]
    preact = jnp.dot(inputs_low, base_in, preferred_element_type=jnp.float32).reshape(
        groups, members, hidden
    ) + jnp.einsum("gjr,jrf->gjf", up_low, in_right, preferred_element_type=jnp.float32)
    hidden_low = jax.nn.gelu(preact).astype(jnp.bfloat16)
    hidden_grad = dot_last(grads_low, base_out).reshape(groups, members, hidden) + jnp.einsum(
        "gjr,jfr->gjf", back_low, out_left, preferred_element_type=jnp.float32
    )
    preact_grad = gelu_backward(preact, hidden_grad).astype(jnp.bfloat16)
    slot_term = dot_last(preact_grad.reshape(groups * members, hidden), base_in)
    down_term = jnp.einsum(
        "gjf,jrf->gjr", preact_grad, in_right, preferred_element_type=jnp.float32
    )
    value_term = jnp.einsum(
        "gjf,jfr->gjr", hidden_low, out_left, preferred_element_type=jnp.float32
    )
    slot_term = slot_term.astype(jnp.bfloat16).reshape(groups, places, owned, groups, slice_width)
    slot_term = slot_term.transpose(3, 1, 0, 2, 4)
    rank_term = jnp.concatenate([down_term, value_term], axis=2).astype(jnp.bfloat16)
    rank_term = rank_term.reshape(groups, places, owned, 2 * rank).transpose(1, 0, 2, 3)
    rank_term = jnp.broadcast_to(rank_term, (groups,) + rank_term.shape)
    third = jnp.concatenate([slot_term, rank_term], axis=4)
    third = third.reshape((ring,) + third.shape[2:])
    third = lax.all_to_all(third, "seq", 0, 0, tiled=True)
    third = home(jnp.sum(third.astype(jnp.float32), axis=0), groups, ring)
    down_own = third[..., slice_width : slice_width + rank].astype(jnp.bfloat16)
    value_own = third[..., slice_width + rank :].astype(jnp.bfloat16)
    slot_grads_own = (
        third[..., :slice_width]
        + jnp.einsum("gjr,jdr->gjd", down_own, in_left, preferred_element_type=jnp.float32)
    ).astype(jnp.bfloat16)
    shift_part = jnp.sum(slot_grads_own.astype(jnp.float32) * slot_inputs, axis=2)
    stats = jnp.stack([*split(peak), *split(total), *split(shift_part)], axis=2)
    stats = jnp.pad(stats, ((0, 0), (0, 0), (0, STATS - 6)))
    fourth = jnp.concatenate([slot_grads_own, stats], axis=2)[:, None]
    fourth = exchange(jnp.broadcast_to(fourth, (groups, ring) + fourth.shape[2:]))
    slot_grads = fourth[..., :slice_width].transpose(1, 2, 0, 3).reshape(slots, width)
    stats = fourth[..., slice_width:].astype(jnp.float32).reshape(groups, slots, STATS)
    slot_peak = stats[0, :, 0] + stats[0, :, 1]
    slot_total = stats[0, :, 2] + stats[0, :, 3]
    shift_back = jnp.sum(stats[:, :, 4] + stats[:, :, 5], axis=0)

    dispatch = jnp.exp(logits - slot_peak) / slot_total
    dispatch_low = dispatch.astype(jnp.bfloat16)
    weight_grad = dot_last(image_rows, slot_grads)
    dispatch_logit = dispatch * (weight_grad - shift_back)
    mixing_grad = dot_last(cot_rows, saved_outputs)
    combine_logit = combine * (mixing_grad - jnp.sum(combine * mixing_grad, axis=1, keepdims=True))
    logit_grad = (dispatch_logit + combine_logit).astype(jnp.bfloat16)
    token_grad = (
        jnp.dot(dispatch_low, slot_grads, preferred_element_type=jnp.float32)
        + dot_last(logit_grad, router)
    ).astype(jnp.bfloat16)
    grad_in_right = jnp.einsum(
        "gjr,gjf->jrf", up_low, preact_grad, preferred_element_type=jnp.float32
    ).astype(jnp.bfloat16)
    grad_out_left = jnp.einsum(
        "gjf,gjr->jfr", hidden_low, back_low, preferred_element_type=jnp.float32
    ).astype(jnp.bfloat16)
    grad_in_left = jnp.einsum(
        "gjd,gjr->jdr", inputs_own, down_own, preferred_element_type=jnp.float32
    ).astype(jnp.bfloat16)
    grad_out_right = jnp.einsum(
        "gjr,gjd->jrd", value_own, grads_own, preferred_element_type=jnp.float32
    ).astype(jnp.bfloat16)
    return (token_grad[None], grad_in_left, grad_in_right, grad_out_left, grad_out_right)


def solution(mesh):
    in_specs = (
        P("dp", "seq", None),
        P("dp", "seq", None),
        P(),
        P("dp", None, None),
        P(None, "seq"),
        P("seq", None),
        P("seq", "dp", None),
        P("dp", None, "seq"),
        P("dp", "seq", None),
        P("seq", None, "dp"),
    )
    out_specs = (
        P("dp", "seq", None),
        P("seq", "dp", None),
        P("dp", None, "seq"),
        P("dp", "seq", None),
        P("seq", None, "dp"),
    )
    return jax.shard_map(local, mesh=mesh, in_specs=in_specs, out_specs=out_specs, check_vma=False)
```

```python
import functools

import jax
import jax.numpy as jnp
from jax import lax
from jax.experimental import pallas as pl
from jax.experimental.pallas import tpu as pltpu
from jax.sharding import PartitionSpec as P

BOTH = ("dp", "seq")
STATS = 128


def gelu_backward(preact, upstream):
    return jax.vjp(jax.nn.gelu, preact)[1](upstream)[0]


def dot_first(left, right):
    return lax.dot_general(
        left, right, (((0,), (0,)), ((), ())), preferred_element_type=jnp.float32
    )


def dot_last(left, right):
    return lax.dot_general(
        left, right, (((1,), (1,)), ((), ())), preferred_element_type=jnp.float32
    )


def split(value):
    high = lax.reduce_precision(value, 8, 7)
    low = lax.reduce_precision(value - high, 8, 7)
    return high.astype(jnp.bfloat16), low.astype(jnp.bfloat16)


def joined(high, low):
    return high.astype(jnp.float32) + low.astype(jnp.float32)


def exchange(blocks):
    flat = blocks.reshape((-1,) + blocks.shape[2:])
    return lax.all_to_all(flat, BOTH, 0, 0, tiled=True).reshape(blocks.shape)


def local_plain(
    tokens,
    cotangent,
    router,
    slot_outputs,
    base_in,
    base_out,
    in_left,
    in_right,
    out_left,
    out_right,
):
    groups, ring = lax.axis_size("dp"), lax.axis_size("seq")
    image_rows = tokens[0]
    cot_rows = cotangent[0]
    saved_outputs = slot_outputs[0]
    width = image_rows.shape[1]
    slots = router.shape[1]
    owned, slice_width, rank = in_left.shape
    members = in_right.shape[0]
    places = members // owned
    group, place = lax.axis_index("dp"), lax.axis_index("seq")

    logits = jnp.dot(image_rows, router, preferred_element_type=jnp.float32)
    peak_high, peak_low = split(jnp.max(logits, axis=0))
    near = jnp.exp(logits - joined(peak_high, peak_low))
    total_high, total_low = split(jnp.sum(near, axis=0))
    combine = jax.nn.softmax(logits, axis=1)
    sums = jnp.stack(
        [
            dot_first(near.astype(jnp.bfloat16), image_rows),
            dot_first(combine.astype(jnp.bfloat16), cot_rows),
        ],
        axis=1,
    ).astype(jnp.bfloat16)
    sums = sums.reshape(ring, owned, 2, groups, slice_width).transpose(3, 0, 1, 2, 4)
    sums = sums.reshape(groups, ring, owned, 2 * slice_width)
    stats = jnp.stack([peak_high, peak_low, total_high, total_low], axis=1)
    stats = jnp.pad(stats, ((0, 0), (0, STATS - 4))).reshape(1, ring, owned, STATS)
    stats = jnp.broadcast_to(stats, (groups, ring, owned, STATS))
    first = exchange(jnp.concatenate([sums, stats], axis=3))

    tail = 2 * slice_width
    peaks = joined(first[..., tail], first[..., tail + 1])
    totals = joined(first[..., tail + 2], first[..., tail + 3])
    peak = jnp.max(peaks, axis=1)
    near_scale = jnp.exp(peaks - peak[:, None])
    total = jnp.sum(near_scale * totals, axis=1)
    near_scale = near_scale / total[:, None]
    parts = first[..., :tail].astype(jnp.float32)
    slot_inputs = jnp.sum(parts[..., :slice_width] * near_scale[..., None], axis=1)
    inputs_own = slot_inputs.astype(jnp.bfloat16)
    grads_own = jnp.sum(parts[..., slice_width:], axis=1).astype(jnp.bfloat16)
    up_part = jnp.einsum("gjd,jdr->gjr", inputs_own, in_left, preferred_element_type=jnp.float32)
    back_part = jnp.einsum("gjd,jrd->gjr", grads_own, out_right, preferred_element_type=jnp.float32)
    second = jnp.concatenate(
        [inputs_own, grads_own, *split(up_part), *split(back_part)], axis=2
    )
    second = exchange(jnp.broadcast_to(second, (groups, ring) + second.shape))
    second = lax.dynamic_slice_in_dim(second, group * places, places, 1)

    def gathered(start):
        piece = second[..., start : start + slice_width]
        return piece.transpose(2, 1, 3, 0, 4).reshape(groups * members, width)

    def ranks(start):
        piece = joined(
            second[..., start : start + rank], second[..., start + rank : start + 2 * rank]
        )
        piece = jnp.sum(piece, axis=0).transpose(1, 0, 2, 3)
        return piece.reshape(groups, members, rank).astype(jnp.bfloat16)

    inputs_low, grads_low = gathered(0), gathered(slice_width)
    up_low, back_low = ranks(tail), ranks(tail + 2 * rank)
    hidden = base_in.shape[1]
    preact = jnp.dot(inputs_low, base_in, preferred_element_type=jnp.float32).reshape(
        groups, members, hidden
    ) + jnp.einsum("gjr,jrf->gjf", up_low, in_right, preferred_element_type=jnp.float32)
    hidden_low = jax.nn.gelu(preact).astype(jnp.bfloat16)
    hidden_grad = dot_last(grads_low, base_out).reshape(groups, members, hidden) + jnp.einsum(
        "gjr,jfr->gjf", back_low, out_left, preferred_element_type=jnp.float32
    )
    preact_grad = gelu_backward(preact, hidden_grad).astype(jnp.bfloat16)
    slot_term = dot_last(preact_grad.reshape(groups * members, hidden), base_in)
    down_term = jnp.einsum(
        "gjf,jrf->gjr", preact_grad, in_right, preferred_element_type=jnp.float32
    )
    value_term = jnp.einsum(
        "gjf,jfr->gjr", hidden_low, out_left, preferred_element_type=jnp.float32
    )
    slot_term = slot_term.astype(jnp.bfloat16).reshape(groups, places, owned, groups, slice_width)
    slot_term = slot_term.transpose(3, 1, 0, 2, 4)
    rank_term = jnp.concatenate([down_term, value_term], axis=2).astype(jnp.bfloat16)
    rank_term = rank_term.reshape(groups, places, owned, 2 * rank).transpose(1, 0, 2, 3)
    rank_term = jnp.broadcast_to(rank_term, (groups,) + rank_term.shape)
    third = jnp.concatenate([slot_term, rank_term], axis=4)
    third = lax.dynamic_update_slice_in_dim(
        jnp.zeros((groups, ring) + third.shape[2:], jnp.bfloat16), third, group * places, 1
    )
    third = exchange(third)
    third = lax.dynamic_index_in_dim(third, place // places, 0, keepdims=False)
    third = jnp.sum(third.astype(jnp.float32), axis=0)
    down_own = third[..., slice_width : slice_width + rank].astype(jnp.bfloat16)
    value_own = third[..., slice_width + rank :].astype(jnp.bfloat16)
    slot_grads_own = (
        third[..., :slice_width]
        + jnp.einsum("gjr,jdr->gjd", down_own, in_left, preferred_element_type=jnp.float32)
    ).astype(jnp.bfloat16)
    shift_part = jnp.sum(slot_grads_own.astype(jnp.float32) * slot_inputs, axis=2)
    stats = jnp.stack([*split(peak), *split(total), *split(shift_part)], axis=2)
    stats = jnp.pad(stats, ((0, 0), (0, 0), (0, STATS - 6)))
    fourth = jnp.concatenate([slot_grads_own, stats], axis=2)[:, None]
    fourth = exchange(jnp.broadcast_to(fourth, (groups, ring) + fourth.shape[2:]))
    slot_grads = fourth[..., :slice_width].transpose(1, 2, 0, 3).reshape(slots, width)
    stats = fourth[..., slice_width:].astype(jnp.float32).reshape(groups, slots, STATS)
    slot_peak = stats[0, :, 0] + stats[0, :, 1]
    slot_total = stats[0, :, 2] + stats[0, :, 3]
    shift_back = jnp.sum(stats[:, :, 4] + stats[:, :, 5], axis=0)

    dispatch = jnp.exp(logits - slot_peak) / slot_total
    dispatch_low = dispatch.astype(jnp.bfloat16)
    weight_grad = dot_last(image_rows, slot_grads)
    dispatch_logit = dispatch * (weight_grad - shift_back)
    mixing_grad = dot_last(cot_rows, saved_outputs)
    combine_logit = combine * (mixing_grad - jnp.sum(combine * mixing_grad, axis=1, keepdims=True))
    logit_grad = (dispatch_logit + combine_logit).astype(jnp.bfloat16)
    token_grad = (
        jnp.dot(dispatch_low, slot_grads, preferred_element_type=jnp.float32)
        + dot_last(logit_grad, router)
    ).astype(jnp.bfloat16)
    grad_in_right = jnp.einsum(
        "gjr,gjf->jrf", up_low, preact_grad, preferred_element_type=jnp.float32
    ).astype(jnp.bfloat16)
    grad_out_left = jnp.einsum(
        "gjf,gjr->jfr", hidden_low, back_low, preferred_element_type=jnp.float32
    ).astype(jnp.bfloat16)
    grad_in_left = jnp.einsum(
        "gjd,gjr->jdr", inputs_own, down_own, preferred_element_type=jnp.float32
    ).astype(jnp.bfloat16)
    grad_out_right = jnp.einsum(
        "gjr,gjd->jrd", value_own, grads_own, preferred_element_type=jnp.float32
    ).astype(jnp.bfloat16)
    return (token_grad[None], grad_in_left, grad_in_right, grad_out_left, grad_out_right)


def dot_plain(left, right):
    return jnp.dot(left, right, preferred_element_type=jnp.float32)


def halves(value):
    high = value.astype(jnp.bfloat16).astype(jnp.float32)
    low = (value - high).astype(jnp.bfloat16).astype(jnp.float32)
    return high, low


def in_lanes(columns, shape):
    lane = lax.broadcasted_iota(jnp.int32, shape, len(shape) - 1)
    out = jnp.zeros(shape, jnp.float32)
    for number, column in enumerate(columns):
        out = jnp.where(lane == number, column, out)
    return out


def own_block(value, owned):
    rows, rank = value.shape
    wide = jnp.concatenate([value] * owned, axis=1)
    shape = (rows, owned * rank)
    block = lax.broadcasted_iota(jnp.int32, shape, 1) // rank
    expert = lax.broadcasted_iota(jnp.int32, shape, 0) % owned
    return jnp.where(block == expert, wide, 0.0).astype(jnp.bfloat16)


def from_own_block(value, owned):
    rows, wide = value.shape
    rank = wide // owned
    block = lax.broadcasted_iota(jnp.int32, value.shape, 1) // rank
    expert = lax.broadcasted_iota(jnp.int32, value.shape, 0) % owned
    kept = jnp.where(block == expert, value, 0.0)
    out = kept[:, :rank]
    for number in range(1, owned):
        out = out + kept[:, number * rank : (number + 1) * rank]
    return out


def sums_kernel(owned, groups, tokens, cotangent, router, first, logits_out, combine_out):
    ring = first.shape[0] // groups
    image_rows, cot_rows = tokens[...], cotangent[...]
    logits = dot_last(router[...], image_rows)
    high, low = halves(jnp.max(logits, axis=1, keepdims=True))
    near = jnp.exp(logits - (high + low))
    total_high, total_low = halves(jnp.sum(near, axis=1, keepdims=True))
    spread = jnp.exp(logits - jnp.max(logits, axis=0, keepdims=True))
    combine = spread / jnp.sum(spread, axis=0, keepdims=True)
    logits_out[...] = logits
    combine_out[...] = combine
    stats = in_lanes([high, low, total_high, total_low], (logits.shape[0], STATS))
    stats = stats.astype(jnp.bfloat16)
    inputs = dot_plain(near.astype(jnp.bfloat16), image_rows).astype(jnp.bfloat16)
    grads = dot_plain(combine.astype(jnp.bfloat16), cot_rows).astype(jnp.bfloat16)
    width = inputs.shape[1] // groups
    for group in range(groups):
        columns = slice(group * width, (group + 1) * width)
        for place in range(ring):
            rows = slice(place * owned, (place + 1) * owned)
            block = group * ring + place
            first[block, :, :width] = inputs[rows, columns]
            first[block, :, width : 2 * width] = grads[rows, columns]
            first[block, :, 2 * width :] = stats[rows, :]


def mixing_kernel(cotangent, saved, combine, out):
    mixing = dot_last(saved[...], cotangent[...])
    weights = combine[...]
    out[...] = weights * (mixing - jnp.sum(weights * mixing, axis=0, keepdims=True))


def owner_kernel(groups, first, in_left, out_right, second, inputs_out, lows_out, stats_out):
    ring = first.shape[0] // groups
    owned, rank, width = in_left.shape
    inputs, grads, stats_rows = [], [], []
    for group in range(groups):
        rows = slice(group * ring, (group + 1) * ring)
        stats = first[rows, :, 2 * width :].astype(jnp.float32)
        peaks = stats[:, :, 0:1] + stats[:, :, 1:2]
        totals = stats[:, :, 2:3] + stats[:, :, 3:4]
        peak = jnp.max(peaks, axis=0)
        scale = jnp.exp(peaks - peak[None])
        total = jnp.sum(scale * totals, axis=0)
        scale = scale / total[None]
        inputs.append(jnp.sum(first[rows, :, :width].astype(jnp.float32) * scale, axis=0))
        grads.append(jnp.sum(first[rows, :, width : 2 * width].astype(jnp.float32), axis=0))
        stats_rows.append(in_lanes([*halves(peak), *halves(total)], (owned, STATS)))
    inputs, grads = jnp.concatenate(inputs, axis=0), jnp.concatenate(grads, axis=0)
    inputs_out[...] = inputs
    stats_out[...] = jnp.concatenate(stats_rows, axis=0)
    inputs_low, grads_low = inputs.astype(jnp.bfloat16), grads.astype(jnp.bfloat16)
    lows_out[0] = inputs_low
    lows_out[1] = grads_low
    up = dot_last(inputs_low, in_left[...].reshape(owned * rank, width))
    back = dot_last(grads_low, out_right[...].reshape(owned * rank, width))
    ranks = [*halves(from_own_block(up, owned)), *halves(from_own_block(back, owned))]
    ranks = jnp.concatenate(ranks, axis=1).astype(jnp.bfloat16)
    block = jnp.concatenate([inputs_low, grads_low, ranks], axis=1)
    for place in range(second.shape[0]):
        second[place] = block


def hidden_kernel(
    groups, second, base_in, base_out, in_right, out_left, third, pair_out, ranks_out
):
    members, rank, hidden = in_right.shape
    rows = second.shape[1]
    owned = rows // groups
    places = members // owned
    width = base_in.shape[1] // groups
    ring = third.shape[0] // groups
    group = lax.axis_index("dp")

    def gathered(columns):
        taken = [
            second[pl.ds(half * ring + group * places, places), :, columns].astype(jnp.float32)
            for half in range(groups)
        ]
        return [part.reshape(places * rows, part.shape[2]) for part in taken]

    def low_rank(value, table):
        value = value.astype(jnp.float32)
        taken = []
        for place in range(places):
            own = own_block(value[place * rows : (place + 1) * rows], owned)
            part = table[place * owned : (place + 1) * owned].reshape(owned * rank, hidden)
            taken.append(dot_plain(own, part))
        return jnp.concatenate(taken, axis=0)

    def to_rank(value, table):
        taken = []
        for place in range(places):
            part = table[place * owned : (place + 1) * owned].reshape(owned * rank, hidden)
            wide = dot_last(value[place * rows : (place + 1) * rows].astype(jnp.bfloat16), part)
            taken.append(from_own_block(wide, owned))
        return jnp.concatenate(taken, axis=0)

    ranks = functools.reduce(jnp.add, gathered(slice(2 * width, 2 * width + 4 * rank)))
    up = (ranks[:, :rank] + ranks[:, rank : 2 * rank]).astype(jnp.bfloat16)
    back = (ranks[:, 2 * rank : 3 * rank] + ranks[:, 3 * rank :]).astype(jnp.bfloat16)
    preact = low_rank(up, in_right)
    for half, part in enumerate(gathered(slice(0, width))):
        columns = slice(half * width, (half + 1) * width)
        preact = preact + dot_last(part.astype(jnp.bfloat16), base_in[:, columns])
    hidden_grad = low_rank(back, out_left)
    for half, part in enumerate(gathered(slice(width, 2 * width))):
        columns = slice(half * width, (half + 1) * width)
        hidden_grad = hidden_grad + dot_last(part.astype(jnp.bfloat16), base_out[:, columns])
    root = 0.7978845608028654
    bent = jnp.tanh(root * (preact + 0.044715 * (preact * preact * preact)))
    hidden_value = 0.5 * preact * (1.0 + bent)
    slope = 0.5 * (1.0 + bent) + 0.5 * preact * (1.0 - bent * bent) * (
        root * (1.0 + 3.0 * 0.044715 * (preact * preact))
    )
    hidden_low = hidden_value.astype(jnp.bfloat16).astype(jnp.float32)
    preact_grad = (hidden_grad * slope).astype(jnp.bfloat16).astype(jnp.float32)
    pair_out[0] = preact_grad
    pair_out[1] = hidden_low
    ranks_out[0] = up.astype(jnp.float32)
    ranks_out[1] = back.astype(jnp.float32)
    slot_term = dot_plain(preact_grad.astype(jnp.bfloat16), base_in[...]).astype(jnp.bfloat16)
    down = to_rank(preact_grad, in_right)
    value = to_rank(hidden_low, out_left)
    ranks = jnp.concatenate([down, value], axis=1).astype(jnp.bfloat16)
    third[...] = jnp.zeros(third.shape, jnp.bfloat16)
    for half in range(groups):
        columns = slice(half * width, (half + 1) * width)
        for place in range(places):
            taken = slice(place * rows, (place + 1) * rows)
            block = half * ring + group * places + place
            third[block, :, :width] = slot_term[taken, columns]
            third[block, :, width:] = ranks[taken]


def outer_kernel(owned, left_rows, right_rows, *outs):
    rows = left_rows.shape[1] // (outs[0].shape[0] // owned)
    for number, out in enumerate(outs):
        for place in range(out.shape[0] // owned):
            taken = slice(place * rows, (place + 1) * rows)
            own = own_block(left_rows[number, taken], owned)
            product = dot_first(own, right_rows[number, taken].astype(jnp.bfloat16))
            out[place * owned : (place + 1) * owned] = product.astype(jnp.bfloat16).reshape(
                (owned,) + out.shape[1:]
            )


def finish_kernel(groups, ring, third, in_left, inputs, stats, fourth, ranks_out):
    owned, rank, width = in_left.shape
    members = ring // groups
    sender = lax.axis_index("seq") // members
    summed = jnp.sum(third[pl.ds(sender * ring, ring)].astype(jnp.float32), axis=0)
    ranks = summed[:, width:].astype(jnp.bfloat16).astype(jnp.float32)
    ranks_out[0] = ranks[:, :rank]
    ranks_out[1] = ranks[:, rank:]
    down = own_block(ranks[:, :rank], owned)
    grads = summed[:, :width] + dot_plain(down, in_left[...].reshape(owned * rank, width))
    grads = grads.astype(jnp.bfloat16).astype(jnp.float32)
    high, low = halves(jnp.sum(grads * inputs[...], axis=1, keepdims=True))
    lane = lax.broadcasted_iota(jnp.int32, stats.shape, 1)
    tail = jnp.where(lane == 4, high, jnp.where(lane == 5, low, stats[...]))
    block = jnp.concatenate([grads, tail], axis=1).astype(jnp.bfloat16)
    for group in range(groups):
        rows = block[group * owned : (group + 1) * owned]
        for place in range(ring):
            fourth[group * ring + place] = rows


def tokens_kernel(groups, fourth, tokens, router, logits, mixing, out):
    blocks, owned, _ = fourth.shape
    ring = blocks // groups
    width = tokens.shape[1] // groups

    def rows(half, columns):
        taken = [
            fourth[half * ring + place, :, columns].astype(jnp.float32) for place in range(ring)
        ]
        return jnp.concatenate(taken, axis=0)

    grads = jnp.concatenate([rows(half, slice(0, width)) for half in range(groups)], axis=1)
    grads = grads.astype(jnp.bfloat16)
    stats = [rows(half, slice(width, width + STATS)) for half in range(groups)]
    peak = stats[0][:, 0:1] + stats[0][:, 1:2]
    total = stats[0][:, 2:3] + stats[0][:, 3:4]
    shift = functools.reduce(jnp.add, [part[:, 4:5] + part[:, 5:6] for part in stats])
    dispatch = jnp.exp(logits[...] - peak) / total
    weight_grad = dot_last(grads, tokens[...])
    logit_grad = dispatch * (weight_grad - shift) + mixing[...]
    left = jnp.concatenate([dispatch, logit_grad], axis=0).astype(jnp.bfloat16)
    right = jnp.concatenate([grads, router[...]], axis=0)
    out[...] = dot_first(left, right).astype(jnp.bfloat16)


def call(kernel, outs, args, flops):
    size = sum(array.size * array.dtype.itemsize for array in args)
    size += sum(out.size * out.dtype.itemsize for out in outs)
    return pl.pallas_call(
        kernel,
        out_shape=outs,
        cost_estimate=pl.CostEstimate(flops=flops, bytes_accessed=size, transcendentals=0),
        compiler_params=pltpu.CompilerParams(vmem_limit_bytes=24 * 2**20),
    )(*args)


def array(dtype, *shape):
    return jax.ShapeDtypeStruct(shape, dtype)


def local(
    tokens,
    cotangent,
    router,
    slot_outputs,
    base_in,
    base_out,
    in_left,
    in_right,
    out_left,
    out_right,
):
    groups, ring = lax.axis_size("dp"), lax.axis_size("seq")
    devices = groups * ring
    _, count, width = tokens.shape
    slots = router.shape[1]
    owned, slice_width, rank = in_left.shape
    members, _, hidden = in_right.shape
    rows = groups * owned
    if slice_width % 128 or rows % 8 or members % owned:
        return local_plain(
            tokens,
            cotangent,
            router,
            slot_outputs,
            base_in,
            base_out,
            in_left,
            in_right,
            out_left,
            out_right,
        )
    low, full = jnp.bfloat16, jnp.float32
    image_rows, cot_rows, saved = tokens[0], cotangent[0], slot_outputs[0]
    router, base_in = router.T, base_in.T
    in_left, out_left = in_left.swapaxes(1, 2), out_left.swapaxes(1, 2)
    first, logits, combine = call(
        functools.partial(sums_kernel, owned, groups),
        [
            array(low, devices, owned, 2 * slice_width + STATS),
            array(full, slots, count),
            array(full, slots, count),
        ],
        [image_rows, cot_rows, router],
        6 * count * slots * width,
    )
    first = lax.all_to_all(first, BOTH, 0, 0, tiled=True)
    (mixing,) = call(
        mixing_kernel,
        [array(full, slots, count)],
        [cot_rows, saved, combine],
        2 * count * slots * width,
    )
    second, inputs, lows, stats = call(
        functools.partial(owner_kernel, groups),
        [
            array(low, devices, rows, 2 * slice_width + 4 * rank),
            array(full, rows, slice_width),
            array(low, 2, rows, slice_width),
            array(full, rows, STATS),
        ],
        [first, in_left, out_right],
        4 * rows * owned * rank * slice_width,
    )
    second = lax.all_to_all(second, BOTH, 0, 0, tiled=True)
    total_rows = groups * members
    third, pair, ranks = call(
        functools.partial(hidden_kernel, groups),
        [
            array(low, devices, rows, slice_width + 2 * rank),
            array(full, 2, total_rows, hidden),
            array(full, 2, total_rows, rank),
        ],
        [second, base_in, base_out, in_right, out_left],
        6 * total_rows * hidden * (width + owned * rank),
    )
    third = lax.all_to_all(third, BOTH, 0, 0, tiled=True)
    grad_in_right, grad_out_left = call(
        functools.partial(outer_kernel, owned),
        [array(low, members, rank, hidden)] * 2,
        [ranks, pair],
        4 * members * rank * hidden * rows,
    )
    fourth, ranks = call(
        functools.partial(finish_kernel, groups, ring),
        [array(low, devices, owned, slice_width + STATS), array(full, 2, rows, rank)],
        [third, in_left, inputs, stats],
        2 * rows * owned * rank * slice_width,
    )
    fourth = lax.all_to_all(fourth, BOTH, 0, 0, tiled=True)
    grad_in_left, grad_out_right = call(
        functools.partial(outer_kernel, owned),
        [array(low, owned, rank, slice_width)] * 2,
        [ranks, lows],
        4 * owned * rank * slice_width * rows,
    )
    (token_grad,) = call(
        functools.partial(tokens_kernel, groups),
        [array(low, count, width)],
        [fourth, image_rows, router, logits, mixing],
        6 * count * slots * width,
    )
    return (
        token_grad[None],
        grad_in_left.swapaxes(1, 2),
        grad_in_right,
        grad_out_left.swapaxes(1, 2),
        grad_out_right,
    )


def solution(mesh):
    in_specs = (
        P("dp", "seq", None),
        P("dp", "seq", None),
        P(),
        P("dp", None, None),
        P(None, "seq"),
        P("seq", None),
        P("seq", "dp", None),
        P("dp", None, "seq"),
        P("dp", "seq", None),
        P("seq", None, "dp"),
    )
    out_specs = (
        P("dp", "seq", None),
        P("seq", "dp", None),
        P("dp", None, "seq"),
        P("dp", "seq", None),
        P("seq", None, "dp"),
    )
    return jax.shard_map(local, mesh=mesh, in_specs=in_specs, out_specs=out_specs, check_vma=False)
```

```python
import functools

import jax
import jax.numpy as jnp
from jax import lax
from jax.experimental import pallas as pl
from jax.experimental.pallas import tpu as pltpu
from jax.sharding import PartitionSpec as P

BOTH = ("dp", "seq")
STATS = 128


def gelu_backward(preact, upstream):
    return jax.vjp(jax.nn.gelu, preact)[1](upstream)[0]


def dot_first(left, right):
    return lax.dot_general(
        left, right, (((0,), (0,)), ((), ())), preferred_element_type=jnp.float32
    )


def dot_last(left, right):
    return lax.dot_general(
        left, right, (((1,), (1,)), ((), ())), preferred_element_type=jnp.float32
    )


def split(value):
    high = lax.reduce_precision(value, 8, 7)
    low = lax.reduce_precision(value - high, 8, 7)
    return high.astype(jnp.bfloat16), low.astype(jnp.bfloat16)


def joined(high, low):
    return high.astype(jnp.float32) + low.astype(jnp.float32)


def exchange(blocks):
    flat = blocks.reshape((-1,) + blocks.shape[2:])
    return lax.all_to_all(flat, BOTH, 0, 0, tiled=True).reshape(blocks.shape)


def local_plain(
    tokens,
    cotangent,
    router,
    slot_outputs,
    base_in,
    base_out,
    in_left,
    in_right,
    out_left,
    out_right,
):
    groups, ring = lax.axis_size("dp"), lax.axis_size("seq")
    image_rows = tokens[0]
    cot_rows = cotangent[0]
    saved_outputs = slot_outputs[0]
    width = image_rows.shape[1]
    slots = router.shape[1]
    owned, slice_width, rank = in_left.shape
    members = in_right.shape[0]
    places = members // owned
    group, place = lax.axis_index("dp"), lax.axis_index("seq")

    logits = jnp.dot(image_rows, router, preferred_element_type=jnp.float32)
    peak_high, peak_low = split(jnp.max(logits, axis=0))
    near = jnp.exp(logits - joined(peak_high, peak_low))
    total_high, total_low = split(jnp.sum(near, axis=0))
    combine = jax.nn.softmax(logits, axis=1)
    sums = jnp.stack(
        [
            dot_first(near.astype(jnp.bfloat16), image_rows),
            dot_first(combine.astype(jnp.bfloat16), cot_rows),
        ],
        axis=1,
    ).astype(jnp.bfloat16)
    sums = sums.reshape(ring, owned, 2, groups, slice_width).transpose(3, 0, 1, 2, 4)
    sums = sums.reshape(groups, ring, owned, 2 * slice_width)
    stats = jnp.stack([peak_high, peak_low, total_high, total_low], axis=1)
    stats = jnp.pad(stats, ((0, 0), (0, STATS - 4))).reshape(1, ring, owned, STATS)
    stats = jnp.broadcast_to(stats, (groups, ring, owned, STATS))
    first = exchange(jnp.concatenate([sums, stats], axis=3))

    tail = 2 * slice_width
    peaks = joined(first[..., tail], first[..., tail + 1])
    totals = joined(first[..., tail + 2], first[..., tail + 3])
    peak = jnp.max(peaks, axis=1)
    near_scale = jnp.exp(peaks - peak[:, None])
    total = jnp.sum(near_scale * totals, axis=1)
    near_scale = near_scale / total[:, None]
    parts = first[..., :tail].astype(jnp.float32)
    slot_inputs = jnp.sum(parts[..., :slice_width] * near_scale[..., None], axis=1)
    inputs_own = slot_inputs.astype(jnp.bfloat16)
    grads_own = jnp.sum(parts[..., slice_width:], axis=1).astype(jnp.bfloat16)
    up_part = jnp.einsum("gjd,jdr->gjr", inputs_own, in_left, preferred_element_type=jnp.float32)
    back_part = jnp.einsum("gjd,jrd->gjr", grads_own, out_right, preferred_element_type=jnp.float32)
    second = jnp.concatenate(
        [inputs_own, grads_own, *split(up_part), *split(back_part)], axis=2
    )
    second = exchange(jnp.broadcast_to(second, (groups, ring) + second.shape))
    second = lax.dynamic_slice_in_dim(second, group * places, places, 1)

    def gathered(start):
        piece = second[..., start : start + slice_width]
        return piece.transpose(2, 1, 3, 0, 4).reshape(groups * members, width)

    def ranks(start):
        piece = joined(
            second[..., start : start + rank], second[..., start + rank : start + 2 * rank]
        )
        piece = jnp.sum(piece, axis=0).transpose(1, 0, 2, 3)
        return piece.reshape(groups, members, rank).astype(jnp.bfloat16)

    inputs_low, grads_low = gathered(0), gathered(slice_width)
    up_low, back_low = ranks(tail), ranks(tail + 2 * rank)
    hidden = base_in.shape[1]
    preact = jnp.dot(inputs_low, base_in, preferred_element_type=jnp.float32).reshape(
        groups, members, hidden
    ) + jnp.einsum("gjr,jrf->gjf", up_low, in_right, preferred_element_type=jnp.float32)
    hidden_low = jax.nn.gelu(preact).astype(jnp.bfloat16)
    hidden_grad = dot_last(grads_low, base_out).reshape(groups, members, hidden) + jnp.einsum(
        "gjr,jfr->gjf", back_low, out_left, preferred_element_type=jnp.float32
    )
    preact_grad = gelu_backward(preact, hidden_grad).astype(jnp.bfloat16)
    slot_term = dot_last(preact_grad.reshape(groups * members, hidden), base_in)
    down_term = jnp.einsum(
        "gjf,jrf->gjr", preact_grad, in_right, preferred_element_type=jnp.float32
    )
    value_term = jnp.einsum(
        "gjf,jfr->gjr", hidden_low, out_left, preferred_element_type=jnp.float32
    )
    slot_term = slot_term.astype(jnp.bfloat16).reshape(groups, places, owned, groups, slice_width)
    slot_term = slot_term.transpose(3, 1, 0, 2, 4)
    rank_term = jnp.concatenate([down_term, value_term], axis=2).astype(jnp.bfloat16)
    rank_term = rank_term.reshape(groups, places, owned, 2 * rank).transpose(1, 0, 2, 3)
    rank_term = jnp.broadcast_to(rank_term, (groups,) + rank_term.shape)
    third = jnp.concatenate([slot_term, rank_term], axis=4)
    third = lax.dynamic_update_slice_in_dim(
        jnp.zeros((groups, ring) + third.shape[2:], jnp.bfloat16), third, group * places, 1
    )
    third = exchange(third)
    third = lax.dynamic_index_in_dim(third, place // places, 0, keepdims=False)
    third = jnp.sum(third.astype(jnp.float32), axis=0)
    down_own = third[..., slice_width : slice_width + rank].astype(jnp.bfloat16)
    value_own = third[..., slice_width + rank :].astype(jnp.bfloat16)
    slot_grads_own = (
        third[..., :slice_width]
        + jnp.einsum("gjr,jdr->gjd", down_own, in_left, preferred_element_type=jnp.float32)
    ).astype(jnp.bfloat16)
    shift_part = jnp.sum(slot_grads_own.astype(jnp.float32) * slot_inputs, axis=2)
    stats = jnp.stack([*split(peak), *split(total), *split(shift_part)], axis=2)
    stats = jnp.pad(stats, ((0, 0), (0, 0), (0, STATS - 6)))
    fourth = jnp.concatenate([slot_grads_own, stats], axis=2)[:, None]
    fourth = exchange(jnp.broadcast_to(fourth, (groups, ring) + fourth.shape[2:]))
    slot_grads = fourth[..., :slice_width].transpose(1, 2, 0, 3).reshape(slots, width)
    stats = fourth[..., slice_width:].astype(jnp.float32).reshape(groups, slots, STATS)
    slot_peak = stats[0, :, 0] + stats[0, :, 1]
    slot_total = stats[0, :, 2] + stats[0, :, 3]
    shift_back = jnp.sum(stats[:, :, 4] + stats[:, :, 5], axis=0)

    dispatch = jnp.exp(logits - slot_peak) / slot_total
    dispatch_low = dispatch.astype(jnp.bfloat16)
    weight_grad = dot_last(image_rows, slot_grads)
    dispatch_logit = dispatch * (weight_grad - shift_back)
    mixing_grad = dot_last(cot_rows, saved_outputs)
    combine_logit = combine * (mixing_grad - jnp.sum(combine * mixing_grad, axis=1, keepdims=True))
    logit_grad = (dispatch_logit + combine_logit).astype(jnp.bfloat16)
    token_grad = (
        jnp.dot(dispatch_low, slot_grads, preferred_element_type=jnp.float32)
        + dot_last(logit_grad, router)
    ).astype(jnp.bfloat16)
    grad_in_right = jnp.einsum(
        "gjr,gjf->jrf", up_low, preact_grad, preferred_element_type=jnp.float32
    ).astype(jnp.bfloat16)
    grad_out_left = jnp.einsum(
        "gjf,gjr->jfr", hidden_low, back_low, preferred_element_type=jnp.float32
    ).astype(jnp.bfloat16)
    grad_in_left = jnp.einsum(
        "gjd,gjr->jdr", inputs_own, down_own, preferred_element_type=jnp.float32
    ).astype(jnp.bfloat16)
    grad_out_right = jnp.einsum(
        "gjr,gjd->jrd", value_own, grads_own, preferred_element_type=jnp.float32
    ).astype(jnp.bfloat16)
    return (token_grad[None], grad_in_left, grad_in_right, grad_out_left, grad_out_right)


def dot_plain(left, right):
    return jnp.dot(left, right, preferred_element_type=jnp.float32)


def halves(value):
    high = value.astype(jnp.bfloat16).astype(jnp.float32)
    low = (value - high).astype(jnp.bfloat16).astype(jnp.float32)
    return high, low


def in_lanes(columns, shape):
    lane = lax.broadcasted_iota(jnp.int32, shape, len(shape) - 1)
    out = jnp.zeros(shape, jnp.float32)
    for number, column in enumerate(columns):
        out = jnp.where(lane == number, column, out)
    return out


def own_block(value, owned):
    rows, rank = value.shape
    wide = jnp.concatenate([value] * owned, axis=1)
    shape = (rows, owned * rank)
    block = lax.broadcasted_iota(jnp.int32, shape, 1) // rank
    expert = lax.broadcasted_iota(jnp.int32, shape, 0) % owned
    return jnp.where(block == expert, wide, 0.0).astype(jnp.bfloat16)


def from_own_block(value, owned):
    rows, wide = value.shape
    rank = wide // owned
    block = lax.broadcasted_iota(jnp.int32, value.shape, 1) // rank
    expert = lax.broadcasted_iota(jnp.int32, value.shape, 0) % owned
    kept = jnp.where(block == expert, value, 0.0)
    out = kept[:, :rank]
    for number in range(1, owned):
        out = out + kept[:, number * rank : (number + 1) * rank]
    return out


def sums_kernel(
    owned,
    groups,
    tokens_far,
    cotangent_far,
    router_far,
    first,
    logits_out,
    combine_out,
    tokens,
    cotangent,
    router,
    arrived,
):
    ring = first.shape[0] // groups
    copies = [
        pltpu.make_async_copy(far, near, arrived.at[number])
        for number, (far, near) in enumerate(
            [(router_far, router), (tokens_far, tokens), (cotangent_far, cotangent)]
        )
    ]
    for copy in copies:
        copy.start()
    copies[0].wait()
    copies[1].wait()
    image_rows = tokens[...]
    logits = dot_last(router[...], image_rows)
    high, low = halves(jnp.max(logits, axis=1, keepdims=True))
    near = jnp.exp(logits - (high + low))
    total_high, total_low = halves(jnp.sum(near, axis=1, keepdims=True))
    spread = jnp.exp(logits - jnp.max(logits, axis=0, keepdims=True))
    combine = spread / jnp.sum(spread, axis=0, keepdims=True)
    logits_out[...] = logits
    combine_out[...] = combine
    stats = in_lanes([high, low, total_high, total_low], (logits.shape[0], STATS))
    stats = stats.astype(jnp.bfloat16)
    inputs = dot_plain(near.astype(jnp.bfloat16), image_rows).astype(jnp.bfloat16)
    copies[2].wait()
    grads = dot_plain(combine.astype(jnp.bfloat16), cotangent[...]).astype(jnp.bfloat16)
    width = inputs.shape[1] // groups
    for group in range(groups):
        columns = slice(group * width, (group + 1) * width)
        for place in range(ring):
            rows = slice(place * owned, (place + 1) * owned)
            block = group * ring + place
            first[block, :, :width] = inputs[rows, columns]
            first[block, :, width : 2 * width] = grads[rows, columns]
            first[block, :, 2 * width :] = stats[rows, :]


def mixing_kernel(cotangent, saved, combine, out):
    mixing = dot_last(saved[...], cotangent[...])
    weights = combine[...]
    out[...] = weights * (mixing - jnp.sum(weights * mixing, axis=0, keepdims=True))


def owner_kernel(groups, first, in_left, out_right, second, inputs_out, lows_out, stats_out):
    ring = first.shape[0] // groups
    owned, rank, width = in_left.shape
    inputs, grads, stats_rows = [], [], []
    for group in range(groups):
        rows = slice(group * ring, (group + 1) * ring)
        stats = first[rows, :, 2 * width :].astype(jnp.float32)
        peaks = stats[:, :, 0:1] + stats[:, :, 1:2]
        totals = stats[:, :, 2:3] + stats[:, :, 3:4]
        peak = jnp.max(peaks, axis=0)
        scale = jnp.exp(peaks - peak[None])
        total = jnp.sum(scale * totals, axis=0)
        scale = scale / total[None]
        inputs.append(jnp.sum(first[rows, :, :width].astype(jnp.float32) * scale, axis=0))
        grads.append(jnp.sum(first[rows, :, width : 2 * width].astype(jnp.float32), axis=0))
        stats_rows.append(in_lanes([*halves(peak), *halves(total)], (owned, STATS)))
    inputs, grads = jnp.concatenate(inputs, axis=0), jnp.concatenate(grads, axis=0)
    inputs_out[...] = inputs
    stats_out[...] = jnp.concatenate(stats_rows, axis=0)
    inputs_low, grads_low = inputs.astype(jnp.bfloat16), grads.astype(jnp.bfloat16)
    lows_out[0] = inputs_low
    lows_out[1] = grads_low
    up = dot_last(inputs_low, in_left[...].reshape(owned * rank, width))
    back = dot_last(grads_low, out_right[...].reshape(owned * rank, width))
    ranks = [*halves(from_own_block(up, owned)), *halves(from_own_block(back, owned))]
    ranks = jnp.concatenate(ranks, axis=1).astype(jnp.bfloat16)
    block = jnp.concatenate([inputs_low, grads_low, ranks], axis=1)
    second[...] = block


def pack_kernel(groups, own, beside, across, out):
    places = out.shape[0]
    group = lax.axis_index("dp")
    here = group == lax.axis_index("seq") // places
    near = jnp.where(here, own[...], beside[...])
    far = jnp.where(here, beside[...], across[...])
    first, last = jnp.where(group == 0, near, far), jnp.where(group == 0, far, near)
    for place in range(places):
        out[place, 0] = first
        out[place, 1] = last


def hidden_kernel(
    groups,
    second,
    base_in,
    base_out_far,
    in_right,
    out_left,
    third,
    pair_out,
    ranks_out,
    base_out,
    arrived,
):
    copy = pltpu.make_async_copy(base_out_far, base_out, arrived)
    copy.start()
    members, rank, hidden = in_right.shape
    rows = second.shape[2]
    owned = rows // groups
    places = members // owned
    width = base_in.shape[1] // groups
    ring = third.shape[0] // groups
    group = lax.axis_index("dp")

    def gathered(columns):
        taken = [
            second[:, half, :, columns].astype(jnp.float32)
            for half in range(groups)
        ]
        return [part.reshape(places * rows, part.shape[2]) for part in taken]

    def low_rank(value, table):
        value = value.astype(jnp.float32)
        taken = []
        for place in range(places):
            own = own_block(value[place * rows : (place + 1) * rows], owned)
            part = table[place * owned : (place + 1) * owned].reshape(owned * rank, hidden)
            taken.append(dot_plain(own, part))
        return jnp.concatenate(taken, axis=0)

    def to_rank(value, table):
        taken = []
        for place in range(places):
            part = table[place * owned : (place + 1) * owned].reshape(owned * rank, hidden)
            wide = dot_last(value[place * rows : (place + 1) * rows].astype(jnp.bfloat16), part)
            taken.append(from_own_block(wide, owned))
        return jnp.concatenate(taken, axis=0)

    ranks = functools.reduce(jnp.add, gathered(slice(2 * width, 2 * width + 4 * rank)))
    up = (ranks[:, :rank] + ranks[:, rank : 2 * rank]).astype(jnp.bfloat16)
    back = (ranks[:, 2 * rank : 3 * rank] + ranks[:, 3 * rank :]).astype(jnp.bfloat16)
    preact = low_rank(up, in_right)
    for half, part in enumerate(gathered(slice(0, width))):
        columns = slice(half * width, (half + 1) * width)
        preact = preact + dot_last(part.astype(jnp.bfloat16), base_in[:, columns])
    hidden_grad = low_rank(back, out_left)
    copy.wait()
    for half, part in enumerate(gathered(slice(width, 2 * width))):
        columns = slice(half * width, (half + 1) * width)
        hidden_grad = hidden_grad + dot_last(part.astype(jnp.bfloat16), base_out[:, columns])
    root = 0.7978845608028654
    bent = jnp.tanh(root * (preact + 0.044715 * (preact * preact * preact)))
    hidden_value = 0.5 * preact * (1.0 + bent)
    slope = 0.5 * (1.0 + bent) + 0.5 * preact * (1.0 - bent * bent) * (
        root * (1.0 + 3.0 * 0.044715 * (preact * preact))
    )
    hidden_low = hidden_value.astype(jnp.bfloat16).astype(jnp.float32)
    preact_grad = (hidden_grad * slope).astype(jnp.bfloat16).astype(jnp.float32)
    pair_out[0] = preact_grad
    pair_out[1] = hidden_low
    ranks_out[0] = up.astype(jnp.float32)
    ranks_out[1] = back.astype(jnp.float32)
    slot_term = dot_plain(preact_grad.astype(jnp.bfloat16), base_in[...]).astype(jnp.bfloat16)
    down = to_rank(preact_grad, in_right)
    value = to_rank(hidden_low, out_left)
    ranks = jnp.concatenate([down, value], axis=1).astype(jnp.bfloat16)
    third[...] = jnp.zeros(third.shape, jnp.bfloat16)
    for half in range(groups):
        columns = slice(half * width, (half + 1) * width)
        for place in range(places):
            taken = slice(place * rows, (place + 1) * rows)
            block = half * ring + group * places + place
            third[block, :, :width] = slot_term[taken, columns]
            third[block, :, width:] = ranks[taken]


def outer_kernel(owned, left_rows, right_rows, *outs):
    rows = left_rows.shape[1] // (outs[0].shape[0] // owned)
    for number, out in enumerate(outs):
        for place in range(out.shape[0] // owned):
            taken = slice(place * rows, (place + 1) * rows)
            own = own_block(left_rows[number, taken], owned)
            product = dot_first(own, right_rows[number, taken].astype(jnp.bfloat16))
            out[place * owned : (place + 1) * owned] = product.astype(jnp.bfloat16).reshape(
                (owned,) + out.shape[1:]
            )


def finish_kernel(groups, ring, third, in_left, inputs, stats, fourth, ranks_out):
    owned, rank, width = in_left.shape
    members = ring // groups
    sender = lax.axis_index("seq") // members
    summed = jnp.sum(third[pl.ds(sender * ring, ring)].astype(jnp.float32), axis=0)
    ranks = summed[:, width:].astype(jnp.bfloat16).astype(jnp.float32)
    ranks_out[0] = ranks[:, :rank]
    ranks_out[1] = ranks[:, rank:]
    down = own_block(ranks[:, :rank], owned)
    grads = summed[:, :width] + dot_plain(down, in_left[...].reshape(owned * rank, width))
    grads = grads.astype(jnp.bfloat16).astype(jnp.float32)
    high, low = halves(jnp.sum(grads * inputs[...], axis=1, keepdims=True))
    lane = lax.broadcasted_iota(jnp.int32, stats.shape, 1)
    tail = jnp.where(lane == 4, high, jnp.where(lane == 5, low, stats[...]))
    block = jnp.concatenate([grads, tail], axis=1).astype(jnp.bfloat16)
    for group in range(groups):
        rows = block[group * owned : (group + 1) * owned]
        for place in range(ring):
            fourth[group * ring + place] = rows


def tokens_kernel(groups, fourth, tokens, router, logits, mixing, out):
    blocks, owned, _ = fourth.shape
    ring = blocks // groups
    width = tokens.shape[1] // groups

    def rows(half, columns):
        taken = [
            fourth[half * ring + place, :, columns].astype(jnp.float32) for place in range(ring)
        ]
        return jnp.concatenate(taken, axis=0)

    grads = jnp.concatenate([rows(half, slice(0, width)) for half in range(groups)], axis=1)
    grads = grads.astype(jnp.bfloat16)
    stats = [rows(half, slice(width, width + STATS)) for half in range(groups)]
    peak = stats[0][:, 0:1] + stats[0][:, 1:2]
    total = stats[0][:, 2:3] + stats[0][:, 3:4]
    shift = functools.reduce(jnp.add, [part[:, 4:5] + part[:, 5:6] for part in stats])
    dispatch = jnp.exp(logits[...] - peak) / total
    weight_grad = dot_last(grads, tokens[...])
    logit_grad = dispatch * (weight_grad - shift) + mixing[...]
    left = jnp.concatenate([dispatch, logit_grad], axis=0).astype(jnp.bfloat16)
    right = jnp.concatenate([grads, router[...]], axis=0)
    out[...] = dot_first(left, right).astype(jnp.bfloat16)


def to_group(block, ring):
    places = ring // 2

    def device(group, half, place):
        return group * ring + half * places + place

    beside, across = [], []
    for place in range(places):
        for half in range(2):
            beside.append((device(half, half, place), device(half, 1 - half, place)))
            beside.append((device(1 - half, half, place), device(half, half, place)))
            across.append((device(1 - half, half, place), device(half, 1 - half, place)))
    beside = lax.ppermute(block, BOTH, beside)
    across = lax.ppermute(block, BOTH, across)
    (blocks,) = call(
        functools.partial(pack_kernel, 2),
        [array(block.dtype, places, 2, *block.shape)],
        [block, beside, across],
        0,
    )
    halves = [[half * places + place for place in range(places)] for half in range(2)]
    return lax.all_to_all(blocks, "seq", 0, 0, axis_index_groups=halves, tiled=True)


def call(kernel, outs, args, flops, far=(), scratch=()):
    size = sum(array.size * array.dtype.itemsize for array in args)
    size += sum(out.size * out.dtype.itemsize for out in outs)
    spaces = [pltpu.HBM if number in far else pltpu.VMEM for number in range(len(args))]
    return pl.pallas_call(
        kernel,
        out_shape=outs,
        in_specs=[pl.BlockSpec(memory_space=space) for space in spaces],
        out_specs=[pl.BlockSpec(memory_space=pltpu.VMEM) for _ in outs],
        scratch_shapes=scratch,
        cost_estimate=pl.CostEstimate(flops=flops, bytes_accessed=size, transcendentals=0),
        compiler_params=pltpu.CompilerParams(vmem_limit_bytes=24 * 2**20),
    )(*args)


def array(dtype, *shape):
    return jax.ShapeDtypeStruct(shape, dtype)


def local(
    tokens,
    cotangent,
    router,
    slot_outputs,
    base_in,
    base_out,
    in_left,
    in_right,
    out_left,
    out_right,
):
    groups, ring = lax.axis_size("dp"), lax.axis_size("seq")
    devices = groups * ring
    _, count, width = tokens.shape
    slots = router.shape[1]
    owned, slice_width, rank = in_left.shape
    members, _, hidden = in_right.shape
    rows = groups * owned
    if groups != 2 or ring % 2 or slice_width % 128 or rows % 8 or members % owned:
        return local_plain(
            tokens,
            cotangent,
            router,
            slot_outputs,
            base_in,
            base_out,
            in_left,
            in_right,
            out_left,
            out_right,
        )
    low, full = jnp.bfloat16, jnp.float32
    image_rows, cot_rows, saved = tokens[0], cotangent[0], slot_outputs[0]
    router, base_in = router.T, base_in.T
    in_left, out_left = in_left.swapaxes(1, 2), out_left.swapaxes(1, 2)
    first, logits, combine = call(
        functools.partial(sums_kernel, owned, groups),
        [
            array(low, devices, owned, 2 * slice_width + STATS),
            array(full, slots, count),
            array(full, slots, count),
        ],
        [image_rows, cot_rows, router],
        6 * count * slots * width,
        (0, 1, 2),
        [pltpu.VMEM((count, width), low)] * 2
        + [pltpu.VMEM((slots, width), low), pltpu.SemaphoreType.DMA((3,))],
    )
    first = lax.all_to_all(first, BOTH, 0, 0, tiled=True)
    (mixing,) = call(
        mixing_kernel,
        [array(full, slots, count)],
        [cot_rows, saved, combine],
        2 * count * slots * width,
    )
    second, inputs, lows, stats = call(
        functools.partial(owner_kernel, groups),
        [
            array(low, rows, 2 * slice_width + 4 * rank),
            array(full, rows, slice_width),
            array(low, 2, rows, slice_width),
            array(full, rows, STATS),
        ],
        [first, in_left, out_right],
        4 * rows * owned * rank * slice_width,
    )
    second = to_group(second, ring)
    total_rows = groups * members
    third, pair, ranks = call(
        functools.partial(hidden_kernel, groups),
        [
            array(low, devices, rows, slice_width + 2 * rank),
            array(full, 2, total_rows, hidden),
            array(full, 2, total_rows, rank),
        ],
        [second, base_in, base_out, in_right, out_left],
        6 * total_rows * hidden * (width + owned * rank),
        (2,),
        [pltpu.VMEM((hidden, width), low), pltpu.SemaphoreType.DMA],
    )
    third = lax.all_to_all(third, BOTH, 0, 0, tiled=True)
    grad_in_right, grad_out_left = call(
        functools.partial(outer_kernel, owned),
        [array(low, members, rank, hidden)] * 2,
        [ranks, pair],
        4 * members * rank * hidden * rows,
    )
    fourth, ranks = call(
        functools.partial(finish_kernel, groups, ring),
        [array(low, devices, owned, slice_width + STATS), array(full, 2, rows, rank)],
        [third, in_left, inputs, stats],
        2 * rows * owned * rank * slice_width,
    )
    fourth = lax.all_to_all(fourth, BOTH, 0, 0, tiled=True)
    grad_in_left, grad_out_right = call(
        functools.partial(outer_kernel, owned),
        [array(low, owned, rank, slice_width)] * 2,
        [ranks, lows],
        4 * owned * rank * slice_width * rows,
    )
    (token_grad,) = call(
        functools.partial(tokens_kernel, groups),
        [array(low, count, width)],
        [fourth, image_rows, router, logits, mixing],
        6 * count * slots * width,
    )
    return (
        token_grad[None],
        grad_in_left.swapaxes(1, 2),
        grad_in_right,
        grad_out_left.swapaxes(1, 2),
        grad_out_right,
    )


def solution(mesh):
    in_specs = (
        P("dp", "seq", None),
        P("dp", "seq", None),
        P(),
        P("dp", None, None),
        P(None, "seq"),
        P("seq", None),
        P("seq", "dp", None),
        P("dp", None, "seq"),
        P("dp", "seq", None),
        P("seq", None, "dp"),
    )
    out_specs = (
        P("dp", "seq", None),
        P("seq", "dp", None),
        P("dp", None, "seq"),
        P("dp", "seq", None),
        P("seq", None, "dp"),
    )
    return jax.shard_map(local, mesh=mesh, in_specs=in_specs, out_specs=out_specs, check_vma=False)
```

```python
import functools

import jax
import jax.numpy as jnp
from jax import lax
from jax.experimental import pallas as pl
from jax.experimental.pallas import tpu as pltpu
from jax.sharding import PartitionSpec as P

SEQ = ("half", "place")
BOTH = ("dp", *SEQ)
STATS = 128


def gelu_backward(preact, upstream):
    return jax.vjp(jax.nn.gelu, preact)[1](upstream)[0]


def dot_first(left, right):
    return lax.dot_general(
        left, right, (((0,), (0,)), ((), ())), preferred_element_type=jnp.float32
    )


def dot_last(left, right):
    return lax.dot_general(
        left, right, (((1,), (1,)), ((), ())), preferred_element_type=jnp.float32
    )


def split(value):
    high = lax.reduce_precision(value, 8, 7)
    low = lax.reduce_precision(value - high, 8, 7)
    return high.astype(jnp.bfloat16), low.astype(jnp.bfloat16)


def joined(high, low):
    return high.astype(jnp.float32) + low.astype(jnp.float32)


def exchange(blocks):
    flat = blocks.reshape((-1,) + blocks.shape[2:])
    return lax.all_to_all(flat, BOTH, 0, 0, tiled=True).reshape(blocks.shape)


def local_plain(
    tokens,
    cotangent,
    router,
    slot_outputs,
    base_in,
    base_out,
    in_left,
    in_right,
    out_left,
    out_right,
):
    groups, ring = lax.axis_size("dp"), lax.axis_size(SEQ)
    image_rows = tokens[0]
    cot_rows = cotangent[0]
    saved_outputs = slot_outputs[0]
    width = image_rows.shape[1]
    slots = router.shape[1]
    owned, slice_width, rank = in_left.shape
    members = in_right.shape[0]
    places = members // owned
    group, place = lax.axis_index("dp"), lax.axis_index(SEQ)

    logits = jnp.dot(image_rows, router, preferred_element_type=jnp.float32)
    peak_high, peak_low = split(jnp.max(logits, axis=0))
    near = jnp.exp(logits - joined(peak_high, peak_low))
    total_high, total_low = split(jnp.sum(near, axis=0))
    combine = jax.nn.softmax(logits, axis=1)
    sums = jnp.stack(
        [
            dot_first(near.astype(jnp.bfloat16), image_rows),
            dot_first(combine.astype(jnp.bfloat16), cot_rows),
        ],
        axis=1,
    ).astype(jnp.bfloat16)
    sums = sums.reshape(ring, owned, 2, groups, slice_width).transpose(3, 0, 1, 2, 4)
    sums = sums.reshape(groups, ring, owned, 2 * slice_width)
    stats = jnp.stack([peak_high, peak_low, total_high, total_low], axis=1)
    stats = jnp.pad(stats, ((0, 0), (0, STATS - 4))).reshape(1, ring, owned, STATS)
    stats = jnp.broadcast_to(stats, (groups, ring, owned, STATS))
    first = exchange(jnp.concatenate([sums, stats], axis=3))

    tail = 2 * slice_width
    peaks = joined(first[..., tail], first[..., tail + 1])
    totals = joined(first[..., tail + 2], first[..., tail + 3])
    peak = jnp.max(peaks, axis=1)
    near_scale = jnp.exp(peaks - peak[:, None])
    total = jnp.sum(near_scale * totals, axis=1)
    near_scale = near_scale / total[:, None]
    parts = first[..., :tail].astype(jnp.float32)
    slot_inputs = jnp.sum(parts[..., :slice_width] * near_scale[..., None], axis=1)
    inputs_own = slot_inputs.astype(jnp.bfloat16)
    grads_own = jnp.sum(parts[..., slice_width:], axis=1).astype(jnp.bfloat16)
    up_part = jnp.einsum("gjd,jdr->gjr", inputs_own, in_left, preferred_element_type=jnp.float32)
    back_part = jnp.einsum("gjd,jrd->gjr", grads_own, out_right, preferred_element_type=jnp.float32)
    second = jnp.concatenate(
        [inputs_own, grads_own, *split(up_part), *split(back_part)], axis=2
    )
    second = exchange(jnp.broadcast_to(second, (groups, ring) + second.shape))
    second = lax.dynamic_slice_in_dim(second, group * places, places, 1)

    def gathered(start):
        piece = second[..., start : start + slice_width]
        return piece.transpose(2, 1, 3, 0, 4).reshape(groups * members, width)

    def ranks(start):
        piece = joined(
            second[..., start : start + rank], second[..., start + rank : start + 2 * rank]
        )
        piece = jnp.sum(piece, axis=0).transpose(1, 0, 2, 3)
        return piece.reshape(groups, members, rank).astype(jnp.bfloat16)

    inputs_low, grads_low = gathered(0), gathered(slice_width)
    up_low, back_low = ranks(tail), ranks(tail + 2 * rank)
    hidden = base_in.shape[1]
    preact = jnp.dot(inputs_low, base_in, preferred_element_type=jnp.float32).reshape(
        groups, members, hidden
    ) + jnp.einsum("gjr,jrf->gjf", up_low, in_right, preferred_element_type=jnp.float32)
    hidden_low = jax.nn.gelu(preact).astype(jnp.bfloat16)
    hidden_grad = dot_last(grads_low, base_out).reshape(groups, members, hidden) + jnp.einsum(
        "gjr,jfr->gjf", back_low, out_left, preferred_element_type=jnp.float32
    )
    preact_grad = gelu_backward(preact, hidden_grad).astype(jnp.bfloat16)
    slot_term = dot_last(preact_grad.reshape(groups * members, hidden), base_in)
    down_term = jnp.einsum(
        "gjf,jrf->gjr", preact_grad, in_right, preferred_element_type=jnp.float32
    )
    value_term = jnp.einsum(
        "gjf,jfr->gjr", hidden_low, out_left, preferred_element_type=jnp.float32
    )
    slot_term = slot_term.astype(jnp.bfloat16).reshape(groups, places, owned, groups, slice_width)
    slot_term = slot_term.transpose(3, 1, 0, 2, 4)
    rank_term = jnp.concatenate([down_term, value_term], axis=2).astype(jnp.bfloat16)
    rank_term = rank_term.reshape(groups, places, owned, 2 * rank).transpose(1, 0, 2, 3)
    rank_term = jnp.broadcast_to(rank_term, (groups,) + rank_term.shape)
    third = jnp.concatenate([slot_term, rank_term], axis=4)
    third = lax.dynamic_update_slice_in_dim(
        jnp.zeros((groups, ring) + third.shape[2:], jnp.bfloat16), third, group * places, 1
    )
    third = exchange(third)
    third = lax.dynamic_index_in_dim(third, place // places, 0, keepdims=False)
    third = jnp.sum(third.astype(jnp.float32), axis=0)
    down_own = third[..., slice_width : slice_width + rank].astype(jnp.bfloat16)
    value_own = third[..., slice_width + rank :].astype(jnp.bfloat16)
    slot_grads_own = (
        third[..., :slice_width]
        + jnp.einsum("gjr,jdr->gjd", down_own, in_left, preferred_element_type=jnp.float32)
    ).astype(jnp.bfloat16)
    shift_part = jnp.sum(slot_grads_own.astype(jnp.float32) * slot_inputs, axis=2)
    stats = jnp.stack([*split(peak), *split(total), *split(shift_part)], axis=2)
    stats = jnp.pad(stats, ((0, 0), (0, 0), (0, STATS - 6)))
    fourth = jnp.concatenate([slot_grads_own, stats], axis=2)[:, None]
    fourth = exchange(jnp.broadcast_to(fourth, (groups, ring) + fourth.shape[2:]))
    slot_grads = fourth[..., :slice_width].transpose(1, 2, 0, 3).reshape(slots, width)
    stats = fourth[..., slice_width:].astype(jnp.float32).reshape(groups, slots, STATS)
    slot_peak = stats[0, :, 0] + stats[0, :, 1]
    slot_total = stats[0, :, 2] + stats[0, :, 3]
    shift_back = jnp.sum(stats[:, :, 4] + stats[:, :, 5], axis=0)

    dispatch = jnp.exp(logits - slot_peak) / slot_total
    dispatch_low = dispatch.astype(jnp.bfloat16)
    weight_grad = dot_last(image_rows, slot_grads)
    dispatch_logit = dispatch * (weight_grad - shift_back)
    mixing_grad = dot_last(cot_rows, saved_outputs)
    combine_logit = combine * (mixing_grad - jnp.sum(combine * mixing_grad, axis=1, keepdims=True))
    logit_grad = (dispatch_logit + combine_logit).astype(jnp.bfloat16)
    token_grad = (
        jnp.dot(dispatch_low, slot_grads, preferred_element_type=jnp.float32)
        + dot_last(logit_grad, router)
    ).astype(jnp.bfloat16)
    grad_in_right = jnp.einsum(
        "gjr,gjf->jrf", up_low, preact_grad, preferred_element_type=jnp.float32
    ).astype(jnp.bfloat16)
    grad_out_left = jnp.einsum(
        "gjf,gjr->jfr", hidden_low, back_low, preferred_element_type=jnp.float32
    ).astype(jnp.bfloat16)
    grad_in_left = jnp.einsum(
        "gjd,gjr->jdr", inputs_own, down_own, preferred_element_type=jnp.float32
    ).astype(jnp.bfloat16)
    grad_out_right = jnp.einsum(
        "gjr,gjd->jrd", value_own, grads_own, preferred_element_type=jnp.float32
    ).astype(jnp.bfloat16)
    return (token_grad[None], grad_in_left, grad_in_right, grad_out_left, grad_out_right)


def dot_plain(left, right):
    return jnp.dot(left, right, preferred_element_type=jnp.float32)


def halves(value):
    high = value.astype(jnp.bfloat16).astype(jnp.float32)
    low = (value - high).astype(jnp.bfloat16).astype(jnp.float32)
    return high, low


def in_lanes(columns, shape):
    lane = lax.broadcasted_iota(jnp.int32, shape, len(shape) - 1)
    out = jnp.zeros(shape, jnp.float32)
    for number, column in enumerate(columns):
        out = jnp.where(lane == number, column, out)
    return out


def own_block(value, owned):
    rows, rank = value.shape
    wide = jnp.concatenate([value] * owned, axis=1)
    shape = (rows, owned * rank)
    block = lax.broadcasted_iota(jnp.int32, shape, 1) // rank
    expert = lax.broadcasted_iota(jnp.int32, shape, 0) % owned
    return jnp.where(block == expert, wide, 0.0).astype(jnp.bfloat16)


def from_own_block(value, owned):
    rows, wide = value.shape
    rank = wide // owned
    block = lax.broadcasted_iota(jnp.int32, value.shape, 1) // rank
    expert = lax.broadcasted_iota(jnp.int32, value.shape, 0) % owned
    kept = jnp.where(block == expert, value, 0.0)
    out = kept[:, :rank]
    for number in range(1, owned):
        out = out + kept[:, number * rank : (number + 1) * rank]
    return out


def sums_kernel(
    owned,
    groups,
    tokens_far,
    cotangent_far,
    router_far,
    first,
    logits_out,
    combine_out,
    tokens,
    cotangent,
    router,
    arrived,
):
    ring = first.shape[0] // groups
    copies = [
        pltpu.make_async_copy(far, near, arrived.at[number])
        for number, (far, near) in enumerate(
            [(router_far, router), (tokens_far, tokens), (cotangent_far, cotangent)]
        )
    ]
    for copy in copies:
        copy.start()
    copies[0].wait()
    copies[1].wait()
    image_rows = tokens[...]
    logits = dot_last(router[...], image_rows)
    high, low = halves(jnp.max(logits, axis=1, keepdims=True))
    near = jnp.exp(logits - (high + low))
    total_high, total_low = halves(jnp.sum(near, axis=1, keepdims=True))
    spread = jnp.exp(logits - jnp.max(logits, axis=0, keepdims=True))
    combine = spread / jnp.sum(spread, axis=0, keepdims=True)
    logits_out[...] = logits
    combine_out[...] = combine
    stats = in_lanes([high, low, total_high, total_low], (logits.shape[0], STATS))
    stats = stats.astype(jnp.bfloat16)
    inputs = dot_plain(near.astype(jnp.bfloat16), image_rows).astype(jnp.bfloat16)
    copies[2].wait()
    grads = dot_plain(combine.astype(jnp.bfloat16), cotangent[...]).astype(jnp.bfloat16)
    width = inputs.shape[1] // groups
    for group in range(groups):
        columns = slice(group * width, (group + 1) * width)
        for place in range(ring):
            rows = slice(place * owned, (place + 1) * owned)
            block = group * ring + place
            first[block, :, :width] = inputs[rows, columns]
            first[block, :, width : 2 * width] = grads[rows, columns]
            first[block, :, 2 * width :] = stats[rows, :]


def mixing_kernel(cotangent, saved, combine, *rest):
    *_, out = rest
    mixing = dot_last(saved[...], cotangent[...])
    weights = combine[...]
    out[...] = weights * (mixing - jnp.sum(weights * mixing, axis=0, keepdims=True))


def owner_kernel(groups, first, in_left, out_right, second, inputs_out, lows_out, stats_out):
    ring = first.shape[0] // groups
    owned, rank, width = in_left.shape
    inputs, grads, stats_rows = [], [], []
    for group in range(groups):
        rows = slice(group * ring, (group + 1) * ring)
        stats = first[rows, :, 2 * width :].astype(jnp.float32)
        peaks = stats[:, :, 0:1] + stats[:, :, 1:2]
        totals = stats[:, :, 2:3] + stats[:, :, 3:4]
        peak = jnp.max(peaks, axis=0)
        scale = jnp.exp(peaks - peak[None])
        total = jnp.sum(scale * totals, axis=0)
        scale = scale / total[None]
        inputs.append(jnp.sum(first[rows, :, :width].astype(jnp.float32) * scale, axis=0))
        grads.append(jnp.sum(first[rows, :, width : 2 * width].astype(jnp.float32), axis=0))
        stats_rows.append(in_lanes([*halves(peak), *halves(total)], (owned, STATS)))
    inputs, grads = jnp.concatenate(inputs, axis=0), jnp.concatenate(grads, axis=0)
    inputs_out[...] = inputs
    stats_out[...] = jnp.concatenate(stats_rows, axis=0)
    inputs_low, grads_low = inputs.astype(jnp.bfloat16), grads.astype(jnp.bfloat16)
    lows_out[0] = inputs_low
    lows_out[1] = grads_low
    up = dot_last(inputs_low, in_left[...].reshape(owned * rank, width))
    back = dot_last(grads_low, out_right[...].reshape(owned * rank, width))
    ranks = [*halves(from_own_block(up, owned)), *halves(from_own_block(back, owned))]
    ranks = jnp.concatenate(ranks, axis=1).astype(jnp.bfloat16)
    block = jnp.concatenate([inputs_low, grads_low, ranks], axis=1)
    second[...] = block


def spread_kernel(block, out):
    for group in range(2):
        for half in range(2):
            out[group, half] = block[...]


def pack_kernel(blocks, out):
    group = lax.axis_index("dp")
    for number in range(2):
        block = blocks[2 * number + group]
        for place in range(out.shape[0]):
            out[place, number] = block


def hidden_kernel(
    groups,
    second,
    base_in,
    base_out,
    in_right,
    out_left,
    third,
    pair_out,
    ranks_out,
):
    members, rank, hidden = in_right.shape
    rows = second.shape[2]
    owned = rows // groups
    places = members // owned
    width = base_in.shape[1] // groups
    ring = third.shape[0] // groups
    group = lax.axis_index("dp")

    def gathered(columns):
        taken = [
            second[:, half, :, columns].astype(jnp.float32)
            for half in range(groups)
        ]
        return [part.reshape(places * rows, part.shape[2]) for part in taken]

    def low_rank(value, table):
        value = value.astype(jnp.float32)
        taken = []
        for place in range(places):
            own = own_block(value[place * rows : (place + 1) * rows], owned)
            part = table[place * owned : (place + 1) * owned].reshape(owned * rank, hidden)
            taken.append(dot_plain(own, part))
        return jnp.concatenate(taken, axis=0)

    def to_rank(value, table):
        taken = []
        for place in range(places):
            part = table[place * owned : (place + 1) * owned].reshape(owned * rank, hidden)
            wide = dot_last(value[place * rows : (place + 1) * rows].astype(jnp.bfloat16), part)
            taken.append(from_own_block(wide, owned))
        return jnp.concatenate(taken, axis=0)

    ranks = functools.reduce(jnp.add, gathered(slice(2 * width, 2 * width + 4 * rank)))
    up = (ranks[:, :rank] + ranks[:, rank : 2 * rank]).astype(jnp.bfloat16)
    back = (ranks[:, 2 * rank : 3 * rank] + ranks[:, 3 * rank :]).astype(jnp.bfloat16)
    preact = low_rank(up, in_right)
    for half, part in enumerate(gathered(slice(0, width))):
        columns = slice(half * width, (half + 1) * width)
        preact = preact + dot_last(part.astype(jnp.bfloat16), base_in[:, columns])
    hidden_grad = low_rank(back, out_left)
    for half, part in enumerate(gathered(slice(width, 2 * width))):
        columns = slice(half * width, (half + 1) * width)
        hidden_grad = hidden_grad + dot_last(part.astype(jnp.bfloat16), base_out[:, columns])
    root = 0.7978845608028654
    bent = jnp.tanh(root * (preact + 0.044715 * (preact * preact * preact)))
    hidden_value = 0.5 * preact * (1.0 + bent)
    slope = 0.5 * (1.0 + bent) + 0.5 * preact * (1.0 - bent * bent) * (
        root * (1.0 + 3.0 * 0.044715 * (preact * preact))
    )
    hidden_low = hidden_value.astype(jnp.bfloat16).astype(jnp.float32)
    preact_grad = (hidden_grad * slope).astype(jnp.bfloat16).astype(jnp.float32)
    pair_out[0] = preact_grad
    pair_out[1] = hidden_low
    ranks_out[0] = up.astype(jnp.float32)
    ranks_out[1] = back.astype(jnp.float32)
    slot_term = dot_plain(preact_grad.astype(jnp.bfloat16), base_in[...]).astype(jnp.bfloat16)
    down = to_rank(preact_grad, in_right)
    value = to_rank(hidden_low, out_left)
    ranks = jnp.concatenate([down, value], axis=1).astype(jnp.bfloat16)
    third[...] = jnp.zeros(third.shape, jnp.bfloat16)
    for half in range(groups):
        columns = slice(half * width, (half + 1) * width)
        for place in range(places):
            taken = slice(place * rows, (place + 1) * rows)
            block = half * ring + group * places + place
            third[block, :, :width] = slot_term[taken, columns]
            third[block, :, width:] = ranks[taken]


def outer_kernel(owned, left_rows, right_rows, *outs):
    rows = left_rows.shape[1] // (outs[0].shape[0] // owned)
    for number, out in enumerate(outs):
        for place in range(out.shape[0] // owned):
            taken = slice(place * rows, (place + 1) * rows)
            own = own_block(left_rows[number, taken], owned)
            product = dot_first(own, right_rows[number, taken].astype(jnp.bfloat16))
            out[place * owned : (place + 1) * owned] = product.astype(jnp.bfloat16).reshape(
                (owned,) + out.shape[1:]
            )


def finish_kernel(groups, ring, third, in_left, inputs, stats, fourth, ranks_out):
    owned, rank, width = in_left.shape
    sender = lax.axis_index("half")
    summed = jnp.sum(third[pl.ds(sender * ring, ring)].astype(jnp.float32), axis=0)
    ranks = summed[:, width:].astype(jnp.bfloat16).astype(jnp.float32)
    ranks_out[0] = ranks[:, :rank]
    ranks_out[1] = ranks[:, rank:]
    down = own_block(ranks[:, :rank], owned)
    grads = summed[:, :width] + dot_plain(down, in_left[...].reshape(owned * rank, width))
    grads = grads.astype(jnp.bfloat16).astype(jnp.float32)
    high, low = halves(jnp.sum(grads * inputs[...], axis=1, keepdims=True))
    lane = lax.broadcasted_iota(jnp.int32, stats.shape, 1)
    tail = jnp.where(lane == 4, high, jnp.where(lane == 5, low, stats[...]))
    block = jnp.concatenate([grads, tail], axis=1).astype(jnp.bfloat16)
    for group in range(groups):
        rows = block[group * owned : (group + 1) * owned]
        for place in range(ring):
            fourth[group * ring + place] = rows


def tokens_kernel(groups, fourth, tokens, router, logits, mixing, out):
    blocks, owned, _ = fourth.shape
    ring = blocks // groups
    width = tokens.shape[1] // groups

    def rows(half, columns):
        taken = [
            fourth[half * ring + place, :, columns].astype(jnp.float32) for place in range(ring)
        ]
        return jnp.concatenate(taken, axis=0)

    grads = jnp.concatenate([rows(half, slice(0, width)) for half in range(groups)], axis=1)
    grads = grads.astype(jnp.bfloat16)
    stats = [rows(half, slice(width, width + STATS)) for half in range(groups)]
    peak = stats[0][:, 0:1] + stats[0][:, 1:2]
    total = stats[0][:, 2:3] + stats[0][:, 3:4]
    shift = functools.reduce(jnp.add, [part[:, 4:5] + part[:, 5:6] for part in stats])
    dispatch = jnp.exp(logits[...] - peak) / total
    weight_grad = dot_last(grads, tokens[...])
    logit_grad = dispatch * (weight_grad - shift) + mixing[...]
    left = jnp.concatenate([dispatch, logit_grad], axis=0).astype(jnp.bfloat16)
    right = jnp.concatenate([grads, router[...]], axis=0)
    out[...] = dot_first(left, right).astype(jnp.bfloat16)


def to_group(block):
    places = lax.axis_size("place")
    (blocks,) = call(
        spread_kernel, [array(block.dtype, 2, 2, *block.shape)], [block], 0
    )
    blocks = lax.all_to_all(blocks.reshape(4, *block.shape), ("dp", "half"), 0, 0, tiled=True)
    (blocks,) = call(
        pack_kernel, [array(block.dtype, places, 2, *block.shape)], [blocks], 0
    )
    return lax.all_to_all(blocks, "place", 0, 0, tiled=True)


def call(kernel, outs, args, flops, far=(), scratch=(), grant=24):
    size = sum(array.size * array.dtype.itemsize for array in args)
    size += sum(out.size * out.dtype.itemsize for out in outs)
    spaces = [pltpu.HBM if number in far else pltpu.VMEM for number in range(len(args))]
    return pl.pallas_call(
        kernel,
        out_shape=outs,
        in_specs=[pl.BlockSpec(memory_space=space) for space in spaces],
        out_specs=[pl.BlockSpec(memory_space=pltpu.VMEM) for _ in outs],
        scratch_shapes=scratch,
        cost_estimate=pl.CostEstimate(flops=flops, bytes_accessed=size, transcendentals=0),
        compiler_params=pltpu.CompilerParams(vmem_limit_bytes=grant * 2**20),
    )(*args)


def array(dtype, *shape):
    return jax.ShapeDtypeStruct(shape, dtype)


def local(
    tokens,
    cotangent,
    router,
    slot_outputs,
    base_in,
    base_out,
    in_left,
    in_right,
    out_left,
    out_right,
):
    groups, ring = lax.axis_size("dp"), lax.axis_size(SEQ)
    devices = groups * ring
    _, count, width = tokens.shape
    slots = router.shape[1]
    owned, slice_width, rank = in_left.shape
    members, _, hidden = in_right.shape
    rows = groups * owned
    if groups != 2 or ring % 2 or slice_width % 128 or rows % 8 or members % owned:
        return local_plain(
            tokens,
            cotangent,
            router,
            slot_outputs,
            base_in,
            base_out,
            in_left,
            in_right,
            out_left,
            out_right,
        )
    low, full = jnp.bfloat16, jnp.float32
    image_rows, cot_rows, saved = tokens[0], cotangent[0], slot_outputs[0]
    router, base_in = router.T, base_in.T
    in_left, out_left = in_left.swapaxes(1, 2), out_left.swapaxes(1, 2)
    first, logits, combine = call(
        functools.partial(sums_kernel, owned, groups),
        [
            array(low, devices, owned, 2 * slice_width + STATS),
            array(full, slots, count),
            array(full, slots, count),
        ],
        [image_rows, cot_rows, router],
        6 * count * slots * width,
        (0, 1, 2),
        [pltpu.VMEM((count, width), low)] * 2
        + [pltpu.VMEM((slots, width), low), pltpu.SemaphoreType.DMA((3,))],
        60,
    )
    first = lax.all_to_all(first, BOTH, 0, 0, tiled=True)
    (mixing,) = call(
        mixing_kernel,
        [array(full, slots, count)],
        [cot_rows, saved, combine, out_right, base_out],
        2 * count * slots * width,
    )
    first, mixing = lax.optimization_barrier((first, mixing))
    second, inputs, lows, stats = call(
        functools.partial(owner_kernel, groups),
        [
            array(low, rows, 2 * slice_width + 4 * rank),
            array(full, rows, slice_width),
            array(low, 2, rows, slice_width),
            array(full, rows, STATS),
        ],
        [first, in_left, out_right],
        4 * rows * owned * rank * slice_width,
    )
    second = to_group(second)
    total_rows = groups * members
    third, pair, ranks = call(
        functools.partial(hidden_kernel, groups),
        [
            array(low, devices, rows, slice_width + 2 * rank),
            array(full, 2, total_rows, hidden),
            array(full, 2, total_rows, rank),
        ],
        [second, base_in, base_out, in_right, out_left],
        6 * total_rows * hidden * (width + owned * rank),
    )
    third = lax.all_to_all(third, BOTH, 0, 0, tiled=True)
    grad_in_right, grad_out_left = call(
        functools.partial(outer_kernel, owned),
        [array(low, members, rank, hidden)] * 2,
        [ranks, pair],
        4 * members * rank * hidden * rows,
    )
    fourth, ranks = call(
        functools.partial(finish_kernel, groups, ring),
        [array(low, devices, owned, slice_width + STATS), array(full, 2, rows, rank)],
        [third, in_left, inputs, stats],
        2 * rows * owned * rank * slice_width,
    )
    fourth = lax.all_to_all(fourth, BOTH, 0, 0, tiled=True)
    grad_in_left, grad_out_right = call(
        functools.partial(outer_kernel, owned),
        [array(low, owned, rank, slice_width)] * 2,
        [ranks, lows],
        4 * owned * rank * slice_width * rows,
    )
    (token_grad,) = call(
        functools.partial(tokens_kernel, groups),
        [array(low, count, width)],
        [fourth, image_rows, router, logits, mixing],
        6 * count * slots * width,
    )
    return (
        token_grad[None],
        grad_in_left.swapaxes(1, 2),
        grad_in_right,
        grad_out_left.swapaxes(1, 2),
        grad_out_right,
    )


def solution(mesh):
    groups, ring = mesh.shape["dp"], mesh.shape["seq"]
    split = mesh.devices.reshape(groups, groups, ring // groups)
    mesh = jax.sharding.Mesh(split, BOTH)
    in_specs = (
        P("dp", SEQ, None),
        P("dp", SEQ, None),
        P(),
        P("dp", None, None),
        P(None, SEQ),
        P(SEQ, None),
        P(SEQ, "dp", None),
        P("dp", None, SEQ),
        P("dp", SEQ, None),
        P(SEQ, None, "dp"),
    )
    out_specs = (
        P("dp", SEQ, None),
        P(SEQ, "dp", None),
        P("dp", None, SEQ),
        P("dp", SEQ, None),
        P(SEQ, None, "dp"),
    )
    return jax.shard_map(local, mesh=mesh, in_specs=in_specs, out_specs=out_specs, check_vma=False)
```

```python
import functools

import jax
import jax.numpy as jnp
from jax import lax
from jax.experimental import pallas as pl
from jax.experimental.pallas import tpu as pltpu
from jax.sharding import PartitionSpec as P

SEQ = ("half", "place")
BOTH = ("dp", *SEQ)
STATS = 128


def gelu_backward(preact, upstream):
    return jax.vjp(jax.nn.gelu, preact)[1](upstream)[0]


def dot_first(left, right):
    return lax.dot_general(
        left, right, (((0,), (0,)), ((), ())), preferred_element_type=jnp.float32
    )


def dot_last(left, right):
    return lax.dot_general(
        left, right, (((1,), (1,)), ((), ())), preferred_element_type=jnp.float32
    )


def split(value):
    high = lax.reduce_precision(value, 8, 7)
    low = lax.reduce_precision(value - high, 8, 7)
    return high.astype(jnp.bfloat16), low.astype(jnp.bfloat16)


def joined(high, low):
    return high.astype(jnp.float32) + low.astype(jnp.float32)


def exchange(blocks):
    flat = blocks.reshape((-1,) + blocks.shape[2:])
    return lax.all_to_all(flat, BOTH, 0, 0, tiled=True).reshape(blocks.shape)


def local_plain(
    tokens,
    cotangent,
    router,
    slot_outputs,
    base_in,
    base_out,
    in_left,
    in_right,
    out_left,
    out_right,
):
    groups, ring = lax.axis_size("dp"), lax.axis_size(SEQ)
    image_rows = tokens[0]
    cot_rows = cotangent[0]
    saved_outputs = slot_outputs[0]
    width = image_rows.shape[1]
    slots = router.shape[1]
    owned, slice_width, rank = in_left.shape
    members = in_right.shape[0]
    places = members // owned
    group, place = lax.axis_index("dp"), lax.axis_index(SEQ)

    logits = jnp.dot(image_rows, router, preferred_element_type=jnp.float32)
    peak_high, peak_low = split(jnp.max(logits, axis=0))
    near = jnp.exp(logits - joined(peak_high, peak_low))
    total_high, total_low = split(jnp.sum(near, axis=0))
    combine = jax.nn.softmax(logits, axis=1)
    sums = jnp.stack(
        [
            dot_first(near.astype(jnp.bfloat16), image_rows),
            dot_first(combine.astype(jnp.bfloat16), cot_rows),
        ],
        axis=1,
    ).astype(jnp.bfloat16)
    sums = sums.reshape(ring, owned, 2, groups, slice_width).transpose(3, 0, 1, 2, 4)
    sums = sums.reshape(groups, ring, owned, 2 * slice_width)
    stats = jnp.stack([peak_high, peak_low, total_high, total_low], axis=1)
    stats = jnp.pad(stats, ((0, 0), (0, STATS - 4))).reshape(1, ring, owned, STATS)
    stats = jnp.broadcast_to(stats, (groups, ring, owned, STATS))
    first = exchange(jnp.concatenate([sums, stats], axis=3))

    tail = 2 * slice_width
    peaks = joined(first[..., tail], first[..., tail + 1])
    totals = joined(first[..., tail + 2], first[..., tail + 3])
    peak = jnp.max(peaks, axis=1)
    near_scale = jnp.exp(peaks - peak[:, None])
    total = jnp.sum(near_scale * totals, axis=1)
    near_scale = near_scale / total[:, None]
    parts = first[..., :tail].astype(jnp.float32)
    slot_inputs = jnp.sum(parts[..., :slice_width] * near_scale[..., None], axis=1)
    inputs_own = slot_inputs.astype(jnp.bfloat16)
    grads_own = jnp.sum(parts[..., slice_width:], axis=1).astype(jnp.bfloat16)
    up_part = jnp.einsum("gjd,jdr->gjr", inputs_own, in_left, preferred_element_type=jnp.float32)
    back_part = jnp.einsum("gjd,jrd->gjr", grads_own, out_right, preferred_element_type=jnp.float32)
    second = jnp.concatenate(
        [inputs_own, grads_own, *split(up_part), *split(back_part)], axis=2
    )
    second = exchange(jnp.broadcast_to(second, (groups, ring) + second.shape))
    second = lax.dynamic_slice_in_dim(second, group * places, places, 1)

    def gathered(start):
        piece = second[..., start : start + slice_width]
        return piece.transpose(2, 1, 3, 0, 4).reshape(groups * members, width)

    def ranks(start):
        piece = joined(
            second[..., start : start + rank], second[..., start + rank : start + 2 * rank]
        )
        piece = jnp.sum(piece, axis=0).transpose(1, 0, 2, 3)
        return piece.reshape(groups, members, rank).astype(jnp.bfloat16)

    inputs_low, grads_low = gathered(0), gathered(slice_width)
    up_low, back_low = ranks(tail), ranks(tail + 2 * rank)
    hidden = base_in.shape[1]
    preact = jnp.dot(inputs_low, base_in, preferred_element_type=jnp.float32).reshape(
        groups, members, hidden
    ) + jnp.einsum("gjr,jrf->gjf", up_low, in_right, preferred_element_type=jnp.float32)
    hidden_low = jax.nn.gelu(preact).astype(jnp.bfloat16)
    hidden_grad = dot_last(grads_low, base_out).reshape(groups, members, hidden) + jnp.einsum(
        "gjr,jfr->gjf", back_low, out_left, preferred_element_type=jnp.float32
    )
    preact_grad = gelu_backward(preact, hidden_grad).astype(jnp.bfloat16)
    slot_term = dot_last(preact_grad.reshape(groups * members, hidden), base_in)
    down_term = jnp.einsum(
        "gjf,jrf->gjr", preact_grad, in_right, preferred_element_type=jnp.float32
    )
    value_term = jnp.einsum(
        "gjf,jfr->gjr", hidden_low, out_left, preferred_element_type=jnp.float32
    )
    slot_term = slot_term.astype(jnp.bfloat16).reshape(groups, places, owned, groups, slice_width)
    slot_term = slot_term.transpose(3, 1, 0, 2, 4)
    rank_term = jnp.concatenate([down_term, value_term], axis=2).astype(jnp.bfloat16)
    rank_term = rank_term.reshape(groups, places, owned, 2 * rank).transpose(1, 0, 2, 3)
    rank_term = jnp.broadcast_to(rank_term, (groups,) + rank_term.shape)
    third = jnp.concatenate([slot_term, rank_term], axis=4)
    third = lax.dynamic_update_slice_in_dim(
        jnp.zeros((groups, ring) + third.shape[2:], jnp.bfloat16), third, group * places, 1
    )
    third = exchange(third)
    third = lax.dynamic_index_in_dim(third, place // places, 0, keepdims=False)
    third = jnp.sum(third.astype(jnp.float32), axis=0)
    down_own = third[..., slice_width : slice_width + rank].astype(jnp.bfloat16)
    value_own = third[..., slice_width + rank :].astype(jnp.bfloat16)
    slot_grads_own = (
        third[..., :slice_width]
        + jnp.einsum("gjr,jdr->gjd", down_own, in_left, preferred_element_type=jnp.float32)
    ).astype(jnp.bfloat16)
    shift_part = jnp.sum(slot_grads_own.astype(jnp.float32) * slot_inputs, axis=2)
    stats = jnp.stack([*split(peak), *split(total), *split(shift_part)], axis=2)
    stats = jnp.pad(stats, ((0, 0), (0, 0), (0, STATS - 6)))
    fourth = jnp.concatenate([slot_grads_own, stats], axis=2)[:, None]
    fourth = exchange(jnp.broadcast_to(fourth, (groups, ring) + fourth.shape[2:]))
    slot_grads = fourth[..., :slice_width].transpose(1, 2, 0, 3).reshape(slots, width)
    stats = fourth[..., slice_width:].astype(jnp.float32).reshape(groups, slots, STATS)
    slot_peak = stats[0, :, 0] + stats[0, :, 1]
    slot_total = stats[0, :, 2] + stats[0, :, 3]
    shift_back = jnp.sum(stats[:, :, 4] + stats[:, :, 5], axis=0)

    dispatch = jnp.exp(logits - slot_peak) / slot_total
    dispatch_low = dispatch.astype(jnp.bfloat16)
    weight_grad = dot_last(image_rows, slot_grads)
    dispatch_logit = dispatch * (weight_grad - shift_back)
    mixing_grad = dot_last(cot_rows, saved_outputs)
    combine_logit = combine * (mixing_grad - jnp.sum(combine * mixing_grad, axis=1, keepdims=True))
    logit_grad = (dispatch_logit + combine_logit).astype(jnp.bfloat16)
    token_grad = (
        jnp.dot(dispatch_low, slot_grads, preferred_element_type=jnp.float32)
        + dot_last(logit_grad, router)
    ).astype(jnp.bfloat16)
    grad_in_right = jnp.einsum(
        "gjr,gjf->jrf", up_low, preact_grad, preferred_element_type=jnp.float32
    ).astype(jnp.bfloat16)
    grad_out_left = jnp.einsum(
        "gjf,gjr->jfr", hidden_low, back_low, preferred_element_type=jnp.float32
    ).astype(jnp.bfloat16)
    grad_in_left = jnp.einsum(
        "gjd,gjr->jdr", inputs_own, down_own, preferred_element_type=jnp.float32
    ).astype(jnp.bfloat16)
    grad_out_right = jnp.einsum(
        "gjr,gjd->jrd", value_own, grads_own, preferred_element_type=jnp.float32
    ).astype(jnp.bfloat16)
    return (token_grad[None], grad_in_left, grad_in_right, grad_out_left, grad_out_right)


def dot_plain(left, right):
    return jnp.dot(left, right, preferred_element_type=jnp.float32)


def halves(value):
    high = value.astype(jnp.bfloat16).astype(jnp.float32)
    low = (value - high).astype(jnp.bfloat16).astype(jnp.float32)
    return high, low


def in_lanes(columns, shape):
    lane = lax.broadcasted_iota(jnp.int32, shape, len(shape) - 1)
    out = jnp.zeros(shape, jnp.float32)
    for number, column in enumerate(columns):
        out = jnp.where(lane == number, column, out)
    return out


def own_block(value, owned):
    rows, rank = value.shape
    wide = jnp.concatenate([value] * owned, axis=1)
    shape = (rows, owned * rank)
    block = lax.broadcasted_iota(jnp.int32, shape, 1) // rank
    expert = lax.broadcasted_iota(jnp.int32, shape, 0) % owned
    return jnp.where(block == expert, wide, 0.0).astype(jnp.bfloat16)


def from_own_block(value, owned):
    rows, wide = value.shape
    rank = wide // owned
    block = lax.broadcasted_iota(jnp.int32, value.shape, 1) // rank
    expert = lax.broadcasted_iota(jnp.int32, value.shape, 0) % owned
    kept = jnp.where(block == expert, value, 0.0)
    out = kept[:, :rank]
    for number in range(1, owned):
        out = out + kept[:, number * rank : (number + 1) * rank]
    return out


def sums_kernel(
    owned,
    groups,
    tokens_far,
    cotangent_far,
    router_far,
    first,
    logits_out,
    combine_out,
    tokens,
    cotangent,
    router,
    arrived,
):
    ring = first.shape[0] // groups
    copies = [
        pltpu.make_async_copy(far, near, arrived.at[number])
        for number, (far, near) in enumerate(
            [(router_far, router), (tokens_far, tokens), (cotangent_far, cotangent)]
        )
    ]
    for copy in copies:
        copy.start()
    copies[0].wait()
    copies[1].wait()
    image_rows = tokens[...]
    logits = dot_last(router[...], image_rows)
    high, low = halves(jnp.max(logits, axis=1, keepdims=True))
    near = jnp.exp(logits - (high + low))
    total_high, total_low = halves(jnp.sum(near, axis=1, keepdims=True))
    spread = jnp.exp(logits - jnp.max(logits, axis=0, keepdims=True))
    combine = spread / jnp.sum(spread, axis=0, keepdims=True)
    logits_out[...] = logits
    combine_out[...] = combine
    stats = in_lanes([high, low, total_high, total_low], (logits.shape[0], STATS))
    stats = stats.astype(jnp.bfloat16)
    inputs = dot_plain(near.astype(jnp.bfloat16), image_rows).astype(jnp.bfloat16)
    copies[2].wait()
    grads = dot_plain(combine.astype(jnp.bfloat16), cotangent[...]).astype(jnp.bfloat16)
    width = inputs.shape[1] // groups
    for group in range(groups):
        columns = slice(group * width, (group + 1) * width)
        for place in range(ring):
            rows = slice(place * owned, (place + 1) * owned)
            block = group * ring + place
            first[block, :, :width] = inputs[rows, columns]
            first[block, :, width : 2 * width] = grads[rows, columns]
            first[block, :, 2 * width :] = stats[rows, :]


def mixing_kernel(cotangent, saved, combine, *rest):
    *_, out = rest
    mixing = dot_last(saved[...], cotangent[...])
    weights = combine[...]
    out[...] = weights * (mixing - jnp.sum(weights * mixing, axis=0, keepdims=True))


def owner_kernel(groups, first, in_left, out_right, second, inputs_out, lows_out, stats_out):
    ring = first.shape[0] // groups
    owned, rank, width = in_left.shape
    inputs, grads, stats_rows = [], [], []
    for group in range(groups):
        rows = slice(group * ring, (group + 1) * ring)
        stats = first[rows, :, 2 * width :].astype(jnp.float32)
        peaks = stats[:, :, 0:1] + stats[:, :, 1:2]
        totals = stats[:, :, 2:3] + stats[:, :, 3:4]
        peak = jnp.max(peaks, axis=0)
        scale = jnp.exp(peaks - peak[None])
        total = jnp.sum(scale * totals, axis=0)
        scale = scale / total[None]
        inputs.append(jnp.sum(first[rows, :, :width].astype(jnp.float32) * scale, axis=0))
        grads.append(jnp.sum(first[rows, :, width : 2 * width].astype(jnp.float32), axis=0))
        stats_rows.append(in_lanes([*halves(peak), *halves(total)], (owned, STATS)))
    inputs, grads = jnp.concatenate(inputs, axis=0), jnp.concatenate(grads, axis=0)
    inputs_out[...] = inputs
    stats_out[...] = jnp.concatenate(stats_rows, axis=0)
    inputs_low, grads_low = inputs.astype(jnp.bfloat16), grads.astype(jnp.bfloat16)
    lows_out[0] = inputs_low
    lows_out[1] = grads_low
    up = dot_last(inputs_low, in_left[...].reshape(owned * rank, width))
    back = dot_last(grads_low, out_right[...].reshape(owned * rank, width))
    ranks = [*halves(from_own_block(up, owned)), *halves(from_own_block(back, owned))]
    ranks = jnp.concatenate(ranks, axis=1).astype(jnp.bfloat16)
    block = jnp.concatenate([inputs_low, grads_low, ranks], axis=1)
    second[...] = block


def spread_kernel(block, out):
    for group in range(2):
        for half in range(2):
            out[group, half] = block[...]


def pack_kernel(blocks, out):
    group = lax.axis_index("dp")
    for number in range(2):
        block = blocks[2 * number + group]
        for place in range(out.shape[0]):
            out[place, number] = block


def hidden_kernel(
    groups,
    second,
    base_in,
    base_out,
    in_right,
    out_left,
    third,
    pair_out,
    ranks_out,
):
    members, rank, hidden = in_right.shape
    rows = second.shape[2]
    owned = rows // groups
    places = members // owned
    width = base_in.shape[1] // groups
    ring = third.shape[0] // groups
    group = lax.axis_index("dp")

    def gathered(columns):
        taken = [
            second[:, half, :, columns].astype(jnp.float32)
            for half in range(groups)
        ]
        return [part.reshape(places * rows, part.shape[2]) for part in taken]

    def low_rank(value, table):
        value = value.astype(jnp.float32)
        taken = []
        for place in range(places):
            own = own_block(value[place * rows : (place + 1) * rows], owned)
            part = table[place * owned : (place + 1) * owned].reshape(owned * rank, hidden)
            taken.append(dot_plain(own, part))
        return jnp.concatenate(taken, axis=0)

    def to_rank(value, table):
        taken = []
        for place in range(places):
            part = table[place * owned : (place + 1) * owned].reshape(owned * rank, hidden)
            wide = dot_last(value[place * rows : (place + 1) * rows].astype(jnp.bfloat16), part)
            taken.append(from_own_block(wide, owned))
        return jnp.concatenate(taken, axis=0)

    ranks = functools.reduce(jnp.add, gathered(slice(2 * width, 2 * width + 4 * rank)))
    up = (ranks[:, :rank] + ranks[:, rank : 2 * rank]).astype(jnp.bfloat16)
    back = (ranks[:, 2 * rank : 3 * rank] + ranks[:, 3 * rank :]).astype(jnp.bfloat16)
    preact = low_rank(up, in_right)
    for half, part in enumerate(gathered(slice(0, width))):
        columns = slice(half * width, (half + 1) * width)
        preact = preact + dot_last(part.astype(jnp.bfloat16), base_in[:, columns])
    hidden_grad = low_rank(back, out_left)
    for half, part in enumerate(gathered(slice(width, 2 * width))):
        columns = slice(half * width, (half + 1) * width)
        hidden_grad = hidden_grad + dot_last(part.astype(jnp.bfloat16), base_out[:, columns])
    root = 0.7978845608028654
    bent = jnp.tanh(root * (preact + 0.044715 * (preact * preact * preact)))
    hidden_value = 0.5 * preact * (1.0 + bent)
    slope = 0.5 * (1.0 + bent) + 0.5 * preact * (1.0 - bent * bent) * (
        root * (1.0 + 3.0 * 0.044715 * (preact * preact))
    )
    hidden_low = hidden_value.astype(jnp.bfloat16).astype(jnp.float32)
    preact_grad = (hidden_grad * slope).astype(jnp.bfloat16).astype(jnp.float32)
    pair_out[0] = preact_grad
    pair_out[1] = hidden_low
    ranks_out[0] = up.astype(jnp.float32)
    ranks_out[1] = back.astype(jnp.float32)
    slot_term = dot_plain(preact_grad.astype(jnp.bfloat16), base_in[...]).astype(jnp.bfloat16)
    down = to_rank(preact_grad, in_right)
    value = to_rank(hidden_low, out_left)
    ranks = jnp.concatenate([down, value], axis=1).astype(jnp.bfloat16)
    third[...] = jnp.zeros(third.shape, jnp.bfloat16)
    for half in range(groups):
        columns = slice(half * width, (half + 1) * width)
        for place in range(places):
            taken = slice(place * rows, (place + 1) * rows)
            block = half * ring + group * places + place
            third[block, :, :width] = slot_term[taken, columns]
            third[block, :, width:] = ranks[taken]


def outer_kernel(owned, left_rows, right_rows, *outs):
    rows = left_rows.shape[1] // (outs[0].shape[0] // owned)
    for number, out in enumerate(outs):
        for place in range(out.shape[0] // owned):
            taken = slice(place * rows, (place + 1) * rows)
            own = own_block(left_rows[number, taken], owned)
            product = dot_first(own, right_rows[number, taken].astype(jnp.bfloat16))
            out[place * owned : (place + 1) * owned] = product.astype(jnp.bfloat16).reshape(
                (owned,) + out.shape[1:]
            )


def finish_kernel(groups, ring, third, in_left, inputs, stats, fourth, ranks_out):
    owned, rank, width = in_left.shape
    sender = lax.axis_index("half")
    summed = jnp.sum(third[pl.ds(sender * ring, ring)].astype(jnp.float32), axis=0)
    ranks = summed[:, width:].astype(jnp.bfloat16).astype(jnp.float32)
    ranks_out[0] = ranks[:, :rank]
    ranks_out[1] = ranks[:, rank:]
    down = own_block(ranks[:, :rank], owned)
    grads = summed[:, :width] + dot_plain(down, in_left[...].reshape(owned * rank, width))
    grads = grads.astype(jnp.bfloat16).astype(jnp.float32)
    high, low = halves(jnp.sum(grads * inputs[...], axis=1, keepdims=True))
    lane = lax.broadcasted_iota(jnp.int32, stats.shape, 1)
    tail = jnp.where(lane == 4, high, jnp.where(lane == 5, low, stats[...]))
    block = jnp.concatenate([grads, tail], axis=1).astype(jnp.bfloat16)
    for group in range(groups):
        rows = block[group * owned : (group + 1) * owned]
        for place in range(ring):
            fourth[group * ring + place] = rows


def tokens_kernel(groups, fourth, tokens, router, logits, mixing, out):
    blocks, owned, _ = fourth.shape
    ring = blocks // groups
    width = tokens.shape[1] // groups

    def rows(half, columns):
        taken = [
            fourth[half * ring + place, :, columns].astype(jnp.float32) for place in range(ring)
        ]
        return jnp.concatenate(taken, axis=0)

    grads = jnp.concatenate([rows(half, slice(0, width)) for half in range(groups)], axis=1)
    grads = grads.astype(jnp.bfloat16)
    stats = [rows(half, slice(width, width + STATS)) for half in range(groups)]
    peak = stats[0][:, 0:1] + stats[0][:, 1:2]
    total = stats[0][:, 2:3] + stats[0][:, 3:4]
    shift = functools.reduce(jnp.add, [part[:, 4:5] + part[:, 5:6] for part in stats])
    dispatch = jnp.exp(logits[...] - peak) / total
    weight_grad = dot_last(grads, tokens[...])
    logit_grad = dispatch * (weight_grad - shift) + mixing[...]
    left = jnp.concatenate([dispatch, logit_grad], axis=0).astype(jnp.bfloat16)
    right = jnp.concatenate([grads, router[...]], axis=0)
    out[...] = dot_first(left, right).astype(jnp.bfloat16)


def to_group(block):
    places = lax.axis_size("place")
    (blocks,) = call(
        spread_kernel, [array(block.dtype, 2, 2, *block.shape)], [block], 0
    )
    blocks = lax.all_to_all(blocks.reshape(4, *block.shape), ("dp", "half"), 0, 0, tiled=True)
    (blocks,) = call(
        pack_kernel, [array(block.dtype, places, 2, *block.shape)], [blocks], 0
    )
    return lax.all_to_all(blocks, "place", 0, 0, tiled=True)


def call(kernel, outs, args, flops, far=(), scratch=(), grant=24):
    size = sum(array.size * array.dtype.itemsize for array in args)
    size += sum(out.size * out.dtype.itemsize for out in outs)
    spaces = [pltpu.HBM if number in far else pltpu.VMEM for number in range(len(args))]
    return pl.pallas_call(
        kernel,
        out_shape=outs,
        in_specs=[pl.BlockSpec(memory_space=space) for space in spaces],
        out_specs=[pl.BlockSpec(memory_space=pltpu.VMEM) for _ in outs],
        scratch_shapes=scratch,
        cost_estimate=pl.CostEstimate(flops=flops, bytes_accessed=size, transcendentals=0),
        compiler_params=pltpu.CompilerParams(vmem_limit_bytes=grant * 2**20),
    )(*args)


def array(dtype, *shape):
    return jax.ShapeDtypeStruct(shape, dtype)


def local(
    tokens,
    cotangent,
    router,
    slot_outputs,
    base_in,
    base_out,
    in_left,
    in_right,
    out_left,
    out_right,
):
    groups, ring = lax.axis_size("dp"), lax.axis_size(SEQ)
    devices = groups * ring
    _, count, width = tokens.shape
    slots = router.shape[1]
    owned, slice_width, rank = in_left.shape
    members, _, hidden = in_right.shape
    rows = groups * owned
    if groups != 2 or ring % 2 or slice_width % 128 or rows % 8 or members % owned:
        return local_plain(
            tokens,
            cotangent,
            router,
            slot_outputs,
            base_in,
            base_out,
            in_left,
            in_right,
            out_left,
            out_right,
        )
    low, full = jnp.bfloat16, jnp.float32
    image_rows, cot_rows, saved = tokens[0], cotangent[0], slot_outputs[0]
    router, base_in = router.T, base_in.T
    in_left, out_left = in_left.swapaxes(1, 2), out_left.swapaxes(1, 2)
    first, logits, combine = call(
        functools.partial(sums_kernel, owned, groups),
        [
            array(low, devices, owned, 2 * slice_width + STATS),
            array(full, slots, count),
            array(full, slots, count),
        ],
        [image_rows, cot_rows, router],
        6 * count * slots * width,
        (0, 1, 2),
        [pltpu.VMEM((count, width), low)] * 2
        + [pltpu.VMEM((slots, width), low), pltpu.SemaphoreType.DMA((3,))],
        60,
    )
    first = lax.all_to_all(first, BOTH, 0, 0, tiled=True)
    (mixing,) = call(
        mixing_kernel,
        [array(full, slots, count)],
        [cot_rows, saved, combine, in_left, out_right, base_in, base_out, in_right, out_left],
        2 * count * slots * width,
    )
    first, mixing = lax.optimization_barrier((first, mixing))
    second, inputs, lows, stats = call(
        functools.partial(owner_kernel, groups),
        [
            array(low, rows, 2 * slice_width + 4 * rank),
            array(full, rows, slice_width),
            array(low, 2, rows, slice_width),
            array(full, rows, STATS),
        ],
        [first, in_left, out_right],
        4 * rows * owned * rank * slice_width,
    )
    second = to_group(second)
    total_rows = groups * members
    third, pair, ranks = call(
        functools.partial(hidden_kernel, groups),
        [
            array(low, devices, rows, slice_width + 2 * rank),
            array(full, 2, total_rows, hidden),
            array(full, 2, total_rows, rank),
        ],
        [second, base_in, base_out, in_right, out_left],
        6 * total_rows * hidden * (width + owned * rank),
    )
    third = lax.all_to_all(third, BOTH, 0, 0, tiled=True)
    grad_in_right, grad_out_left = call(
        functools.partial(outer_kernel, owned),
        [array(low, members, rank, hidden)] * 2,
        [ranks, pair],
        4 * members * rank * hidden * rows,
    )
    fourth, ranks = call(
        functools.partial(finish_kernel, groups, ring),
        [array(low, devices, owned, slice_width + STATS), array(full, 2, rows, rank)],
        [third, in_left, inputs, stats],
        2 * rows * owned * rank * slice_width,
    )
    fourth = lax.all_to_all(fourth, BOTH, 0, 0, tiled=True)
    grad_in_left, grad_out_right = call(
        functools.partial(outer_kernel, owned),
        [array(low, owned, rank, slice_width)] * 2,
        [ranks, lows],
        4 * owned * rank * slice_width * rows,
    )
    (token_grad,) = call(
        functools.partial(tokens_kernel, groups),
        [array(low, count, width)],
        [fourth, image_rows, router, logits, mixing],
        6 * count * slots * width,
    )
    return (
        token_grad[None],
        grad_in_left.swapaxes(1, 2),
        grad_in_right,
        grad_out_left.swapaxes(1, 2),
        grad_out_right,
    )


def solution(mesh):
    groups, ring = mesh.shape["dp"], mesh.shape["seq"]
    split = mesh.devices.reshape(groups, groups, ring // groups)
    mesh = jax.sharding.Mesh(split, BOTH)
    in_specs = (
        P("dp", SEQ, None),
        P("dp", SEQ, None),
        P(),
        P("dp", None, None),
        P(None, SEQ),
        P(SEQ, None),
        P(SEQ, "dp", None),
        P("dp", None, SEQ),
        P("dp", SEQ, None),
        P(SEQ, None, "dp"),
    )
    out_specs = (
        P("dp", SEQ, None),
        P(SEQ, "dp", None),
        P("dp", None, SEQ),
        P("dp", SEQ, None),
        P(SEQ, None, "dp"),
    )
    return jax.shard_map(local, mesh=mesh, in_specs=in_specs, out_specs=out_specs, check_vma=False)
```

```python
import functools

import jax
import jax.numpy as jnp
from jax import lax
from jax.experimental import pallas as pl
from jax.experimental.pallas import tpu as pltpu
from jax.sharding import PartitionSpec as P

SEQ = ("half", "place")
BOTH = ("dp", *SEQ)
STATS = 128


def gelu_backward(preact, upstream):
    return jax.vjp(jax.nn.gelu, preact)[1](upstream)[0]


def dot_first(left, right):
    return lax.dot_general(
        left, right, (((0,), (0,)), ((), ())), preferred_element_type=jnp.float32
    )


def dot_last(left, right):
    return lax.dot_general(
        left, right, (((1,), (1,)), ((), ())), preferred_element_type=jnp.float32
    )


def split(value):
    high = lax.reduce_precision(value, 8, 7)
    low = lax.reduce_precision(value - high, 8, 7)
    return high.astype(jnp.bfloat16), low.astype(jnp.bfloat16)


def joined(high, low):
    return high.astype(jnp.float32) + low.astype(jnp.float32)


def exchange(blocks):
    flat = blocks.reshape((-1,) + blocks.shape[2:])
    return lax.all_to_all(flat, BOTH, 0, 0, tiled=True).reshape(blocks.shape)


def local_plain(
    tokens,
    cotangent,
    router,
    slot_outputs,
    base_in,
    base_out,
    in_left,
    in_right,
    out_left,
    out_right,
):
    groups, ring = lax.axis_size("dp"), lax.axis_size(SEQ)
    image_rows = tokens[0]
    cot_rows = cotangent[0]
    saved_outputs = slot_outputs[0]
    width = image_rows.shape[1]
    slots = router.shape[1]
    owned, slice_width, rank = in_left.shape
    members = in_right.shape[0]
    places = members // owned
    group, place = lax.axis_index("dp"), lax.axis_index(SEQ)

    logits = jnp.dot(image_rows, router, preferred_element_type=jnp.float32)
    peak_high, peak_low = split(jnp.max(logits, axis=0))
    near = jnp.exp(logits - joined(peak_high, peak_low))
    total_high, total_low = split(jnp.sum(near, axis=0))
    combine = jax.nn.softmax(logits, axis=1)
    sums = jnp.stack(
        [
            dot_first(near.astype(jnp.bfloat16), image_rows),
            dot_first(combine.astype(jnp.bfloat16), cot_rows),
        ],
        axis=1,
    ).astype(jnp.bfloat16)
    sums = sums.reshape(ring, owned, 2, groups, slice_width).transpose(3, 0, 1, 2, 4)
    sums = sums.reshape(groups, ring, owned, 2 * slice_width)
    stats = jnp.stack([peak_high, peak_low, total_high, total_low], axis=1)
    stats = jnp.pad(stats, ((0, 0), (0, STATS - 4))).reshape(1, ring, owned, STATS)
    stats = jnp.broadcast_to(stats, (groups, ring, owned, STATS))
    first = exchange(jnp.concatenate([sums, stats], axis=3))

    tail = 2 * slice_width
    peaks = joined(first[..., tail], first[..., tail + 1])
    totals = joined(first[..., tail + 2], first[..., tail + 3])
    peak = jnp.max(peaks, axis=1)
    near_scale = jnp.exp(peaks - peak[:, None])
    total = jnp.sum(near_scale * totals, axis=1)
    near_scale = near_scale / total[:, None]
    parts = first[..., :tail].astype(jnp.float32)
    slot_inputs = jnp.sum(parts[..., :slice_width] * near_scale[..., None], axis=1)
    inputs_own = slot_inputs.astype(jnp.bfloat16)
    grads_own = jnp.sum(parts[..., slice_width:], axis=1).astype(jnp.bfloat16)
    up_part = jnp.einsum("gjd,jdr->gjr", inputs_own, in_left, preferred_element_type=jnp.float32)
    back_part = jnp.einsum("gjd,jrd->gjr", grads_own, out_right, preferred_element_type=jnp.float32)
    second = jnp.concatenate(
        [inputs_own, grads_own, *split(up_part), *split(back_part)], axis=2
    )
    second = exchange(jnp.broadcast_to(second, (groups, ring) + second.shape))
    second = lax.dynamic_slice_in_dim(second, group * places, places, 1)

    def gathered(start):
        piece = second[..., start : start + slice_width]
        return piece.transpose(2, 1, 3, 0, 4).reshape(groups * members, width)

    def ranks(start):
        piece = joined(
            second[..., start : start + rank], second[..., start + rank : start + 2 * rank]
        )
        piece = jnp.sum(piece, axis=0).transpose(1, 0, 2, 3)
        return piece.reshape(groups, members, rank).astype(jnp.bfloat16)

    inputs_low, grads_low = gathered(0), gathered(slice_width)
    up_low, back_low = ranks(tail), ranks(tail + 2 * rank)
    hidden = base_in.shape[1]
    preact = jnp.dot(inputs_low, base_in, preferred_element_type=jnp.float32).reshape(
        groups, members, hidden
    ) + jnp.einsum("gjr,jrf->gjf", up_low, in_right, preferred_element_type=jnp.float32)
    hidden_low = jax.nn.gelu(preact).astype(jnp.bfloat16)
    hidden_grad = dot_last(grads_low, base_out).reshape(groups, members, hidden) + jnp.einsum(
        "gjr,jfr->gjf", back_low, out_left, preferred_element_type=jnp.float32
    )
    preact_grad = gelu_backward(preact, hidden_grad).astype(jnp.bfloat16)
    slot_term = dot_last(preact_grad.reshape(groups * members, hidden), base_in)
    down_term = jnp.einsum(
        "gjf,jrf->gjr", preact_grad, in_right, preferred_element_type=jnp.float32
    )
    value_term = jnp.einsum(
        "gjf,jfr->gjr", hidden_low, out_left, preferred_element_type=jnp.float32
    )
    slot_term = slot_term.astype(jnp.bfloat16).reshape(groups, places, owned, groups, slice_width)
    slot_term = slot_term.transpose(3, 1, 0, 2, 4)
    rank_term = jnp.concatenate([down_term, value_term], axis=2).astype(jnp.bfloat16)
    rank_term = rank_term.reshape(groups, places, owned, 2 * rank).transpose(1, 0, 2, 3)
    rank_term = jnp.broadcast_to(rank_term, (groups,) + rank_term.shape)
    third = jnp.concatenate([slot_term, rank_term], axis=4)
    third = lax.dynamic_update_slice_in_dim(
        jnp.zeros((groups, ring) + third.shape[2:], jnp.bfloat16), third, group * places, 1
    )
    third = exchange(third)
    third = lax.dynamic_index_in_dim(third, place // places, 0, keepdims=False)
    third = jnp.sum(third.astype(jnp.float32), axis=0)
    down_own = third[..., slice_width : slice_width + rank].astype(jnp.bfloat16)
    value_own = third[..., slice_width + rank :].astype(jnp.bfloat16)
    slot_grads_own = (
        third[..., :slice_width]
        + jnp.einsum("gjr,jdr->gjd", down_own, in_left, preferred_element_type=jnp.float32)
    ).astype(jnp.bfloat16)
    shift_part = jnp.sum(slot_grads_own.astype(jnp.float32) * slot_inputs, axis=2)
    stats = jnp.stack([*split(peak), *split(total), *split(shift_part)], axis=2)
    stats = jnp.pad(stats, ((0, 0), (0, 0), (0, STATS - 6)))
    fourth = jnp.concatenate([slot_grads_own, stats], axis=2)[:, None]
    fourth = exchange(jnp.broadcast_to(fourth, (groups, ring) + fourth.shape[2:]))
    slot_grads = fourth[..., :slice_width].transpose(1, 2, 0, 3).reshape(slots, width)
    stats = fourth[..., slice_width:].astype(jnp.float32).reshape(groups, slots, STATS)
    slot_peak = stats[0, :, 0] + stats[0, :, 1]
    slot_total = stats[0, :, 2] + stats[0, :, 3]
    shift_back = jnp.sum(stats[:, :, 4] + stats[:, :, 5], axis=0)

    dispatch = jnp.exp(logits - slot_peak) / slot_total
    dispatch_low = dispatch.astype(jnp.bfloat16)
    weight_grad = dot_last(image_rows, slot_grads)
    dispatch_logit = dispatch * (weight_grad - shift_back)
    mixing_grad = dot_last(cot_rows, saved_outputs)
    combine_logit = combine * (mixing_grad - jnp.sum(combine * mixing_grad, axis=1, keepdims=True))
    logit_grad = (dispatch_logit + combine_logit).astype(jnp.bfloat16)
    token_grad = (
        jnp.dot(dispatch_low, slot_grads, preferred_element_type=jnp.float32)
        + dot_last(logit_grad, router)
    ).astype(jnp.bfloat16)
    grad_in_right = jnp.einsum(
        "gjr,gjf->jrf", up_low, preact_grad, preferred_element_type=jnp.float32
    ).astype(jnp.bfloat16)
    grad_out_left = jnp.einsum(
        "gjf,gjr->jfr", hidden_low, back_low, preferred_element_type=jnp.float32
    ).astype(jnp.bfloat16)
    grad_in_left = jnp.einsum(
        "gjd,gjr->jdr", inputs_own, down_own, preferred_element_type=jnp.float32
    ).astype(jnp.bfloat16)
    grad_out_right = jnp.einsum(
        "gjr,gjd->jrd", value_own, grads_own, preferred_element_type=jnp.float32
    ).astype(jnp.bfloat16)
    return (token_grad[None], grad_in_left, grad_in_right, grad_out_left, grad_out_right)


def dot_plain(left, right):
    return jnp.dot(left, right, preferred_element_type=jnp.float32)


def halves(value):
    high = value.astype(jnp.bfloat16).astype(jnp.float32)
    low = (value - high).astype(jnp.bfloat16).astype(jnp.float32)
    return high, low


def in_lanes(columns, shape):
    lane = lax.broadcasted_iota(jnp.int32, shape, len(shape) - 1)
    out = jnp.zeros(shape, jnp.float32)
    for number, column in enumerate(columns):
        out = jnp.where(lane == number, column, out)
    return out


def own_block(value, owned):
    rows, rank = value.shape
    wide = jnp.concatenate([value] * owned, axis=1)
    shape = (rows, owned * rank)
    block = lax.broadcasted_iota(jnp.int32, shape, 1) // rank
    expert = lax.broadcasted_iota(jnp.int32, shape, 0) % owned
    return jnp.where(block == expert, wide, 0.0).astype(jnp.bfloat16)


def from_own_block(value, owned):
    rows, wide = value.shape
    rank = wide // owned
    block = lax.broadcasted_iota(jnp.int32, value.shape, 1) // rank
    expert = lax.broadcasted_iota(jnp.int32, value.shape, 0) % owned
    kept = jnp.where(block == expert, value, 0.0)
    out = kept[:, :rank]
    for number in range(1, owned):
        out = out + kept[:, number * rank : (number + 1) * rank]
    return out


def sums_kernel(
    owned,
    groups,
    tokens_far,
    cotangent_far,
    router_far,
    first,
    logits_out,
    combine_out,
    tokens,
    cotangent,
    router,
    arrived,
):
    ring = first.shape[0] // groups
    copies = [
        pltpu.make_async_copy(far, near, arrived.at[number])
        for number, (far, near) in enumerate(
            [(router_far, router), (tokens_far, tokens), (cotangent_far, cotangent)]
        )
    ]
    for copy in copies:
        copy.start()
    copies[0].wait()
    copies[1].wait()
    image_rows = tokens[...]
    logits = dot_last(router[...], image_rows)
    high, low = halves(jnp.max(logits, axis=1, keepdims=True))
    near = jnp.exp(logits - (high + low))
    total_high, total_low = halves(jnp.sum(near, axis=1, keepdims=True))
    spread = jnp.exp(logits - jnp.max(logits, axis=0, keepdims=True))
    combine = spread / jnp.sum(spread, axis=0, keepdims=True)
    logits_out[...] = logits
    combine_out[...] = combine
    stats = in_lanes([high, low, total_high, total_low], (logits.shape[0], STATS))
    stats = stats.astype(jnp.bfloat16)
    inputs = dot_plain(near.astype(jnp.bfloat16), image_rows).astype(jnp.bfloat16)
    copies[2].wait()
    grads = dot_plain(combine.astype(jnp.bfloat16), cotangent[...]).astype(jnp.bfloat16)
    width = inputs.shape[1] // groups
    for group in range(groups):
        columns = slice(group * width, (group + 1) * width)
        for place in range(ring):
            rows = slice(place * owned, (place + 1) * owned)
            block = group * ring + place
            first[block, :, :width] = inputs[rows, columns]
            first[block, :, width : 2 * width] = grads[rows, columns]
            first[block, :, 2 * width :] = stats[rows, :]


def mixing_kernel(cotangent, saved, combine, *rest):
    *_, table, out, table_out = rest
    table_out[...] = table[...]
    mixing = dot_last(saved[...], cotangent[...])
    weights = combine[...]
    out[...] = weights * (mixing - jnp.sum(weights * mixing, axis=0, keepdims=True))


def owner_kernel(groups, first, in_left, out_right, second, inputs_out, lows_out, stats_out):
    ring = first.shape[0] // groups
    owned, rank, width = in_left.shape
    inputs, grads, stats_rows = [], [], []
    for group in range(groups):
        rows = slice(group * ring, (group + 1) * ring)
        stats = first[rows, :, 2 * width :].astype(jnp.float32)
        peaks = stats[:, :, 0:1] + stats[:, :, 1:2]
        totals = stats[:, :, 2:3] + stats[:, :, 3:4]
        peak = jnp.max(peaks, axis=0)
        scale = jnp.exp(peaks - peak[None])
        total = jnp.sum(scale * totals, axis=0)
        scale = scale / total[None]
        inputs.append(jnp.sum(first[rows, :, :width].astype(jnp.float32) * scale, axis=0))
        grads.append(jnp.sum(first[rows, :, width : 2 * width].astype(jnp.float32), axis=0))
        stats_rows.append(in_lanes([*halves(peak), *halves(total)], (owned, STATS)))
    inputs, grads = jnp.concatenate(inputs, axis=0), jnp.concatenate(grads, axis=0)
    inputs_out[...] = inputs
    stats_out[...] = jnp.concatenate(stats_rows, axis=0)
    inputs_low, grads_low = inputs.astype(jnp.bfloat16), grads.astype(jnp.bfloat16)
    lows_out[0] = inputs_low
    lows_out[1] = grads_low
    up = dot_last(inputs_low, in_left[...].reshape(owned * rank, width))
    back = dot_last(grads_low, out_right[...].reshape(owned * rank, width))
    ranks = [*halves(from_own_block(up, owned)), *halves(from_own_block(back, owned))]
    ranks = jnp.concatenate(ranks, axis=1).astype(jnp.bfloat16)
    block = jnp.concatenate([inputs_low, grads_low, ranks], axis=1)
    second[...] = block


def spread_kernel(block, out):
    for group in range(2):
        for half in range(2):
            out[group, half] = block[...]


def pack_kernel(blocks, out):
    group = lax.axis_index("dp")
    for number in range(2):
        block = blocks[2 * number + group]
        for place in range(out.shape[0]):
            out[place, number] = block


def hidden_kernel(
    groups,
    second,
    base_in,
    base_out,
    in_right,
    out_left,
    third,
    pair_out,
    ranks_out,
):
    members, rank, hidden = in_right.shape
    rows = second.shape[2]
    owned = rows // groups
    places = members // owned
    width = base_in.shape[1] // groups
    ring = third.shape[0] // groups
    group = lax.axis_index("dp")

    def gathered(columns):
        taken = [
            second[:, half, :, columns].astype(jnp.float32)
            for half in range(groups)
        ]
        return [part.reshape(places * rows, part.shape[2]) for part in taken]

    def low_rank(value, table):
        value = value.astype(jnp.float32)
        taken = []
        for place in range(places):
            own = own_block(value[place * rows : (place + 1) * rows], owned)
            part = table[place * owned : (place + 1) * owned].reshape(owned * rank, hidden)
            taken.append(dot_plain(own, part))
        return jnp.concatenate(taken, axis=0)

    def to_rank(value, table):
        taken = []
        for place in range(places):
            part = table[place * owned : (place + 1) * owned].reshape(owned * rank, hidden)
            wide = dot_last(value[place * rows : (place + 1) * rows].astype(jnp.bfloat16), part)
            taken.append(from_own_block(wide, owned))
        return jnp.concatenate(taken, axis=0)

    ranks = functools.reduce(jnp.add, gathered(slice(2 * width, 2 * width + 4 * rank)))
    up = (ranks[:, :rank] + ranks[:, rank : 2 * rank]).astype(jnp.bfloat16)
    back = (ranks[:, 2 * rank : 3 * rank] + ranks[:, 3 * rank :]).astype(jnp.bfloat16)
    preact = low_rank(up, in_right)
    for half, part in enumerate(gathered(slice(0, width))):
        columns = slice(half * width, (half + 1) * width)
        preact = preact + dot_last(part.astype(jnp.bfloat16), base_in[:, columns])
    hidden_grad = low_rank(back, out_left)
    for half, part in enumerate(gathered(slice(width, 2 * width))):
        columns = slice(half * width, (half + 1) * width)
        hidden_grad = hidden_grad + dot_last(part.astype(jnp.bfloat16), base_out[:, columns])
    root = 0.7978845608028654
    bent = jnp.tanh(root * (preact + 0.044715 * (preact * preact * preact)))
    hidden_value = 0.5 * preact * (1.0 + bent)
    slope = 0.5 * (1.0 + bent) + 0.5 * preact * (1.0 - bent * bent) * (
        root * (1.0 + 3.0 * 0.044715 * (preact * preact))
    )
    hidden_low = hidden_value.astype(jnp.bfloat16).astype(jnp.float32)
    preact_grad = (hidden_grad * slope).astype(jnp.bfloat16).astype(jnp.float32)
    pair_out[0] = preact_grad
    pair_out[1] = hidden_low
    ranks_out[0] = up.astype(jnp.float32)
    ranks_out[1] = back.astype(jnp.float32)
    slot_term = dot_plain(preact_grad.astype(jnp.bfloat16), base_in[...]).astype(jnp.bfloat16)
    down = to_rank(preact_grad, in_right)
    value = to_rank(hidden_low, out_left)
    ranks = jnp.concatenate([down, value], axis=1).astype(jnp.bfloat16)
    third[...] = jnp.zeros(third.shape, jnp.bfloat16)
    for half in range(groups):
        columns = slice(half * width, (half + 1) * width)
        for place in range(places):
            taken = slice(place * rows, (place + 1) * rows)
            block = half * ring + group * places + place
            third[block, :, :width] = slot_term[taken, columns]
            third[block, :, width:] = ranks[taken]


def outer_kernel(owned, left_rows, right_rows, *outs):
    rows = left_rows.shape[1] // (outs[0].shape[0] // owned)
    for number, out in enumerate(outs):
        for place in range(out.shape[0] // owned):
            taken = slice(place * rows, (place + 1) * rows)
            own = own_block(left_rows[number, taken], owned)
            product = dot_first(own, right_rows[number, taken].astype(jnp.bfloat16))
            out[place * owned : (place + 1) * owned] = product.astype(jnp.bfloat16).reshape(
                (owned,) + out.shape[1:]
            )


def finish_kernel(groups, ring, third, in_left, inputs, stats, fourth, ranks_out):
    owned, rank, width = in_left.shape
    sender = lax.axis_index("half")
    summed = jnp.sum(third[pl.ds(sender * ring, ring)].astype(jnp.float32), axis=0)
    ranks = summed[:, width:].astype(jnp.bfloat16).astype(jnp.float32)
    ranks_out[0] = ranks[:, :rank]
    ranks_out[1] = ranks[:, rank:]
    down = own_block(ranks[:, :rank], owned)
    grads = summed[:, :width] + dot_plain(down, in_left[...].reshape(owned * rank, width))
    grads = grads.astype(jnp.bfloat16).astype(jnp.float32)
    high, low = halves(jnp.sum(grads * inputs[...], axis=1, keepdims=True))
    lane = lax.broadcasted_iota(jnp.int32, stats.shape, 1)
    tail = jnp.where(lane == 4, high, jnp.where(lane == 5, low, stats[...]))
    block = jnp.concatenate([grads, tail], axis=1).astype(jnp.bfloat16)
    for group in range(groups):
        rows = block[group * owned : (group + 1) * owned]
        for place in range(ring):
            fourth[group * ring + place] = rows


def tokens_kernel(groups, fourth, tokens, router, logits, mixing, out):
    blocks, owned, _ = fourth.shape
    ring = blocks // groups
    width = tokens.shape[1] // groups

    def rows(half, columns):
        taken = [
            fourth[half * ring + place, :, columns].astype(jnp.float32) for place in range(ring)
        ]
        return jnp.concatenate(taken, axis=0)

    grads = jnp.concatenate([rows(half, slice(0, width)) for half in range(groups)], axis=1)
    grads = grads.astype(jnp.bfloat16)
    stats = [rows(half, slice(width, width + STATS)) for half in range(groups)]
    peak = stats[0][:, 0:1] + stats[0][:, 1:2]
    total = stats[0][:, 2:3] + stats[0][:, 3:4]
    shift = functools.reduce(jnp.add, [part[:, 4:5] + part[:, 5:6] for part in stats])
    dispatch = jnp.exp(logits[...] - peak) / total
    weight_grad = dot_last(grads, tokens[...])
    logit_grad = dispatch * (weight_grad - shift) + mixing[...]
    left = jnp.concatenate([dispatch, logit_grad], axis=0).astype(jnp.bfloat16)
    right = jnp.concatenate([grads, router[...]], axis=0)
    out[...] = dot_first(left, right).astype(jnp.bfloat16)


def to_group(block):
    places = lax.axis_size("place")
    (blocks,) = call(
        spread_kernel, [array(block.dtype, 2, 2, *block.shape)], [block], 0
    )
    blocks = lax.all_to_all(blocks.reshape(4, *block.shape), ("dp", "half"), 0, 0, tiled=True)
    (blocks,) = call(
        pack_kernel, [array(block.dtype, places, 2, *block.shape)], [blocks], 0
    )
    return lax.all_to_all(blocks, "place", 0, 0, tiled=True)


def call(kernel, outs, args, flops, far=(), scratch=(), grant=24):
    size = sum(array.size * array.dtype.itemsize for array in args)
    size += sum(out.size * out.dtype.itemsize for out in outs)
    spaces = [pltpu.HBM if number in far else pltpu.VMEM for number in range(len(args))]
    return pl.pallas_call(
        kernel,
        out_shape=outs,
        in_specs=[pl.BlockSpec(memory_space=space) for space in spaces],
        out_specs=[pl.BlockSpec(memory_space=pltpu.VMEM) for _ in outs],
        scratch_shapes=scratch,
        cost_estimate=pl.CostEstimate(flops=flops, bytes_accessed=size, transcendentals=0),
        compiler_params=pltpu.CompilerParams(vmem_limit_bytes=grant * 2**20),
    )(*args)


def array(dtype, *shape):
    return jax.ShapeDtypeStruct(shape, dtype)


def local(
    tokens,
    cotangent,
    router,
    slot_outputs,
    base_in,
    base_out,
    in_left,
    in_right,
    out_left,
    out_right,
):
    groups, ring = lax.axis_size("dp"), lax.axis_size(SEQ)
    devices = groups * ring
    _, count, width = tokens.shape
    slots = router.shape[1]
    owned, slice_width, rank = in_left.shape
    members, _, hidden = in_right.shape
    rows = groups * owned
    if groups != 2 or ring % 2 or slice_width % 128 or rows % 8 or members % owned:
        return local_plain(
            tokens,
            cotangent,
            router,
            slot_outputs,
            base_in,
            base_out,
            in_left,
            in_right,
            out_left,
            out_right,
        )
    low, full = jnp.bfloat16, jnp.float32
    image_rows, cot_rows, saved = tokens[0], cotangent[0], slot_outputs[0]
    router, base_in = router.T, base_in.T
    in_left, out_left = in_left.swapaxes(1, 2), out_left.swapaxes(1, 2)
    first, logits, combine = call(
        functools.partial(sums_kernel, owned, groups),
        [
            array(low, devices, owned, 2 * slice_width + STATS),
            array(full, slots, count),
            array(full, slots, count),
        ],
        [image_rows, cot_rows, router],
        6 * count * slots * width,
        (0, 1, 2),
        [pltpu.VMEM((count, width), low)] * 2
        + [pltpu.VMEM((slots, width), low), pltpu.SemaphoreType.DMA((3,))],
        60,
    )
    first = lax.all_to_all(first, BOTH, 0, 0, tiled=True)
    mixing, out_left = call(
        mixing_kernel,
        [array(full, slots, count), array(low, *out_left.shape)],
        [cot_rows, saved, combine, out_right, base_out, out_left],
        2 * count * slots * width,
    )
    first, mixing, out_left = lax.optimization_barrier((first, mixing, out_left))
    second, inputs, lows, stats = call(
        functools.partial(owner_kernel, groups),
        [
            array(low, rows, 2 * slice_width + 4 * rank),
            array(full, rows, slice_width),
            array(low, 2, rows, slice_width),
            array(full, rows, STATS),
        ],
        [first, in_left, out_right],
        4 * rows * owned * rank * slice_width,
    )
    second = to_group(second)
    total_rows = groups * members
    third, pair, ranks = call(
        functools.partial(hidden_kernel, groups),
        [
            array(low, devices, rows, slice_width + 2 * rank),
            array(full, 2, total_rows, hidden),
            array(full, 2, total_rows, rank),
        ],
        [second, base_in, base_out, in_right, out_left],
        6 * total_rows * hidden * (width + owned * rank),
    )
    third = lax.all_to_all(third, BOTH, 0, 0, tiled=True)
    grad_in_right, grad_out_left = call(
        functools.partial(outer_kernel, owned),
        [array(low, members, rank, hidden)] * 2,
        [ranks, pair],
        4 * members * rank * hidden * rows,
    )
    fourth, ranks = call(
        functools.partial(finish_kernel, groups, ring),
        [array(low, devices, owned, slice_width + STATS), array(full, 2, rows, rank)],
        [third, in_left, inputs, stats],
        2 * rows * owned * rank * slice_width,
    )
    fourth = lax.all_to_all(fourth, BOTH, 0, 0, tiled=True)
    grad_in_left, grad_out_right = call(
        functools.partial(outer_kernel, owned),
        [array(low, owned, rank, slice_width)] * 2,
        [ranks, lows],
        4 * owned * rank * slice_width * rows,
    )
    (token_grad,) = call(
        functools.partial(tokens_kernel, groups),
        [array(low, count, width)],
        [fourth, image_rows, router, logits, mixing],
        6 * count * slots * width,
    )
    return (
        token_grad[None],
        grad_in_left.swapaxes(1, 2),
        grad_in_right,
        grad_out_left.swapaxes(1, 2),
        grad_out_right,
    )


def solution(mesh):
    groups, ring = mesh.shape["dp"], mesh.shape["seq"]
    split = mesh.devices.reshape(groups, groups, ring // groups)
    mesh = jax.sharding.Mesh(split, BOTH)
    in_specs = (
        P("dp", SEQ, None),
        P("dp", SEQ, None),
        P(),
        P("dp", None, None),
        P(None, SEQ),
        P(SEQ, None),
        P(SEQ, "dp", None),
        P("dp", None, SEQ),
        P("dp", SEQ, None),
        P(SEQ, None, "dp"),
    )
    out_specs = (
        P("dp", SEQ, None),
        P(SEQ, "dp", None),
        P("dp", None, SEQ),
        P("dp", SEQ, None),
        P(SEQ, None, "dp"),
    )
    return jax.shard_map(local, mesh=mesh, in_specs=in_specs, out_specs=out_specs, check_vma=False)
```

```python
import functools

import jax
import jax.numpy as jnp
from jax import lax
from jax.experimental import pallas as pl
from jax.experimental.pallas import tpu as pltpu
from jax.sharding import PartitionSpec as P

SEQ = ("half", "place")
BOTH = ("dp", *SEQ)
STATS = 128


def gelu_backward(preact, upstream):
    return jax.vjp(jax.nn.gelu, preact)[1](upstream)[0]


def dot_first(left, right):
    return lax.dot_general(
        left, right, (((0,), (0,)), ((), ())), preferred_element_type=jnp.float32
    )


def dot_last(left, right):
    return lax.dot_general(
        left, right, (((1,), (1,)), ((), ())), preferred_element_type=jnp.float32
    )


def split(value):
    high = lax.reduce_precision(value, 8, 7)
    low = lax.reduce_precision(value - high, 8, 7)
    return high.astype(jnp.bfloat16), low.astype(jnp.bfloat16)


def joined(high, low):
    return high.astype(jnp.float32) + low.astype(jnp.float32)


def exchange(blocks):
    flat = blocks.reshape((-1,) + blocks.shape[2:])
    return lax.all_to_all(flat, BOTH, 0, 0, tiled=True).reshape(blocks.shape)


def local_plain(
    tokens,
    cotangent,
    router,
    slot_outputs,
    base_in,
    base_out,
    in_left,
    in_right,
    out_left,
    out_right,
):
    groups, ring = lax.axis_size("dp"), lax.axis_size(SEQ)
    image_rows = tokens[0]
    cot_rows = cotangent[0]
    saved_outputs = slot_outputs[0]
    width = image_rows.shape[1]
    slots = router.shape[1]
    owned, slice_width, rank = in_left.shape
    members = in_right.shape[0]
    places = members // owned
    group, place = lax.axis_index("dp"), lax.axis_index(SEQ)

    logits = jnp.dot(image_rows, router, preferred_element_type=jnp.float32)
    peak_high, peak_low = split(jnp.max(logits, axis=0))
    near = jnp.exp(logits - joined(peak_high, peak_low))
    total_high, total_low = split(jnp.sum(near, axis=0))
    combine = jax.nn.softmax(logits, axis=1)
    sums = jnp.stack(
        [
            dot_first(near.astype(jnp.bfloat16), image_rows),
            dot_first(combine.astype(jnp.bfloat16), cot_rows),
        ],
        axis=1,
    ).astype(jnp.bfloat16)
    sums = sums.reshape(ring, owned, 2, groups, slice_width).transpose(3, 0, 1, 2, 4)
    sums = sums.reshape(groups, ring, owned, 2 * slice_width)
    stats = jnp.stack([peak_high, peak_low, total_high, total_low], axis=1)
    stats = jnp.pad(stats, ((0, 0), (0, STATS - 4))).reshape(1, ring, owned, STATS)
    stats = jnp.broadcast_to(stats, (groups, ring, owned, STATS))
    first = exchange(jnp.concatenate([sums, stats], axis=3))

    tail = 2 * slice_width
    peaks = joined(first[..., tail], first[..., tail + 1])
    totals = joined(first[..., tail + 2], first[..., tail + 3])
    peak = jnp.max(peaks, axis=1)
    near_scale = jnp.exp(peaks - peak[:, None])
    total = jnp.sum(near_scale * totals, axis=1)
    near_scale = near_scale / total[:, None]
    parts = first[..., :tail].astype(jnp.float32)
    slot_inputs = jnp.sum(parts[..., :slice_width] * near_scale[..., None], axis=1)
    inputs_own = slot_inputs.astype(jnp.bfloat16)
    grads_own = jnp.sum(parts[..., slice_width:], axis=1).astype(jnp.bfloat16)
    up_part = jnp.einsum("gjd,jdr->gjr", inputs_own, in_left, preferred_element_type=jnp.float32)
    back_part = jnp.einsum("gjd,jrd->gjr", grads_own, out_right, preferred_element_type=jnp.float32)
    second = jnp.concatenate(
        [inputs_own, grads_own, *split(up_part), *split(back_part)], axis=2
    )
    second = exchange(jnp.broadcast_to(second, (groups, ring) + second.shape))
    second = lax.dynamic_slice_in_dim(second, group * places, places, 1)

    def gathered(start):
        piece = second[..., start : start + slice_width]
        return piece.transpose(2, 1, 3, 0, 4).reshape(groups * members, width)

    def ranks(start):
        piece = joined(
            second[..., start : start + rank], second[..., start + rank : start + 2 * rank]
        )
        piece = jnp.sum(piece, axis=0).transpose(1, 0, 2, 3)
        return piece.reshape(groups, members, rank).astype(jnp.bfloat16)

    inputs_low, grads_low = gathered(0), gathered(slice_width)
    up_low, back_low = ranks(tail), ranks(tail + 2 * rank)
    hidden = base_in.shape[1]
    preact = jnp.dot(inputs_low, base_in, preferred_element_type=jnp.float32).reshape(
        groups, members, hidden
    ) + jnp.einsum("gjr,jrf->gjf", up_low, in_right, preferred_element_type=jnp.float32)
    hidden_low = jax.nn.gelu(preact).astype(jnp.bfloat16)
    hidden_grad = dot_last(grads_low, base_out).reshape(groups, members, hidden) + jnp.einsum(
        "gjr,jfr->gjf", back_low, out_left, preferred_element_type=jnp.float32
    )
    preact_grad = gelu_backward(preact, hidden_grad).astype(jnp.bfloat16)
    slot_term = dot_last(preact_grad.reshape(groups * members, hidden), base_in)
    down_term = jnp.einsum(
        "gjf,jrf->gjr", preact_grad, in_right, preferred_element_type=jnp.float32
    )
    value_term = jnp.einsum(
        "gjf,jfr->gjr", hidden_low, out_left, preferred_element_type=jnp.float32
    )
    slot_term = slot_term.astype(jnp.bfloat16).reshape(groups, places, owned, groups, slice_width)
    slot_term = slot_term.transpose(3, 1, 0, 2, 4)
    rank_term = jnp.concatenate([down_term, value_term], axis=2).astype(jnp.bfloat16)
    rank_term = rank_term.reshape(groups, places, owned, 2 * rank).transpose(1, 0, 2, 3)
    rank_term = jnp.broadcast_to(rank_term, (groups,) + rank_term.shape)
    third = jnp.concatenate([slot_term, rank_term], axis=4)
    third = lax.dynamic_update_slice_in_dim(
        jnp.zeros((groups, ring) + third.shape[2:], jnp.bfloat16), third, group * places, 1
    )
    third = exchange(third)
    third = lax.dynamic_index_in_dim(third, place // places, 0, keepdims=False)
    third = jnp.sum(third.astype(jnp.float32), axis=0)
    down_own = third[..., slice_width : slice_width + rank].astype(jnp.bfloat16)
    value_own = third[..., slice_width + rank :].astype(jnp.bfloat16)
    slot_grads_own = (
        third[..., :slice_width]
        + jnp.einsum("gjr,jdr->gjd", down_own, in_left, preferred_element_type=jnp.float32)
    ).astype(jnp.bfloat16)
    shift_part = jnp.sum(slot_grads_own.astype(jnp.float32) * slot_inputs, axis=2)
    stats = jnp.stack([*split(peak), *split(total), *split(shift_part)], axis=2)
    stats = jnp.pad(stats, ((0, 0), (0, 0), (0, STATS - 6)))
    fourth = jnp.concatenate([slot_grads_own, stats], axis=2)[:, None]
    fourth = exchange(jnp.broadcast_to(fourth, (groups, ring) + fourth.shape[2:]))
    slot_grads = fourth[..., :slice_width].transpose(1, 2, 0, 3).reshape(slots, width)
    stats = fourth[..., slice_width:].astype(jnp.float32).reshape(groups, slots, STATS)
    slot_peak = stats[0, :, 0] + stats[0, :, 1]
    slot_total = stats[0, :, 2] + stats[0, :, 3]
    shift_back = jnp.sum(stats[:, :, 4] + stats[:, :, 5], axis=0)

    dispatch = jnp.exp(logits - slot_peak) / slot_total
    dispatch_low = dispatch.astype(jnp.bfloat16)
    weight_grad = dot_last(image_rows, slot_grads)
    dispatch_logit = dispatch * (weight_grad - shift_back)
    mixing_grad = dot_last(cot_rows, saved_outputs)
    combine_logit = combine * (mixing_grad - jnp.sum(combine * mixing_grad, axis=1, keepdims=True))
    logit_grad = (dispatch_logit + combine_logit).astype(jnp.bfloat16)
    token_grad = (
        jnp.dot(dispatch_low, slot_grads, preferred_element_type=jnp.float32)
        + dot_last(logit_grad, router)
    ).astype(jnp.bfloat16)
    grad_in_right = jnp.einsum(
        "gjr,gjf->jrf", up_low, preact_grad, preferred_element_type=jnp.float32
    ).astype(jnp.bfloat16)
    grad_out_left = jnp.einsum(
        "gjf,gjr->jfr", hidden_low, back_low, preferred_element_type=jnp.float32
    ).astype(jnp.bfloat16)
    grad_in_left = jnp.einsum(
        "gjd,gjr->jdr", inputs_own, down_own, preferred_element_type=jnp.float32
    ).astype(jnp.bfloat16)
    grad_out_right = jnp.einsum(
        "gjr,gjd->jrd", value_own, grads_own, preferred_element_type=jnp.float32
    ).astype(jnp.bfloat16)
    return (token_grad[None], grad_in_left, grad_in_right, grad_out_left, grad_out_right)


def dot_plain(left, right):
    return jnp.dot(left, right, preferred_element_type=jnp.float32)


def halves(value):
    high = value.astype(jnp.bfloat16).astype(jnp.float32)
    low = (value - high).astype(jnp.bfloat16).astype(jnp.float32)
    return high, low


def in_lanes(columns, shape):
    lane = lax.broadcasted_iota(jnp.int32, shape, len(shape) - 1)
    out = jnp.zeros(shape, jnp.float32)
    for number, column in enumerate(columns):
        out = jnp.where(lane == number, column, out)
    return out


def own_block(value, owned):
    rows, rank = value.shape
    wide = jnp.concatenate([value] * owned, axis=1)
    shape = (rows, owned * rank)
    block = lax.broadcasted_iota(jnp.int32, shape, 1) // rank
    expert = lax.broadcasted_iota(jnp.int32, shape, 0) % owned
    return jnp.where(block == expert, wide, 0.0).astype(jnp.bfloat16)


def from_own_block(value, owned):
    rows, wide = value.shape
    rank = wide // owned
    block = lax.broadcasted_iota(jnp.int32, value.shape, 1) // rank
    expert = lax.broadcasted_iota(jnp.int32, value.shape, 0) % owned
    kept = jnp.where(block == expert, value, 0.0)
    out = kept[:, :rank]
    for number in range(1, owned):
        out = out + kept[:, number * rank : (number + 1) * rank]
    return out


def sums_kernel(
    owned,
    groups,
    tokens_far,
    cotangent_far,
    router_far,
    first,
    logits_out,
    combine_out,
    tokens,
    cotangent,
    router,
    arrived,
):
    ring = first.shape[0] // groups
    copies = [
        pltpu.make_async_copy(far, near, arrived.at[number])
        for number, (far, near) in enumerate(
            [(router_far, router), (tokens_far, tokens), (cotangent_far, cotangent)]
        )
    ]
    for copy in copies:
        copy.start()
    copies[0].wait()
    copies[1].wait()
    image_rows = tokens[...]
    logits = dot_last(router[...], image_rows)
    high, low = halves(jnp.max(logits, axis=1, keepdims=True))
    near = jnp.exp(logits - (high + low))
    total_high, total_low = halves(jnp.sum(near, axis=1, keepdims=True))
    spread = jnp.exp(logits - jnp.max(logits, axis=0, keepdims=True))
    combine = spread / jnp.sum(spread, axis=0, keepdims=True)
    logits_out[...] = logits
    combine_out[...] = combine
    stats = in_lanes([high, low, total_high, total_low], (logits.shape[0], STATS))
    stats = stats.astype(jnp.bfloat16)
    inputs = dot_plain(near.astype(jnp.bfloat16), image_rows).astype(jnp.bfloat16)
    copies[2].wait()
    grads = dot_plain(combine.astype(jnp.bfloat16), cotangent[...]).astype(jnp.bfloat16)
    width = inputs.shape[1] // groups
    places = ring // groups
    for group in range(groups):
        for half in range(groups):
            columns = slice(half * width, (half + 1) * width)
            for place in range(places):
                start = (group * places + place) * owned
                rows = slice(start, start + owned)
                block = group * ring + half * places + place
                first[block, :, :width] = inputs[rows, columns]
                first[block, :, width : 2 * width] = grads[rows, columns]
                first[block, :, 2 * width :] = stats[rows, :]


def mixing_kernel(cotangent, saved, combine, *rest):
    *_, out_left, in_right, out, out_left_near, in_right_near = rest
    out_left_near[...] = out_left[...]
    in_right_near[...] = in_right[...]
    mixing = dot_last(saved[...], cotangent[...])
    weights = combine[...]
    out[...] = weights * (mixing - jnp.sum(weights * mixing, axis=0, keepdims=True))


def owner_kernel(groups, width, first, second, across):
    ring = first.shape[0] // groups
    owned = first.shape[1]
    inputs, grads, stats_rows = [], [], []
    for group in range(groups):
        rows = slice(group * ring, (group + 1) * ring)
        stats = first[rows, :, 2 * width :].astype(jnp.float32)
        peaks = stats[:, :, 0:1] + stats[:, :, 1:2]
        totals = stats[:, :, 2:3] + stats[:, :, 3:4]
        peak = jnp.max(peaks, axis=0)
        scale = jnp.exp(peaks - peak[None])
        total = jnp.sum(scale * totals, axis=0)
        scale = scale / total[None]
        inputs.append(jnp.sum(first[rows, :, :width].astype(jnp.float32) * scale, axis=0))
        grads.append(jnp.sum(first[rows, :, width : 2 * width].astype(jnp.float32), axis=0))
        stats_rows.append(in_lanes([*halves(peak), *halves(total)], (owned, STATS)))
    inputs, grads = jnp.concatenate(inputs, axis=0), jnp.concatenate(grads, axis=0)
    stats = jnp.concatenate(stats_rows, axis=0)
    high, low = halves(inputs)
    block = jnp.concatenate([high, grads], axis=1).astype(jnp.bfloat16)
    for place in range(second.shape[0]):
        second[place] = block
    across[...] = jnp.concatenate([high, grads, low, stats], axis=1).astype(jnp.bfloat16)


def rank_kernel(across, in_left, out_right, ranks, inputs_out, lows_out, stats_out):
    owned, rank, width = in_left.shape
    inputs_low, grads_low = across[:, :width], across[:, width : 2 * width]
    inputs_out[...] = inputs_low.astype(jnp.float32) + across[
        :, 2 * width : 3 * width
    ].astype(jnp.float32)
    stats_out[...] = across[:, 3 * width :].astype(jnp.float32)
    lows_out[0] = inputs_low
    lows_out[1] = grads_low
    up = dot_last(inputs_low, in_left[...].reshape(owned * rank, width))
    back = dot_last(grads_low, out_right[...].reshape(owned * rank, width))
    block = [*halves(from_own_block(up, owned)), *halves(from_own_block(back, owned))]
    block = jnp.concatenate(block, axis=1).astype(jnp.bfloat16)
    for place in range(ranks.shape[0]):
        ranks[place] = block


def hidden_kernel(
    groups,
    second,
    factors,
    base_in,
    base_out,
    in_right,
    out_left,
    third,
    pair_out,
    ranks_out,
):
    members, rank, hidden = in_right.shape
    rows = second.shape[1]
    owned = rows // groups
    places = members // owned
    width = base_in.shape[1] // groups
    ring = third.shape[0] // groups
    group = lax.axis_index("dp")

    def gathered(columns):
        taken = [
            second[half * places : (half + 1) * places, :, columns].astype(jnp.float32)
            for half in range(groups)
        ]
        return [part.reshape(places * rows, part.shape[2]) for part in taken]

    def low_rank(value, table):
        value = value.astype(jnp.float32)
        taken = []
        for place in range(places):
            own = own_block(value[place * rows : (place + 1) * rows], owned)
            part = table[place * owned : (place + 1) * owned].reshape(owned * rank, hidden)
            taken.append(dot_plain(own, part))
        return jnp.concatenate(taken, axis=0)

    def to_rank(value, table):
        taken = []
        for place in range(places):
            part = table[place * owned : (place + 1) * owned].reshape(owned * rank, hidden)
            wide = dot_last(value[place * rows : (place + 1) * rows].astype(jnp.bfloat16), part)
            taken.append(from_own_block(wide, owned))
        return jnp.concatenate(taken, axis=0)

    ranks = jnp.zeros((places * rows, 4 * rank), jnp.float32)
    for half in range(groups):
        part = factors[pl.ds(half * ring + group * places, places)].astype(jnp.float32)
        ranks = ranks + part.reshape(ranks.shape)
    up = (ranks[:, :rank] + ranks[:, rank : 2 * rank]).astype(jnp.bfloat16)
    back = (ranks[:, 2 * rank : 3 * rank] + ranks[:, 3 * rank :]).astype(jnp.bfloat16)
    preact = low_rank(up, in_right)
    for half, part in enumerate(gathered(slice(0, width))):
        columns = slice(half * width, (half + 1) * width)
        preact = preact + dot_last(part.astype(jnp.bfloat16), base_in[:, columns])
    hidden_grad = low_rank(back, out_left)
    for half, part in enumerate(gathered(slice(width, 2 * width))):
        columns = slice(half * width, (half + 1) * width)
        hidden_grad = hidden_grad + dot_last(part.astype(jnp.bfloat16), base_out[:, columns])
    root = 0.7978845608028654
    bent = jnp.tanh(root * (preact + 0.044715 * (preact * preact * preact)))
    hidden_value = 0.5 * preact * (1.0 + bent)
    slope = 0.5 * (1.0 + bent) + 0.5 * preact * (1.0 - bent * bent) * (
        root * (1.0 + 3.0 * 0.044715 * (preact * preact))
    )
    hidden_low = hidden_value.astype(jnp.bfloat16).astype(jnp.float32)
    preact_grad = (hidden_grad * slope).astype(jnp.bfloat16).astype(jnp.float32)
    pair_out[0] = preact_grad
    pair_out[1] = hidden_low
    ranks_out[0] = up.astype(jnp.float32)
    ranks_out[1] = back.astype(jnp.float32)
    slot_term = dot_plain(preact_grad.astype(jnp.bfloat16), base_in[...]).astype(jnp.bfloat16)
    down = to_rank(preact_grad, in_right)
    value = to_rank(hidden_low, out_left)
    ranks = jnp.concatenate([down, value], axis=1).astype(jnp.bfloat16)
    third[...] = jnp.zeros(third.shape, jnp.bfloat16)
    for half in range(groups):
        columns = slice(half * width, (half + 1) * width)
        for place in range(places):
            taken = slice(place * rows, (place + 1) * rows)
            block = half * ring + group * places + place
            third[block, :, :width] = slot_term[taken, columns]
            third[block, :, width:] = ranks[taken]


def outer_kernel(owned, left_rows, right_rows, *outs):
    rows = left_rows.shape[1] // (outs[0].shape[0] // owned)
    for number, out in enumerate(outs):
        for place in range(out.shape[0] // owned):
            taken = slice(place * rows, (place + 1) * rows)
            own = own_block(left_rows[number, taken], owned)
            product = dot_first(own, right_rows[number, taken].astype(jnp.bfloat16))
            out[place * owned : (place + 1) * owned] = product.astype(jnp.bfloat16).reshape(
                (owned,) + out.shape[1:]
            )


def finish_kernel(groups, ring, third, in_left, inputs, stats, fourth, ranks_out):
    owned, rank, width = in_left.shape
    sender = lax.axis_index("half")
    summed = jnp.sum(third[pl.ds(sender * ring, ring)].astype(jnp.float32), axis=0)
    ranks = summed[:, width:].astype(jnp.bfloat16).astype(jnp.float32)
    ranks_out[0] = ranks[:, :rank]
    ranks_out[1] = ranks[:, rank:]
    down = own_block(ranks[:, :rank], owned)
    grads = summed[:, :width] + dot_plain(down, in_left[...].reshape(owned * rank, width))
    grads = grads.astype(jnp.bfloat16).astype(jnp.float32)
    high, low = halves(jnp.sum(grads * inputs[...], axis=1, keepdims=True))
    lane = lax.broadcasted_iota(jnp.int32, stats.shape, 1)
    tail = jnp.where(lane == 4, high, jnp.where(lane == 5, low, stats[...]))
    block = jnp.concatenate([grads, tail], axis=1).astype(jnp.bfloat16)
    for group in range(groups):
        rows = block[group * owned : (group + 1) * owned]
        for place in range(ring):
            fourth[group * ring + place] = rows


def tokens_kernel(groups, fourth, tokens, router, logits, mixing, out):
    blocks, owned, _ = fourth.shape
    ring = blocks // groups
    width = tokens.shape[1] // groups

    def rows(half, columns):
        taken = [
            fourth[half * ring + place, :, columns].astype(jnp.float32) for place in range(ring)
        ]
        return jnp.concatenate(taken, axis=0)

    grads = jnp.concatenate([rows(half, slice(0, width)) for half in range(groups)], axis=1)
    grads = grads.astype(jnp.bfloat16)
    stats = [rows(half, slice(width, width + STATS)) for half in range(groups)]
    peak = stats[0][:, 0:1] + stats[0][:, 1:2]
    total = stats[0][:, 2:3] + stats[0][:, 3:4]
    shift = functools.reduce(jnp.add, [part[:, 4:5] + part[:, 5:6] for part in stats])
    dispatch = jnp.exp(logits[...] - peak) / total
    weight_grad = dot_last(grads, tokens[...])
    logit_grad = dispatch * (weight_grad - shift) + mixing[...]
    left = jnp.concatenate([dispatch, logit_grad], axis=0).astype(jnp.bfloat16)
    right = jnp.concatenate([grads, router[...]], axis=0)
    out[...] = dot_first(left, right).astype(jnp.bfloat16)


def to_home(block):
    places = lax.axis_size("place")
    ring = 2 * places
    pairs = [
        (group * ring + half * places + place, half * ring + group * places + place)
        for group in range(2)
        for half in range(2)
        for place in range(places)
    ]
    return lax.ppermute(block, BOTH, pairs)


def call(kernel, outs, args, flops, far=(), scratch=(), grant=24):
    size = sum(array.size * array.dtype.itemsize for array in args)
    size += sum(out.size * out.dtype.itemsize for out in outs)
    spaces = [pltpu.HBM if number in far else pltpu.VMEM for number in range(len(args))]
    return pl.pallas_call(
        kernel,
        out_shape=outs,
        in_specs=[pl.BlockSpec(memory_space=space) for space in spaces],
        out_specs=[pl.BlockSpec(memory_space=pltpu.VMEM) for _ in outs],
        scratch_shapes=scratch,
        cost_estimate=pl.CostEstimate(flops=flops, bytes_accessed=size, transcendentals=0),
        compiler_params=pltpu.CompilerParams(vmem_limit_bytes=grant * 2**20),
    )(*args)


def array(dtype, *shape):
    return jax.ShapeDtypeStruct(shape, dtype)


def local(
    tokens,
    cotangent,
    router,
    slot_outputs,
    base_in,
    base_out,
    in_left,
    in_right,
    out_left,
    out_right,
):
    groups, ring = lax.axis_size("dp"), lax.axis_size(SEQ)
    devices = groups * ring
    _, count, width = tokens.shape
    slots = router.shape[1]
    owned, slice_width, rank = in_left.shape
    members, _, hidden = in_right.shape
    rows = groups * owned
    if groups != 2 or ring % 2 or slice_width % 128 or rows % 8 or members % owned:
        return local_plain(
            tokens,
            cotangent,
            router,
            slot_outputs,
            base_in,
            base_out,
            in_left,
            in_right,
            out_left,
            out_right,
        )
    low, full = jnp.bfloat16, jnp.float32
    image_rows, cot_rows, saved = tokens[0], cotangent[0], slot_outputs[0]
    router, base_in = router.T, base_in.T
    in_left, out_left = in_left.swapaxes(1, 2), out_left.swapaxes(1, 2)
    first, logits, combine = call(
        functools.partial(sums_kernel, owned, groups),
        [
            array(low, devices, owned, 2 * slice_width + STATS),
            array(full, slots, count),
            array(full, slots, count),
        ],
        [image_rows, cot_rows, router],
        6 * count * slots * width,
        (0, 1, 2),
        [pltpu.VMEM((count, width), low)] * 2
        + [pltpu.VMEM((slots, width), low), pltpu.SemaphoreType.DMA((3,))],
        60,
    )
    first = lax.all_to_all(first, BOTH, 0, 0, tiled=True)
    mixing, out_left, in_right = call(
        mixing_kernel,
        [array(full, slots, count), array(low, *out_left.shape), array(low, *in_right.shape)],
        [cot_rows, saved, combine, out_right, base_out, out_left, in_right],
        2 * count * slots * width,
    )
    first, mixing, out_left, in_right = lax.optimization_barrier(
        (first, mixing, out_left, in_right)
    )
    second, across = call(
        functools.partial(owner_kernel, groups, slice_width),
        [
            array(low, ring, rows, 2 * slice_width),
            array(low, rows, 3 * slice_width + STATS),
        ],
        [first],
        0,
    )
    across = to_home(across)
    second = lax.all_to_all(second, SEQ, 0, 0, tiled=True)
    factors, inputs, lows, stats = call(
        rank_kernel,
        [
            array(low, devices, rows, 4 * rank),
            array(full, rows, slice_width),
            array(low, 2, rows, slice_width),
            array(full, rows, STATS),
        ],
        [across, in_left, out_right],
        4 * rows * owned * rank * slice_width,
    )
    factors = lax.all_to_all(factors, BOTH, 0, 0, tiled=True)
    total_rows = groups * members
    third, pair, ranks = call(
        functools.partial(hidden_kernel, groups),
        [
            array(low, devices, rows, slice_width + 2 * rank),
            array(full, 2, total_rows, hidden),
            array(full, 2, total_rows, rank),
        ],
        [second, factors, base_in, base_out, in_right, out_left],
        6 * total_rows * hidden * (width + owned * rank),
    )
    third = lax.all_to_all(third, BOTH, 0, 0, tiled=True)
    grad_in_right, grad_out_left = call(
        functools.partial(outer_kernel, owned),
        [array(low, members, rank, hidden)] * 2,
        [ranks, pair],
        4 * members * rank * hidden * rows,
    )
    fourth, ranks = call(
        functools.partial(finish_kernel, groups, ring),
        [array(low, devices, owned, slice_width + STATS), array(full, 2, rows, rank)],
        [third, in_left, inputs, stats],
        2 * rows * owned * rank * slice_width,
    )
    fourth = lax.all_to_all(fourth, BOTH, 0, 0, tiled=True)
    grad_in_left, grad_out_right = call(
        functools.partial(outer_kernel, owned),
        [array(low, owned, rank, slice_width)] * 2,
        [ranks, lows],
        4 * owned * rank * slice_width * rows,
    )
    (token_grad,) = call(
        functools.partial(tokens_kernel, groups),
        [array(low, count, width)],
        [fourth, image_rows, router, logits, mixing],
        6 * count * slots * width,
    )
    return (
        token_grad[None],
        grad_in_left.swapaxes(1, 2),
        grad_in_right,
        grad_out_left.swapaxes(1, 2),
        grad_out_right,
    )


def solution(mesh):
    groups, ring = mesh.shape["dp"], mesh.shape["seq"]
    split = mesh.devices.reshape(groups, groups, ring // groups)
    mesh = jax.sharding.Mesh(split, BOTH)
    in_specs = (
        P("dp", SEQ, None),
        P("dp", SEQ, None),
        P(),
        P("dp", None, None),
        P(None, SEQ),
        P(SEQ, None),
        P(SEQ, "dp", None),
        P("dp", None, SEQ),
        P("dp", SEQ, None),
        P(SEQ, None, "dp"),
    )
    out_specs = (
        P("dp", SEQ, None),
        P(SEQ, "dp", None),
        P("dp", None, SEQ),
        P("dp", SEQ, None),
        P(SEQ, None, "dp"),
    )
    return jax.shard_map(local, mesh=mesh, in_specs=in_specs, out_specs=out_specs, check_vma=False)
```

```python
import functools

import jax
import jax.numpy as jnp
from jax import lax
from jax.experimental import pallas as pl
from jax.experimental.pallas import tpu as pltpu
from jax.sharding import PartitionSpec as P

SEQ = ("half", "place")
BOTH = ("dp", *SEQ)
HALF = ("dp", "place")
STATS = 128


def gelu_backward(preact, upstream):
    return jax.vjp(jax.nn.gelu, preact)[1](upstream)[0]


def dot_first(left, right):
    return lax.dot_general(
        left, right, (((0,), (0,)), ((), ())), preferred_element_type=jnp.float32
    )


def dot_last(left, right):
    return lax.dot_general(
        left, right, (((1,), (1,)), ((), ())), preferred_element_type=jnp.float32
    )


def split(value):
    high = lax.reduce_precision(value, 8, 7)
    low = lax.reduce_precision(value - high, 8, 7)
    return high.astype(jnp.bfloat16), low.astype(jnp.bfloat16)


def joined(high, low):
    return high.astype(jnp.float32) + low.astype(jnp.float32)


def exchange(blocks):
    flat = blocks.reshape((-1,) + blocks.shape[2:])
    return lax.all_to_all(flat, BOTH, 0, 0, tiled=True).reshape(blocks.shape)


def local_plain(
    tokens,
    cotangent,
    router,
    slot_outputs,
    base_in,
    base_out,
    in_left,
    in_right,
    out_left,
    out_right,
):
    groups, ring = lax.axis_size("dp"), lax.axis_size(SEQ)
    image_rows = tokens[0]
    cot_rows = cotangent[0]
    saved_outputs = slot_outputs[0]
    width = image_rows.shape[1]
    slots = router.shape[1]
    owned, slice_width, rank = in_left.shape
    members = in_right.shape[0]
    places = members // owned
    group, place = lax.axis_index("dp"), lax.axis_index(SEQ)

    logits = jnp.dot(image_rows, router, preferred_element_type=jnp.float32)
    peak_high, peak_low = split(jnp.max(logits, axis=0))
    near = jnp.exp(logits - joined(peak_high, peak_low))
    total_high, total_low = split(jnp.sum(near, axis=0))
    combine = jax.nn.softmax(logits, axis=1)
    sums = jnp.stack(
        [
            dot_first(near.astype(jnp.bfloat16), image_rows),
            dot_first(combine.astype(jnp.bfloat16), cot_rows),
        ],
        axis=1,
    ).astype(jnp.bfloat16)
    sums = sums.reshape(ring, owned, 2, groups, slice_width).transpose(3, 0, 1, 2, 4)
    sums = sums.reshape(groups, ring, owned, 2 * slice_width)
    stats = jnp.stack([peak_high, peak_low, total_high, total_low], axis=1)
    stats = jnp.pad(stats, ((0, 0), (0, STATS - 4))).reshape(1, ring, owned, STATS)
    stats = jnp.broadcast_to(stats, (groups, ring, owned, STATS))
    first = exchange(jnp.concatenate([sums, stats], axis=3))

    tail = 2 * slice_width
    peaks = joined(first[..., tail], first[..., tail + 1])
    totals = joined(first[..., tail + 2], first[..., tail + 3])
    peak = jnp.max(peaks, axis=1)
    near_scale = jnp.exp(peaks - peak[:, None])
    total = jnp.sum(near_scale * totals, axis=1)
    near_scale = near_scale / total[:, None]
    parts = first[..., :tail].astype(jnp.float32)
    slot_inputs = jnp.sum(parts[..., :slice_width] * near_scale[..., None], axis=1)
    inputs_own = slot_inputs.astype(jnp.bfloat16)
    grads_own = jnp.sum(parts[..., slice_width:], axis=1).astype(jnp.bfloat16)
    up_part = jnp.einsum("gjd,jdr->gjr", inputs_own, in_left, preferred_element_type=jnp.float32)
    back_part = jnp.einsum("gjd,jrd->gjr", grads_own, out_right, preferred_element_type=jnp.float32)
    second = jnp.concatenate(
        [inputs_own, grads_own, *split(up_part), *split(back_part)], axis=2
    )
    second = exchange(jnp.broadcast_to(second, (groups, ring) + second.shape))
    second = lax.dynamic_slice_in_dim(second, group * places, places, 1)

    def gathered(start):
        piece = second[..., start : start + slice_width]
        return piece.transpose(2, 1, 3, 0, 4).reshape(groups * members, width)

    def ranks(start):
        piece = joined(
            second[..., start : start + rank], second[..., start + rank : start + 2 * rank]
        )
        piece = jnp.sum(piece, axis=0).transpose(1, 0, 2, 3)
        return piece.reshape(groups, members, rank).astype(jnp.bfloat16)

    inputs_low, grads_low = gathered(0), gathered(slice_width)
    up_low, back_low = ranks(tail), ranks(tail + 2 * rank)
    hidden = base_in.shape[1]
    preact = jnp.dot(inputs_low, base_in, preferred_element_type=jnp.float32).reshape(
        groups, members, hidden
    ) + jnp.einsum("gjr,jrf->gjf", up_low, in_right, preferred_element_type=jnp.float32)
    hidden_low = jax.nn.gelu(preact).astype(jnp.bfloat16)
    hidden_grad = dot_last(grads_low, base_out).reshape(groups, members, hidden) + jnp.einsum(
        "gjr,jfr->gjf", back_low, out_left, preferred_element_type=jnp.float32
    )
    preact_grad = gelu_backward(preact, hidden_grad).astype(jnp.bfloat16)
    slot_term = dot_last(preact_grad.reshape(groups * members, hidden), base_in)
    down_term = jnp.einsum(
        "gjf,jrf->gjr", preact_grad, in_right, preferred_element_type=jnp.float32
    )
    value_term = jnp.einsum(
        "gjf,jfr->gjr", hidden_low, out_left, preferred_element_type=jnp.float32
    )
    slot_term = slot_term.astype(jnp.bfloat16).reshape(groups, places, owned, groups, slice_width)
    slot_term = slot_term.transpose(3, 1, 0, 2, 4)
    rank_term = jnp.concatenate([down_term, value_term], axis=2).astype(jnp.bfloat16)
    rank_term = rank_term.reshape(groups, places, owned, 2 * rank).transpose(1, 0, 2, 3)
    rank_term = jnp.broadcast_to(rank_term, (groups,) + rank_term.shape)
    third = jnp.concatenate([slot_term, rank_term], axis=4)
    third = lax.dynamic_update_slice_in_dim(
        jnp.zeros((groups, ring) + third.shape[2:], jnp.bfloat16), third, group * places, 1
    )
    third = exchange(third)
    third = lax.dynamic_index_in_dim(third, place // places, 0, keepdims=False)
    third = jnp.sum(third.astype(jnp.float32), axis=0)
    down_own = third[..., slice_width : slice_width + rank].astype(jnp.bfloat16)
    value_own = third[..., slice_width + rank :].astype(jnp.bfloat16)
    slot_grads_own = (
        third[..., :slice_width]
        + jnp.einsum("gjr,jdr->gjd", down_own, in_left, preferred_element_type=jnp.float32)
    ).astype(jnp.bfloat16)
    shift_part = jnp.sum(slot_grads_own.astype(jnp.float32) * slot_inputs, axis=2)
    stats = jnp.stack([*split(peak), *split(total), *split(shift_part)], axis=2)
    stats = jnp.pad(stats, ((0, 0), (0, 0), (0, STATS - 6)))
    fourth = jnp.concatenate([slot_grads_own, stats], axis=2)[:, None]
    fourth = exchange(jnp.broadcast_to(fourth, (groups, ring) + fourth.shape[2:]))
    slot_grads = fourth[..., :slice_width].transpose(1, 2, 0, 3).reshape(slots, width)
    stats = fourth[..., slice_width:].astype(jnp.float32).reshape(groups, slots, STATS)
    slot_peak = stats[0, :, 0] + stats[0, :, 1]
    slot_total = stats[0, :, 2] + stats[0, :, 3]
    shift_back = jnp.sum(stats[:, :, 4] + stats[:, :, 5], axis=0)

    dispatch = jnp.exp(logits - slot_peak) / slot_total
    dispatch_low = dispatch.astype(jnp.bfloat16)
    weight_grad = dot_last(image_rows, slot_grads)
    dispatch_logit = dispatch * (weight_grad - shift_back)
    mixing_grad = dot_last(cot_rows, saved_outputs)
    combine_logit = combine * (mixing_grad - jnp.sum(combine * mixing_grad, axis=1, keepdims=True))
    logit_grad = (dispatch_logit + combine_logit).astype(jnp.bfloat16)
    token_grad = (
        jnp.dot(dispatch_low, slot_grads, preferred_element_type=jnp.float32)
        + dot_last(logit_grad, router)
    ).astype(jnp.bfloat16)
    grad_in_right = jnp.einsum(
        "gjr,gjf->jrf", up_low, preact_grad, preferred_element_type=jnp.float32
    ).astype(jnp.bfloat16)
    grad_out_left = jnp.einsum(
        "gjf,gjr->jfr", hidden_low, back_low, preferred_element_type=jnp.float32
    ).astype(jnp.bfloat16)
    grad_in_left = jnp.einsum(
        "gjd,gjr->jdr", inputs_own, down_own, preferred_element_type=jnp.float32
    ).astype(jnp.bfloat16)
    grad_out_right = jnp.einsum(
        "gjr,gjd->jrd", value_own, grads_own, preferred_element_type=jnp.float32
    ).astype(jnp.bfloat16)
    return (token_grad[None], grad_in_left, grad_in_right, grad_out_left, grad_out_right)


def dot_plain(left, right):
    return jnp.dot(left, right, preferred_element_type=jnp.float32)


def halves(value):
    high = value.astype(jnp.bfloat16).astype(jnp.float32)
    low = (value - high).astype(jnp.bfloat16).astype(jnp.float32)
    return high, low


def in_lanes(columns, shape):
    lane = lax.broadcasted_iota(jnp.int32, shape, len(shape) - 1)
    out = jnp.zeros(shape, jnp.float32)
    for number, column in enumerate(columns):
        out = jnp.where(lane == number, column, out)
    return out


def own_block(value, owned):
    rows, rank = value.shape
    wide = jnp.concatenate([value] * owned, axis=1)
    shape = (rows, owned * rank)
    block = lax.broadcasted_iota(jnp.int32, shape, 1) // rank
    expert = lax.broadcasted_iota(jnp.int32, shape, 0) % owned
    return jnp.where(block == expert, wide, 0.0).astype(jnp.bfloat16)


def from_own_block(value, owned):
    rows, wide = value.shape
    rank = wide // owned
    block = lax.broadcasted_iota(jnp.int32, value.shape, 1) // rank
    expert = lax.broadcasted_iota(jnp.int32, value.shape, 0) % owned
    kept = jnp.where(block == expert, value, 0.0)
    out = kept[:, :rank]
    for number in range(1, owned):
        out = out + kept[:, number * rank : (number + 1) * rank]
    return out


def sums_kernel(
    owned,
    groups,
    tokens_far,
    cotangent_far,
    router_far,
    first,
    logits_out,
    combine_out,
    tokens,
    cotangent,
    router,
    arrived,
):
    ring = first.shape[0] // groups
    copies = [
        pltpu.make_async_copy(far, near, arrived.at[number])
        for number, (far, near) in enumerate(
            [(router_far, router), (tokens_far, tokens), (cotangent_far, cotangent)]
        )
    ]
    for copy in copies:
        copy.start()
    copies[0].wait()
    copies[1].wait()
    image_rows = tokens[...]
    logits = dot_last(router[...], image_rows)
    high, low = halves(jnp.max(logits, axis=1, keepdims=True))
    near = jnp.exp(logits - (high + low))
    total_high, total_low = halves(jnp.sum(near, axis=1, keepdims=True))
    spread = jnp.exp(logits - jnp.max(logits, axis=0, keepdims=True))
    combine = spread / jnp.sum(spread, axis=0, keepdims=True)
    logits_out[...] = logits
    combine_out[...] = combine
    stats = in_lanes([high, low, total_high, total_low], (logits.shape[0], STATS))
    stats = stats.astype(jnp.bfloat16)
    inputs = dot_plain(near.astype(jnp.bfloat16), image_rows).astype(jnp.bfloat16)
    copies[2].wait()
    grads = dot_plain(combine.astype(jnp.bfloat16), cotangent[...]).astype(jnp.bfloat16)
    width = inputs.shape[1] // groups
    for group in range(groups):
        columns = slice(group * width, (group + 1) * width)
        for place in range(ring):
            rows = slice(place * owned, (place + 1) * owned)
            block = group * ring + place
            first[block, :, :width] = inputs[rows, columns]
            first[block, :, width : 2 * width] = grads[rows, columns]
            first[block, :, 2 * width :] = stats[rows, :]


def mixing_kernel(cotangent, saved, combine, *rest):
    *_, out_left, in_right, out, out_left_near, in_right_near = rest
    out_left_near[...] = out_left[...]
    in_right_near[...] = in_right[...]
    mixing = dot_last(saved[...], cotangent[...])
    weights = combine[...]
    out[...] = weights * (mixing - jnp.sum(weights * mixing, axis=0, keepdims=True))


def owner_kernel(groups, first, in_left, out_right, second, inputs_out, lows_out, stats_out):
    ring = first.shape[0] // groups
    owned, rank, width = in_left.shape
    inputs, grads, stats_rows = [], [], []
    for group in range(groups):
        rows = slice(group * ring, (group + 1) * ring)
        stats = first[rows, :, 2 * width :].astype(jnp.float32)
        peaks = stats[:, :, 0:1] + stats[:, :, 1:2]
        totals = stats[:, :, 2:3] + stats[:, :, 3:4]
        peak = jnp.max(peaks, axis=0)
        scale = jnp.exp(peaks - peak[None])
        total = jnp.sum(scale * totals, axis=0)
        scale = scale / total[None]
        inputs.append(jnp.sum(first[rows, :, :width].astype(jnp.float32) * scale, axis=0))
        grads.append(jnp.sum(first[rows, :, width : 2 * width].astype(jnp.float32), axis=0))
        stats_rows.append(in_lanes([*halves(peak), *halves(total)], (owned, STATS)))
    inputs, grads = jnp.concatenate(inputs, axis=0), jnp.concatenate(grads, axis=0)
    inputs_out[...] = inputs
    stats_out[...] = jnp.concatenate(stats_rows, axis=0)
    inputs_low, grads_low = inputs.astype(jnp.bfloat16), grads.astype(jnp.bfloat16)
    lows_out[0] = inputs_low
    lows_out[1] = grads_low
    up = dot_last(inputs_low, in_left[...].reshape(owned * rank, width))
    back = dot_last(grads_low, out_right[...].reshape(owned * rank, width))
    ranks = [*halves(from_own_block(up, owned)), *halves(from_own_block(back, owned))]
    ranks = jnp.concatenate(ranks, axis=1).astype(jnp.bfloat16)
    block = jnp.concatenate([inputs_low, grads_low, ranks], axis=1)
    second[...] = block


def pack_kernel(blocks, out):
    for group in range(out.shape[0]):
        for place in range(out.shape[1]):
            out[group, place] = blocks[group]


def hidden_kernel(
    groups,
    second,
    base_in,
    base_out,
    in_right,
    out_left,
    third,
    pair_out,
    ranks_out,
):
    members, rank, hidden = in_right.shape
    rows = second.shape[1]
    owned = rows // groups
    places = members // owned
    width = base_in.shape[1] // groups

    def gathered(columns):
        taken = [
            second[half * places : (half + 1) * places, :, columns].astype(jnp.float32)
            for half in range(groups)
        ]
        return [part.reshape(places * rows, part.shape[2]) for part in taken]

    def low_rank(value, table):
        value = value.astype(jnp.float32)
        taken = []
        for place in range(places):
            own = own_block(value[place * rows : (place + 1) * rows], owned)
            part = table[place * owned : (place + 1) * owned].reshape(owned * rank, hidden)
            taken.append(dot_plain(own, part))
        return jnp.concatenate(taken, axis=0)

    def to_rank(value, table):
        taken = []
        for place in range(places):
            part = table[place * owned : (place + 1) * owned].reshape(owned * rank, hidden)
            wide = dot_last(value[place * rows : (place + 1) * rows].astype(jnp.bfloat16), part)
            taken.append(from_own_block(wide, owned))
        return jnp.concatenate(taken, axis=0)

    ranks = functools.reduce(jnp.add, gathered(slice(2 * width, 2 * width + 4 * rank)))
    up = (ranks[:, :rank] + ranks[:, rank : 2 * rank]).astype(jnp.bfloat16)
    back = (ranks[:, 2 * rank : 3 * rank] + ranks[:, 3 * rank :]).astype(jnp.bfloat16)
    preact = low_rank(up, in_right)
    for half, part in enumerate(gathered(slice(0, width))):
        columns = slice(half * width, (half + 1) * width)
        preact = preact + dot_last(part.astype(jnp.bfloat16), base_in[:, columns])
    hidden_grad = low_rank(back, out_left)
    for half, part in enumerate(gathered(slice(width, 2 * width))):
        columns = slice(half * width, (half + 1) * width)
        hidden_grad = hidden_grad + dot_last(part.astype(jnp.bfloat16), base_out[:, columns])
    root = 0.7978845608028654
    bent = jnp.tanh(root * (preact + 0.044715 * (preact * preact * preact)))
    hidden_value = 0.5 * preact * (1.0 + bent)
    slope = 0.5 * (1.0 + bent) + 0.5 * preact * (1.0 - bent * bent) * (
        root * (1.0 + 3.0 * 0.044715 * (preact * preact))
    )
    hidden_low = hidden_value.astype(jnp.bfloat16).astype(jnp.float32)
    preact_grad = (hidden_grad * slope).astype(jnp.bfloat16).astype(jnp.float32)
    pair_out[0] = preact_grad
    pair_out[1] = hidden_low
    ranks_out[0] = up.astype(jnp.float32)
    ranks_out[1] = back.astype(jnp.float32)
    slot_term = dot_plain(preact_grad.astype(jnp.bfloat16), base_in[...]).astype(jnp.bfloat16)
    down = to_rank(preact_grad, in_right)
    value = to_rank(hidden_low, out_left)
    ranks = jnp.concatenate([down, value], axis=1).astype(jnp.bfloat16)
    for half in range(groups):
        columns = slice(half * width, (half + 1) * width)
        for place in range(places):
            taken = slice(place * rows, (place + 1) * rows)
            block = half * places + place
            third[block, :, :width] = slot_term[taken, columns]
            third[block, :, width:] = ranks[taken]


def outer_kernel(owned, left_rows, right_rows, *outs):
    rows = left_rows.shape[1] // (outs[0].shape[0] // owned)
    for number, out in enumerate(outs):
        for place in range(out.shape[0] // owned):
            taken = slice(place * rows, (place + 1) * rows)
            own = own_block(left_rows[number, taken], owned)
            product = dot_first(own, right_rows[number, taken].astype(jnp.bfloat16))
            out[place * owned : (place + 1) * owned] = product.astype(jnp.bfloat16).reshape(
                (owned,) + out.shape[1:]
            )


def halves_kernel(third, own, other):
    places = third.shape[0] // 2
    here = lax.axis_index("half")
    for out, group in ((own, here), (other, 1 - here)):
        taken = third[pl.ds(group * places, places)].astype(jnp.float32)
        out[...] = jnp.sum(taken, axis=0)


def finish_kernel(groups, ring, own, others, in_left, inputs, stats, fourth, ranks_out):
    owned, rank, width = in_left.shape
    summed = own[...] + others[1 - lax.axis_index("half")]
    ranks = summed[:, width:].astype(jnp.bfloat16).astype(jnp.float32)
    ranks_out[0] = ranks[:, :rank]
    ranks_out[1] = ranks[:, rank:]
    down = own_block(ranks[:, :rank], owned)
    grads = summed[:, :width] + dot_plain(down, in_left[...].reshape(owned * rank, width))
    grads = grads.astype(jnp.bfloat16).astype(jnp.float32)
    high, low = halves(jnp.sum(grads * inputs[...], axis=1, keepdims=True))
    lane = lax.broadcasted_iota(jnp.int32, stats.shape, 1)
    tail = jnp.where(lane == 4, high, jnp.where(lane == 5, low, stats[...]))
    block = jnp.concatenate([grads, tail], axis=1).astype(jnp.bfloat16)
    for group in range(groups):
        rows = block[group * owned : (group + 1) * owned]
        for place in range(ring):
            fourth[group * ring + place] = rows


def tokens_kernel(groups, fourth, tokens, router, logits, mixing, out):
    blocks, owned, _ = fourth.shape
    ring = blocks // groups
    width = tokens.shape[1] // groups

    def rows(half, columns):
        taken = [
            fourth[half * ring + place, :, columns].astype(jnp.float32) for place in range(ring)
        ]
        return jnp.concatenate(taken, axis=0)

    grads = jnp.concatenate([rows(half, slice(0, width)) for half in range(groups)], axis=1)
    grads = grads.astype(jnp.bfloat16)
    stats = [rows(half, slice(width, width + STATS)) for half in range(groups)]
    peak = stats[0][:, 0:1] + stats[0][:, 1:2]
    total = stats[0][:, 2:3] + stats[0][:, 3:4]
    shift = functools.reduce(jnp.add, [part[:, 4:5] + part[:, 5:6] for part in stats])
    dispatch = jnp.exp(logits[...] - peak) / total
    weight_grad = dot_last(grads, tokens[...])
    logit_grad = dispatch * (weight_grad - shift) + mixing[...]
    left = jnp.concatenate([dispatch, logit_grad], axis=0).astype(jnp.bfloat16)
    right = jnp.concatenate([grads, router[...]], axis=0)
    out[...] = dot_first(left, right).astype(jnp.bfloat16)


def to_group(block, groups):
    places = lax.axis_size("place")
    blocks = lax.all_gather(block, "half", axis=0)
    (blocks,) = call(
        pack_kernel, [array(block.dtype, groups, places, *block.shape)], [blocks], 0
    )
    blocks = blocks.reshape(groups * places, *block.shape)
    return lax.all_to_all(blocks, HALF, 0, 0, tiled=True)


def call(kernel, outs, args, flops, far=(), scratch=(), grant=24):
    size = sum(array.size * array.dtype.itemsize for array in args)
    size += sum(out.size * out.dtype.itemsize for out in outs)
    spaces = [pltpu.HBM if number in far else pltpu.VMEM for number in range(len(args))]
    return pl.pallas_call(
        kernel,
        out_shape=outs,
        in_specs=[pl.BlockSpec(memory_space=space) for space in spaces],
        out_specs=[pl.BlockSpec(memory_space=pltpu.VMEM) for _ in outs],
        scratch_shapes=scratch,
        cost_estimate=pl.CostEstimate(flops=flops, bytes_accessed=size, transcendentals=0),
        compiler_params=pltpu.CompilerParams(vmem_limit_bytes=grant * 2**20),
    )(*args)


def array(dtype, *shape):
    return jax.ShapeDtypeStruct(shape, dtype)


def local(
    tokens,
    cotangent,
    router,
    slot_outputs,
    base_in,
    base_out,
    in_left,
    in_right,
    out_left,
    out_right,
):
    groups, ring = lax.axis_size("dp"), lax.axis_size(SEQ)
    devices = groups * ring
    _, count, width = tokens.shape
    slots = router.shape[1]
    owned, slice_width, rank = in_left.shape
    members, _, hidden = in_right.shape
    rows = groups * owned
    if groups != 2 or ring % 2 or slice_width % 128 or rows % 8 or members % owned:
        return local_plain(
            tokens,
            cotangent,
            router,
            slot_outputs,
            base_in,
            base_out,
            in_left,
            in_right,
            out_left,
            out_right,
        )
    low, full = jnp.bfloat16, jnp.float32
    image_rows, cot_rows, saved = tokens[0], cotangent[0], slot_outputs[0]
    router, base_in = router.T, base_in.T
    in_left, out_left = in_left.swapaxes(1, 2), out_left.swapaxes(1, 2)
    first, logits, combine = call(
        functools.partial(sums_kernel, owned, groups),
        [
            array(low, devices, owned, 2 * slice_width + STATS),
            array(full, slots, count),
            array(full, slots, count),
        ],
        [image_rows, cot_rows, router],
        6 * count * slots * width,
        (0, 1, 2),
        [pltpu.VMEM((count, width), low)] * 2
        + [pltpu.VMEM((slots, width), low), pltpu.SemaphoreType.DMA((3,))],
        60,
    )
    first = lax.all_to_all(first, BOTH, 0, 0, tiled=True)
    mixing, out_left, in_right = call(
        mixing_kernel,
        [array(full, slots, count), array(low, *out_left.shape), array(low, *in_right.shape)],
        [cot_rows, saved, combine, out_right, base_out, out_left, in_right],
        2 * count * slots * width,
    )
    first, mixing, out_left, in_right = lax.optimization_barrier(
        (first, mixing, out_left, in_right)
    )
    second, inputs, lows, stats = call(
        functools.partial(owner_kernel, groups),
        [
            array(low, rows, 2 * slice_width + 4 * rank),
            array(full, rows, slice_width),
            array(low, 2, rows, slice_width),
            array(full, rows, STATS),
        ],
        [first, in_left, out_right],
        4 * rows * owned * rank * slice_width,
    )
    second = to_group(second, groups)
    total_rows = groups * members
    third, pair, ranks = call(
        functools.partial(hidden_kernel, groups),
        [
            array(low, ring, rows, slice_width + 2 * rank),
            array(full, 2, total_rows, hidden),
            array(full, 2, total_rows, rank),
        ],
        [second, base_in, base_out, in_right, out_left],
        6 * total_rows * hidden * (width + owned * rank),
    )
    third = lax.all_to_all(third, HALF, 0, 0, tiled=True)
    grad_in_right, grad_out_left = call(
        functools.partial(outer_kernel, owned),
        [array(low, members, rank, hidden)] * 2,
        [ranks, pair],
        4 * members * rank * hidden * rows,
    )
    own, other = call(halves_kernel, [array(full, rows, slice_width + 2 * rank)] * 2, [third], 0)
    others = lax.all_gather(other, "half", axis=0)
    fourth, ranks = call(
        functools.partial(finish_kernel, groups, ring),
        [array(low, devices, owned, slice_width + STATS), array(full, 2, rows, rank)],
        [own, others, in_left, inputs, stats],
        2 * rows * owned * rank * slice_width,
    )
    fourth = lax.all_to_all(fourth, BOTH, 0, 0, tiled=True)
    grad_in_left, grad_out_right = call(
        functools.partial(outer_kernel, owned),
        [array(low, owned, rank, slice_width)] * 2,
        [ranks, lows],
        4 * owned * rank * slice_width * rows,
    )
    (token_grad,) = call(
        functools.partial(tokens_kernel, groups),
        [array(low, count, width)],
        [fourth, image_rows, router, logits, mixing],
        6 * count * slots * width,
    )
    return (
        token_grad[None],
        grad_in_left.swapaxes(1, 2),
        grad_in_right,
        grad_out_left.swapaxes(1, 2),
        grad_out_right,
    )


def solution(mesh):
    groups, ring = mesh.shape["dp"], mesh.shape["seq"]
    split = mesh.devices.reshape(groups, groups, ring // groups)
    mesh = jax.sharding.Mesh(split, BOTH)
    in_specs = (
        P("dp", SEQ, None),
        P("dp", SEQ, None),
        P(),
        P("dp", None, None),
        P(None, SEQ),
        P(SEQ, None),
        P(SEQ, "dp", None),
        P("dp", None, SEQ),
        P("dp", SEQ, None),
        P(SEQ, None, "dp"),
    )
    out_specs = (
        P("dp", SEQ, None),
        P(SEQ, "dp", None),
        P("dp", None, SEQ),
        P("dp", SEQ, None),
        P(SEQ, None, "dp"),
    )
    return jax.shard_map(local, mesh=mesh, in_specs=in_specs, out_specs=out_specs, check_vma=False)
```

```python
import functools

import jax
import jax.numpy as jnp
from jax import lax
from jax.experimental import pallas as pl
from jax.experimental.pallas import tpu as pltpu
from jax.sharding import PartitionSpec as P

SEQ = ("half", "place")
BOTH = ("dp", *SEQ)
HALF = ("dp", "place")
STATS = 128


def gelu_backward(preact, upstream):
    return jax.vjp(jax.nn.gelu, preact)[1](upstream)[0]


def dot_first(left, right):
    return lax.dot_general(
        left, right, (((0,), (0,)), ((), ())), preferred_element_type=jnp.float32
    )


def dot_last(left, right):
    return lax.dot_general(
        left, right, (((1,), (1,)), ((), ())), preferred_element_type=jnp.float32
    )


def split(value):
    high = lax.reduce_precision(value, 8, 7)
    low = lax.reduce_precision(value - high, 8, 7)
    return high.astype(jnp.bfloat16), low.astype(jnp.bfloat16)


def joined(high, low):
    return high.astype(jnp.float32) + low.astype(jnp.float32)


def exchange(blocks):
    flat = blocks.reshape((-1,) + blocks.shape[2:])
    return lax.all_to_all(flat, BOTH, 0, 0, tiled=True).reshape(blocks.shape)


def local_plain(
    tokens,
    cotangent,
    router,
    slot_outputs,
    base_in,
    base_out,
    in_left,
    in_right,
    out_left,
    out_right,
):
    groups, ring = lax.axis_size("dp"), lax.axis_size(SEQ)
    image_rows = tokens[0]
    cot_rows = cotangent[0]
    saved_outputs = slot_outputs[0]
    width = image_rows.shape[1]
    slots = router.shape[1]
    owned, slice_width, rank = in_left.shape
    members = in_right.shape[0]
    places = members // owned
    group, place = lax.axis_index("dp"), lax.axis_index(SEQ)

    logits = jnp.dot(image_rows, router, preferred_element_type=jnp.float32)
    peak_high, peak_low = split(jnp.max(logits, axis=0))
    near = jnp.exp(logits - joined(peak_high, peak_low))
    total_high, total_low = split(jnp.sum(near, axis=0))
    combine = jax.nn.softmax(logits, axis=1)
    sums = jnp.stack(
        [
            dot_first(near.astype(jnp.bfloat16), image_rows),
            dot_first(combine.astype(jnp.bfloat16), cot_rows),
        ],
        axis=1,
    ).astype(jnp.bfloat16)
    sums = sums.reshape(ring, owned, 2, groups, slice_width).transpose(3, 0, 1, 2, 4)
    sums = sums.reshape(groups, ring, owned, 2 * slice_width)
    stats = jnp.stack([peak_high, peak_low, total_high, total_low], axis=1)
    stats = jnp.pad(stats, ((0, 0), (0, STATS - 4))).reshape(1, ring, owned, STATS)
    stats = jnp.broadcast_to(stats, (groups, ring, owned, STATS))
    first = exchange(jnp.concatenate([sums, stats], axis=3))

    tail = 2 * slice_width
    peaks = joined(first[..., tail], first[..., tail + 1])
    totals = joined(first[..., tail + 2], first[..., tail + 3])
    peak = jnp.max(peaks, axis=1)
    near_scale = jnp.exp(peaks - peak[:, None])
    total = jnp.sum(near_scale * totals, axis=1)
    near_scale = near_scale / total[:, None]
    parts = first[..., :tail].astype(jnp.float32)
    slot_inputs = jnp.sum(parts[..., :slice_width] * near_scale[..., None], axis=1)
    inputs_own = slot_inputs.astype(jnp.bfloat16)
    grads_own = jnp.sum(parts[..., slice_width:], axis=1).astype(jnp.bfloat16)
    up_part = jnp.einsum("gjd,jdr->gjr", inputs_own, in_left, preferred_element_type=jnp.float32)
    back_part = jnp.einsum("gjd,jrd->gjr", grads_own, out_right, preferred_element_type=jnp.float32)
    second = jnp.concatenate(
        [inputs_own, grads_own, *split(up_part), *split(back_part)], axis=2
    )
    second = exchange(jnp.broadcast_to(second, (groups, ring) + second.shape))
    second = lax.dynamic_slice_in_dim(second, group * places, places, 1)

    def gathered(start):
        piece = second[..., start : start + slice_width]
        return piece.transpose(2, 1, 3, 0, 4).reshape(groups * members, width)

    def ranks(start):
        piece = joined(
            second[..., start : start + rank], second[..., start + rank : start + 2 * rank]
        )
        piece = jnp.sum(piece, axis=0).transpose(1, 0, 2, 3)
        return piece.reshape(groups, members, rank).astype(jnp.bfloat16)

    inputs_low, grads_low = gathered(0), gathered(slice_width)
    up_low, back_low = ranks(tail), ranks(tail + 2 * rank)
    hidden = base_in.shape[1]
    preact = jnp.dot(inputs_low, base_in, preferred_element_type=jnp.float32).reshape(
        groups, members, hidden
    ) + jnp.einsum("gjr,jrf->gjf", up_low, in_right, preferred_element_type=jnp.float32)
    hidden_low = jax.nn.gelu(preact).astype(jnp.bfloat16)
    hidden_grad = dot_last(grads_low, base_out).reshape(groups, members, hidden) + jnp.einsum(
        "gjr,jfr->gjf", back_low, out_left, preferred_element_type=jnp.float32
    )
    preact_grad = gelu_backward(preact, hidden_grad).astype(jnp.bfloat16)
    slot_term = dot_last(preact_grad.reshape(groups * members, hidden), base_in)
    down_term = jnp.einsum(
        "gjf,jrf->gjr", preact_grad, in_right, preferred_element_type=jnp.float32
    )
    value_term = jnp.einsum(
        "gjf,jfr->gjr", hidden_low, out_left, preferred_element_type=jnp.float32
    )
    slot_term = slot_term.astype(jnp.bfloat16).reshape(groups, places, owned, groups, slice_width)
    slot_term = slot_term.transpose(3, 1, 0, 2, 4)
    rank_term = jnp.concatenate([down_term, value_term], axis=2).astype(jnp.bfloat16)
    rank_term = rank_term.reshape(groups, places, owned, 2 * rank).transpose(1, 0, 2, 3)
    rank_term = jnp.broadcast_to(rank_term, (groups,) + rank_term.shape)
    third = jnp.concatenate([slot_term, rank_term], axis=4)
    third = lax.dynamic_update_slice_in_dim(
        jnp.zeros((groups, ring) + third.shape[2:], jnp.bfloat16), third, group * places, 1
    )
    third = exchange(third)
    third = lax.dynamic_index_in_dim(third, place // places, 0, keepdims=False)
    third = jnp.sum(third.astype(jnp.float32), axis=0)
    down_own = third[..., slice_width : slice_width + rank].astype(jnp.bfloat16)
    value_own = third[..., slice_width + rank :].astype(jnp.bfloat16)
    slot_grads_own = (
        third[..., :slice_width]
        + jnp.einsum("gjr,jdr->gjd", down_own, in_left, preferred_element_type=jnp.float32)
    ).astype(jnp.bfloat16)
    shift_part = jnp.sum(slot_grads_own.astype(jnp.float32) * slot_inputs, axis=2)
    stats = jnp.stack([*split(peak), *split(total), *split(shift_part)], axis=2)
    stats = jnp.pad(stats, ((0, 0), (0, 0), (0, STATS - 6)))
    fourth = jnp.concatenate([slot_grads_own, stats], axis=2)[:, None]
    fourth = exchange(jnp.broadcast_to(fourth, (groups, ring) + fourth.shape[2:]))
    slot_grads = fourth[..., :slice_width].transpose(1, 2, 0, 3).reshape(slots, width)
    stats = fourth[..., slice_width:].astype(jnp.float32).reshape(groups, slots, STATS)
    slot_peak = stats[0, :, 0] + stats[0, :, 1]
    slot_total = stats[0, :, 2] + stats[0, :, 3]
    shift_back = jnp.sum(stats[:, :, 4] + stats[:, :, 5], axis=0)

    dispatch = jnp.exp(logits - slot_peak) / slot_total
    dispatch_low = dispatch.astype(jnp.bfloat16)
    weight_grad = dot_last(image_rows, slot_grads)
    dispatch_logit = dispatch * (weight_grad - shift_back)
    mixing_grad = dot_last(cot_rows, saved_outputs)
    combine_logit = combine * (mixing_grad - jnp.sum(combine * mixing_grad, axis=1, keepdims=True))
    logit_grad = (dispatch_logit + combine_logit).astype(jnp.bfloat16)
    token_grad = (
        jnp.dot(dispatch_low, slot_grads, preferred_element_type=jnp.float32)
        + dot_last(logit_grad, router)
    ).astype(jnp.bfloat16)
    grad_in_right = jnp.einsum(
        "gjr,gjf->jrf", up_low, preact_grad, preferred_element_type=jnp.float32
    ).astype(jnp.bfloat16)
    grad_out_left = jnp.einsum(
        "gjf,gjr->jfr", hidden_low, back_low, preferred_element_type=jnp.float32
    ).astype(jnp.bfloat16)
    grad_in_left = jnp.einsum(
        "gjd,gjr->jdr", inputs_own, down_own, preferred_element_type=jnp.float32
    ).astype(jnp.bfloat16)
    grad_out_right = jnp.einsum(
        "gjr,gjd->jrd", value_own, grads_own, preferred_element_type=jnp.float32
    ).astype(jnp.bfloat16)
    return (token_grad[None], grad_in_left, grad_in_right, grad_out_left, grad_out_right)


def dot_plain(left, right):
    return jnp.dot(left, right, preferred_element_type=jnp.float32)


def halves(value):
    high = value.astype(jnp.bfloat16).astype(jnp.float32)
    low = (value - high).astype(jnp.bfloat16).astype(jnp.float32)
    return high, low


def in_lanes(columns, shape):
    lane = lax.broadcasted_iota(jnp.int32, shape, len(shape) - 1)
    out = jnp.zeros(shape, jnp.float32)
    for number, column in enumerate(columns):
        out = jnp.where(lane == number, column, out)
    return out


def own_block(value, owned):
    rows, rank = value.shape
    wide = jnp.concatenate([value] * owned, axis=1)
    shape = (rows, owned * rank)
    block = lax.broadcasted_iota(jnp.int32, shape, 1) // rank
    expert = lax.broadcasted_iota(jnp.int32, shape, 0) % owned
    return jnp.where(block == expert, wide, 0.0).astype(jnp.bfloat16)


def from_own_block(value, owned):
    rows, wide = value.shape
    rank = wide // owned
    block = lax.broadcasted_iota(jnp.int32, value.shape, 1) // rank
    expert = lax.broadcasted_iota(jnp.int32, value.shape, 0) % owned
    kept = jnp.where(block == expert, value, 0.0)
    out = kept[:, :rank]
    for number in range(1, owned):
        out = out + kept[:, number * rank : (number + 1) * rank]
    return out


def sums_kernel(
    owned,
    groups,
    tokens_far,
    cotangent_far,
    router_far,
    first,
    logits_out,
    combine_out,
    tokens,
    cotangent,
    router,
    arrived,
):
    ring = first.shape[0] // groups
    copies = [
        pltpu.make_async_copy(far, near, arrived.at[number])
        for number, (far, near) in enumerate(
            [(router_far, router), (tokens_far, tokens), (cotangent_far, cotangent)]
        )
    ]
    for copy in copies:
        copy.start()
    copies[0].wait()
    copies[1].wait()
    image_rows = tokens[...]
    logits = dot_last(router[...], image_rows)
    high, low = halves(jnp.max(logits, axis=1, keepdims=True))
    near = jnp.exp(logits - (high + low))
    total_high, total_low = halves(jnp.sum(near, axis=1, keepdims=True))
    spread = jnp.exp(logits - jnp.max(logits, axis=0, keepdims=True))
    combine = spread / jnp.sum(spread, axis=0, keepdims=True)
    logits_out[...] = logits
    combine_out[...] = combine
    stats = in_lanes([high, low, total_high, total_low], (logits.shape[0], STATS))
    stats = stats.astype(jnp.bfloat16)
    inputs = dot_plain(near.astype(jnp.bfloat16), image_rows).astype(jnp.bfloat16)
    copies[2].wait()
    grads = dot_plain(combine.astype(jnp.bfloat16), cotangent[...]).astype(jnp.bfloat16)
    width = inputs.shape[1] // groups
    for group in range(groups):
        columns = slice(group * width, (group + 1) * width)
        for place in range(ring):
            rows = slice(place * owned, (place + 1) * owned)
            block = group * ring + place
            first[block, :, :width] = inputs[rows, columns]
            first[block, :, width : 2 * width] = grads[rows, columns]
            first[block, :, 2 * width :] = stats[rows, :]


def mixing_kernel(cotangent, saved, combine, out):
    mixing = dot_last(saved[...], cotangent[...])
    weights = combine[...]
    out[...] = weights * (mixing - jnp.sum(weights * mixing, axis=0, keepdims=True))


def load_kernel(after, *refs):
    count = len(refs) // 2
    arrived = refs[-1]
    copies = [
        pltpu.make_async_copy(refs[number], refs[count + number], arrived.at[number])
        for number in range(count)
    ]
    for copy in copies:
        copy.start()
    for copy in copies:
        copy.wait()


def owner_kernel(groups, first, in_left, out_right, second, inputs_out, lows_out, stats_out):
    ring = first.shape[0] // groups
    owned, rank, width = in_left.shape
    inputs, grads, stats_rows = [], [], []
    for group in range(groups):
        rows = slice(group * ring, (group + 1) * ring)
        stats = first[rows, :, 2 * width :].astype(jnp.float32)
        peaks = stats[:, :, 0:1] + stats[:, :, 1:2]
        totals = stats[:, :, 2:3] + stats[:, :, 3:4]
        peak = jnp.max(peaks, axis=0)
        scale = jnp.exp(peaks - peak[None])
        total = jnp.sum(scale * totals, axis=0)
        scale = scale / total[None]
        inputs.append(jnp.sum(first[rows, :, :width].astype(jnp.float32) * scale, axis=0))
        grads.append(jnp.sum(first[rows, :, width : 2 * width].astype(jnp.float32), axis=0))
        stats_rows.append(in_lanes([*halves(peak), *halves(total)], (owned, STATS)))
    inputs, grads = jnp.concatenate(inputs, axis=0), jnp.concatenate(grads, axis=0)
    inputs_out[...] = inputs
    stats_out[...] = jnp.concatenate(stats_rows, axis=0)
    inputs_low, grads_low = inputs.astype(jnp.bfloat16), grads.astype(jnp.bfloat16)
    lows_out[0] = inputs_low
    lows_out[1] = grads_low
    up = dot_last(inputs_low, in_left[...].reshape(owned * rank, width))
    back = dot_last(grads_low, out_right[...].reshape(owned * rank, width))
    ranks = [*halves(from_own_block(up, owned)), *halves(from_own_block(back, owned))]
    ranks = jnp.concatenate(ranks, axis=1).astype(jnp.bfloat16)
    block = jnp.concatenate([inputs_low, grads_low, ranks], axis=1)
    second[...] = block


def pack_kernel(blocks, out):
    for group in range(out.shape[0]):
        for place in range(out.shape[1]):
            out[group, place] = blocks[group]


def hidden_kernel(
    groups,
    second,
    base_in,
    base_out,
    in_right,
    out_left,
    third,
    pair_out,
    ranks_out,
):
    members, rank, hidden = in_right.shape
    rows = second.shape[1]
    owned = rows // groups
    places = members // owned
    width = base_in.shape[1] // groups

    def gathered(columns):
        taken = [
            second[half * places : (half + 1) * places, :, columns].astype(jnp.float32)
            for half in range(groups)
        ]
        return [part.reshape(places * rows, part.shape[2]) for part in taken]

    def low_rank(value, table):
        value = value.astype(jnp.float32)
        taken = []
        for place in range(places):
            own = own_block(value[place * rows : (place + 1) * rows], owned)
            part = table[place * owned : (place + 1) * owned].reshape(owned * rank, hidden)
            taken.append(dot_plain(own, part))
        return jnp.concatenate(taken, axis=0)

    def to_rank(value, table):
        taken = []
        for place in range(places):
            part = table[place * owned : (place + 1) * owned].reshape(owned * rank, hidden)
            wide = dot_last(value[place * rows : (place + 1) * rows].astype(jnp.bfloat16), part)
            taken.append(from_own_block(wide, owned))
        return jnp.concatenate(taken, axis=0)

    ranks = functools.reduce(jnp.add, gathered(slice(2 * width, 2 * width + 4 * rank)))
    up = (ranks[:, :rank] + ranks[:, rank : 2 * rank]).astype(jnp.bfloat16)
    back = (ranks[:, 2 * rank : 3 * rank] + ranks[:, 3 * rank :]).astype(jnp.bfloat16)
    preact = low_rank(up, in_right)
    for half, part in enumerate(gathered(slice(0, width))):
        columns = slice(half * width, (half + 1) * width)
        preact = preact + dot_last(part.astype(jnp.bfloat16), base_in[:, columns])
    hidden_grad = low_rank(back, out_left)
    for half, part in enumerate(gathered(slice(width, 2 * width))):
        columns = slice(half * width, (half + 1) * width)
        hidden_grad = hidden_grad + dot_last(part.astype(jnp.bfloat16), base_out[:, columns])
    root = 0.7978845608028654
    bent = jnp.tanh(root * (preact + 0.044715 * (preact * preact * preact)))
    hidden_value = 0.5 * preact * (1.0 + bent)
    slope = 0.5 * (1.0 + bent) + 0.5 * preact * (1.0 - bent * bent) * (
        root * (1.0 + 3.0 * 0.044715 * (preact * preact))
    )
    hidden_low = hidden_value.astype(jnp.bfloat16).astype(jnp.float32)
    preact_grad = (hidden_grad * slope).astype(jnp.bfloat16).astype(jnp.float32)
    pair_out[0] = preact_grad
    pair_out[1] = hidden_low
    ranks_out[0] = up.astype(jnp.float32)
    ranks_out[1] = back.astype(jnp.float32)
    slot_term = dot_plain(preact_grad.astype(jnp.bfloat16), base_in[...]).astype(jnp.bfloat16)
    down = to_rank(preact_grad, in_right)
    value = to_rank(hidden_low, out_left)
    ranks = jnp.concatenate([down, value], axis=1).astype(jnp.bfloat16)
    for half in range(groups):
        columns = slice(half * width, (half + 1) * width)
        for place in range(places):
            taken = slice(place * rows, (place + 1) * rows)
            block = half * places + place
            third[block, :, :width] = slot_term[taken, columns]
            third[block, :, width:] = ranks[taken]


def outer_kernel(owned, left_rows, right_rows, *outs):
    rows = left_rows.shape[1] // (outs[0].shape[0] // owned)
    for number, out in enumerate(outs):
        for place in range(out.shape[0] // owned):
            taken = slice(place * rows, (place + 1) * rows)
            own = own_block(left_rows[number, taken], owned)
            product = dot_first(own, right_rows[number, taken].astype(jnp.bfloat16))
            out[place * owned : (place + 1) * owned] = product.astype(jnp.bfloat16).reshape(
                (owned,) + out.shape[1:]
            )


def halves_kernel(third, own, other):
    places = third.shape[0] // 2
    here = lax.axis_index("half")
    for out, group in ((own, here), (other, 1 - here)):
        taken = third[pl.ds(group * places, places)].astype(jnp.float32)
        out[...] = jnp.sum(taken, axis=0)


def finish_kernel(groups, ring, own, others, in_left, inputs, stats, fourth, ranks_out):
    owned, rank, width = in_left.shape
    summed = own[...] + others[1 - lax.axis_index("half")]
    ranks = summed[:, width:].astype(jnp.bfloat16).astype(jnp.float32)
    ranks_out[0] = ranks[:, :rank]
    ranks_out[1] = ranks[:, rank:]
    down = own_block(ranks[:, :rank], owned)
    grads = summed[:, :width] + dot_plain(down, in_left[...].reshape(owned * rank, width))
    grads = grads.astype(jnp.bfloat16).astype(jnp.float32)
    high, low = halves(jnp.sum(grads * inputs[...], axis=1, keepdims=True))
    lane = lax.broadcasted_iota(jnp.int32, stats.shape, 1)
    tail = jnp.where(lane == 4, high, jnp.where(lane == 5, low, stats[...]))
    block = jnp.concatenate([grads, tail], axis=1).astype(jnp.bfloat16)
    for group in range(groups):
        rows = block[group * owned : (group + 1) * owned]
        for place in range(ring):
            fourth[group * ring + place] = rows


def tokens_kernel(groups, fourth, tokens, router, logits, mixing, out):
    blocks, owned, _ = fourth.shape
    ring = blocks // groups
    width = tokens.shape[1] // groups

    def rows(half, columns):
        taken = [
            fourth[half * ring + place, :, columns].astype(jnp.float32) for place in range(ring)
        ]
        return jnp.concatenate(taken, axis=0)

    grads = jnp.concatenate([rows(half, slice(0, width)) for half in range(groups)], axis=1)
    grads = grads.astype(jnp.bfloat16)
    stats = [rows(half, slice(width, width + STATS)) for half in range(groups)]
    peak = stats[0][:, 0:1] + stats[0][:, 1:2]
    total = stats[0][:, 2:3] + stats[0][:, 3:4]
    shift = functools.reduce(jnp.add, [part[:, 4:5] + part[:, 5:6] for part in stats])
    dispatch = jnp.exp(logits[...] - peak) / total
    weight_grad = dot_last(grads, tokens[...])
    logit_grad = dispatch * (weight_grad - shift) + mixing[...]
    left = jnp.concatenate([dispatch, logit_grad], axis=0).astype(jnp.bfloat16)
    right = jnp.concatenate([grads, router[...]], axis=0)
    out[...] = dot_first(left, right).astype(jnp.bfloat16)


def to_group(block, groups):
    places = lax.axis_size("place")
    blocks = lax.all_gather(block, "half", axis=0)
    (blocks,) = call(
        pack_kernel, [array(block.dtype, groups, places, *block.shape)], [blocks], 0
    )
    blocks = blocks.reshape(groups * places, *block.shape)
    return lax.all_to_all(blocks, HALF, 0, 0, tiled=True)


def call(kernel, outs, args, flops, far=(), scratch=(), grant=24):
    size = sum(array.size * array.dtype.itemsize for array in args)
    size += sum(out.size * out.dtype.itemsize for out in outs)
    spaces = [pltpu.HBM if number in far else pltpu.VMEM for number in range(len(args))]
    return pl.pallas_call(
        kernel,
        out_shape=outs,
        in_specs=[pl.BlockSpec(memory_space=space) for space in spaces],
        out_specs=[pl.BlockSpec(memory_space=pltpu.VMEM) for _ in outs],
        scratch_shapes=scratch,
        cost_estimate=pl.CostEstimate(flops=flops, bytes_accessed=size, transcendentals=0),
        compiler_params=pltpu.CompilerParams(vmem_limit_bytes=grant * 2**20),
    )(*args)


def array(dtype, *shape):
    return jax.ShapeDtypeStruct(shape, dtype)


def local(
    tokens,
    cotangent,
    router,
    slot_outputs,
    base_in,
    base_out,
    in_left,
    in_right,
    out_left,
    out_right,
):
    groups, ring = lax.axis_size("dp"), lax.axis_size(SEQ)
    devices = groups * ring
    _, count, width = tokens.shape
    slots = router.shape[1]
    owned, slice_width, rank = in_left.shape
    members, _, hidden = in_right.shape
    rows = groups * owned
    if groups != 2 or ring % 2 or slice_width % 128 or rows % 8 or members % owned:
        return local_plain(
            tokens,
            cotangent,
            router,
            slot_outputs,
            base_in,
            base_out,
            in_left,
            in_right,
            out_left,
            out_right,
        )
    low, full = jnp.bfloat16, jnp.float32
    image_rows, cot_rows, saved = tokens[0], cotangent[0], slot_outputs[0]
    router, base_in = router.T, base_in.T
    in_left, out_left = in_left.swapaxes(1, 2), out_left.swapaxes(1, 2)
    first, logits, combine = call(
        functools.partial(sums_kernel, owned, groups),
        [
            array(low, devices, owned, 2 * slice_width + STATS),
            array(full, slots, count),
            array(full, slots, count),
        ],
        [image_rows, cot_rows, router],
        6 * count * slots * width,
        (0, 1, 2),
        [pltpu.VMEM((count, width), low)] * 2
        + [pltpu.VMEM((slots, width), low), pltpu.SemaphoreType.DMA((3,))],
        60,
    )
    first = lax.all_to_all(first, BOTH, 0, 0, tiled=True)
    weights = [in_left, out_right, base_in, base_out, in_right, out_left]
    weights = call(
        load_kernel,
        [array(low, *weight.shape) for weight in weights],
        [combine, *weights],
        0,
        range(len(weights) + 1),
        [pltpu.SemaphoreType.DMA((len(weights),))],
        46,
    )
    first, *weights = lax.optimization_barrier((first, *weights))
    in_left, out_right, base_in, base_out, in_right, out_left = weights
    second, inputs, lows, stats = call(
        functools.partial(owner_kernel, groups),
        [
            array(low, rows, 2 * slice_width + 4 * rank),
            array(full, rows, slice_width),
            array(low, 2, rows, slice_width),
            array(full, rows, STATS),
        ],
        [first, in_left, out_right],
        4 * rows * owned * rank * slice_width,
    )
    second = to_group(second, groups)
    total_rows = groups * members
    third, pair, ranks = call(
        functools.partial(hidden_kernel, groups),
        [
            array(low, ring, rows, slice_width + 2 * rank),
            array(full, 2, total_rows, hidden),
            array(full, 2, total_rows, rank),
        ],
        [second, base_in, base_out, in_right, out_left],
        6 * total_rows * hidden * (width + owned * rank),
    )
    third = lax.all_to_all(third, HALF, 0, 0, tiled=True)
    grad_in_right, grad_out_left = call(
        functools.partial(outer_kernel, owned),
        [array(low, members, rank, hidden)] * 2,
        [ranks, pair],
        4 * members * rank * hidden * rows,
    )
    own, other = call(halves_kernel, [array(full, rows, slice_width + 2 * rank)] * 2, [third], 0)
    others = lax.all_gather(other, "half", axis=0)
    fourth, ranks = call(
        functools.partial(finish_kernel, groups, ring),
        [array(low, devices, owned, slice_width + STATS), array(full, 2, rows, rank)],
        [own, others, in_left, inputs, stats],
        2 * rows * owned * rank * slice_width,
    )
    (mixing,) = call(
        mixing_kernel,
        [array(full, slots, count)],
        [cot_rows, saved, combine],
        2 * count * slots * width,
    )
    fourth = lax.all_to_all(fourth, BOTH, 0, 0, tiled=True)
    grad_in_left, grad_out_right = call(
        functools.partial(outer_kernel, owned),
        [array(low, owned, rank, slice_width)] * 2,
        [ranks, lows],
        4 * owned * rank * slice_width * rows,
    )
    (token_grad,) = call(
        functools.partial(tokens_kernel, groups),
        [array(low, count, width)],
        [fourth, image_rows, router, logits, mixing],
        6 * count * slots * width,
    )
    return (
        token_grad[None],
        grad_in_left.swapaxes(1, 2),
        grad_in_right,
        grad_out_left.swapaxes(1, 2),
        grad_out_right,
    )


def solution(mesh):
    groups, ring = mesh.shape["dp"], mesh.shape["seq"]
    split = mesh.devices.reshape(groups, groups, ring // groups)
    mesh = jax.sharding.Mesh(split, BOTH)
    in_specs = (
        P("dp", SEQ, None),
        P("dp", SEQ, None),
        P(),
        P("dp", None, None),
        P(None, SEQ),
        P(SEQ, None),
        P(SEQ, "dp", None),
        P("dp", None, SEQ),
        P("dp", SEQ, None),
        P(SEQ, None, "dp"),
    )
    out_specs = (
        P("dp", SEQ, None),
        P(SEQ, "dp", None),
        P("dp", None, SEQ),
        P("dp", SEQ, None),
        P(SEQ, None, "dp"),
    )
    return jax.shard_map(local, mesh=mesh, in_specs=in_specs, out_specs=out_specs, check_vma=False)
```

```python
import functools

import jax
import jax.numpy as jnp
from jax import lax
from jax.experimental import pallas as pl
from jax.experimental.pallas import tpu as pltpu
from jax.sharding import PartitionSpec as P

SEQ = ("half", "place")
BOTH = ("dp", *SEQ)
HALF = ("dp", "place")
STATS = 128


def gelu_backward(preact, upstream):
    return jax.vjp(jax.nn.gelu, preact)[1](upstream)[0]


def dot_first(left, right):
    return lax.dot_general(
        left, right, (((0,), (0,)), ((), ())), preferred_element_type=jnp.float32
    )


def dot_last(left, right):
    return lax.dot_general(
        left, right, (((1,), (1,)), ((), ())), preferred_element_type=jnp.float32
    )


def split(value):
    high = lax.reduce_precision(value, 8, 7)
    low = lax.reduce_precision(value - high, 8, 7)
    return high.astype(jnp.bfloat16), low.astype(jnp.bfloat16)


def joined(high, low):
    return high.astype(jnp.float32) + low.astype(jnp.float32)


def exchange(blocks):
    flat = blocks.reshape((-1,) + blocks.shape[2:])
    return lax.all_to_all(flat, BOTH, 0, 0, tiled=True).reshape(blocks.shape)


def local_plain(
    tokens,
    cotangent,
    router,
    slot_outputs,
    base_in,
    base_out,
    in_left,
    in_right,
    out_left,
    out_right,
):
    groups, ring = lax.axis_size("dp"), lax.axis_size(SEQ)
    image_rows = tokens[0]
    cot_rows = cotangent[0]
    saved_outputs = slot_outputs[0]
    width = image_rows.shape[1]
    slots = router.shape[1]
    owned, slice_width, rank = in_left.shape
    members = in_right.shape[0]
    places = members // owned
    group, place = lax.axis_index("dp"), lax.axis_index(SEQ)

    logits = jnp.dot(image_rows, router, preferred_element_type=jnp.float32)
    peak_high, peak_low = split(jnp.max(logits, axis=0))
    near = jnp.exp(logits - joined(peak_high, peak_low))
    total_high, total_low = split(jnp.sum(near, axis=0))
    combine = jax.nn.softmax(logits, axis=1)
    sums = jnp.stack(
        [
            dot_first(near.astype(jnp.bfloat16), image_rows),
            dot_first(combine.astype(jnp.bfloat16), cot_rows),
        ],
        axis=1,
    ).astype(jnp.bfloat16)
    sums = sums.reshape(ring, owned, 2, groups, slice_width).transpose(3, 0, 1, 2, 4)
    sums = sums.reshape(groups, ring, owned, 2 * slice_width)
    stats = jnp.stack([peak_high, peak_low, total_high, total_low], axis=1)
    stats = jnp.pad(stats, ((0, 0), (0, STATS - 4))).reshape(1, ring, owned, STATS)
    stats = jnp.broadcast_to(stats, (groups, ring, owned, STATS))
    first = exchange(jnp.concatenate([sums, stats], axis=3))

    tail = 2 * slice_width
    peaks = joined(first[..., tail], first[..., tail + 1])
    totals = joined(first[..., tail + 2], first[..., tail + 3])
    peak = jnp.max(peaks, axis=1)
    near_scale = jnp.exp(peaks - peak[:, None])
    total = jnp.sum(near_scale * totals, axis=1)
    near_scale = near_scale / total[:, None]
    parts = first[..., :tail].astype(jnp.float32)
    slot_inputs = jnp.sum(parts[..., :slice_width] * near_scale[..., None], axis=1)
    inputs_own = slot_inputs.astype(jnp.bfloat16)
    grads_own = jnp.sum(parts[..., slice_width:], axis=1).astype(jnp.bfloat16)
    up_part = jnp.einsum("gjd,jdr->gjr", inputs_own, in_left, preferred_element_type=jnp.float32)
    back_part = jnp.einsum("gjd,jrd->gjr", grads_own, out_right, preferred_element_type=jnp.float32)
    second = jnp.concatenate(
        [inputs_own, grads_own, *split(up_part), *split(back_part)], axis=2
    )
    second = exchange(jnp.broadcast_to(second, (groups, ring) + second.shape))
    second = lax.dynamic_slice_in_dim(second, group * places, places, 1)

    def gathered(start):
        piece = second[..., start : start + slice_width]
        return piece.transpose(2, 1, 3, 0, 4).reshape(groups * members, width)

    def ranks(start):
        piece = joined(
            second[..., start : start + rank], second[..., start + rank : start + 2 * rank]
        )
        piece = jnp.sum(piece, axis=0).transpose(1, 0, 2, 3)
        return piece.reshape(groups, members, rank).astype(jnp.bfloat16)

    inputs_low, grads_low = gathered(0), gathered(slice_width)
    up_low, back_low = ranks(tail), ranks(tail + 2 * rank)
    hidden = base_in.shape[1]
    preact = jnp.dot(inputs_low, base_in, preferred_element_type=jnp.float32).reshape(
        groups, members, hidden
    ) + jnp.einsum("gjr,jrf->gjf", up_low, in_right, preferred_element_type=jnp.float32)
    hidden_low = jax.nn.gelu(preact).astype(jnp.bfloat16)
    hidden_grad = dot_last(grads_low, base_out).reshape(groups, members, hidden) + jnp.einsum(
        "gjr,jfr->gjf", back_low, out_left, preferred_element_type=jnp.float32
    )
    preact_grad = gelu_backward(preact, hidden_grad).astype(jnp.bfloat16)
    slot_term = dot_last(preact_grad.reshape(groups * members, hidden), base_in)
    down_term = jnp.einsum(
        "gjf,jrf->gjr", preact_grad, in_right, preferred_element_type=jnp.float32
    )
    value_term = jnp.einsum(
        "gjf,jfr->gjr", hidden_low, out_left, preferred_element_type=jnp.float32
    )
    slot_term = slot_term.astype(jnp.bfloat16).reshape(groups, places, owned, groups, slice_width)
    slot_term = slot_term.transpose(3, 1, 0, 2, 4)
    rank_term = jnp.concatenate([down_term, value_term], axis=2).astype(jnp.bfloat16)
    rank_term = rank_term.reshape(groups, places, owned, 2 * rank).transpose(1, 0, 2, 3)
    rank_term = jnp.broadcast_to(rank_term, (groups,) + rank_term.shape)
    third = jnp.concatenate([slot_term, rank_term], axis=4)
    third = lax.dynamic_update_slice_in_dim(
        jnp.zeros((groups, ring) + third.shape[2:], jnp.bfloat16), third, group * places, 1
    )
    third = exchange(third)
    third = lax.dynamic_index_in_dim(third, place // places, 0, keepdims=False)
    third = jnp.sum(third.astype(jnp.float32), axis=0)
    down_own = third[..., slice_width : slice_width + rank].astype(jnp.bfloat16)
    value_own = third[..., slice_width + rank :].astype(jnp.bfloat16)
    slot_grads_own = (
        third[..., :slice_width]
        + jnp.einsum("gjr,jdr->gjd", down_own, in_left, preferred_element_type=jnp.float32)
    ).astype(jnp.bfloat16)
    shift_part = jnp.sum(slot_grads_own.astype(jnp.float32) * slot_inputs, axis=2)
    stats = jnp.stack([*split(peak), *split(total), *split(shift_part)], axis=2)
    stats = jnp.pad(stats, ((0, 0), (0, 0), (0, STATS - 6)))
    fourth = jnp.concatenate([slot_grads_own, stats], axis=2)[:, None]
    fourth = exchange(jnp.broadcast_to(fourth, (groups, ring) + fourth.shape[2:]))
    slot_grads = fourth[..., :slice_width].transpose(1, 2, 0, 3).reshape(slots, width)
    stats = fourth[..., slice_width:].astype(jnp.float32).reshape(groups, slots, STATS)
    slot_peak = stats[0, :, 0] + stats[0, :, 1]
    slot_total = stats[0, :, 2] + stats[0, :, 3]
    shift_back = jnp.sum(stats[:, :, 4] + stats[:, :, 5], axis=0)

    dispatch = jnp.exp(logits - slot_peak) / slot_total
    dispatch_low = dispatch.astype(jnp.bfloat16)
    weight_grad = dot_last(image_rows, slot_grads)
    dispatch_logit = dispatch * (weight_grad - shift_back)
    mixing_grad = dot_last(cot_rows, saved_outputs)
    combine_logit = combine * (mixing_grad - jnp.sum(combine * mixing_grad, axis=1, keepdims=True))
    logit_grad = (dispatch_logit + combine_logit).astype(jnp.bfloat16)
    token_grad = (
        jnp.dot(dispatch_low, slot_grads, preferred_element_type=jnp.float32)
        + dot_last(logit_grad, router)
    ).astype(jnp.bfloat16)
    grad_in_right = jnp.einsum(
        "gjr,gjf->jrf", up_low, preact_grad, preferred_element_type=jnp.float32
    ).astype(jnp.bfloat16)
    grad_out_left = jnp.einsum(
        "gjf,gjr->jfr", hidden_low, back_low, preferred_element_type=jnp.float32
    ).astype(jnp.bfloat16)
    grad_in_left = jnp.einsum(
        "gjd,gjr->jdr", inputs_own, down_own, preferred_element_type=jnp.float32
    ).astype(jnp.bfloat16)
    grad_out_right = jnp.einsum(
        "gjr,gjd->jrd", value_own, grads_own, preferred_element_type=jnp.float32
    ).astype(jnp.bfloat16)
    return (token_grad[None], grad_in_left, grad_in_right, grad_out_left, grad_out_right)


def dot_plain(left, right):
    return jnp.dot(left, right, preferred_element_type=jnp.float32)


def halves(value):
    high = value.astype(jnp.bfloat16).astype(jnp.float32)
    low = (value - high).astype(jnp.bfloat16).astype(jnp.float32)
    return high, low


def in_lanes(columns, shape):
    lane = lax.broadcasted_iota(jnp.int32, shape, len(shape) - 1)
    out = jnp.zeros(shape, jnp.float32)
    for number, column in enumerate(columns):
        out = jnp.where(lane == number, column, out)
    return out


def own_block(value, owned):
    rows, rank = value.shape
    wide = jnp.concatenate([value] * owned, axis=1)
    shape = (rows, owned * rank)
    block = lax.broadcasted_iota(jnp.int32, shape, 1) // rank
    expert = lax.broadcasted_iota(jnp.int32, shape, 0) % owned
    return jnp.where(block == expert, wide, 0.0).astype(jnp.bfloat16)


def from_own_block(value, owned):
    rows, wide = value.shape
    rank = wide // owned
    block = lax.broadcasted_iota(jnp.int32, value.shape, 1) // rank
    expert = lax.broadcasted_iota(jnp.int32, value.shape, 0) % owned
    kept = jnp.where(block == expert, value, 0.0)
    out = kept[:, :rank]
    for number in range(1, owned):
        out = out + kept[:, number * rank : (number + 1) * rank]
    return out


def sums_kernel(
    owned,
    groups,
    tokens_far,
    cotangent_far,
    router_far,
    first,
    logits_out,
    combine_out,
    tokens,
    cotangent,
    router,
    arrived,
):
    ring = first.shape[0] // groups
    copies = [
        pltpu.make_async_copy(far, near, arrived.at[number])
        for number, (far, near) in enumerate(
            [(router_far, router), (tokens_far, tokens), (cotangent_far, cotangent)]
        )
    ]
    for copy in copies:
        copy.start()
    copies[0].wait()
    copies[1].wait()
    image_rows = tokens[...]
    logits = dot_last(router[...], image_rows)
    high, low = halves(jnp.max(logits, axis=1, keepdims=True))
    near = jnp.exp(logits - (high + low))
    total_high, total_low = halves(jnp.sum(near, axis=1, keepdims=True))
    spread = jnp.exp(logits - jnp.max(logits, axis=0, keepdims=True))
    combine = spread / jnp.sum(spread, axis=0, keepdims=True)
    logits_out[...] = logits
    combine_out[...] = combine
    stats = in_lanes([high, low, total_high, total_low], (logits.shape[0], STATS))
    stats = stats.astype(jnp.bfloat16)
    inputs = dot_plain(near.astype(jnp.bfloat16), image_rows).astype(jnp.bfloat16)
    copies[2].wait()
    grads = dot_plain(combine.astype(jnp.bfloat16), cotangent[...]).astype(jnp.bfloat16)
    width = inputs.shape[1] // groups
    for group in range(groups):
        columns = slice(group * width, (group + 1) * width)
        for place in range(ring):
            rows = slice(place * owned, (place + 1) * owned)
            block = group * ring + place
            first[block, :, :width] = inputs[rows, columns]
            first[block, :, width : 2 * width] = grads[rows, columns]
            first[block, :, 2 * width :] = stats[rows, :]


def mixing_kernel(cotangent, saved, combine, out):
    mixing = dot_last(saved[...], cotangent[...])
    weights = combine[...]
    out[...] = weights * (mixing - jnp.sum(weights * mixing, axis=0, keepdims=True))


def owner_kernel(groups, first, in_left, out_right, second, inputs_out, lows_out, stats_out):
    ring = first.shape[0] // groups
    owned, rank, width = in_left.shape
    inputs, grads, stats_rows = [], [], []
    for group in range(groups):
        rows = slice(group * ring, (group + 1) * ring)
        stats = first[rows, :, 2 * width :].astype(jnp.float32)
        peaks = stats[:, :, 0:1] + stats[:, :, 1:2]
        totals = stats[:, :, 2:3] + stats[:, :, 3:4]
        peak = jnp.max(peaks, axis=0)
        scale = jnp.exp(peaks - peak[None])
        total = jnp.sum(scale * totals, axis=0)
        scale = scale / total[None]
        inputs.append(jnp.sum(first[rows, :, :width].astype(jnp.float32) * scale, axis=0))
        grads.append(jnp.sum(first[rows, :, width : 2 * width].astype(jnp.float32), axis=0))
        stats_rows.append(in_lanes([*halves(peak), *halves(total)], (owned, STATS)))
    inputs, grads = jnp.concatenate(inputs, axis=0), jnp.concatenate(grads, axis=0)
    inputs_out[...] = inputs
    stats_out[...] = jnp.concatenate(stats_rows, axis=0)
    inputs_low, grads_low = inputs.astype(jnp.bfloat16), grads.astype(jnp.bfloat16)
    lows_out[0] = inputs_low
    lows_out[1] = grads_low
    up = dot_last(inputs_low, in_left[...].reshape(owned * rank, width))
    back = dot_last(grads_low, out_right[...].reshape(owned * rank, width))
    ranks = [*halves(from_own_block(up, owned)), *halves(from_own_block(back, owned))]
    ranks = jnp.concatenate(ranks, axis=1).astype(jnp.bfloat16)
    block = jnp.concatenate([inputs_low, grads_low, ranks], axis=1)
    second[...] = block


def pack_kernel(blocks, out):
    for group in range(out.shape[0]):
        for place in range(out.shape[1]):
            out[group, place] = blocks[group]


def hidden_kernel(
    groups,
    second,
    base_in,
    base_out,
    in_right,
    out_left,
    third,
    pair_out,
    ranks_out,
):
    members, rank, hidden = in_right.shape
    rows = second.shape[1]
    owned = rows // groups
    places = members // owned
    width = base_in.shape[1] // groups

    def gathered(columns):
        taken = [
            second[half * places : (half + 1) * places, :, columns].astype(jnp.float32)
            for half in range(groups)
        ]
        return [part.reshape(places * rows, part.shape[2]) for part in taken]

    def low_rank(value, table):
        value = value.astype(jnp.float32)
        taken = []
        for place in range(places):
            own = own_block(value[place * rows : (place + 1) * rows], owned)
            part = table[place * owned : (place + 1) * owned].reshape(owned * rank, hidden)
            taken.append(dot_plain(own, part))
        return jnp.concatenate(taken, axis=0)

    def to_rank(value, table):
        taken = []
        for place in range(places):
            part = table[place * owned : (place + 1) * owned].reshape(owned * rank, hidden)
            wide = dot_last(value[place * rows : (place + 1) * rows].astype(jnp.bfloat16), part)
            taken.append(from_own_block(wide, owned))
        return jnp.concatenate(taken, axis=0)

    ranks = functools.reduce(jnp.add, gathered(slice(2 * width, 2 * width + 4 * rank)))
    up = (ranks[:, :rank] + ranks[:, rank : 2 * rank]).astype(jnp.bfloat16)
    back = (ranks[:, 2 * rank : 3 * rank] + ranks[:, 3 * rank :]).astype(jnp.bfloat16)
    preact = low_rank(up, in_right)
    for half, part in enumerate(gathered(slice(0, width))):
        columns = slice(half * width, (half + 1) * width)
        preact = preact + dot_last(part.astype(jnp.bfloat16), base_in[:, columns])
    hidden_grad = low_rank(back, out_left)
    for half, part in enumerate(gathered(slice(width, 2 * width))):
        columns = slice(half * width, (half + 1) * width)
        hidden_grad = hidden_grad + dot_last(part.astype(jnp.bfloat16), base_out[:, columns])
    root = 0.7978845608028654
    bent = jnp.tanh(root * (preact + 0.044715 * (preact * preact * preact)))
    hidden_value = 0.5 * preact * (1.0 + bent)
    slope = 0.5 * (1.0 + bent) + 0.5 * preact * (1.0 - bent * bent) * (
        root * (1.0 + 3.0 * 0.044715 * (preact * preact))
    )
    hidden_low = hidden_value.astype(jnp.bfloat16).astype(jnp.float32)
    preact_grad = (hidden_grad * slope).astype(jnp.bfloat16).astype(jnp.float32)
    pair_out[0] = preact_grad
    pair_out[1] = hidden_low
    ranks_out[0] = up.astype(jnp.float32)
    ranks_out[1] = back.astype(jnp.float32)
    slot_term = dot_plain(preact_grad.astype(jnp.bfloat16), base_in[...]).astype(jnp.bfloat16)
    down = to_rank(preact_grad, in_right)
    value = to_rank(hidden_low, out_left)
    ranks = jnp.concatenate([down, value], axis=1).astype(jnp.bfloat16)
    for half in range(groups):
        columns = slice(half * width, (half + 1) * width)
        for place in range(places):
            taken = slice(place * rows, (place + 1) * rows)
            block = half * places + place
            third[block, :, :width] = slot_term[taken, columns]
            third[block, :, width:] = ranks[taken]


def outer_kernel(owned, left_rows, right_rows, *outs):
    rows = left_rows.shape[1] // (outs[0].shape[0] // owned)
    for number, out in enumerate(outs):
        for place in range(out.shape[0] // owned):
            taken = slice(place * rows, (place + 1) * rows)
            own = own_block(left_rows[number, taken], owned)
            product = dot_first(own, right_rows[number, taken].astype(jnp.bfloat16))
            out[place * owned : (place + 1) * owned] = product.astype(jnp.bfloat16).reshape(
                (owned,) + out.shape[1:]
            )


def halves_kernel(third, own, other):
    places = third.shape[0] // 2
    here = lax.axis_index("half")
    for out, group in ((own, here), (other, 1 - here)):
        taken = third[pl.ds(group * places, places)].astype(jnp.float32)
        out[...] = jnp.sum(taken, axis=0)


def finish_kernel(groups, ring, own, others, in_left, inputs, stats, fourth, ranks_out):
    owned, rank, width = in_left.shape
    summed = own[...] + others[1 - lax.axis_index("half")]
    ranks = summed[:, width:].astype(jnp.bfloat16).astype(jnp.float32)
    ranks_out[0] = ranks[:, :rank]
    ranks_out[1] = ranks[:, rank:]
    down = own_block(ranks[:, :rank], owned)
    grads = summed[:, :width] + dot_plain(down, in_left[...].reshape(owned * rank, width))
    grads = grads.astype(jnp.bfloat16).astype(jnp.float32)
    high, low = halves(jnp.sum(grads * inputs[...], axis=1, keepdims=True))
    lane = lax.broadcasted_iota(jnp.int32, stats.shape, 1)
    tail = jnp.where(lane == 4, high, jnp.where(lane == 5, low, stats[...]))
    block = jnp.concatenate([grads, tail], axis=1).astype(jnp.bfloat16)
    for group in range(groups):
        rows = block[group * owned : (group + 1) * owned]
        for place in range(ring):
            fourth[group * ring + place] = rows


def tokens_kernel(groups, fourth, tokens, router, logits, mixing, out):
    blocks, owned, _ = fourth.shape
    ring = blocks // groups
    width = tokens.shape[1] // groups

    def rows(half, columns):
        taken = [
            fourth[half * ring + place, :, columns].astype(jnp.float32) for place in range(ring)
        ]
        return jnp.concatenate(taken, axis=0)

    grads = jnp.concatenate([rows(half, slice(0, width)) for half in range(groups)], axis=1)
    grads = grads.astype(jnp.bfloat16)
    stats = [rows(half, slice(width, width + STATS)) for half in range(groups)]
    peak = stats[0][:, 0:1] + stats[0][:, 1:2]
    total = stats[0][:, 2:3] + stats[0][:, 3:4]
    shift = functools.reduce(jnp.add, [part[:, 4:5] + part[:, 5:6] for part in stats])
    dispatch = jnp.exp(logits[...] - peak) / total
    weight_grad = dot_last(grads, tokens[...])
    logit_grad = dispatch * (weight_grad - shift) + mixing[...]
    left = jnp.concatenate([dispatch, logit_grad], axis=0).astype(jnp.bfloat16)
    right = jnp.concatenate([grads, router[...]], axis=0)
    out[...] = dot_first(left, right).astype(jnp.bfloat16)


def to_group(block, groups):
    places = lax.axis_size("place")
    blocks = lax.all_gather(block, "half", axis=0)
    (blocks,) = call(
        pack_kernel, [array(block.dtype, groups, places, *block.shape)], [blocks], 0
    )
    blocks = blocks.reshape(groups * places, *block.shape)
    return lax.all_to_all(blocks, HALF, 0, 0, tiled=True)


def call(kernel, outs, args, flops, far=(), scratch=(), grant=24):
    size = sum(array.size * array.dtype.itemsize for array in args)
    size += sum(out.size * out.dtype.itemsize for out in outs)
    spaces = [pltpu.HBM if number in far else pltpu.VMEM for number in range(len(args))]
    return pl.pallas_call(
        kernel,
        out_shape=outs,
        in_specs=[pl.BlockSpec(memory_space=space) for space in spaces],
        out_specs=[pl.BlockSpec(memory_space=pltpu.VMEM) for _ in outs],
        scratch_shapes=scratch,
        cost_estimate=pl.CostEstimate(flops=flops, bytes_accessed=size, transcendentals=0),
        compiler_params=pltpu.CompilerParams(vmem_limit_bytes=grant * 2**20),
    )(*args)


def array(dtype, *shape):
    return jax.ShapeDtypeStruct(shape, dtype)


def local(
    tokens,
    cotangent,
    router,
    slot_outputs,
    base_in,
    base_out,
    in_left,
    in_right,
    out_left,
    out_right,
):
    groups, ring = lax.axis_size("dp"), lax.axis_size(SEQ)
    devices = groups * ring
    _, count, width = tokens.shape
    slots = router.shape[1]
    owned, slice_width, rank = in_left.shape
    members, _, hidden = in_right.shape
    rows = groups * owned
    if groups != 2 or ring % 2 or slice_width % 128 or rows % 8 or members % owned:
        return local_plain(
            tokens,
            cotangent,
            router,
            slot_outputs,
            base_in,
            base_out,
            in_left,
            in_right,
            out_left,
            out_right,
        )
    low, full = jnp.bfloat16, jnp.float32
    image_rows, cot_rows, saved = tokens[0], cotangent[0], slot_outputs[0]
    router, base_in = router.T, base_in.T
    in_left, out_left = in_left.swapaxes(1, 2), out_left.swapaxes(1, 2)
    first, logits, combine = call(
        functools.partial(sums_kernel, owned, groups),
        [
            array(low, devices, owned, 2 * slice_width + STATS),
            array(full, slots, count),
            array(full, slots, count),
        ],
        [image_rows, cot_rows, router],
        6 * count * slots * width,
        (0, 1, 2),
        [pltpu.VMEM((count, width), low)] * 2
        + [pltpu.VMEM((slots, width), low), pltpu.SemaphoreType.DMA((3,))],
        60,
    )
    first = lax.all_to_all(first, BOTH, 0, 0, tiled=True)
    second, inputs, lows, stats = call(
        functools.partial(owner_kernel, groups),
        [
            array(low, rows, 2 * slice_width + 4 * rank),
            array(full, rows, slice_width),
            array(low, 2, rows, slice_width),
            array(full, rows, STATS),
        ],
        [first, in_left, out_right],
        4 * rows * owned * rank * slice_width,
    )
    second = to_group(second, groups)
    total_rows = groups * members
    third, pair, ranks = call(
        functools.partial(hidden_kernel, groups),
        [
            array(low, ring, rows, slice_width + 2 * rank),
            array(full, 2, total_rows, hidden),
            array(full, 2, total_rows, rank),
        ],
        [second, base_in, base_out, in_right, out_left],
        6 * total_rows * hidden * (width + owned * rank),
    )
    third = lax.all_to_all(third, HALF, 0, 0, tiled=True)
    grad_in_right, grad_out_left = call(
        functools.partial(outer_kernel, owned),
        [array(low, members, rank, hidden)] * 2,
        [ranks, pair],
        4 * members * rank * hidden * rows,
    )
    own, other = call(halves_kernel, [array(full, rows, slice_width + 2 * rank)] * 2, [third], 0)
    others = lax.all_gather(other, "half", axis=0)
    fourth, ranks = call(
        functools.partial(finish_kernel, groups, ring),
        [array(low, devices, owned, slice_width + STATS), array(full, 2, rows, rank)],
        [own, others, in_left, inputs, stats],
        2 * rows * owned * rank * slice_width,
    )
    (mixing,) = call(
        mixing_kernel,
        [array(full, slots, count)],
        [cot_rows, saved, combine],
        2 * count * slots * width,
    )
    fourth = lax.all_to_all(fourth, BOTH, 0, 0, tiled=True)
    grad_in_left, grad_out_right = call(
        functools.partial(outer_kernel, owned),
        [array(low, owned, rank, slice_width)] * 2,
        [ranks, lows],
        4 * owned * rank * slice_width * rows,
    )
    (token_grad,) = call(
        functools.partial(tokens_kernel, groups),
        [array(low, count, width)],
        [fourth, image_rows, router, logits, mixing],
        6 * count * slots * width,
    )
    return (
        token_grad[None],
        grad_in_left.swapaxes(1, 2),
        grad_in_right,
        grad_out_left.swapaxes(1, 2),
        grad_out_right,
    )


def solution(mesh):
    groups, ring = mesh.shape["dp"], mesh.shape["seq"]
    split = mesh.devices.reshape(groups, groups, ring // groups)
    mesh = jax.sharding.Mesh(split, BOTH)
    in_specs = (
        P("dp", SEQ, None),
        P("dp", SEQ, None),
        P(),
        P("dp", None, None),
        P(None, SEQ),
        P(SEQ, None),
        P(SEQ, "dp", None),
        P("dp", None, SEQ),
        P("dp", SEQ, None),
        P(SEQ, None, "dp"),
    )
    out_specs = (
        P("dp", SEQ, None),
        P(SEQ, "dp", None),
        P("dp", None, SEQ),
        P("dp", SEQ, None),
        P(SEQ, None, "dp"),
    )
    return jax.shard_map(local, mesh=mesh, in_specs=in_specs, out_specs=out_specs, check_vma=False)
```

```python
import functools

import jax
import jax.numpy as jnp
from jax import lax
from jax.experimental import pallas as pl
from jax.experimental.pallas import tpu as pltpu
from jax.sharding import PartitionSpec as P

SEQ = ("half", "place")
BOTH = ("dp", *SEQ)
HALF = ("dp", "place")
STATS = 128
FLOPS_BESIDE_EXCHANGE = 10**10


def gelu_backward(preact, upstream):
    return jax.vjp(jax.nn.gelu, preact)[1](upstream)[0]


def dot_first(left, right):
    return lax.dot_general(
        left, right, (((0,), (0,)), ((), ())), preferred_element_type=jnp.float32
    )


def dot_last(left, right):
    return lax.dot_general(
        left, right, (((1,), (1,)), ((), ())), preferred_element_type=jnp.float32
    )


def split(value):
    high = lax.reduce_precision(value, 8, 7)
    low = lax.reduce_precision(value - high, 8, 7)
    return high.astype(jnp.bfloat16), low.astype(jnp.bfloat16)


def joined(high, low):
    return high.astype(jnp.float32) + low.astype(jnp.float32)


def exchange(blocks):
    flat = blocks.reshape((-1,) + blocks.shape[2:])
    return lax.all_to_all(flat, BOTH, 0, 0, tiled=True).reshape(blocks.shape)


def local_plain(
    tokens,
    cotangent,
    router,
    slot_outputs,
    base_in,
    base_out,
    in_left,
    in_right,
    out_left,
    out_right,
):
    groups, ring = lax.axis_size("dp"), lax.axis_size(SEQ)
    image_rows = tokens[0]
    cot_rows = cotangent[0]
    saved_outputs = slot_outputs[0]
    width = image_rows.shape[1]
    slots = router.shape[1]
    owned, slice_width, rank = in_left.shape
    members = in_right.shape[0]
    places = members // owned
    group, place = lax.axis_index("dp"), lax.axis_index(SEQ)

    logits = jnp.dot(image_rows, router, preferred_element_type=jnp.float32)
    peak_high, peak_low = split(jnp.max(logits, axis=0))
    near = jnp.exp(logits - joined(peak_high, peak_low))
    total_high, total_low = split(jnp.sum(near, axis=0))
    combine = jax.nn.softmax(logits, axis=1)
    sums = jnp.stack(
        [
            dot_first(near.astype(jnp.bfloat16), image_rows),
            dot_first(combine.astype(jnp.bfloat16), cot_rows),
        ],
        axis=1,
    ).astype(jnp.bfloat16)
    sums = sums.reshape(ring, owned, 2, groups, slice_width).transpose(3, 0, 1, 2, 4)
    sums = sums.reshape(groups, ring, owned, 2 * slice_width)
    stats = jnp.stack([peak_high, peak_low, total_high, total_low], axis=1)
    stats = jnp.pad(stats, ((0, 0), (0, STATS - 4))).reshape(1, ring, owned, STATS)
    stats = jnp.broadcast_to(stats, (groups, ring, owned, STATS))
    first = exchange(jnp.concatenate([sums, stats], axis=3))

    tail = 2 * slice_width
    peaks = joined(first[..., tail], first[..., tail + 1])
    totals = joined(first[..., tail + 2], first[..., tail + 3])
    peak = jnp.max(peaks, axis=1)
    near_scale = jnp.exp(peaks - peak[:, None])
    total = jnp.sum(near_scale * totals, axis=1)
    near_scale = near_scale / total[:, None]
    parts = first[..., :tail].astype(jnp.float32)
    slot_inputs = jnp.sum(parts[..., :slice_width] * near_scale[..., None], axis=1)
    inputs_own = slot_inputs.astype(jnp.bfloat16)
    grads_own = jnp.sum(parts[..., slice_width:], axis=1).astype(jnp.bfloat16)
    up_part = jnp.einsum("gjd,jdr->gjr", inputs_own, in_left, preferred_element_type=jnp.float32)
    back_part = jnp.einsum("gjd,jrd->gjr", grads_own, out_right, preferred_element_type=jnp.float32)
    second = jnp.concatenate(
        [inputs_own, grads_own, *split(up_part), *split(back_part)], axis=2
    )
    second = exchange(jnp.broadcast_to(second, (groups, ring) + second.shape))
    second = lax.dynamic_slice_in_dim(second, group * places, places, 1)

    def gathered(start):
        piece = second[..., start : start + slice_width]
        return piece.transpose(2, 1, 3, 0, 4).reshape(groups * members, width)

    def ranks(start):
        piece = joined(
            second[..., start : start + rank], second[..., start + rank : start + 2 * rank]
        )
        piece = jnp.sum(piece, axis=0).transpose(1, 0, 2, 3)
        return piece.reshape(groups, members, rank).astype(jnp.bfloat16)

    inputs_low, grads_low = gathered(0), gathered(slice_width)
    up_low, back_low = ranks(tail), ranks(tail + 2 * rank)
    hidden = base_in.shape[1]
    preact = jnp.dot(inputs_low, base_in, preferred_element_type=jnp.float32).reshape(
        groups, members, hidden
    ) + jnp.einsum("gjr,jrf->gjf", up_low, in_right, preferred_element_type=jnp.float32)
    hidden_low = jax.nn.gelu(preact).astype(jnp.bfloat16)
    hidden_grad = dot_last(grads_low, base_out).reshape(groups, members, hidden) + jnp.einsum(
        "gjr,jfr->gjf", back_low, out_left, preferred_element_type=jnp.float32
    )
    preact_grad = gelu_backward(preact, hidden_grad).astype(jnp.bfloat16)
    slot_term = dot_last(preact_grad.reshape(groups * members, hidden), base_in)
    down_term = jnp.einsum(
        "gjf,jrf->gjr", preact_grad, in_right, preferred_element_type=jnp.float32
    )
    value_term = jnp.einsum(
        "gjf,jfr->gjr", hidden_low, out_left, preferred_element_type=jnp.float32
    )
    slot_term = slot_term.astype(jnp.bfloat16).reshape(groups, places, owned, groups, slice_width)
    slot_term = slot_term.transpose(3, 1, 0, 2, 4)
    rank_term = jnp.concatenate([down_term, value_term], axis=2).astype(jnp.bfloat16)
    rank_term = rank_term.reshape(groups, places, owned, 2 * rank).transpose(1, 0, 2, 3)
    rank_term = jnp.broadcast_to(rank_term, (groups,) + rank_term.shape)
    third = jnp.concatenate([slot_term, rank_term], axis=4)
    third = lax.dynamic_update_slice_in_dim(
        jnp.zeros((groups, ring) + third.shape[2:], jnp.bfloat16), third, group * places, 1
    )
    third = exchange(third)
    third = lax.dynamic_index_in_dim(third, place // places, 0, keepdims=False)
    third = jnp.sum(third.astype(jnp.float32), axis=0)
    down_own = third[..., slice_width : slice_width + rank].astype(jnp.bfloat16)
    value_own = third[..., slice_width + rank :].astype(jnp.bfloat16)
    slot_grads_own = (
        third[..., :slice_width]
        + jnp.einsum("gjr,jdr->gjd", down_own, in_left, preferred_element_type=jnp.float32)
    ).astype(jnp.bfloat16)
    shift_part = jnp.sum(slot_grads_own.astype(jnp.float32) * slot_inputs, axis=2)
    stats = jnp.stack([*split(peak), *split(total), *split(shift_part)], axis=2)
    stats = jnp.pad(stats, ((0, 0), (0, 0), (0, STATS - 6)))
    fourth = jnp.concatenate([slot_grads_own, stats], axis=2)[:, None]
    fourth = exchange(jnp.broadcast_to(fourth, (groups, ring) + fourth.shape[2:]))
    slot_grads = fourth[..., :slice_width].transpose(1, 2, 0, 3).reshape(slots, width)
    stats = fourth[..., slice_width:].astype(jnp.float32).reshape(groups, slots, STATS)
    slot_peak = stats[0, :, 0] + stats[0, :, 1]
    slot_total = stats[0, :, 2] + stats[0, :, 3]
    shift_back = jnp.sum(stats[:, :, 4] + stats[:, :, 5], axis=0)

    dispatch = jnp.exp(logits - slot_peak) / slot_total
    dispatch_low = dispatch.astype(jnp.bfloat16)
    weight_grad = dot_last(image_rows, slot_grads)
    dispatch_logit = dispatch * (weight_grad - shift_back)
    mixing_grad = dot_last(cot_rows, saved_outputs)
    combine_logit = combine * (mixing_grad - jnp.sum(combine * mixing_grad, axis=1, keepdims=True))
    logit_grad = (dispatch_logit + combine_logit).astype(jnp.bfloat16)
    token_grad = (
        jnp.dot(dispatch_low, slot_grads, preferred_element_type=jnp.float32)
        + dot_last(logit_grad, router)
    ).astype(jnp.bfloat16)
    grad_in_right = jnp.einsum(
        "gjr,gjf->jrf", up_low, preact_grad, preferred_element_type=jnp.float32
    ).astype(jnp.bfloat16)
    grad_out_left = jnp.einsum(
        "gjf,gjr->jfr", hidden_low, back_low, preferred_element_type=jnp.float32
    ).astype(jnp.bfloat16)
    grad_in_left = jnp.einsum(
        "gjd,gjr->jdr", inputs_own, down_own, preferred_element_type=jnp.float32
    ).astype(jnp.bfloat16)
    grad_out_right = jnp.einsum(
        "gjr,gjd->jrd", value_own, grads_own, preferred_element_type=jnp.float32
    ).astype(jnp.bfloat16)
    return (token_grad[None], grad_in_left, grad_in_right, grad_out_left, grad_out_right)


def dot_plain(left, right):
    return jnp.dot(left, right, preferred_element_type=jnp.float32)


def halves(value):
    high = value.astype(jnp.bfloat16).astype(jnp.float32)
    low = (value - high).astype(jnp.bfloat16).astype(jnp.float32)
    return high, low


def in_lanes(columns, shape):
    lane = lax.broadcasted_iota(jnp.int32, shape, len(shape) - 1)
    out = jnp.zeros(shape, jnp.float32)
    for number, column in enumerate(columns):
        out = jnp.where(lane == number, column, out)
    return out


def own_block(value, owned):
    rows, rank = value.shape
    wide = jnp.concatenate([value] * owned, axis=1)
    shape = (rows, owned * rank)
    block = lax.broadcasted_iota(jnp.int32, shape, 1) // rank
    expert = lax.broadcasted_iota(jnp.int32, shape, 0) % owned
    return jnp.where(block == expert, wide, 0.0).astype(jnp.bfloat16)


def from_own_block(value, owned):
    rows, wide = value.shape
    rank = wide // owned
    block = lax.broadcasted_iota(jnp.int32, value.shape, 1) // rank
    expert = lax.broadcasted_iota(jnp.int32, value.shape, 0) % owned
    kept = jnp.where(block == expert, value, 0.0)
    out = kept[:, :rank]
    for number in range(1, owned):
        out = out + kept[:, number * rank : (number + 1) * rank]
    return out


def sums_kernel(
    owned,
    groups,
    tokens_far,
    cotangent_far,
    router_far,
    first,
    logits_out,
    combine_out,
    tokens,
    cotangent,
    router,
    arrived,
):
    ring = first.shape[0] // groups
    copies = [
        pltpu.make_async_copy(far, near, arrived.at[number])
        for number, (far, near) in enumerate(
            [(router_far, router), (tokens_far, tokens), (cotangent_far, cotangent)]
        )
    ]
    for copy in copies:
        copy.start()
    copies[0].wait()
    copies[1].wait()
    image_rows = tokens[...]
    logits = dot_last(router[...], image_rows)
    high, low = halves(jnp.max(logits, axis=1, keepdims=True))
    near = jnp.exp(logits - (high + low))
    total_high, total_low = halves(jnp.sum(near, axis=1, keepdims=True))
    spread = jnp.exp(logits - jnp.max(logits, axis=0, keepdims=True))
    combine = spread / jnp.sum(spread, axis=0, keepdims=True)
    logits_out[...] = logits
    combine_out[...] = combine
    stats = in_lanes([high, low, total_high, total_low], (logits.shape[0], STATS))
    stats = stats.astype(jnp.bfloat16)
    inputs = dot_plain(near.astype(jnp.bfloat16), image_rows).astype(jnp.bfloat16)
    copies[2].wait()
    grads = dot_plain(combine.astype(jnp.bfloat16), cotangent[...]).astype(jnp.bfloat16)
    width = inputs.shape[1] // groups
    for group in range(groups):
        columns = slice(group * width, (group + 1) * width)
        for place in range(ring):
            rows = slice(place * owned, (place + 1) * owned)
            block = group * ring + place
            first[block, :, :width] = inputs[rows, columns]
            first[block, :, width : 2 * width] = grads[rows, columns]
            first[block, :, 2 * width :] = stats[rows, :]


def mixing_kernel(cotangent, saved, combine, out):
    mixing = dot_last(saved[...], cotangent[...])
    weights = combine[...]
    out[...] = weights * (mixing - jnp.sum(weights * mixing, axis=0, keepdims=True))


def owner_kernel(groups, first, in_left, out_right, second, inputs_out, lows_out, stats_out):
    ring = first.shape[0] // groups
    owned, rank, width = in_left.shape
    inputs, grads, stats_rows = [], [], []
    for group in range(groups):
        rows = slice(group * ring, (group + 1) * ring)
        stats = first[rows, :, 2 * width :].astype(jnp.float32)
        peaks = stats[:, :, 0:1] + stats[:, :, 1:2]
        totals = stats[:, :, 2:3] + stats[:, :, 3:4]
        peak = jnp.max(peaks, axis=0)
        scale = jnp.exp(peaks - peak[None])
        total = jnp.sum(scale * totals, axis=0)
        scale = scale / total[None]
        inputs.append(jnp.sum(first[rows, :, :width].astype(jnp.float32) * scale, axis=0))
        grads.append(jnp.sum(first[rows, :, width : 2 * width].astype(jnp.float32), axis=0))
        stats_rows.append(in_lanes([*halves(peak), *halves(total)], (owned, STATS)))
    inputs, grads = jnp.concatenate(inputs, axis=0), jnp.concatenate(grads, axis=0)
    inputs_out[...] = inputs
    stats_out[...] = jnp.concatenate(stats_rows, axis=0)
    inputs_low, grads_low = inputs.astype(jnp.bfloat16), grads.astype(jnp.bfloat16)
    lows_out[0] = inputs_low
    lows_out[1] = grads_low
    up = dot_last(inputs_low, in_left[...].reshape(owned * rank, width))
    back = dot_last(grads_low, out_right[...].reshape(owned * rank, width))
    ranks = [*halves(from_own_block(up, owned)), *halves(from_own_block(back, owned))]
    ranks = jnp.concatenate(ranks, axis=1).astype(jnp.bfloat16)
    block = jnp.concatenate([inputs_low, grads_low, ranks], axis=1)
    second[...] = block


def pack_kernel(blocks, out):
    for group in range(out.shape[0]):
        for place in range(out.shape[1]):
            out[group, place] = blocks[group]


def hidden_kernel(
    groups,
    second,
    base_in,
    base_out,
    in_right,
    out_left,
    third,
    pair_out,
    ranks_out,
):
    members, rank, hidden = in_right.shape
    rows = second.shape[1]
    owned = rows // groups
    places = members // owned
    width = base_in.shape[1] // groups

    def gathered(columns):
        taken = [
            second[half * places : (half + 1) * places, :, columns].astype(jnp.float32)
            for half in range(groups)
        ]
        return [part.reshape(places * rows, part.shape[2]) for part in taken]

    def low_rank(value, table):
        value = value.astype(jnp.float32)
        taken = []
        for place in range(places):
            own = own_block(value[place * rows : (place + 1) * rows], owned)
            part = table[place * owned : (place + 1) * owned].reshape(owned * rank, hidden)
            taken.append(dot_plain(own, part))
        return jnp.concatenate(taken, axis=0)

    def to_rank(value, table):
        taken = []
        for place in range(places):
            part = table[place * owned : (place + 1) * owned].reshape(owned * rank, hidden)
            wide = dot_last(value[place * rows : (place + 1) * rows].astype(jnp.bfloat16), part)
            taken.append(from_own_block(wide, owned))
        return jnp.concatenate(taken, axis=0)

    ranks = functools.reduce(jnp.add, gathered(slice(2 * width, 2 * width + 4 * rank)))
    up = (ranks[:, :rank] + ranks[:, rank : 2 * rank]).astype(jnp.bfloat16)
    back = (ranks[:, 2 * rank : 3 * rank] + ranks[:, 3 * rank :]).astype(jnp.bfloat16)
    preact = low_rank(up, in_right)
    for half, part in enumerate(gathered(slice(0, width))):
        columns = slice(half * width, (half + 1) * width)
        preact = preact + dot_last(part.astype(jnp.bfloat16), base_in[:, columns])
    hidden_grad = low_rank(back, out_left)
    for half, part in enumerate(gathered(slice(width, 2 * width))):
        columns = slice(half * width, (half + 1) * width)
        hidden_grad = hidden_grad + dot_last(part.astype(jnp.bfloat16), base_out[:, columns])
    root = 0.7978845608028654
    bent = jnp.tanh(root * (preact + 0.044715 * (preact * preact * preact)))
    hidden_value = 0.5 * preact * (1.0 + bent)
    slope = 0.5 * (1.0 + bent) + 0.5 * preact * (1.0 - bent * bent) * (
        root * (1.0 + 3.0 * 0.044715 * (preact * preact))
    )
    hidden_low = hidden_value.astype(jnp.bfloat16).astype(jnp.float32)
    preact_grad = (hidden_grad * slope).astype(jnp.bfloat16).astype(jnp.float32)
    pair_out[0] = preact_grad
    pair_out[1] = hidden_low
    ranks_out[0] = up.astype(jnp.float32)
    ranks_out[1] = back.astype(jnp.float32)
    slot_term = dot_plain(preact_grad.astype(jnp.bfloat16), base_in[...]).astype(jnp.bfloat16)
    down = to_rank(preact_grad, in_right)
    value = to_rank(hidden_low, out_left)
    ranks = jnp.concatenate([down, value], axis=1).astype(jnp.bfloat16)
    for half in range(groups):
        columns = slice(half * width, (half + 1) * width)
        for place in range(places):
            taken = slice(place * rows, (place + 1) * rows)
            block = half * places + place
            third[block, :, :width] = slot_term[taken, columns]
            third[block, :, width:] = ranks[taken]


def outer_kernel(owned, left_rows, right_rows, *outs):
    rows = left_rows.shape[1] // (outs[0].shape[0] // owned)
    for number, out in enumerate(outs):
        for place in range(out.shape[0] // owned):
            taken = slice(place * rows, (place + 1) * rows)
            own = own_block(left_rows[number, taken], owned)
            product = dot_first(own, right_rows[number, taken].astype(jnp.bfloat16))
            out[place * owned : (place + 1) * owned] = product.astype(jnp.bfloat16).reshape(
                (owned,) + out.shape[1:]
            )


def halves_kernel(third, own, other):
    places = third.shape[0] // 2
    here = lax.axis_index("half")
    for out, group in ((own, here), (other, 1 - here)):
        taken = third[pl.ds(group * places, places)].astype(jnp.float32)
        out[...] = jnp.sum(taken, axis=0)


def finish_kernel(groups, ring, own, others, in_left, inputs, stats, fourth, ranks_out):
    owned, rank, width = in_left.shape
    summed = own[...] + others[1 - lax.axis_index("half")]
    ranks = summed[:, width:].astype(jnp.bfloat16).astype(jnp.float32)
    ranks_out[0] = ranks[:, :rank]
    ranks_out[1] = ranks[:, rank:]
    down = own_block(ranks[:, :rank], owned)
    grads = summed[:, :width] + dot_plain(down, in_left[...].reshape(owned * rank, width))
    grads = grads.astype(jnp.bfloat16).astype(jnp.float32)
    high, low = halves(jnp.sum(grads * inputs[...], axis=1, keepdims=True))
    lane = lax.broadcasted_iota(jnp.int32, stats.shape, 1)
    tail = jnp.where(lane == 4, high, jnp.where(lane == 5, low, stats[...]))
    block = jnp.concatenate([grads, tail], axis=1).astype(jnp.bfloat16)
    for group in range(groups):
        rows = block[group * owned : (group + 1) * owned]
        for place in range(ring):
            fourth[group * ring + place] = rows


def tokens_kernel(groups, fourth, tokens, router, logits, mixing, out):
    blocks, owned, _ = fourth.shape
    ring = blocks // groups
    width = tokens.shape[1] // groups

    def rows(half, columns):
        taken = [
            fourth[half * ring + place, :, columns].astype(jnp.float32) for place in range(ring)
        ]
        return jnp.concatenate(taken, axis=0)

    grads = jnp.concatenate([rows(half, slice(0, width)) for half in range(groups)], axis=1)
    grads = grads.astype(jnp.bfloat16)
    stats = [rows(half, slice(width, width + STATS)) for half in range(groups)]
    peak = stats[0][:, 0:1] + stats[0][:, 1:2]
    total = stats[0][:, 2:3] + stats[0][:, 3:4]
    shift = functools.reduce(jnp.add, [part[:, 4:5] + part[:, 5:6] for part in stats])
    dispatch = jnp.exp(logits[...] - peak) / total
    weight_grad = dot_last(grads, tokens[...])
    logit_grad = dispatch * (weight_grad - shift) + mixing[...]
    left = jnp.concatenate([dispatch, logit_grad], axis=0).astype(jnp.bfloat16)
    right = jnp.concatenate([grads, router[...]], axis=0)
    out[...] = dot_first(left, right).astype(jnp.bfloat16)


def to_group(block, groups):
    places = lax.axis_size("place")
    blocks = lax.all_gather(block, "half", axis=0)
    (blocks,) = call(
        pack_kernel, [array(block.dtype, groups, places, *block.shape)], [blocks], FLOPS_BESIDE_EXCHANGE
    )
    blocks = blocks.reshape(groups * places, *block.shape)
    return lax.all_to_all(blocks, HALF, 0, 0, tiled=True)


def call(kernel, outs, args, flops, far=(), scratch=(), grant=24):
    size = sum(array.size * array.dtype.itemsize for array in args)
    size += sum(out.size * out.dtype.itemsize for out in outs)
    spaces = [pltpu.HBM if number in far else pltpu.VMEM for number in range(len(args))]
    return pl.pallas_call(
        kernel,
        out_shape=outs,
        in_specs=[pl.BlockSpec(memory_space=space) for space in spaces],
        out_specs=[pl.BlockSpec(memory_space=pltpu.VMEM) for _ in outs],
        scratch_shapes=scratch,
        cost_estimate=pl.CostEstimate(flops=flops, bytes_accessed=size, transcendentals=0),
        compiler_params=pltpu.CompilerParams(vmem_limit_bytes=grant * 2**20),
    )(*args)


def array(dtype, *shape):
    return jax.ShapeDtypeStruct(shape, dtype)


def local(
    tokens,
    cotangent,
    router,
    slot_outputs,
    base_in,
    base_out,
    in_left,
    in_right,
    out_left,
    out_right,
):
    groups, ring = lax.axis_size("dp"), lax.axis_size(SEQ)
    devices = groups * ring
    _, count, width = tokens.shape
    slots = router.shape[1]
    owned, slice_width, rank = in_left.shape
    members, _, hidden = in_right.shape
    rows = groups * owned
    if groups != 2 or ring % 2 or slice_width % 128 or rows % 8 or members % owned:
        return local_plain(
            tokens,
            cotangent,
            router,
            slot_outputs,
            base_in,
            base_out,
            in_left,
            in_right,
            out_left,
            out_right,
        )
    low, full = jnp.bfloat16, jnp.float32
    image_rows, cot_rows, saved = tokens[0], cotangent[0], slot_outputs[0]
    router, base_in = router.T, base_in.T
    in_left, out_left = in_left.swapaxes(1, 2), out_left.swapaxes(1, 2)
    first, logits, combine = call(
        functools.partial(sums_kernel, owned, groups),
        [
            array(low, devices, owned, 2 * slice_width + STATS),
            array(full, slots, count),
            array(full, slots, count),
        ],
        [image_rows, cot_rows, router],
        6 * count * slots * width + FLOPS_BESIDE_EXCHANGE,
        (0, 1, 2),
        [pltpu.VMEM((count, width), low)] * 2
        + [pltpu.VMEM((slots, width), low), pltpu.SemaphoreType.DMA((3,))],
        60,
    )
    first = lax.all_to_all(first, BOTH, 0, 0, tiled=True)
    second, inputs, lows, stats = call(
        functools.partial(owner_kernel, groups),
        [
            array(low, rows, 2 * slice_width + 4 * rank),
            array(full, rows, slice_width),
            array(low, 2, rows, slice_width),
            array(full, rows, STATS),
        ],
        [first, in_left, out_right],
        4 * rows * owned * rank * slice_width,
    )
    second = to_group(second, groups)
    total_rows = groups * members
    third, pair, ranks = call(
        functools.partial(hidden_kernel, groups),
        [
            array(low, ring, rows, slice_width + 2 * rank),
            array(full, 2, total_rows, hidden),
            array(full, 2, total_rows, rank),
        ],
        [second, base_in, base_out, in_right, out_left],
        6 * total_rows * hidden * (width + owned * rank),
    )
    third = lax.all_to_all(third, HALF, 0, 0, tiled=True)
    grad_in_right, grad_out_left = call(
        functools.partial(outer_kernel, owned),
        [array(low, members, rank, hidden)] * 2,
        [ranks, pair],
        4 * members * rank * hidden * rows,
    )
    own, other = call(halves_kernel, [array(full, rows, slice_width + 2 * rank)] * 2, [third], 0)
    others = lax.all_gather(other, "half", axis=0)
    fourth, ranks = call(
        functools.partial(finish_kernel, groups, ring),
        [array(low, devices, owned, slice_width + STATS), array(full, 2, rows, rank)],
        [own, others, in_left, inputs, stats],
        2 * rows * owned * rank * slice_width,
    )
    (mixing,) = call(
        mixing_kernel,
        [array(full, slots, count)],
        [cot_rows, saved, combine],
        2 * count * slots * width,
    )
    fourth = lax.all_to_all(fourth, BOTH, 0, 0, tiled=True)
    grad_in_left, grad_out_right = call(
        functools.partial(outer_kernel, owned),
        [array(low, owned, rank, slice_width)] * 2,
        [ranks, lows],
        4 * owned * rank * slice_width * rows,
    )
    (token_grad,) = call(
        functools.partial(tokens_kernel, groups),
        [array(low, count, width)],
        [fourth, image_rows, router, logits, mixing],
        6 * count * slots * width,
    )
    return (
        token_grad[None],
        grad_in_left.swapaxes(1, 2),
        grad_in_right,
        grad_out_left.swapaxes(1, 2),
        grad_out_right,
    )


def solution(mesh):
    groups, ring = mesh.shape["dp"], mesh.shape["seq"]
    split = mesh.devices.reshape(groups, groups, ring // groups)
    mesh = jax.sharding.Mesh(split, BOTH)
    in_specs = (
        P("dp", SEQ, None),
        P("dp", SEQ, None),
        P(),
        P("dp", None, None),
        P(None, SEQ),
        P(SEQ, None),
        P(SEQ, "dp", None),
        P("dp", None, SEQ),
        P("dp", SEQ, None),
        P(SEQ, None, "dp"),
    )
    out_specs = (
        P("dp", SEQ, None),
        P(SEQ, "dp", None),
        P("dp", None, SEQ),
        P("dp", SEQ, None),
        P(SEQ, None, "dp"),
    )
    return jax.shard_map(local, mesh=mesh, in_specs=in_specs, out_specs=out_specs, check_vma=False)
```

```python
import functools

import jax
import jax.numpy as jnp
from jax import lax
from jax.experimental import pallas as pl
from jax.experimental.pallas import tpu as pltpu
from jax.sharding import PartitionSpec as P

SEQ = ("half", "place")
BOTH = ("dp", *SEQ)
HALF = ("dp", "place")
STATS = 128
FLOPS_BESIDE_EXCHANGE = 10**10


def gelu_backward(preact, upstream):
    return jax.vjp(jax.nn.gelu, preact)[1](upstream)[0]


def dot_first(left, right):
    return lax.dot_general(
        left, right, (((0,), (0,)), ((), ())), preferred_element_type=jnp.float32
    )


def dot_last(left, right):
    return lax.dot_general(
        left, right, (((1,), (1,)), ((), ())), preferred_element_type=jnp.float32
    )


def split(value):
    high = lax.reduce_precision(value, 8, 7)
    low = lax.reduce_precision(value - high, 8, 7)
    return high.astype(jnp.bfloat16), low.astype(jnp.bfloat16)


def joined(high, low):
    return high.astype(jnp.float32) + low.astype(jnp.float32)


def exchange(blocks):
    flat = blocks.reshape((-1,) + blocks.shape[2:])
    return lax.all_to_all(flat, BOTH, 0, 0, tiled=True).reshape(blocks.shape)


def local_plain(
    tokens,
    cotangent,
    router,
    slot_outputs,
    base_in,
    base_out,
    in_left,
    in_right,
    out_left,
    out_right,
):
    groups, ring = lax.axis_size("dp"), lax.axis_size(SEQ)
    image_rows = tokens[0]
    cot_rows = cotangent[0]
    saved_outputs = slot_outputs[0]
    width = image_rows.shape[1]
    slots = router.shape[1]
    owned, slice_width, rank = in_left.shape
    members = in_right.shape[0]
    places = members // owned
    group, place = lax.axis_index("dp"), lax.axis_index(SEQ)

    logits = jnp.dot(image_rows, router, preferred_element_type=jnp.float32)
    peak_high, peak_low = split(jnp.max(logits, axis=0))
    near = jnp.exp(logits - joined(peak_high, peak_low))
    total_high, total_low = split(jnp.sum(near, axis=0))
    combine = jax.nn.softmax(logits, axis=1)
    sums = jnp.stack(
        [
            dot_first(near.astype(jnp.bfloat16), image_rows),
            dot_first(combine.astype(jnp.bfloat16), cot_rows),
        ],
        axis=1,
    ).astype(jnp.bfloat16)
    sums = sums.reshape(ring, owned, 2, groups, slice_width).transpose(3, 0, 1, 2, 4)
    sums = sums.reshape(groups, ring, owned, 2 * slice_width)
    stats = jnp.stack([peak_high, peak_low, total_high, total_low], axis=1)
    stats = jnp.pad(stats, ((0, 0), (0, STATS - 4))).reshape(1, ring, owned, STATS)
    stats = jnp.broadcast_to(stats, (groups, ring, owned, STATS))
    first = exchange(jnp.concatenate([sums, stats], axis=3))

    tail = 2 * slice_width
    peaks = joined(first[..., tail], first[..., tail + 1])
    totals = joined(first[..., tail + 2], first[..., tail + 3])
    peak = jnp.max(peaks, axis=1)
    near_scale = jnp.exp(peaks - peak[:, None])
    total = jnp.sum(near_scale * totals, axis=1)
    near_scale = near_scale / total[:, None]
    parts = first[..., :tail].astype(jnp.float32)
    slot_inputs = jnp.sum(parts[..., :slice_width] * near_scale[..., None], axis=1)
    inputs_own = slot_inputs.astype(jnp.bfloat16)
    grads_own = jnp.sum(parts[..., slice_width:], axis=1).astype(jnp.bfloat16)
    up_part = jnp.einsum("gjd,jdr->gjr", inputs_own, in_left, preferred_element_type=jnp.float32)
    back_part = jnp.einsum("gjd,jrd->gjr", grads_own, out_right, preferred_element_type=jnp.float32)
    second = jnp.concatenate(
        [inputs_own, grads_own, *split(up_part), *split(back_part)], axis=2
    )
    second = exchange(jnp.broadcast_to(second, (groups, ring) + second.shape))
    second = lax.dynamic_slice_in_dim(second, group * places, places, 1)

    def gathered(start):
        piece = second[..., start : start + slice_width]
        return piece.transpose(2, 1, 3, 0, 4).reshape(groups * members, width)

    def ranks(start):
        piece = joined(
            second[..., start : start + rank], second[..., start + rank : start + 2 * rank]
        )
        piece = jnp.sum(piece, axis=0).transpose(1, 0, 2, 3)
        return piece.reshape(groups, members, rank).astype(jnp.bfloat16)

    inputs_low, grads_low = gathered(0), gathered(slice_width)
    up_low, back_low = ranks(tail), ranks(tail + 2 * rank)
    hidden = base_in.shape[1]
    preact = jnp.dot(inputs_low, base_in, preferred_element_type=jnp.float32).reshape(
        groups, members, hidden
    ) + jnp.einsum("gjr,jrf->gjf", up_low, in_right, preferred_element_type=jnp.float32)
    hidden_low = jax.nn.gelu(preact).astype(jnp.bfloat16)
    hidden_grad = dot_last(grads_low, base_out).reshape(groups, members, hidden) + jnp.einsum(
        "gjr,jfr->gjf", back_low, out_left, preferred_element_type=jnp.float32
    )
    preact_grad = gelu_backward(preact, hidden_grad).astype(jnp.bfloat16)
    slot_term = dot_last(preact_grad.reshape(groups * members, hidden), base_in)
    down_term = jnp.einsum(
        "gjf,jrf->gjr", preact_grad, in_right, preferred_element_type=jnp.float32
    )
    value_term = jnp.einsum(
        "gjf,jfr->gjr", hidden_low, out_left, preferred_element_type=jnp.float32
    )
    slot_term = slot_term.astype(jnp.bfloat16).reshape(groups, places, owned, groups, slice_width)
    slot_term = slot_term.transpose(3, 1, 0, 2, 4)
    rank_term = jnp.concatenate([down_term, value_term], axis=2).astype(jnp.bfloat16)
    rank_term = rank_term.reshape(groups, places, owned, 2 * rank).transpose(1, 0, 2, 3)
    rank_term = jnp.broadcast_to(rank_term, (groups,) + rank_term.shape)
    third = jnp.concatenate([slot_term, rank_term], axis=4)
    third = lax.dynamic_update_slice_in_dim(
        jnp.zeros((groups, ring) + third.shape[2:], jnp.bfloat16), third, group * places, 1
    )
    third = exchange(third)
    third = lax.dynamic_index_in_dim(third, place // places, 0, keepdims=False)
    third = jnp.sum(third.astype(jnp.float32), axis=0)
    down_own = third[..., slice_width : slice_width + rank].astype(jnp.bfloat16)
    value_own = third[..., slice_width + rank :].astype(jnp.bfloat16)
    slot_grads_own = (
        third[..., :slice_width]
        + jnp.einsum("gjr,jdr->gjd", down_own, in_left, preferred_element_type=jnp.float32)
    ).astype(jnp.bfloat16)
    shift_part = jnp.sum(slot_grads_own.astype(jnp.float32) * slot_inputs, axis=2)
    stats = jnp.stack([*split(peak), *split(total), *split(shift_part)], axis=2)
    stats = jnp.pad(stats, ((0, 0), (0, 0), (0, STATS - 6)))
    fourth = jnp.concatenate([slot_grads_own, stats], axis=2)[:, None]
    fourth = exchange(jnp.broadcast_to(fourth, (groups, ring) + fourth.shape[2:]))
    slot_grads = fourth[..., :slice_width].transpose(1, 2, 0, 3).reshape(slots, width)
    stats = fourth[..., slice_width:].astype(jnp.float32).reshape(groups, slots, STATS)
    slot_peak = stats[0, :, 0] + stats[0, :, 1]
    slot_total = stats[0, :, 2] + stats[0, :, 3]
    shift_back = jnp.sum(stats[:, :, 4] + stats[:, :, 5], axis=0)

    dispatch = jnp.exp(logits - slot_peak) / slot_total
    dispatch_low = dispatch.astype(jnp.bfloat16)
    weight_grad = dot_last(image_rows, slot_grads)
    dispatch_logit = dispatch * (weight_grad - shift_back)
    mixing_grad = dot_last(cot_rows, saved_outputs)
    combine_logit = combine * (mixing_grad - jnp.sum(combine * mixing_grad, axis=1, keepdims=True))
    logit_grad = (dispatch_logit + combine_logit).astype(jnp.bfloat16)
    token_grad = (
        jnp.dot(dispatch_low, slot_grads, preferred_element_type=jnp.float32)
        + dot_last(logit_grad, router)
    ).astype(jnp.bfloat16)
    grad_in_right = jnp.einsum(
        "gjr,gjf->jrf", up_low, preact_grad, preferred_element_type=jnp.float32
    ).astype(jnp.bfloat16)
    grad_out_left = jnp.einsum(
        "gjf,gjr->jfr", hidden_low, back_low, preferred_element_type=jnp.float32
    ).astype(jnp.bfloat16)
    grad_in_left = jnp.einsum(
        "gjd,gjr->jdr", inputs_own, down_own, preferred_element_type=jnp.float32
    ).astype(jnp.bfloat16)
    grad_out_right = jnp.einsum(
        "gjr,gjd->jrd", value_own, grads_own, preferred_element_type=jnp.float32
    ).astype(jnp.bfloat16)
    return (token_grad[None], grad_in_left, grad_in_right, grad_out_left, grad_out_right)


def dot_plain(left, right):
    return jnp.dot(left, right, preferred_element_type=jnp.float32)


def halves(value):
    high = value.astype(jnp.bfloat16).astype(jnp.float32)
    low = (value - high).astype(jnp.bfloat16).astype(jnp.float32)
    return high, low


def in_lanes(columns, shape):
    lane = lax.broadcasted_iota(jnp.int32, shape, len(shape) - 1)
    out = jnp.zeros(shape, jnp.float32)
    for number, column in enumerate(columns):
        out = jnp.where(lane == number, column, out)
    return out


def own_block(value, owned):
    rows, rank = value.shape
    wide = jnp.concatenate([value] * owned, axis=1)
    shape = (rows, owned * rank)
    block = lax.broadcasted_iota(jnp.int32, shape, 1) // rank
    expert = lax.broadcasted_iota(jnp.int32, shape, 0) % owned
    return jnp.where(block == expert, wide, 0.0).astype(jnp.bfloat16)


def from_own_block(value, owned):
    rows, wide = value.shape
    rank = wide // owned
    block = lax.broadcasted_iota(jnp.int32, value.shape, 1) // rank
    expert = lax.broadcasted_iota(jnp.int32, value.shape, 0) % owned
    kept = jnp.where(block == expert, value, 0.0)
    out = kept[:, :rank]
    for number in range(1, owned):
        out = out + kept[:, number * rank : (number + 1) * rank]
    return out


def early_kernel(out):
    out[...] = jnp.zeros(out.shape, out.dtype)


def sums_kernel(owned, groups, _, tokens, cotangent, router, first, logits_out, combine_out):
    ring = first.shape[0] // groups
    image_rows = tokens[...]
    logits = dot_last(router[...], image_rows)
    high, low = halves(jnp.max(logits, axis=1, keepdims=True))
    near = jnp.exp(logits - (high + low))
    total_high, total_low = halves(jnp.sum(near, axis=1, keepdims=True))
    spread = jnp.exp(logits - jnp.max(logits, axis=0, keepdims=True))
    combine = spread / jnp.sum(spread, axis=0, keepdims=True)
    logits_out[...] = logits
    combine_out[...] = combine
    stats = in_lanes([high, low, total_high, total_low], (logits.shape[0], STATS))
    stats = stats.astype(jnp.bfloat16)
    inputs = dot_plain(near.astype(jnp.bfloat16), image_rows).astype(jnp.bfloat16)
    grads = dot_plain(combine.astype(jnp.bfloat16), cotangent[...]).astype(jnp.bfloat16)
    width = inputs.shape[1] // groups
    for group in range(groups):
        columns = slice(group * width, (group + 1) * width)
        for place in range(ring):
            rows = slice(place * owned, (place + 1) * owned)
            block = group * ring + place
            first[block, :, :width] = inputs[rows, columns]
            first[block, :, width : 2 * width] = grads[rows, columns]
            first[block, :, 2 * width :] = stats[rows, :]


def mixing_kernel(cotangent, saved, combine, out):
    mixing = dot_last(saved[...], cotangent[...])
    weights = combine[...]
    out[...] = weights * (mixing - jnp.sum(weights * mixing, axis=0, keepdims=True))


def owner_kernel(groups, first, in_left, out_right, second, inputs_out, lows_out, stats_out):
    ring = first.shape[0] // groups
    owned, rank, width = in_left.shape
    inputs, grads, stats_rows = [], [], []
    for group in range(groups):
        rows = slice(group * ring, (group + 1) * ring)
        stats = first[rows, :, 2 * width :].astype(jnp.float32)
        peaks = stats[:, :, 0:1] + stats[:, :, 1:2]
        totals = stats[:, :, 2:3] + stats[:, :, 3:4]
        peak = jnp.max(peaks, axis=0)
        scale = jnp.exp(peaks - peak[None])
        total = jnp.sum(scale * totals, axis=0)
        scale = scale / total[None]
        inputs.append(jnp.sum(first[rows, :, :width].astype(jnp.float32) * scale, axis=0))
        grads.append(jnp.sum(first[rows, :, width : 2 * width].astype(jnp.float32), axis=0))
        stats_rows.append(in_lanes([*halves(peak), *halves(total)], (owned, STATS)))
    inputs, grads = jnp.concatenate(inputs, axis=0), jnp.concatenate(grads, axis=0)
    inputs_out[...] = inputs
    stats_out[...] = jnp.concatenate(stats_rows, axis=0)
    inputs_low, grads_low = inputs.astype(jnp.bfloat16), grads.astype(jnp.bfloat16)
    lows_out[0] = inputs_low
    lows_out[1] = grads_low
    up = dot_last(inputs_low, in_left[...].reshape(owned * rank, width))
    back = dot_last(grads_low, out_right[...].reshape(owned * rank, width))
    ranks = [*halves(from_own_block(up, owned)), *halves(from_own_block(back, owned))]
    ranks = jnp.concatenate(ranks, axis=1).astype(jnp.bfloat16)
    block = jnp.concatenate([inputs_low, grads_low, ranks], axis=1)
    second[...] = block


def pack_kernel(blocks, out):
    for group in range(out.shape[0]):
        for place in range(out.shape[1]):
            out[group, place] = blocks[group]


def hidden_kernel(
    groups,
    second,
    base_in,
    base_out,
    in_right,
    out_left,
    third,
    pair_out,
    ranks_out,
):
    members, rank, hidden = in_right.shape
    rows = second.shape[1]
    owned = rows // groups
    places = members // owned
    width = base_in.shape[1] // groups

    def gathered(columns):
        taken = [
            second[half * places : (half + 1) * places, :, columns].astype(jnp.float32)
            for half in range(groups)
        ]
        return [part.reshape(places * rows, part.shape[2]) for part in taken]

    def low_rank(value, table):
        value = value.astype(jnp.float32)
        taken = []
        for place in range(places):
            own = own_block(value[place * rows : (place + 1) * rows], owned)
            part = table[place * owned : (place + 1) * owned].reshape(owned * rank, hidden)
            taken.append(dot_plain(own, part))
        return jnp.concatenate(taken, axis=0)

    def to_rank(value, table):
        taken = []
        for place in range(places):
            part = table[place * owned : (place + 1) * owned].reshape(owned * rank, hidden)
            wide = dot_last(value[place * rows : (place + 1) * rows].astype(jnp.bfloat16), part)
            taken.append(from_own_block(wide, owned))
        return jnp.concatenate(taken, axis=0)

    ranks = functools.reduce(jnp.add, gathered(slice(2 * width, 2 * width + 4 * rank)))
    up = (ranks[:, :rank] + ranks[:, rank : 2 * rank]).astype(jnp.bfloat16)
    back = (ranks[:, 2 * rank : 3 * rank] + ranks[:, 3 * rank :]).astype(jnp.bfloat16)
    preact = low_rank(up, in_right)
    for half, part in enumerate(gathered(slice(0, width))):
        columns = slice(half * width, (half + 1) * width)
        preact = preact + dot_last(part.astype(jnp.bfloat16), base_in[:, columns])
    hidden_grad = low_rank(back, out_left)
    for half, part in enumerate(gathered(slice(width, 2 * width))):
        columns = slice(half * width, (half + 1) * width)
        hidden_grad = hidden_grad + dot_last(part.astype(jnp.bfloat16), base_out[:, columns])
    root = 0.7978845608028654
    bent = jnp.tanh(root * (preact + 0.044715 * (preact * preact * preact)))
    hidden_value = 0.5 * preact * (1.0 + bent)
    slope = 0.5 * (1.0 + bent) + 0.5 * preact * (1.0 - bent * bent) * (
        root * (1.0 + 3.0 * 0.044715 * (preact * preact))
    )
    hidden_low = hidden_value.astype(jnp.bfloat16).astype(jnp.float32)
    preact_grad = (hidden_grad * slope).astype(jnp.bfloat16).astype(jnp.float32)
    pair_out[0] = preact_grad
    pair_out[1] = hidden_low
    ranks_out[0] = up.astype(jnp.float32)
    ranks_out[1] = back.astype(jnp.float32)
    slot_term = dot_plain(preact_grad.astype(jnp.bfloat16), base_in[...]).astype(jnp.bfloat16)
    down = to_rank(preact_grad, in_right)
    value = to_rank(hidden_low, out_left)
    ranks = jnp.concatenate([down, value], axis=1).astype(jnp.bfloat16)
    for half in range(groups):
        columns = slice(half * width, (half + 1) * width)
        for place in range(places):
            taken = slice(place * rows, (place + 1) * rows)
            block = half * places + place
            third[block, :, :width] = slot_term[taken, columns]
            third[block, :, width:] = ranks[taken]


def outer_kernel(owned, left_rows, right_rows, *outs):
    rows = left_rows.shape[1] // (outs[0].shape[0] // owned)
    for number, out in enumerate(outs):
        for place in range(out.shape[0] // owned):
            taken = slice(place * rows, (place + 1) * rows)
            own = own_block(left_rows[number, taken], owned)
            product = dot_first(own, right_rows[number, taken].astype(jnp.bfloat16))
            out[place * owned : (place + 1) * owned] = product.astype(jnp.bfloat16).reshape(
                (owned,) + out.shape[1:]
            )


def halves_kernel(third, own, other):
    places = third.shape[0] // 2
    here = lax.axis_index("half")
    for out, group in ((own, here), (other, 1 - here)):
        taken = third[pl.ds(group * places, places)].astype(jnp.float32)
        out[...] = jnp.sum(taken, axis=0)


def finish_kernel(groups, ring, own, others, in_left, inputs, stats, fourth, ranks_out):
    owned, rank, width = in_left.shape
    summed = own[...] + others[1 - lax.axis_index("half")]
    ranks = summed[:, width:].astype(jnp.bfloat16).astype(jnp.float32)
    ranks_out[0] = ranks[:, :rank]
    ranks_out[1] = ranks[:, rank:]
    down = own_block(ranks[:, :rank], owned)
    grads = summed[:, :width] + dot_plain(down, in_left[...].reshape(owned * rank, width))
    grads = grads.astype(jnp.bfloat16).astype(jnp.float32)
    high, low = halves(jnp.sum(grads * inputs[...], axis=1, keepdims=True))
    lane = lax.broadcasted_iota(jnp.int32, stats.shape, 1)
    tail = jnp.where(lane == 4, high, jnp.where(lane == 5, low, stats[...]))
    block = jnp.concatenate([grads, tail], axis=1).astype(jnp.bfloat16)
    for group in range(groups):
        rows = block[group * owned : (group + 1) * owned]
        for place in range(ring):
            fourth[group * ring + place] = rows


def tokens_kernel(groups, fourth, tokens, router, logits, mixing, out):
    blocks, owned, _ = fourth.shape
    ring = blocks // groups
    width = tokens.shape[1] // groups

    def rows(half, columns):
        taken = [
            fourth[half * ring + place, :, columns].astype(jnp.float32) for place in range(ring)
        ]
        return jnp.concatenate(taken, axis=0)

    grads = jnp.concatenate([rows(half, slice(0, width)) for half in range(groups)], axis=1)
    grads = grads.astype(jnp.bfloat16)
    stats = [rows(half, slice(width, width + STATS)) for half in range(groups)]
    peak = stats[0][:, 0:1] + stats[0][:, 1:2]
    total = stats[0][:, 2:3] + stats[0][:, 3:4]
    shift = functools.reduce(jnp.add, [part[:, 4:5] + part[:, 5:6] for part in stats])
    dispatch = jnp.exp(logits[...] - peak) / total
    weight_grad = dot_last(grads, tokens[...])
    logit_grad = dispatch * (weight_grad - shift) + mixing[...]
    left = jnp.concatenate([dispatch, logit_grad], axis=0).astype(jnp.bfloat16)
    right = jnp.concatenate([grads, router[...]], axis=0)
    out[...] = dot_first(left, right).astype(jnp.bfloat16)


def to_group(block, groups):
    places = lax.axis_size("place")
    blocks = lax.all_gather(block, "half", axis=0)
    (blocks,) = call(
        pack_kernel, [array(block.dtype, groups, places, *block.shape)], [blocks], FLOPS_BESIDE_EXCHANGE
    )
    blocks = blocks.reshape(groups * places, *block.shape)
    return lax.all_to_all(blocks, HALF, 0, 0, tiled=True)


def call(kernel, outs, args, flops):
    size = sum(array.size * array.dtype.itemsize for array in args)
    size += sum(out.size * out.dtype.itemsize for out in outs)
    return pl.pallas_call(
        kernel,
        out_shape=outs,
        in_specs=[pl.BlockSpec(memory_space=pltpu.VMEM) for _ in args],
        out_specs=[pl.BlockSpec(memory_space=pltpu.VMEM) for _ in outs],
        cost_estimate=pl.CostEstimate(flops=flops, bytes_accessed=size, transcendentals=0),
        compiler_params=pltpu.CompilerParams(vmem_limit_bytes=24 * 2**20),
    )(*args)


def array(dtype, *shape):
    return jax.ShapeDtypeStruct(shape, dtype)


def local(
    tokens,
    cotangent,
    router,
    slot_outputs,
    base_in,
    base_out,
    in_left,
    in_right,
    out_left,
    out_right,
):
    groups, ring = lax.axis_size("dp"), lax.axis_size(SEQ)
    devices = groups * ring
    _, count, width = tokens.shape
    slots = router.shape[1]
    owned, slice_width, rank = in_left.shape
    members, _, hidden = in_right.shape
    rows = groups * owned
    if groups != 2 or ring % 2 or slice_width % 128 or rows % 8 or members % owned:
        return local_plain(
            tokens,
            cotangent,
            router,
            slot_outputs,
            base_in,
            base_out,
            in_left,
            in_right,
            out_left,
            out_right,
        )
    low, full = jnp.bfloat16, jnp.float32
    image_rows, cot_rows, saved = tokens[0], cotangent[0], slot_outputs[0]
    router, base_in = router.T, base_in.T
    in_left, out_left = in_left.swapaxes(1, 2), out_left.swapaxes(1, 2)
    (early,) = call(early_kernel, [array(full, 8, 128)], [], FLOPS_BESIDE_EXCHANGE)
    first, logits, combine = call(
        functools.partial(sums_kernel, owned, groups),
        [
            array(low, devices, owned, 2 * slice_width + STATS),
            array(full, slots, count),
            array(full, slots, count),
        ],
        [early, image_rows, cot_rows, router],
        6 * count * slots * width + FLOPS_BESIDE_EXCHANGE,
    )
    first = lax.all_to_all(first, BOTH, 0, 0, tiled=True)
    second, inputs, lows, stats = call(
        functools.partial(owner_kernel, groups),
        [
            array(low, rows, 2 * slice_width + 4 * rank),
            array(full, rows, slice_width),
            array(low, 2, rows, slice_width),
            array(full, rows, STATS),
        ],
        [first, in_left, out_right],
        4 * rows * owned * rank * slice_width,
    )
    second = to_group(second, groups)
    total_rows = groups * members
    third, pair, ranks = call(
        functools.partial(hidden_kernel, groups),
        [
            array(low, ring, rows, slice_width + 2 * rank),
            array(full, 2, total_rows, hidden),
            array(full, 2, total_rows, rank),
        ],
        [second, base_in, base_out, in_right, out_left],
        6 * total_rows * hidden * (width + owned * rank),
    )
    third = lax.all_to_all(third, HALF, 0, 0, tiled=True)
    grad_in_right, grad_out_left = call(
        functools.partial(outer_kernel, owned),
        [array(low, members, rank, hidden)] * 2,
        [ranks, pair],
        4 * members * rank * hidden * rows,
    )
    own, other = call(halves_kernel, [array(full, rows, slice_width + 2 * rank)] * 2, [third], 0)
    others = lax.all_gather(other, "half", axis=0)
    fourth, ranks = call(
        functools.partial(finish_kernel, groups, ring),
        [array(low, devices, owned, slice_width + STATS), array(full, 2, rows, rank)],
        [own, others, in_left, inputs, stats],
        2 * rows * owned * rank * slice_width,
    )
    (mixing,) = call(
        mixing_kernel,
        [array(full, slots, count)],
        [cot_rows, saved, combine],
        2 * count * slots * width,
    )
    fourth = lax.all_to_all(fourth, BOTH, 0, 0, tiled=True)
    grad_in_left, grad_out_right = call(
        functools.partial(outer_kernel, owned),
        [array(low, owned, rank, slice_width)] * 2,
        [ranks, lows],
        4 * owned * rank * slice_width * rows,
    )
    (token_grad,) = call(
        functools.partial(tokens_kernel, groups),
        [array(low, count, width)],
        [fourth, image_rows, router, logits, mixing],
        6 * count * slots * width,
    )
    return (
        token_grad[None],
        grad_in_left.swapaxes(1, 2),
        grad_in_right,
        grad_out_left.swapaxes(1, 2),
        grad_out_right,
    )


def solution(mesh):
    groups, ring = mesh.shape["dp"], mesh.shape["seq"]
    split = mesh.devices.reshape(groups, groups, ring // groups)
    mesh = jax.sharding.Mesh(split, BOTH)
    in_specs = (
        P("dp", SEQ, None),
        P("dp", SEQ, None),
        P(),
        P("dp", None, None),
        P(None, SEQ),
        P(SEQ, None),
        P(SEQ, "dp", None),
        P("dp", None, SEQ),
        P("dp", SEQ, None),
        P(SEQ, None, "dp"),
    )
    out_specs = (
        P("dp", SEQ, None),
        P(SEQ, "dp", None),
        P("dp", None, SEQ),
        P("dp", SEQ, None),
        P(SEQ, None, "dp"),
    )
    return jax.shard_map(local, mesh=mesh, in_specs=in_specs, out_specs=out_specs, check_vma=False)
```

```python
import functools
import math

import jax
import jax.numpy as jnp
from jax import lax
from jax.experimental import pallas as pl
from jax.experimental.pallas import tpu as pltpu
from jax.sharding import PartitionSpec as P

SEQ = ("half", "place")
BOTH = ("dp", *SEQ)
HALF = ("dp", "place")
STATS = 128
FLOPS_BESIDE_EXCHANGE = 10**10


def gelu_backward(preact, upstream):
    return jax.vjp(jax.nn.gelu, preact)[1](upstream)[0]


def dot_first(left, right):
    return lax.dot_general(
        left, right, (((0,), (0,)), ((), ())), preferred_element_type=jnp.float32
    )


def dot_last(left, right):
    return lax.dot_general(
        left, right, (((1,), (1,)), ((), ())), preferred_element_type=jnp.float32
    )


def split(value):
    high = lax.reduce_precision(value, 8, 7)
    low = lax.reduce_precision(value - high, 8, 7)
    return high.astype(jnp.bfloat16), low.astype(jnp.bfloat16)


def joined(high, low):
    return high.astype(jnp.float32) + low.astype(jnp.float32)


def exchange(blocks):
    flat = blocks.reshape((-1,) + blocks.shape[2:])
    return lax.all_to_all(flat, BOTH, 0, 0, tiled=True).reshape(blocks.shape)


def local_plain(
    tokens,
    cotangent,
    router,
    slot_outputs,
    base_in,
    base_out,
    in_left,
    in_right,
    out_left,
    out_right,
):
    groups, ring = lax.axis_size("dp"), lax.axis_size(SEQ)
    image_rows = tokens[0]
    cot_rows = cotangent[0]
    saved_outputs = slot_outputs[0]
    width = image_rows.shape[1]
    slots = router.shape[1]
    owned, slice_width, rank = in_left.shape
    members = in_right.shape[0]
    places = members // owned
    group, place = lax.axis_index("dp"), lax.axis_index(SEQ)

    logits = jnp.dot(image_rows, router, preferred_element_type=jnp.float32)
    peak_high, peak_low = split(jnp.max(logits, axis=0))
    near = jnp.exp(logits - joined(peak_high, peak_low))
    total_high, total_low = split(jnp.sum(near, axis=0))
    combine = jax.nn.softmax(logits, axis=1)
    sums = jnp.stack(
        [
            dot_first(near.astype(jnp.bfloat16), image_rows),
            dot_first(combine.astype(jnp.bfloat16), cot_rows),
        ],
        axis=1,
    ).astype(jnp.bfloat16)
    sums = sums.reshape(ring, owned, 2, groups, slice_width).transpose(3, 0, 1, 2, 4)
    sums = sums.reshape(groups, ring, owned, 2 * slice_width)
    stats = jnp.stack([peak_high, peak_low, total_high, total_low], axis=1)
    stats = jnp.pad(stats, ((0, 0), (0, STATS - 4))).reshape(1, ring, owned, STATS)
    stats = jnp.broadcast_to(stats, (groups, ring, owned, STATS))
    first = exchange(jnp.concatenate([sums, stats], axis=3))

    tail = 2 * slice_width
    peaks = joined(first[..., tail], first[..., tail + 1])
    totals = joined(first[..., tail + 2], first[..., tail + 3])
    peak = jnp.max(peaks, axis=1)
    near_scale = jnp.exp(peaks - peak[:, None])
    total = jnp.sum(near_scale * totals, axis=1)
    near_scale = near_scale / total[:, None]
    parts = first[..., :tail].astype(jnp.float32)
    slot_inputs = jnp.sum(parts[..., :slice_width] * near_scale[..., None], axis=1)
    inputs_own = slot_inputs.astype(jnp.bfloat16)
    grads_own = jnp.sum(parts[..., slice_width:], axis=1).astype(jnp.bfloat16)
    up_part = jnp.einsum("gjd,jdr->gjr", inputs_own, in_left, preferred_element_type=jnp.float32)
    back_part = jnp.einsum("gjd,jrd->gjr", grads_own, out_right, preferred_element_type=jnp.float32)
    second = jnp.concatenate(
        [inputs_own, grads_own, *split(up_part), *split(back_part)], axis=2
    )
    second = exchange(jnp.broadcast_to(second, (groups, ring) + second.shape))
    second = lax.dynamic_slice_in_dim(second, group * places, places, 1)

    def gathered(start):
        piece = second[..., start : start + slice_width]
        return piece.transpose(2, 1, 3, 0, 4).reshape(groups * members, width)

    def ranks(start):
        piece = joined(
            second[..., start : start + rank], second[..., start + rank : start + 2 * rank]
        )
        piece = jnp.sum(piece, axis=0).transpose(1, 0, 2, 3)
        return piece.reshape(groups, members, rank).astype(jnp.bfloat16)

    inputs_low, grads_low = gathered(0), gathered(slice_width)
    up_low, back_low = ranks(tail), ranks(tail + 2 * rank)
    hidden = base_in.shape[1]
    preact = jnp.dot(inputs_low, base_in, preferred_element_type=jnp.float32).reshape(
        groups, members, hidden
    ) + jnp.einsum("gjr,jrf->gjf", up_low, in_right, preferred_element_type=jnp.float32)
    hidden_low = jax.nn.gelu(preact).astype(jnp.bfloat16)
    hidden_grad = dot_last(grads_low, base_out).reshape(groups, members, hidden) + jnp.einsum(
        "gjr,jfr->gjf", back_low, out_left, preferred_element_type=jnp.float32
    )
    preact_grad = gelu_backward(preact, hidden_grad).astype(jnp.bfloat16)
    slot_term = dot_last(preact_grad.reshape(groups * members, hidden), base_in)
    down_term = jnp.einsum(
        "gjf,jrf->gjr", preact_grad, in_right, preferred_element_type=jnp.float32
    )
    value_term = jnp.einsum(
        "gjf,jfr->gjr", hidden_low, out_left, preferred_element_type=jnp.float32
    )
    slot_term = slot_term.astype(jnp.bfloat16).reshape(groups, places, owned, groups, slice_width)
    slot_term = slot_term.transpose(3, 1, 0, 2, 4)
    rank_term = jnp.concatenate([down_term, value_term], axis=2).astype(jnp.bfloat16)
    rank_term = rank_term.reshape(groups, places, owned, 2 * rank).transpose(1, 0, 2, 3)
    rank_term = jnp.broadcast_to(rank_term, (groups,) + rank_term.shape)
    third = jnp.concatenate([slot_term, rank_term], axis=4)
    third = lax.dynamic_update_slice_in_dim(
        jnp.zeros((groups, ring) + third.shape[2:], jnp.bfloat16), third, group * places, 1
    )
    third = exchange(third)
    third = lax.dynamic_index_in_dim(third, place // places, 0, keepdims=False)
    third = jnp.sum(third.astype(jnp.float32), axis=0)
    down_own = third[..., slice_width : slice_width + rank].astype(jnp.bfloat16)
    value_own = third[..., slice_width + rank :].astype(jnp.bfloat16)
    slot_grads_own = (
        third[..., :slice_width]
        + jnp.einsum("gjr,jdr->gjd", down_own, in_left, preferred_element_type=jnp.float32)
    ).astype(jnp.bfloat16)
    shift_part = jnp.sum(slot_grads_own.astype(jnp.float32) * slot_inputs, axis=2)
    stats = jnp.stack([*split(peak), *split(total), *split(shift_part)], axis=2)
    stats = jnp.pad(stats, ((0, 0), (0, 0), (0, STATS - 6)))
    fourth = jnp.concatenate([slot_grads_own, stats], axis=2)[:, None]
    fourth = exchange(jnp.broadcast_to(fourth, (groups, ring) + fourth.shape[2:]))
    slot_grads = fourth[..., :slice_width].transpose(1, 2, 0, 3).reshape(slots, width)
    stats = fourth[..., slice_width:].astype(jnp.float32).reshape(groups, slots, STATS)
    slot_peak = stats[0, :, 0] + stats[0, :, 1]
    slot_total = stats[0, :, 2] + stats[0, :, 3]
    shift_back = jnp.sum(stats[:, :, 4] + stats[:, :, 5], axis=0)

    dispatch = jnp.exp(logits - slot_peak) / slot_total
    dispatch_low = dispatch.astype(jnp.bfloat16)
    weight_grad = dot_last(image_rows, slot_grads)
    dispatch_logit = dispatch * (weight_grad - shift_back)
    mixing_grad = dot_last(cot_rows, saved_outputs)
    combine_logit = combine * (mixing_grad - jnp.sum(combine * mixing_grad, axis=1, keepdims=True))
    logit_grad = (dispatch_logit + combine_logit).astype(jnp.bfloat16)
    token_grad = (
        jnp.dot(dispatch_low, slot_grads, preferred_element_type=jnp.float32)
        + dot_last(logit_grad, router)
    ).astype(jnp.bfloat16)
    grad_in_right = jnp.einsum(
        "gjr,gjf->jrf", up_low, preact_grad, preferred_element_type=jnp.float32
    ).astype(jnp.bfloat16)
    grad_out_left = jnp.einsum(
        "gjf,gjr->jfr", hidden_low, back_low, preferred_element_type=jnp.float32
    ).astype(jnp.bfloat16)
    grad_in_left = jnp.einsum(
        "gjd,gjr->jdr", inputs_own, down_own, preferred_element_type=jnp.float32
    ).astype(jnp.bfloat16)
    grad_out_right = jnp.einsum(
        "gjr,gjd->jrd", value_own, grads_own, preferred_element_type=jnp.float32
    ).astype(jnp.bfloat16)
    return (token_grad[None], grad_in_left, grad_in_right, grad_out_left, grad_out_right)


def dot_plain(left, right):
    return jnp.dot(left, right, preferred_element_type=jnp.float32)


def halves(value):
    high = value.astype(jnp.bfloat16).astype(jnp.float32)
    low = (value - high).astype(jnp.bfloat16).astype(jnp.float32)
    return high, low


def in_lanes(columns, shape):
    lane = lax.broadcasted_iota(jnp.int32, shape, len(shape) - 1)
    out = jnp.zeros(shape, jnp.float32)
    for number, column in enumerate(columns):
        out = jnp.where(lane == number, column, out)
    return out


def own_block(value, owned):
    rows, rank = value.shape
    wide = jnp.concatenate([value] * owned, axis=1)
    shape = (rows, owned * rank)
    block = lax.broadcasted_iota(jnp.int32, shape, 1) // rank
    expert = lax.broadcasted_iota(jnp.int32, shape, 0) % owned
    return jnp.where(block == expert, wide, 0.0).astype(jnp.bfloat16)


def from_own_block(value, owned):
    rows, wide = value.shape
    rank = wide // owned
    block = lax.broadcasted_iota(jnp.int32, value.shape, 1) // rank
    expert = lax.broadcasted_iota(jnp.int32, value.shape, 0) % owned
    kept = jnp.where(block == expert, value, 0.0)
    out = kept[:, :rank]
    for number in range(1, owned):
        out = out + kept[:, number * rank : (number + 1) * rank]
    return out


def early_kernel(out):
    out[...] = jnp.zeros(out.shape, out.dtype)


def sums_kernel(owned, groups, _, tokens, cotangent, router, first, logits_out, combine_out):
    ring = first.shape[0] // groups
    image_rows = tokens[...]
    logits = dot_last(router[...], image_rows)
    high, low = halves(jnp.max(logits, axis=1, keepdims=True))
    near = jnp.exp(logits - (high + low))
    total_high, total_low = halves(jnp.sum(near, axis=1, keepdims=True))
    spread = jnp.exp(logits - jnp.max(logits, axis=0, keepdims=True))
    combine = spread / jnp.sum(spread, axis=0, keepdims=True)
    logits_out[...] = logits
    combine_out[...] = combine
    stats = in_lanes([high, low, total_high, total_low], (logits.shape[0], STATS))
    stats = stats.astype(jnp.bfloat16)
    inputs = dot_plain(near.astype(jnp.bfloat16), image_rows).astype(jnp.bfloat16)
    grads = dot_plain(combine.astype(jnp.bfloat16), cotangent[...]).astype(jnp.bfloat16)
    width = inputs.shape[1] // groups
    for group in range(groups):
        columns = slice(group * width, (group + 1) * width)
        for place in range(ring):
            rows = slice(place * owned, (place + 1) * owned)
            block = group * ring + place
            first[block, :, :width] = inputs[rows, columns]
            first[block, :, width : 2 * width] = grads[rows, columns]
            first[block, :, 2 * width :] = stats[rows, :]


def mixing_kernel(cotangent, saved, combine, out):
    mixing = dot_last(saved[...], cotangent[...])
    weights = combine[...]
    out[...] = weights * (mixing - jnp.sum(weights * mixing, axis=0, keepdims=True))


def owner_kernel(groups, first, in_left, out_right, second, inputs_out, lows_out, stats_out):
    ring = first.shape[0] // groups
    owned, rank, width = in_left.shape
    inputs, grads, stats_rows = [], [], []
    for group in range(groups):
        rows = slice(group * ring, (group + 1) * ring)
        stats = first[rows, :, 2 * width :].astype(jnp.float32)
        peaks = stats[:, :, 0:1] + stats[:, :, 1:2]
        totals = stats[:, :, 2:3] + stats[:, :, 3:4]
        peak = jnp.max(peaks, axis=0)
        scale = jnp.exp(peaks - peak[None])
        total = jnp.sum(scale * totals, axis=0)
        scale = scale / total[None]
        inputs.append(jnp.sum(first[rows, :, :width].astype(jnp.float32) * scale, axis=0))
        grads.append(jnp.sum(first[rows, :, width : 2 * width].astype(jnp.float32), axis=0))
        stats_rows.append(in_lanes([*halves(peak), *halves(total)], (owned, STATS)))
    inputs, grads = jnp.concatenate(inputs, axis=0), jnp.concatenate(grads, axis=0)
    inputs_out[...] = inputs
    stats_out[...] = jnp.concatenate(stats_rows, axis=0)
    inputs_low, grads_low = inputs.astype(jnp.bfloat16), grads.astype(jnp.bfloat16)
    lows_out[0] = inputs_low
    lows_out[1] = grads_low
    up = dot_last(inputs_low, in_left[...].reshape(owned * rank, width))
    back = dot_last(grads_low, out_right[...].reshape(owned * rank, width))
    ranks = [from_own_block(up, owned), from_own_block(back, owned)]
    ranks = jnp.concatenate(ranks, axis=1).astype(jnp.bfloat16)
    block = jnp.concatenate([inputs_low, grads_low, ranks], axis=1)
    second[...] = block


def pack_kernel(blocks, out):
    for group in range(out.shape[0]):
        for place in range(out.shape[1]):
            out[group, place] = blocks[group]


def hidden_kernel(
    groups,
    second,
    base_in,
    base_out,
    in_right,
    out_left,
    third,
    pair_out,
    ranks_out,
):
    members, rank, hidden = in_right.shape
    rows = second.shape[1]
    owned = rows // groups
    places = members // owned
    width = base_in.shape[1] // groups

    def gathered(columns):
        taken = [
            second[half * places : (half + 1) * places, :, columns].astype(jnp.float32)
            for half in range(groups)
        ]
        return [part.reshape(places * rows, part.shape[2]) for part in taken]

    def low_rank(value, table):
        value = value.astype(jnp.float32)
        taken = []
        for place in range(places):
            own = own_block(value[place * rows : (place + 1) * rows], owned)
            part = table[place * owned : (place + 1) * owned].reshape(owned * rank, hidden)
            taken.append(dot_plain(own, part))
        return jnp.concatenate(taken, axis=0)

    def to_rank(value, table):
        taken = []
        for place in range(places):
            part = table[place * owned : (place + 1) * owned].reshape(owned * rank, hidden)
            wide = dot_last(value[place * rows : (place + 1) * rows].astype(jnp.bfloat16), part)
            taken.append(from_own_block(wide, owned))
        return jnp.concatenate(taken, axis=0)

    ranks = functools.reduce(jnp.add, gathered(slice(2 * width, 2 * width + 2 * rank)))
    up, back = ranks[:, :rank].astype(jnp.bfloat16), ranks[:, rank:].astype(jnp.bfloat16)
    preact = low_rank(up, in_right)
    for half, part in enumerate(gathered(slice(0, width))):
        columns = slice(half * width, (half + 1) * width)
        preact = preact + dot_last(part.astype(jnp.bfloat16), base_in[:, columns])
    hidden_grad = low_rank(back, out_left)
    for half, part in enumerate(gathered(slice(width, 2 * width))):
        columns = slice(half * width, (half + 1) * width)
        hidden_grad = hidden_grad + dot_last(part.astype(jnp.bfloat16), base_out[:, columns])
    root = 0.7978845608028654
    bent = jnp.tanh(root * (preact + 0.044715 * (preact * preact * preact)))
    hidden_value = 0.5 * preact * (1.0 + bent)
    slope = 0.5 * (1.0 + bent) + 0.5 * preact * (1.0 - bent * bent) * (
        root * (1.0 + 3.0 * 0.044715 * (preact * preact))
    )
    hidden_low = hidden_value.astype(jnp.bfloat16).astype(jnp.float32)
    preact_grad = (hidden_grad * slope).astype(jnp.bfloat16).astype(jnp.float32)
    pair_out[0] = preact_grad
    pair_out[1] = hidden_low
    ranks_out[0] = up.astype(jnp.float32)
    ranks_out[1] = back.astype(jnp.float32)
    slot_term = dot_plain(preact_grad.astype(jnp.bfloat16), base_in[...]).astype(jnp.bfloat16)
    down = to_rank(preact_grad, in_right)
    value = to_rank(hidden_low, out_left)
    ranks = jnp.concatenate([down, value], axis=1).astype(jnp.bfloat16)
    for half in range(groups):
        columns = slice(half * width, (half + 1) * width)
        for place in range(places):
            taken = slice(place * rows, (place + 1) * rows)
            block = half * places + place
            third[block, :, :width] = slot_term[taken, columns]
            third[block, :, width:] = ranks[taken]


def outer_kernel(owned, left_rows, right_rows, *outs):
    rows = left_rows.shape[1] // (outs[0].shape[0] // owned)
    for number, out in enumerate(outs):
        for place in range(out.shape[0] // owned):
            taken = slice(place * rows, (place + 1) * rows)
            own = own_block(left_rows[number, taken], owned)
            product = dot_first(own, right_rows[number, taken].astype(jnp.bfloat16))
            out[place * owned : (place + 1) * owned] = product.astype(jnp.bfloat16).reshape(
                (owned,) + out.shape[1:]
            )


def halves_kernel(third, own, other):
    places = third.shape[0] // 2
    here = lax.axis_index("half")
    for out, group in ((own, here), (other, 1 - here)):
        taken = third[pl.ds(group * places, places)].astype(jnp.float32)
        out[...] = jnp.sum(taken, axis=0).astype(out.dtype)


def finish_kernel(groups, ring, own, others, in_left, inputs, stats, fourth, ranks_out):
    owned, rank, width = in_left.shape
    summed = own[...] + others[1 - lax.axis_index("half")].astype(jnp.float32)
    ranks = summed[:, width:].astype(jnp.bfloat16).astype(jnp.float32)
    ranks_out[0] = ranks[:, :rank]
    ranks_out[1] = ranks[:, rank:]
    down = own_block(ranks[:, :rank], owned)
    grads = summed[:, :width] + dot_plain(down, in_left[...].reshape(owned * rank, width))
    grads = grads.astype(jnp.bfloat16).astype(jnp.float32)
    high, low = halves(jnp.sum(grads * inputs[...], axis=1, keepdims=True))
    lane = lax.broadcasted_iota(jnp.int32, stats.shape, 1)
    tail = jnp.where(lane == 4, high, jnp.where(lane == 5, low, stats[...]))
    block = jnp.concatenate([grads, tail], axis=1).astype(jnp.bfloat16)
    for group in range(groups):
        rows = block[group * owned : (group + 1) * owned]
        for place in range(ring):
            fourth[group * ring + place] = rows


def tokens_kernel(groups, fourth, tokens, router, logits, mixing, out_far, out, sent):
    blocks, owned, _ = fourth.shape
    ring = blocks // groups
    width = tokens.shape[1] // groups

    def rows(half, columns):
        taken = [
            fourth[half * ring + place, :, columns].astype(jnp.float32) for place in range(ring)
        ]
        return jnp.concatenate(taken, axis=0)

    grads = jnp.concatenate([rows(half, slice(0, width)) for half in range(groups)], axis=1)
    grads = grads.astype(jnp.bfloat16)
    stats = [rows(half, slice(width, width + STATS)) for half in range(groups)]
    peak = stats[0][:, 0:1] + stats[0][:, 1:2]
    total = stats[0][:, 2:3] + stats[0][:, 3:4]
    shift = functools.reduce(jnp.add, [part[:, 4:5] + part[:, 5:6] for part in stats])
    dispatch = jnp.exp(logits[...] - peak) / total
    weight_grad = dot_last(grads, tokens[...])
    logit_grad = dispatch * (weight_grad - shift) + mixing[...]
    left = jnp.concatenate([dispatch, logit_grad], axis=0).astype(jnp.bfloat16)
    right = jnp.concatenate([grads, router[...]], axis=0)
    parts = sent.shape[0]
    size = out.shape[0] // parts
    copies = []
    for part in range(parts):
        rows = slice(part * size, (part + 1) * size)
        out[rows] = dot_first(left[:, rows], right).astype(jnp.bfloat16)
        copy = pltpu.make_async_copy(out.at[rows], out_far.at[rows], sent.at[part])
        copy.start()
        copies.append(copy)
    for copy in copies:
        copy.wait()


def to_group(block, groups):
    places = lax.axis_size("place")
    blocks = lax.all_gather(block, "half", axis=0)
    (blocks,) = call(
        pack_kernel, [array(block.dtype, groups, places, *block.shape)], [blocks], FLOPS_BESIDE_EXCHANGE
    )
    blocks = blocks.reshape(groups * places, *block.shape)
    return lax.all_to_all(blocks, HALF, 0, 0, tiled=True)


def call(kernel, outs, args, flops, space=pltpu.VMEM, scratch=()):
    size = sum(array.size * array.dtype.itemsize for array in args)
    size += sum(out.size * out.dtype.itemsize for out in outs)
    return pl.pallas_call(
        kernel,
        out_shape=outs,
        in_specs=[pl.BlockSpec(memory_space=pltpu.VMEM) for _ in args],
        out_specs=[pl.BlockSpec(memory_space=space) for _ in outs],
        scratch_shapes=scratch,
        cost_estimate=pl.CostEstimate(flops=flops, bytes_accessed=size, transcendentals=0),
        compiler_params=pltpu.CompilerParams(vmem_limit_bytes=24 * 2**20),
    )(*args)


def array(dtype, *shape):
    return jax.ShapeDtypeStruct(shape, dtype)


def local(
    tokens,
    cotangent,
    router,
    slot_outputs,
    base_in,
    base_out,
    in_left,
    in_right,
    out_left,
    out_right,
):
    groups, ring = lax.axis_size("dp"), lax.axis_size(SEQ)
    devices = groups * ring
    _, count, width = tokens.shape
    slots = router.shape[1]
    owned, slice_width, rank = in_left.shape
    members, _, hidden = in_right.shape
    rows = groups * owned
    if groups != 2 or ring % 2 or slice_width % 128 or rows % 8 or members % owned:
        return local_plain(
            tokens,
            cotangent,
            router,
            slot_outputs,
            base_in,
            base_out,
            in_left,
            in_right,
            out_left,
            out_right,
        )
    low, full = jnp.bfloat16, jnp.float32
    image_rows, cot_rows, saved = tokens[0], cotangent[0], slot_outputs[0]
    router, base_in = router.T, base_in.T
    in_left, out_left = in_left.swapaxes(1, 2), out_left.swapaxes(1, 2)
    (early,) = call(early_kernel, [array(full, 8, 128)], [], FLOPS_BESIDE_EXCHANGE)
    first, logits, combine = call(
        functools.partial(sums_kernel, owned, groups),
        [
            array(low, devices, owned, 2 * slice_width + STATS),
            array(full, slots, count),
            array(full, slots, count),
        ],
        [early, image_rows, cot_rows, router],
        6 * count * slots * width + FLOPS_BESIDE_EXCHANGE,
    )
    first = lax.all_to_all(first, BOTH, 0, 0, tiled=True)
    second, inputs, lows, stats = call(
        functools.partial(owner_kernel, groups),
        [
            array(low, rows, 2 * slice_width + 2 * rank),
            array(full, rows, slice_width),
            array(low, 2, rows, slice_width),
            array(full, rows, STATS),
        ],
        [first, in_left, out_right],
        4 * rows * owned * rank * slice_width,
    )
    second = to_group(second, groups)
    total_rows = groups * members
    third, pair, ranks = call(
        functools.partial(hidden_kernel, groups),
        [
            array(low, ring, rows, slice_width + 2 * rank),
            array(full, 2, total_rows, hidden),
            array(full, 2, total_rows, rank),
        ],
        [second, base_in, base_out, in_right, out_left],
        6 * total_rows * hidden * (width + owned * rank),
    )
    third = lax.all_to_all(third, HALF, 0, 0, tiled=True)
    grad_in_right, grad_out_left = call(
        functools.partial(outer_kernel, owned),
        [array(low, members, rank, hidden)] * 2,
        [ranks, pair],
        4 * members * rank * hidden * rows,
    )
    own, other = call(
        halves_kernel,
        [array(kind, rows, slice_width + 2 * rank) for kind in (full, low)],
        [third],
        0,
    )
    others = lax.all_gather(other, "half", axis=0)
    fourth, ranks = call(
        functools.partial(finish_kernel, groups, ring),
        [array(low, devices, owned, slice_width + STATS), array(full, 2, rows, rank)],
        [own, others, in_left, inputs, stats],
        2 * rows * owned * rank * slice_width,
    )
    (mixing,) = call(
        mixing_kernel,
        [array(full, slots, count)],
        [cot_rows, saved, combine],
        2 * count * slots * width,
    )
    fourth = lax.all_to_all(fourth, BOTH, 0, 0, tiled=True)
    grad_in_left, grad_out_right = call(
        functools.partial(outer_kernel, owned),
        [array(low, owned, rank, slice_width)] * 2,
        [ranks, lows],
        4 * owned * rank * slice_width * rows,
    )
    parts = math.gcd(4, count // 16)
    (token_grad,) = call(
        functools.partial(tokens_kernel, groups),
        [array(low, count, width)],
        [fourth, image_rows, router, logits, mixing],
        6 * count * slots * width,
        pltpu.HBM,
        [pltpu.VMEM((count, width), low), pltpu.SemaphoreType.DMA((parts,))],
    )
    return (
        token_grad[None],
        grad_in_left.swapaxes(1, 2),
        grad_in_right,
        grad_out_left.swapaxes(1, 2),
        grad_out_right,
    )


def solution(mesh):
    groups, ring = mesh.shape["dp"], mesh.shape["seq"]
    split = mesh.devices.reshape(groups, groups, ring // groups)
    mesh = jax.sharding.Mesh(split, BOTH)
    in_specs = (
        P("dp", SEQ, None),
        P("dp", SEQ, None),
        P(),
        P("dp", None, None),
        P(None, SEQ),
        P(SEQ, None),
        P(SEQ, "dp", None),
        P("dp", None, SEQ),
        P("dp", SEQ, None),
        P(SEQ, None, "dp"),
    )
    out_specs = (
        P("dp", SEQ, None),
        P(SEQ, "dp", None),
        P("dp", None, SEQ),
        P("dp", SEQ, None),
        P(SEQ, None, "dp"),
    )
    return jax.shard_map(local, mesh=mesh, in_specs=in_specs, out_specs=out_specs, check_vma=False)
```

```python
import functools
import math

import jax
import jax.numpy as jnp
from jax import lax
from jax.experimental import pallas as pl
from jax.experimental.pallas import tpu as pltpu
from jax.sharding import PartitionSpec as P

PLACE = ("chip", "core")
SEQ = ("half", *PLACE)
BOTH = ("dp", *SEQ)
HALF = ("dp", *PLACE)
SAME_CORE = ("dp", "half", "chip")
STATS = 128
FLOPS_BESIDE_EXCHANGE = 10**10


def gelu_backward(preact, upstream):
    return jax.vjp(jax.nn.gelu, preact)[1](upstream)[0]


def dot_first(left, right):
    return lax.dot_general(
        left, right, (((0,), (0,)), ((), ())), preferred_element_type=jnp.float32
    )


def dot_last(left, right):
    return lax.dot_general(
        left, right, (((1,), (1,)), ((), ())), preferred_element_type=jnp.float32
    )


def split(value):
    high = lax.reduce_precision(value, 8, 7)
    low = lax.reduce_precision(value - high, 8, 7)
    return high.astype(jnp.bfloat16), low.astype(jnp.bfloat16)


def joined(high, low):
    return high.astype(jnp.float32) + low.astype(jnp.float32)


def exchange(blocks):
    flat = blocks.reshape((-1,) + blocks.shape[2:])
    return lax.all_to_all(flat, BOTH, 0, 0, tiled=True).reshape(blocks.shape)


def local_plain(
    tokens,
    cotangent,
    router,
    slot_outputs,
    base_in,
    base_out,
    in_left,
    in_right,
    out_left,
    out_right,
):
    groups, ring = lax.axis_size("dp"), lax.axis_size(SEQ)
    image_rows = tokens[0]
    cot_rows = cotangent[0]
    saved_outputs = slot_outputs[0]
    width = image_rows.shape[1]
    slots = router.shape[1]
    owned, slice_width, rank = in_left.shape
    members = in_right.shape[0]
    places = members // owned
    group, place = lax.axis_index("dp"), lax.axis_index(SEQ)

    logits = jnp.dot(image_rows, router, preferred_element_type=jnp.float32)
    peak_high, peak_low = split(jnp.max(logits, axis=0))
    near = jnp.exp(logits - joined(peak_high, peak_low))
    total_high, total_low = split(jnp.sum(near, axis=0))
    combine = jax.nn.softmax(logits, axis=1)
    sums = jnp.stack(
        [
            dot_first(near.astype(jnp.bfloat16), image_rows),
            dot_first(combine.astype(jnp.bfloat16), cot_rows),
        ],
        axis=1,
    ).astype(jnp.bfloat16)
    sums = sums.reshape(ring, owned, 2, groups, slice_width).transpose(3, 0, 1, 2, 4)
    sums = sums.reshape(groups, ring, owned, 2 * slice_width)
    stats = jnp.stack([peak_high, peak_low, total_high, total_low], axis=1)
    stats = jnp.pad(stats, ((0, 0), (0, STATS - 4))).reshape(1, ring, owned, STATS)
    stats = jnp.broadcast_to(stats, (groups, ring, owned, STATS))
    first = exchange(jnp.concatenate([sums, stats], axis=3))

    tail = 2 * slice_width
    peaks = joined(first[..., tail], first[..., tail + 1])
    totals = joined(first[..., tail + 2], first[..., tail + 3])
    peak = jnp.max(peaks, axis=1)
    near_scale = jnp.exp(peaks - peak[:, None])
    total = jnp.sum(near_scale * totals, axis=1)
    near_scale = near_scale / total[:, None]
    parts = first[..., :tail].astype(jnp.float32)
    slot_inputs = jnp.sum(parts[..., :slice_width] * near_scale[..., None], axis=1)
    inputs_own = slot_inputs.astype(jnp.bfloat16)
    grads_own = jnp.sum(parts[..., slice_width:], axis=1).astype(jnp.bfloat16)
    up_part = jnp.einsum("gjd,jdr->gjr", inputs_own, in_left, preferred_element_type=jnp.float32)
    back_part = jnp.einsum("gjd,jrd->gjr", grads_own, out_right, preferred_element_type=jnp.float32)
    second = jnp.concatenate(
        [inputs_own, grads_own, *split(up_part), *split(back_part)], axis=2
    )
    second = exchange(jnp.broadcast_to(second, (groups, ring) + second.shape))
    second = lax.dynamic_slice_in_dim(second, group * places, places, 1)

    def gathered(start):
        piece = second[..., start : start + slice_width]
        return piece.transpose(2, 1, 3, 0, 4).reshape(groups * members, width)

    def ranks(start):
        piece = joined(
            second[..., start : start + rank], second[..., start + rank : start + 2 * rank]
        )
        piece = jnp.sum(piece, axis=0).transpose(1, 0, 2, 3)
        return piece.reshape(groups, members, rank).astype(jnp.bfloat16)

    inputs_low, grads_low = gathered(0), gathered(slice_width)
    up_low, back_low = ranks(tail), ranks(tail + 2 * rank)
    hidden = base_in.shape[1]
    preact = jnp.dot(inputs_low, base_in, preferred_element_type=jnp.float32).reshape(
        groups, members, hidden
    ) + jnp.einsum("gjr,jrf->gjf", up_low, in_right, preferred_element_type=jnp.float32)
    hidden_low = jax.nn.gelu(preact).astype(jnp.bfloat16)
    hidden_grad = dot_last(grads_low, base_out).reshape(groups, members, hidden) + jnp.einsum(
        "gjr,jfr->gjf", back_low, out_left, preferred_element_type=jnp.float32
    )
    preact_grad = gelu_backward(preact, hidden_grad).astype(jnp.bfloat16)
    slot_term = dot_last(preact_grad.reshape(groups * members, hidden), base_in)
    down_term = jnp.einsum(
        "gjf,jrf->gjr", preact_grad, in_right, preferred_element_type=jnp.float32
    )
    value_term = jnp.einsum(
        "gjf,jfr->gjr", hidden_low, out_left, preferred_element_type=jnp.float32
    )
    slot_term = slot_term.astype(jnp.bfloat16).reshape(groups, places, owned, groups, slice_width)
    slot_term = slot_term.transpose(3, 1, 0, 2, 4)
    rank_term = jnp.concatenate([down_term, value_term], axis=2).astype(jnp.bfloat16)
    rank_term = rank_term.reshape(groups, places, owned, 2 * rank).transpose(1, 0, 2, 3)
    rank_term = jnp.broadcast_to(rank_term, (groups,) + rank_term.shape)
    third = jnp.concatenate([slot_term, rank_term], axis=4)
    third = lax.dynamic_update_slice_in_dim(
        jnp.zeros((groups, ring) + third.shape[2:], jnp.bfloat16), third, group * places, 1
    )
    third = exchange(third)
    third = lax.dynamic_index_in_dim(third, place // places, 0, keepdims=False)
    third = jnp.sum(third.astype(jnp.float32), axis=0)
    down_own = third[..., slice_width : slice_width + rank].astype(jnp.bfloat16)
    value_own = third[..., slice_width + rank :].astype(jnp.bfloat16)
    slot_grads_own = (
        third[..., :slice_width]
        + jnp.einsum("gjr,jdr->gjd", down_own, in_left, preferred_element_type=jnp.float32)
    ).astype(jnp.bfloat16)
    shift_part = jnp.sum(slot_grads_own.astype(jnp.float32) * slot_inputs, axis=2)
    stats = jnp.stack([*split(peak), *split(total), *split(shift_part)], axis=2)
    stats = jnp.pad(stats, ((0, 0), (0, 0), (0, STATS - 6)))
    fourth = jnp.concatenate([slot_grads_own, stats], axis=2)[:, None]
    fourth = exchange(jnp.broadcast_to(fourth, (groups, ring) + fourth.shape[2:]))
    slot_grads = fourth[..., :slice_width].transpose(1, 2, 0, 3).reshape(slots, width)
    stats = fourth[..., slice_width:].astype(jnp.float32).reshape(groups, slots, STATS)
    slot_peak = stats[0, :, 0] + stats[0, :, 1]
    slot_total = stats[0, :, 2] + stats[0, :, 3]
    shift_back = jnp.sum(stats[:, :, 4] + stats[:, :, 5], axis=0)

    dispatch = jnp.exp(logits - slot_peak) / slot_total
    dispatch_low = dispatch.astype(jnp.bfloat16)
    weight_grad = dot_last(image_rows, slot_grads)
    dispatch_logit = dispatch * (weight_grad - shift_back)
    mixing_grad = dot_last(cot_rows, saved_outputs)
    combine_logit = combine * (mixing_grad - jnp.sum(combine * mixing_grad, axis=1, keepdims=True))
    logit_grad = (dispatch_logit + combine_logit).astype(jnp.bfloat16)
    token_grad = (
        jnp.dot(dispatch_low, slot_grads, preferred_element_type=jnp.float32)
        + dot_last(logit_grad, router)
    ).astype(jnp.bfloat16)
    grad_in_right = jnp.einsum(
        "gjr,gjf->jrf", up_low, preact_grad, preferred_element_type=jnp.float32
    ).astype(jnp.bfloat16)
    grad_out_left = jnp.einsum(
        "gjf,gjr->jfr", hidden_low, back_low, preferred_element_type=jnp.float32
    ).astype(jnp.bfloat16)
    grad_in_left = jnp.einsum(
        "gjd,gjr->jdr", inputs_own, down_own, preferred_element_type=jnp.float32
    ).astype(jnp.bfloat16)
    grad_out_right = jnp.einsum(
        "gjr,gjd->jrd", value_own, grads_own, preferred_element_type=jnp.float32
    ).astype(jnp.bfloat16)
    return (token_grad[None], grad_in_left, grad_in_right, grad_out_left, grad_out_right)


def dot_plain(left, right):
    return jnp.dot(left, right, preferred_element_type=jnp.float32)


def halves(value):
    high = value.astype(jnp.bfloat16).astype(jnp.float32)
    low = (value - high).astype(jnp.bfloat16).astype(jnp.float32)
    return high, low


def in_lanes(columns, shape):
    lane = lax.broadcasted_iota(jnp.int32, shape, len(shape) - 1)
    out = jnp.zeros(shape, jnp.float32)
    for number, column in enumerate(columns):
        out = jnp.where(lane == number, column, out)
    return out


def own_block(value, owned):
    rows, rank = value.shape
    wide = jnp.concatenate([value] * owned, axis=1)
    shape = (rows, owned * rank)
    block = lax.broadcasted_iota(jnp.int32, shape, 1) // rank
    expert = lax.broadcasted_iota(jnp.int32, shape, 0) % owned
    return jnp.where(block == expert, wide, 0.0).astype(jnp.bfloat16)


def from_own_block(value, owned):
    rows, wide = value.shape
    rank = wide // owned
    block = lax.broadcasted_iota(jnp.int32, value.shape, 1) // rank
    expert = lax.broadcasted_iota(jnp.int32, value.shape, 0) % owned
    kept = jnp.where(block == expert, value, 0.0)
    out = kept[:, :rank]
    for number in range(1, owned):
        out = out + kept[:, number * rank : (number + 1) * rank]
    return out


def early_kernel(out):
    out[...] = jnp.zeros(out.shape, out.dtype)


def sums_kernel(
    owned, groups, _, tokens, cotangent, router, own, other, logits_out, combine_out
):
    chips = own.shape[0] // groups
    core = lax.axis_index("core")
    image_rows = tokens[...]
    logits = dot_last(router[...], image_rows)
    high, low = halves(jnp.max(logits, axis=1, keepdims=True))
    near = jnp.exp(logits - (high + low))
    total_high, total_low = halves(jnp.sum(near, axis=1, keepdims=True))
    spread = jnp.exp(logits - jnp.max(logits, axis=0, keepdims=True))
    combine = spread / jnp.sum(spread, axis=0, keepdims=True)
    logits_out[...] = logits
    combine_out[...] = combine
    stats = in_lanes([high, low, total_high, total_low], (logits.shape[0], STATS))
    stats = stats.astype(jnp.bfloat16)
    inputs = dot_plain(near.astype(jnp.bfloat16), image_rows).astype(jnp.bfloat16)
    grads = dot_plain(combine.astype(jnp.bfloat16), cotangent[...]).astype(jnp.bfloat16)
    width = inputs.shape[1] // groups

    def block(rows, columns):
        return jnp.concatenate([inputs[rows, columns], grads[rows, columns], stats[rows]], axis=1)

    for group in range(groups):
        columns = slice(group * width, (group + 1) * width)
        for chip in range(chips):
            start = 2 * chip * owned
            even = block(slice(start, start + owned), columns)
            odd = block(slice(start + owned, start + 2 * owned), columns)
            own[group * chips + chip] = jnp.where(core == 0, even, odd)
            other[group * chips + chip] = jnp.where(core == 0, odd, even)


def merge_kernel(width, own, other, out):
    parts = []
    for part in (own, other):
        stats = part[:, :, 2 * width :].astype(jnp.float32)
        parts.append((stats[:, :, 0:1] + stats[:, :, 1:2], stats[:, :, 2:3] + stats[:, :, 3:4]))
    peak = jnp.maximum(parts[0][0], parts[1][0])
    scales = [jnp.exp(part[0] - peak) for part in parts]
    total = scales[0] * parts[0][1] + scales[1] * parts[1][1]
    stats = in_lanes([*halves(peak), *halves(total)], own.shape[:2] + (STATS,))
    inputs = [
        part[:, :, :width].astype(jnp.float32) * scale
        for part, scale in zip((own, other), scales, strict=True)
    ]
    grads = [part[:, :, width : 2 * width].astype(jnp.float32) for part in (own, other)]
    out[:, :, :width] = (inputs[0] + inputs[1]).astype(jnp.bfloat16)
    out[:, :, width : 2 * width] = (grads[0] + grads[1]).astype(jnp.bfloat16)
    out[:, :, 2 * width :] = stats.astype(jnp.bfloat16)


def mixing_kernel(cotangent, saved, combine, out):
    mixing = dot_last(saved[...], cotangent[...])
    weights = combine[...]
    out[...] = weights * (mixing - jnp.sum(weights * mixing, axis=0, keepdims=True))


def owner_kernel(groups, first, in_left, out_right, second, inputs_out, lows_out, stats_out):
    ring = first.shape[0] // groups
    owned, rank, width = in_left.shape
    inputs, grads, stats_rows = [], [], []
    for group in range(groups):
        rows = slice(group * ring, (group + 1) * ring)
        stats = first[rows, :, 2 * width :].astype(jnp.float32)
        peaks = stats[:, :, 0:1] + stats[:, :, 1:2]
        totals = stats[:, :, 2:3] + stats[:, :, 3:4]
        peak = jnp.max(peaks, axis=0)
        scale = jnp.exp(peaks - peak[None])
        total = jnp.sum(scale * totals, axis=0)
        scale = scale / total[None]
        inputs.append(jnp.sum(first[rows, :, :width].astype(jnp.float32) * scale, axis=0))
        grads.append(jnp.sum(first[rows, :, width : 2 * width].astype(jnp.float32), axis=0))
        stats_rows.append(in_lanes([*halves(peak), *halves(total)], (owned, STATS)))
    inputs, grads = jnp.concatenate(inputs, axis=0), jnp.concatenate(grads, axis=0)
    inputs_out[...] = inputs
    stats_out[...] = jnp.concatenate(stats_rows, axis=0)
    inputs_low, grads_low = inputs.astype(jnp.bfloat16), grads.astype(jnp.bfloat16)
    lows_out[0] = inputs_low
    lows_out[1] = grads_low
    up = dot_last(inputs_low, in_left[...].reshape(owned * rank, width))
    back = dot_last(grads_low, out_right[...].reshape(owned * rank, width))
    ranks = [from_own_block(up, owned), from_own_block(back, owned)]
    ranks = jnp.concatenate(ranks, axis=1).astype(jnp.bfloat16)
    block = jnp.concatenate([inputs_low, grads_low, ranks], axis=1)
    second[...] = block


def pack_kernel(blocks, out):
    for group in range(out.shape[0]):
        for place in range(out.shape[1]):
            out[group, place] = blocks[group]


def hidden_kernel(
    groups,
    second,
    base_in,
    base_out,
    in_right,
    out_left,
    third,
    pair_out,
    ranks_out,
):
    members, rank, hidden = in_right.shape
    rows = second.shape[1]
    owned = rows // groups
    places = members // owned
    width = base_in.shape[1] // groups

    def gathered(columns):
        taken = [
            second[half * places : (half + 1) * places, :, columns].astype(jnp.float32)
            for half in range(groups)
        ]
        return [part.reshape(places * rows, part.shape[2]) for part in taken]

    def low_rank(value, table):
        value = value.astype(jnp.float32)
        taken = []
        for place in range(places):
            own = own_block(value[place * rows : (place + 1) * rows], owned)
            part = table[place * owned : (place + 1) * owned].reshape(owned * rank, hidden)
            taken.append(dot_plain(own, part))
        return jnp.concatenate(taken, axis=0)

    def to_rank(value, table):
        taken = []
        for place in range(places):
            part = table[place * owned : (place + 1) * owned].reshape(owned * rank, hidden)
            wide = dot_last(value[place * rows : (place + 1) * rows].astype(jnp.bfloat16), part)
            taken.append(from_own_block(wide, owned))
        return jnp.concatenate(taken, axis=0)

    ranks = functools.reduce(jnp.add, gathered(slice(2 * width, 2 * width + 2 * rank)))
    up, back = ranks[:, :rank].astype(jnp.bfloat16), ranks[:, rank:].astype(jnp.bfloat16)
    preact = low_rank(up, in_right)
    for half, part in enumerate(gathered(slice(0, width))):
        columns = slice(half * width, (half + 1) * width)
        preact = preact + dot_last(part.astype(jnp.bfloat16), base_in[:, columns])
    hidden_grad = low_rank(back, out_left)
    for half, part in enumerate(gathered(slice(width, 2 * width))):
        columns = slice(half * width, (half + 1) * width)
        hidden_grad = hidden_grad + dot_last(part.astype(jnp.bfloat16), base_out[:, columns])
    root = 0.7978845608028654
    bent = jnp.tanh(root * (preact + 0.044715 * (preact * preact * preact)))
    hidden_value = 0.5 * preact * (1.0 + bent)
    slope = 0.5 * (1.0 + bent) + 0.5 * preact * (1.0 - bent * bent) * (
        root * (1.0 + 3.0 * 0.044715 * (preact * preact))
    )
    hidden_low = hidden_value.astype(jnp.bfloat16).astype(jnp.float32)
    preact_grad = (hidden_grad * slope).astype(jnp.bfloat16).astype(jnp.float32)
    pair_out[0] = preact_grad
    pair_out[1] = hidden_low
    ranks_out[0] = up.astype(jnp.float32)
    ranks_out[1] = back.astype(jnp.float32)
    slot_term = dot_plain(preact_grad.astype(jnp.bfloat16), base_in[...]).astype(jnp.bfloat16)
    down = to_rank(preact_grad, in_right)
    value = to_rank(hidden_low, out_left)
    ranks = jnp.concatenate([down, value], axis=1).astype(jnp.bfloat16)
    for half in range(groups):
        columns = slice(half * width, (half + 1) * width)
        for place in range(places):
            taken = slice(place * rows, (place + 1) * rows)
            block = half * places + place
            third[block, :, :width] = slot_term[taken, columns]
            third[block, :, width:] = ranks[taken]


def outer_kernel(owned, left_rows, right_rows, *outs):
    rows = left_rows.shape[1] // (outs[0].shape[0] // owned)
    for number, out in enumerate(outs):
        for place in range(out.shape[0] // owned):
            taken = slice(place * rows, (place + 1) * rows)
            own = own_block(left_rows[number, taken], owned)
            product = dot_first(own, right_rows[number, taken].astype(jnp.bfloat16))
            out[place * owned : (place + 1) * owned] = product.astype(jnp.bfloat16).reshape(
                (owned,) + out.shape[1:]
            )


def halves_kernel(third, own, other):
    places = third.shape[0] // 2
    here = lax.axis_index("half")
    for out, group in ((own, here), (other, 1 - here)):
        taken = third[pl.ds(group * places, places)].astype(jnp.float32)
        out[...] = jnp.sum(taken, axis=0).astype(out.dtype)


def finish_kernel(groups, ring, own, others, in_left, inputs, stats, fourth, ranks_out):
    owned, rank, width = in_left.shape
    summed = own[...] + others[1 - lax.axis_index("half")].astype(jnp.float32)
    ranks = summed[:, width:].astype(jnp.bfloat16).astype(jnp.float32)
    ranks_out[0] = ranks[:, :rank]
    ranks_out[1] = ranks[:, rank:]
    down = own_block(ranks[:, :rank], owned)
    grads = summed[:, :width] + dot_plain(down, in_left[...].reshape(owned * rank, width))
    grads = grads.astype(jnp.bfloat16).astype(jnp.float32)
    high, low = halves(jnp.sum(grads * inputs[...], axis=1, keepdims=True))
    lane = lax.broadcasted_iota(jnp.int32, stats.shape, 1)
    tail = jnp.where(lane == 4, high, jnp.where(lane == 5, low, stats[...]))
    block = jnp.concatenate([grads, tail], axis=1).astype(jnp.bfloat16)
    for group in range(groups):
        rows = block[group * owned : (group + 1) * owned]
        for place in range(ring):
            fourth[group * ring + place] = rows


def tokens_kernel(groups, fourth, tokens, router, logits, mixing, out_far, out, sent):
    blocks, owned, _ = fourth.shape
    ring = blocks // groups
    width = tokens.shape[1] // groups

    def rows(half, columns):
        taken = [
            fourth[half * ring + place, :, columns].astype(jnp.float32) for place in range(ring)
        ]
        return jnp.concatenate(taken, axis=0)

    grads = jnp.concatenate([rows(half, slice(0, width)) for half in range(groups)], axis=1)
    grads = grads.astype(jnp.bfloat16)
    stats = [rows(half, slice(width, width + STATS)) for half in range(groups)]
    peak = stats[0][:, 0:1] + stats[0][:, 1:2]
    total = stats[0][:, 2:3] + stats[0][:, 3:4]
    shift = functools.reduce(jnp.add, [part[:, 4:5] + part[:, 5:6] for part in stats])
    dispatch = jnp.exp(logits[...] - peak) / total
    weight_grad = dot_last(grads, tokens[...])
    logit_grad = dispatch * (weight_grad - shift) + mixing[...]
    left = jnp.concatenate([dispatch, logit_grad], axis=0).astype(jnp.bfloat16)
    right = jnp.concatenate([grads, router[...]], axis=0)
    parts = sent.shape[0]
    size = out.shape[0] // parts
    copies = []
    for part in range(parts):
        rows = slice(part * size, (part + 1) * size)
        out[rows] = dot_first(left[:, rows], right).astype(jnp.bfloat16)
        copy = pltpu.make_async_copy(out.at[rows], out_far.at[rows], sent.at[part])
        copy.start()
        copies.append(copy)
    for copy in copies:
        copy.wait()


def to_group(block, groups):
    places = lax.axis_size(PLACE)
    blocks = lax.all_gather(block, "half", axis=0)
    (blocks,) = call(
        pack_kernel, [array(block.dtype, groups, places, *block.shape)], [blocks], FLOPS_BESIDE_EXCHANGE
    )
    blocks = blocks.reshape(groups * places, *block.shape)
    return lax.all_to_all(blocks, HALF, 0, 0, tiled=True)


def call(kernel, outs, args, flops, space=pltpu.VMEM, scratch=()):
    size = sum(array.size * array.dtype.itemsize for array in args)
    size += sum(out.size * out.dtype.itemsize for out in outs)
    return pl.pallas_call(
        kernel,
        out_shape=outs,
        in_specs=[pl.BlockSpec(memory_space=pltpu.VMEM) for _ in args],
        out_specs=[pl.BlockSpec(memory_space=space) for _ in outs],
        scratch_shapes=scratch,
        cost_estimate=pl.CostEstimate(flops=flops, bytes_accessed=size, transcendentals=0),
        compiler_params=pltpu.CompilerParams(vmem_limit_bytes=24 * 2**20),
    )(*args)


def array(dtype, *shape):
    return jax.ShapeDtypeStruct(shape, dtype)


def local(
    tokens,
    cotangent,
    router,
    slot_outputs,
    base_in,
    base_out,
    in_left,
    in_right,
    out_left,
    out_right,
):
    groups, ring = lax.axis_size("dp"), lax.axis_size(SEQ)
    devices = groups * ring
    _, count, width = tokens.shape
    slots = router.shape[1]
    owned, slice_width, rank = in_left.shape
    members, _, hidden = in_right.shape
    rows = groups * owned
    if groups != 2 or ring % 4 or slice_width % 128 or rows % 8 or members % owned:
        return local_plain(
            tokens,
            cotangent,
            router,
            slot_outputs,
            base_in,
            base_out,
            in_left,
            in_right,
            out_left,
            out_right,
        )
    low, full = jnp.bfloat16, jnp.float32
    image_rows, cot_rows, saved = tokens[0], cotangent[0], slot_outputs[0]
    router, base_in = router.T, base_in.T
    in_left, out_left = in_left.swapaxes(1, 2), out_left.swapaxes(1, 2)
    (early,) = call(early_kernel, [array(full, 8, 128)], [], FLOPS_BESIDE_EXCHANGE)
    first = array(low, devices // 2, owned, 2 * slice_width + STATS)
    own, other, logits, combine = call(
        functools.partial(sums_kernel, owned, groups),
        [first, first, array(full, slots, count), array(full, slots, count)],
        [early, image_rows, cot_rows, router],
        6 * count * slots * width + FLOPS_BESIDE_EXCHANGE,
    )
    other = lax.ppermute(other, "core", [(0, 1), (1, 0)])
    (first,) = call(
        functools.partial(merge_kernel, slice_width), [first], [own, other], FLOPS_BESIDE_EXCHANGE
    )
    first = lax.all_to_all(first, SAME_CORE, 0, 0, tiled=True)
    second, inputs, lows, stats = call(
        functools.partial(owner_kernel, groups),
        [
            array(low, rows, 2 * slice_width + 2 * rank),
            array(full, rows, slice_width),
            array(low, 2, rows, slice_width),
            array(full, rows, STATS),
        ],
        [first, in_left, out_right],
        4 * rows * owned * rank * slice_width,
    )
    second = to_group(second, groups)
    total_rows = groups * members
    third, pair, ranks = call(
        functools.partial(hidden_kernel, groups),
        [
            array(low, ring, rows, slice_width + 2 * rank),
            array(full, 2, total_rows, hidden),
            array(full, 2, total_rows, rank),
        ],
        [second, base_in, base_out, in_right, out_left],
        6 * total_rows * hidden * (width + owned * rank),
    )
    third = lax.all_to_all(third, HALF, 0, 0, tiled=True)
    grad_in_right, grad_out_left = call(
        functools.partial(outer_kernel, owned),
        [array(low, members, rank, hidden)] * 2,
        [ranks, pair],
        4 * members * rank * hidden * rows,
    )
    own, other = call(
        halves_kernel,
        [array(kind, rows, slice_width + 2 * rank) for kind in (full, low)],
        [third],
        0,
    )
    others = lax.all_gather(other, "half", axis=0)
    fourth, ranks = call(
        functools.partial(finish_kernel, groups, ring),
        [array(low, devices, owned, slice_width + STATS), array(full, 2, rows, rank)],
        [own, others, in_left, inputs, stats],
        2 * rows * owned * rank * slice_width,
    )
    (mixing,) = call(
        mixing_kernel,
        [array(full, slots, count)],
        [cot_rows, saved, combine],
        2 * count * slots * width,
    )
    fourth = lax.all_to_all(fourth, BOTH, 0, 0, tiled=True)
    grad_in_left, grad_out_right = call(
        functools.partial(outer_kernel, owned),
        [array(low, owned, rank, slice_width)] * 2,
        [ranks, lows],
        4 * owned * rank * slice_width * rows,
    )
    parts = math.gcd(4, count // 16)
    (token_grad,) = call(
        functools.partial(tokens_kernel, groups),
        [array(low, count, width)],
        [fourth, image_rows, router, logits, mixing],
        6 * count * slots * width,
        pltpu.HBM,
        [pltpu.VMEM((count, width), low), pltpu.SemaphoreType.DMA((parts,))],
    )
    return (
        token_grad[None],
        grad_in_left.swapaxes(1, 2),
        grad_in_right,
        grad_out_left.swapaxes(1, 2),
        grad_out_right,
    )


def solution(mesh):
    groups, ring = mesh.shape["dp"], mesh.shape["seq"]
    cores = math.gcd(2, ring // groups)
    split = mesh.devices.reshape(groups, groups, ring // groups // cores, cores)
    mesh = jax.sharding.Mesh(split, BOTH)
    in_specs = (
        P("dp", SEQ, None),
        P("dp", SEQ, None),
        P(),
        P("dp", None, None),
        P(None, SEQ),
        P(SEQ, None),
        P(SEQ, "dp", None),
        P("dp", None, SEQ),
        P("dp", SEQ, None),
        P(SEQ, None, "dp"),
    )
    out_specs = (
        P("dp", SEQ, None),
        P(SEQ, "dp", None),
        P("dp", None, SEQ),
        P("dp", SEQ, None),
        P(SEQ, None, "dp"),
    )
    return jax.shard_map(local, mesh=mesh, in_specs=in_specs, out_specs=out_specs, check_vma=False)
```

```python
import functools
import math

import jax
import jax.numpy as jnp
from jax import lax
from jax.experimental import pallas as pl
from jax.experimental.pallas import tpu as pltpu
from jax.sharding import PartitionSpec as P

PLACE = ("chip", "core")
SEQ = ("half", *PLACE)
BOTH = ("dp", *SEQ)
HALF_CORE = ("dp", "chip")
SAME_CORE = ("dp", "half", "chip")
STATS = 128
FLOPS_BESIDE_EXCHANGE = 10**10


def gelu_backward(preact, upstream):
    return jax.vjp(jax.nn.gelu, preact)[1](upstream)[0]


def dot_first(left, right):
    return lax.dot_general(
        left, right, (((0,), (0,)), ((), ())), preferred_element_type=jnp.float32
    )


def dot_last(left, right):
    return lax.dot_general(
        left, right, (((1,), (1,)), ((), ())), preferred_element_type=jnp.float32
    )


def split(value):
    high = lax.reduce_precision(value, 8, 7)
    low = lax.reduce_precision(value - high, 8, 7)
    return high.astype(jnp.bfloat16), low.astype(jnp.bfloat16)


def joined(high, low):
    return high.astype(jnp.float32) + low.astype(jnp.float32)


def exchange(blocks):
    flat = blocks.reshape((-1,) + blocks.shape[2:])
    return lax.all_to_all(flat, BOTH, 0, 0, tiled=True).reshape(blocks.shape)


def local_plain(
    tokens,
    cotangent,
    router,
    slot_outputs,
    base_in,
    base_out,
    in_left,
    in_right,
    out_left,
    out_right,
):
    groups, ring = lax.axis_size("dp"), lax.axis_size(SEQ)
    image_rows = tokens[0]
    cot_rows = cotangent[0]
    saved_outputs = slot_outputs[0]
    width = image_rows.shape[1]
    slots = router.shape[1]
    owned, slice_width, rank = in_left.shape
    members = in_right.shape[0]
    places = members // owned
    group, place = lax.axis_index("dp"), lax.axis_index(SEQ)

    logits = jnp.dot(image_rows, router, preferred_element_type=jnp.float32)
    peak_high, peak_low = split(jnp.max(logits, axis=0))
    near = jnp.exp(logits - joined(peak_high, peak_low))
    total_high, total_low = split(jnp.sum(near, axis=0))
    combine = jax.nn.softmax(logits, axis=1)
    sums = jnp.stack(
        [
            dot_first(near.astype(jnp.bfloat16), image_rows),
            dot_first(combine.astype(jnp.bfloat16), cot_rows),
        ],
        axis=1,
    ).astype(jnp.bfloat16)
    sums = sums.reshape(ring, owned, 2, groups, slice_width).transpose(3, 0, 1, 2, 4)
    sums = sums.reshape(groups, ring, owned, 2 * slice_width)
    stats = jnp.stack([peak_high, peak_low, total_high, total_low], axis=1)
    stats = jnp.pad(stats, ((0, 0), (0, STATS - 4))).reshape(1, ring, owned, STATS)
    stats = jnp.broadcast_to(stats, (groups, ring, owned, STATS))
    first = exchange(jnp.concatenate([sums, stats], axis=3))

    tail = 2 * slice_width
    peaks = joined(first[..., tail], first[..., tail + 1])
    totals = joined(first[..., tail + 2], first[..., tail + 3])
    peak = jnp.max(peaks, axis=1)
    near_scale = jnp.exp(peaks - peak[:, None])
    total = jnp.sum(near_scale * totals, axis=1)
    near_scale = near_scale / total[:, None]
    parts = first[..., :tail].astype(jnp.float32)
    slot_inputs = jnp.sum(parts[..., :slice_width] * near_scale[..., None], axis=1)
    inputs_own = slot_inputs.astype(jnp.bfloat16)
    grads_own = jnp.sum(parts[..., slice_width:], axis=1).astype(jnp.bfloat16)
    up_part = jnp.einsum("gjd,jdr->gjr", inputs_own, in_left, preferred_element_type=jnp.float32)
    back_part = jnp.einsum("gjd,jrd->gjr", grads_own, out_right, preferred_element_type=jnp.float32)
    second = jnp.concatenate(
        [inputs_own, grads_own, *split(up_part), *split(back_part)], axis=2
    )
    second = exchange(jnp.broadcast_to(second, (groups, ring) + second.shape))
    second = lax.dynamic_slice_in_dim(second, group * places, places, 1)

    def gathered(start):
        piece = second[..., start : start + slice_width]
        return piece.transpose(2, 1, 3, 0, 4).reshape(groups * members, width)

    def ranks(start):
        piece = joined(
            second[..., start : start + rank], second[..., start + rank : start + 2 * rank]
        )
        piece = jnp.sum(piece, axis=0).transpose(1, 0, 2, 3)
        return piece.reshape(groups, members, rank).astype(jnp.bfloat16)

    inputs_low, grads_low = gathered(0), gathered(slice_width)
    up_low, back_low = ranks(tail), ranks(tail + 2 * rank)
    hidden = base_in.shape[1]
    preact = jnp.dot(inputs_low, base_in, preferred_element_type=jnp.float32).reshape(
        groups, members, hidden
    ) + jnp.einsum("gjr,jrf->gjf", up_low, in_right, preferred_element_type=jnp.float32)
    hidden_low = jax.nn.gelu(preact).astype(jnp.bfloat16)
    hidden_grad = dot_last(grads_low, base_out).reshape(groups, members, hidden) + jnp.einsum(
        "gjr,jfr->gjf", back_low, out_left, preferred_element_type=jnp.float32
    )
    preact_grad = gelu_backward(preact, hidden_grad).astype(jnp.bfloat16)
    slot_term = dot_last(preact_grad.reshape(groups * members, hidden), base_in)
    down_term = jnp.einsum(
        "gjf,jrf->gjr", preact_grad, in_right, preferred_element_type=jnp.float32
    )
    value_term = jnp.einsum(
        "gjf,jfr->gjr", hidden_low, out_left, preferred_element_type=jnp.float32
    )
    slot_term = slot_term.astype(jnp.bfloat16).reshape(groups, places, owned, groups, slice_width)
    slot_term = slot_term.transpose(3, 1, 0, 2, 4)
    rank_term = jnp.concatenate([down_term, value_term], axis=2).astype(jnp.bfloat16)
    rank_term = rank_term.reshape(groups, places, owned, 2 * rank).transpose(1, 0, 2, 3)
    rank_term = jnp.broadcast_to(rank_term, (groups,) + rank_term.shape)
    third = jnp.concatenate([slot_term, rank_term], axis=4)
    third = lax.dynamic_update_slice_in_dim(
        jnp.zeros((groups, ring) + third.shape[2:], jnp.bfloat16), third, group * places, 1
    )
    third = exchange(third)
    third = lax.dynamic_index_in_dim(third, place // places, 0, keepdims=False)
    third = jnp.sum(third.astype(jnp.float32), axis=0)
    down_own = third[..., slice_width : slice_width + rank].astype(jnp.bfloat16)
    value_own = third[..., slice_width + rank :].astype(jnp.bfloat16)
    slot_grads_own = (
        third[..., :slice_width]
        + jnp.einsum("gjr,jdr->gjd", down_own, in_left, preferred_element_type=jnp.float32)
    ).astype(jnp.bfloat16)
    shift_part = jnp.sum(slot_grads_own.astype(jnp.float32) * slot_inputs, axis=2)
    stats = jnp.stack([*split(peak), *split(total), *split(shift_part)], axis=2)
    stats = jnp.pad(stats, ((0, 0), (0, 0), (0, STATS - 6)))
    fourth = jnp.concatenate([slot_grads_own, stats], axis=2)[:, None]
    fourth = exchange(jnp.broadcast_to(fourth, (groups, ring) + fourth.shape[2:]))
    slot_grads = fourth[..., :slice_width].transpose(1, 2, 0, 3).reshape(slots, width)
    stats = fourth[..., slice_width:].astype(jnp.float32).reshape(groups, slots, STATS)
    slot_peak = stats[0, :, 0] + stats[0, :, 1]
    slot_total = stats[0, :, 2] + stats[0, :, 3]
    shift_back = jnp.sum(stats[:, :, 4] + stats[:, :, 5], axis=0)

    dispatch = jnp.exp(logits - slot_peak) / slot_total
    dispatch_low = dispatch.astype(jnp.bfloat16)
    weight_grad = dot_last(image_rows, slot_grads)
    dispatch_logit = dispatch * (weight_grad - shift_back)
    mixing_grad = dot_last(cot_rows, saved_outputs)
    combine_logit = combine * (mixing_grad - jnp.sum(combine * mixing_grad, axis=1, keepdims=True))
    logit_grad = (dispatch_logit + combine_logit).astype(jnp.bfloat16)
    token_grad = (
        jnp.dot(dispatch_low, slot_grads, preferred_element_type=jnp.float32)
        + dot_last(logit_grad, router)
    ).astype(jnp.bfloat16)
    grad_in_right = jnp.einsum(
        "gjr,gjf->jrf", up_low, preact_grad, preferred_element_type=jnp.float32
    ).astype(jnp.bfloat16)
    grad_out_left = jnp.einsum(
        "gjf,gjr->jfr", hidden_low, back_low, preferred_element_type=jnp.float32
    ).astype(jnp.bfloat16)
    grad_in_left = jnp.einsum(
        "gjd,gjr->jdr", inputs_own, down_own, preferred_element_type=jnp.float32
    ).astype(jnp.bfloat16)
    grad_out_right = jnp.einsum(
        "gjr,gjd->jrd", value_own, grads_own, preferred_element_type=jnp.float32
    ).astype(jnp.bfloat16)
    return (token_grad[None], grad_in_left, grad_in_right, grad_out_left, grad_out_right)


def dot_plain(left, right):
    return jnp.dot(left, right, preferred_element_type=jnp.float32)


def halves(value):
    high = value.astype(jnp.bfloat16).astype(jnp.float32)
    low = (value - high).astype(jnp.bfloat16).astype(jnp.float32)
    return high, low


def in_lanes(columns, shape):
    lane = lax.broadcasted_iota(jnp.int32, shape, len(shape) - 1)
    out = jnp.zeros(shape, jnp.float32)
    for number, column in enumerate(columns):
        out = jnp.where(lane == number, column, out)
    return out


def own_block(value, owned):
    rows, rank = value.shape
    wide = jnp.concatenate([value] * owned, axis=1)
    shape = (rows, owned * rank)
    block = lax.broadcasted_iota(jnp.int32, shape, 1) // rank
    expert = lax.broadcasted_iota(jnp.int32, shape, 0) % owned
    return jnp.where(block == expert, wide, 0.0).astype(jnp.bfloat16)


def from_own_block(value, owned):
    rows, wide = value.shape
    rank = wide // owned
    block = lax.broadcasted_iota(jnp.int32, value.shape, 1) // rank
    expert = lax.broadcasted_iota(jnp.int32, value.shape, 0) % owned
    kept = jnp.where(block == expert, value, 0.0)
    out = kept[:, :rank]
    for number in range(1, owned):
        out = out + kept[:, number * rank : (number + 1) * rank]
    return out


def early_kernel(out):
    out[...] = jnp.zeros(out.shape, out.dtype)


def sums_kernel(
    owned, groups, _, tokens, cotangent, router, own, other, logits_out, combine_out
):
    chips = own.shape[0] // groups
    core = lax.axis_index("core")
    image_rows = tokens[...]
    logits = dot_last(router[...], image_rows)
    high, low = halves(jnp.max(logits, axis=1, keepdims=True))
    near = jnp.exp(logits - (high + low))
    total_high, total_low = halves(jnp.sum(near, axis=1, keepdims=True))
    spread = jnp.exp(logits - jnp.max(logits, axis=0, keepdims=True))
    combine = spread / jnp.sum(spread, axis=0, keepdims=True)
    logits_out[...] = logits
    combine_out[...] = combine
    stats = in_lanes([high, low, total_high, total_low], (logits.shape[0], STATS))
    stats = stats.astype(jnp.bfloat16)
    inputs = dot_plain(near.astype(jnp.bfloat16), image_rows).astype(jnp.bfloat16)
    grads = dot_plain(combine.astype(jnp.bfloat16), cotangent[...]).astype(jnp.bfloat16)
    width = inputs.shape[1] // groups

    def block(rows, columns):
        return jnp.concatenate([inputs[rows, columns], grads[rows, columns], stats[rows]], axis=1)

    for group in range(groups):
        columns = slice(group * width, (group + 1) * width)
        for chip in range(chips):
            start = 2 * chip * owned
            even = block(slice(start, start + owned), columns)
            odd = block(slice(start + owned, start + 2 * owned), columns)
            own[group * chips + chip] = jnp.where(core == 0, even, odd)
            other[group * chips + chip] = jnp.where(core == 0, odd, even)


def merge_kernel(width, own, other, out):
    parts = []
    for part in (own, other):
        stats = part[:, :, 2 * width :].astype(jnp.float32)
        parts.append((stats[:, :, 0:1] + stats[:, :, 1:2], stats[:, :, 2:3] + stats[:, :, 3:4]))
    peak = jnp.maximum(parts[0][0], parts[1][0])
    scales = [jnp.exp(part[0] - peak) for part in parts]
    total = scales[0] * parts[0][1] + scales[1] * parts[1][1]
    stats = in_lanes([*halves(peak), *halves(total)], own.shape[:2] + (STATS,))
    inputs = [
        part[:, :, :width].astype(jnp.float32) * scale
        for part, scale in zip((own, other), scales, strict=True)
    ]
    grads = [part[:, :, width : 2 * width].astype(jnp.float32) for part in (own, other)]
    out[:, :, :width] = (inputs[0] + inputs[1]).astype(jnp.bfloat16)
    out[:, :, width : 2 * width] = (grads[0] + grads[1]).astype(jnp.bfloat16)
    out[:, :, 2 * width :] = stats.astype(jnp.bfloat16)


def mixing_kernel(cotangent, saved, combine, out):
    mixing = dot_last(saved[...], cotangent[...])
    weights = combine[...]
    out[...] = weights * (mixing - jnp.sum(weights * mixing, axis=0, keepdims=True))


def owner_kernel(groups, first, in_left, out_right, second, inputs_out, lows_out, stats_out):
    ring = first.shape[0] // groups
    owned, rank, width = in_left.shape
    inputs, grads, stats_rows = [], [], []
    for group in range(groups):
        rows = slice(group * ring, (group + 1) * ring)
        stats = first[rows, :, 2 * width :].astype(jnp.float32)
        peaks = stats[:, :, 0:1] + stats[:, :, 1:2]
        totals = stats[:, :, 2:3] + stats[:, :, 3:4]
        peak = jnp.max(peaks, axis=0)
        scale = jnp.exp(peaks - peak[None])
        total = jnp.sum(scale * totals, axis=0)
        scale = scale / total[None]
        inputs.append(jnp.sum(first[rows, :, :width].astype(jnp.float32) * scale, axis=0))
        grads.append(jnp.sum(first[rows, :, width : 2 * width].astype(jnp.float32), axis=0))
        stats_rows.append(in_lanes([*halves(peak), *halves(total)], (owned, STATS)))
    inputs, grads = jnp.concatenate(inputs, axis=0), jnp.concatenate(grads, axis=0)
    inputs_out[...] = inputs
    stats_out[...] = jnp.concatenate(stats_rows, axis=0)
    inputs_low, grads_low = inputs.astype(jnp.bfloat16), grads.astype(jnp.bfloat16)
    lows_out[0] = inputs_low
    lows_out[1] = grads_low
    up = dot_last(inputs_low, in_left[...].reshape(owned * rank, width))
    back = dot_last(grads_low, out_right[...].reshape(owned * rank, width))
    ranks = [from_own_block(up, owned), from_own_block(back, owned)]
    ranks = jnp.concatenate(ranks, axis=1).astype(jnp.bfloat16)
    block = jnp.concatenate([inputs_low, grads_low, ranks], axis=1)
    second[...] = block


def pack_kernel(blocks, out):
    for group in range(out.shape[0]):
        for place in range(out.shape[1]):
            out[group, place] = blocks[group]


def hidden_kernel(
    groups,
    second,
    second_other,
    base_in,
    base_out,
    in_right,
    out_left,
    third,
    third_other,
    pair_out,
    ranks_out,
):
    first_core = lax.axis_index("core") == 0
    members, rank, hidden = in_right.shape
    rows = second.shape[1]
    owned = rows // groups
    places = members // owned
    width = base_in.shape[1] // groups

    def gathered(columns):
        parts = []
        for half in range(groups):
            taken = []
            for chip in range(places // 2):
                block = half * (places // 2) + chip
                own = second[block, :, columns].astype(jnp.float32)
                other = second_other[block, :, columns].astype(jnp.float32)
                taken.append(jnp.where(first_core, own, other))
                taken.append(jnp.where(first_core, other, own))
            parts.append(jnp.concatenate(taken, axis=0))
        return parts

    def low_rank(value, table):
        value = value.astype(jnp.float32)
        taken = []
        for place in range(places):
            own = own_block(value[place * rows : (place + 1) * rows], owned)
            part = table[place * owned : (place + 1) * owned].reshape(owned * rank, hidden)
            taken.append(dot_plain(own, part))
        return jnp.concatenate(taken, axis=0)

    def to_rank(value, table):
        taken = []
        for place in range(places):
            part = table[place * owned : (place + 1) * owned].reshape(owned * rank, hidden)
            wide = dot_last(value[place * rows : (place + 1) * rows].astype(jnp.bfloat16), part)
            taken.append(from_own_block(wide, owned))
        return jnp.concatenate(taken, axis=0)

    ranks = functools.reduce(jnp.add, gathered(slice(2 * width, 2 * width + 2 * rank)))
    up, back = ranks[:, :rank].astype(jnp.bfloat16), ranks[:, rank:].astype(jnp.bfloat16)
    preact = low_rank(up, in_right)
    for half, part in enumerate(gathered(slice(0, width))):
        columns = slice(half * width, (half + 1) * width)
        preact = preact + dot_last(part.astype(jnp.bfloat16), base_in[:, columns])
    hidden_grad = low_rank(back, out_left)
    for half, part in enumerate(gathered(slice(width, 2 * width))):
        columns = slice(half * width, (half + 1) * width)
        hidden_grad = hidden_grad + dot_last(part.astype(jnp.bfloat16), base_out[:, columns])
    root = 0.7978845608028654
    bent = jnp.tanh(root * (preact + 0.044715 * (preact * preact * preact)))
    hidden_value = 0.5 * preact * (1.0 + bent)
    slope = 0.5 * (1.0 + bent) + 0.5 * preact * (1.0 - bent * bent) * (
        root * (1.0 + 3.0 * 0.044715 * (preact * preact))
    )
    hidden_low = hidden_value.astype(jnp.bfloat16).astype(jnp.float32)
    preact_grad = (hidden_grad * slope).astype(jnp.bfloat16).astype(jnp.float32)
    pair_out[0] = preact_grad
    pair_out[1] = hidden_low
    ranks_out[0] = up.astype(jnp.float32)
    ranks_out[1] = back.astype(jnp.float32)
    slot_term = dot_plain(preact_grad.astype(jnp.bfloat16), base_in[...])
    down = to_rank(preact_grad, in_right)
    value = to_rank(hidden_low, out_left)
    ranks = jnp.concatenate([down, value], axis=1)
    for half in range(groups):
        columns = slice(half * width, (half + 1) * width)

        def block(place):
            taken = slice(place * rows, (place + 1) * rows)
            return jnp.concatenate([slot_term[taken, columns], ranks[taken]], axis=1)

        for chip in range(places // 2):
            even, odd = block(2 * chip), block(2 * chip + 1)
            number = half * (places // 2) + chip
            third[number] = jnp.where(first_core, even, odd).astype(jnp.bfloat16)
            third_other[number] = jnp.where(first_core, odd, even).astype(jnp.bfloat16)


def add_kernel(own, other, out):
    out[...] = (own[...].astype(jnp.float32) + other[...].astype(jnp.float32)).astype(out.dtype)


def outer_kernel(owned, left_rows, right_rows, *outs):
    rows = left_rows.shape[1] // (outs[0].shape[0] // owned)
    for number, out in enumerate(outs):
        for place in range(out.shape[0] // owned):
            taken = slice(place * rows, (place + 1) * rows)
            own = own_block(left_rows[number, taken], owned)
            product = dot_first(own, right_rows[number, taken].astype(jnp.bfloat16))
            out[place * owned : (place + 1) * owned] = product.astype(jnp.bfloat16).reshape(
                (owned,) + out.shape[1:]
            )


def halves_kernel(third, own, other):
    places = third.shape[0] // 2
    here = lax.axis_index("half")
    for out, group in ((own, here), (other, 1 - here)):
        taken = third[pl.ds(group * places, places)].astype(jnp.float32)
        out[...] = jnp.sum(taken, axis=0).astype(out.dtype)


def finish_kernel(groups, own, others, in_left, inputs, stats, fourth, ranks_out):
    owned, rank, width = in_left.shape
    summed = own[...] + others[1 - lax.axis_index("half")].astype(jnp.float32)
    ranks = summed[:, width:].astype(jnp.bfloat16).astype(jnp.float32)
    ranks_out[0] = ranks[:, :rank]
    ranks_out[1] = ranks[:, rank:]
    down = own_block(ranks[:, :rank], owned)
    grads = summed[:, :width] + dot_plain(down, in_left[...].reshape(owned * rank, width))
    grads = grads.astype(jnp.bfloat16).astype(jnp.float32)
    high, low = halves(jnp.sum(grads * inputs[...], axis=1, keepdims=True))
    lane = lax.broadcasted_iota(jnp.int32, stats.shape, 1)
    tail = jnp.where(lane == 4, high, jnp.where(lane == 5, low, stats[...]))
    block = jnp.concatenate([grads, tail], axis=1).astype(jnp.bfloat16)
    for group in range(groups):
        rows = block[group * owned : (group + 1) * owned]
        for place in range(fourth.shape[0] // groups):
            fourth[group * (fourth.shape[0] // groups) + place] = rows


def tokens_kernel(groups, fourth, fourth_other, tokens, router, logits, mixing, out_far, out, sent):
    blocks, owned, _ = fourth.shape
    chips = blocks // groups
    width = tokens.shape[1] // groups
    first_core = lax.axis_index("core") == 0

    def rows(half, columns):
        taken = []
        for chip in range(chips):
            own = fourth[half * chips + chip, :, columns].astype(jnp.float32)
            other = fourth_other[half * chips + chip, :, columns].astype(jnp.float32)
            taken.append(jnp.where(first_core, own, other))
            taken.append(jnp.where(first_core, other, own))
        return jnp.concatenate(taken, axis=0)

    grads = jnp.concatenate([rows(half, slice(0, width)) for half in range(groups)], axis=1)
    grads = grads.astype(jnp.bfloat16)
    stats = [rows(half, slice(width, width + STATS)) for half in range(groups)]
    peak = stats[0][:, 0:1] + stats[0][:, 1:2]
    total = stats[0][:, 2:3] + stats[0][:, 3:4]
    shift = functools.reduce(jnp.add, [part[:, 4:5] + part[:, 5:6] for part in stats])
    dispatch = jnp.exp(logits[...] - peak) / total
    weight_grad = dot_last(grads, tokens[...])
    logit_grad = dispatch * (weight_grad - shift) + mixing[...]
    left = jnp.concatenate([dispatch, logit_grad], axis=0).astype(jnp.bfloat16)
    right = jnp.concatenate([grads, router[...]], axis=0)
    parts = sent.shape[0]
    size = out.shape[0] // parts
    copies = []
    for part in range(parts):
        rows = slice(part * size, (part + 1) * size)
        out[rows] = dot_first(left[:, rows], right).astype(jnp.bfloat16)
        copy = pltpu.make_async_copy(out.at[rows], out_far.at[rows], sent.at[part])
        copy.start()
        copies.append(copy)
    for copy in copies:
        copy.wait()


def swap_cores(blocks):
    return lax.ppermute(blocks, "core", [(0, 1), (1, 0)])


def to_group(block, groups):
    chips = lax.axis_size("chip")
    blocks = lax.all_gather(block, "half", axis=0)
    (blocks,) = call(
        pack_kernel,
        [array(block.dtype, groups, chips, *block.shape)],
        [blocks],
        FLOPS_BESIDE_EXCHANGE,
    )
    blocks = blocks.reshape(groups * chips, *block.shape)
    blocks = lax.all_to_all(blocks, HALF_CORE, 0, 0, tiled=True)
    return blocks, swap_cores(blocks)


def call(kernel, outs, args, flops, space=pltpu.VMEM, scratch=()):
    size = sum(array.size * array.dtype.itemsize for array in args)
    size += sum(out.size * out.dtype.itemsize for out in outs)
    return pl.pallas_call(
        kernel,
        out_shape=outs,
        in_specs=[pl.BlockSpec(memory_space=pltpu.VMEM) for _ in args],
        out_specs=[pl.BlockSpec(memory_space=space) for _ in outs],
        scratch_shapes=scratch,
        cost_estimate=pl.CostEstimate(flops=flops, bytes_accessed=size, transcendentals=0),
        compiler_params=pltpu.CompilerParams(vmem_limit_bytes=24 * 2**20),
    )(*args)


def array(dtype, *shape):
    return jax.ShapeDtypeStruct(shape, dtype)


def local(
    tokens,
    cotangent,
    router,
    slot_outputs,
    base_in,
    base_out,
    in_left,
    in_right,
    out_left,
    out_right,
):
    groups, ring = lax.axis_size("dp"), lax.axis_size(SEQ)
    devices = groups * ring
    _, count, width = tokens.shape
    slots = router.shape[1]
    owned, slice_width, rank = in_left.shape
    members, _, hidden = in_right.shape
    rows = groups * owned
    if groups != 2 or ring % 4 or slice_width % 128 or rows % 8 or members % owned:
        return local_plain(
            tokens,
            cotangent,
            router,
            slot_outputs,
            base_in,
            base_out,
            in_left,
            in_right,
            out_left,
            out_right,
        )
    low, full = jnp.bfloat16, jnp.float32
    image_rows, cot_rows, saved = tokens[0], cotangent[0], slot_outputs[0]
    router, base_in = router.T, base_in.T
    in_left, out_left = in_left.swapaxes(1, 2), out_left.swapaxes(1, 2)
    (early,) = call(early_kernel, [array(full, 8, 128)], [], FLOPS_BESIDE_EXCHANGE)
    first = array(low, devices // 2, owned, 2 * slice_width + STATS)
    own, other, logits, combine = call(
        functools.partial(sums_kernel, owned, groups),
        [first, first, array(full, slots, count), array(full, slots, count)],
        [early, image_rows, cot_rows, router],
        6 * count * slots * width + FLOPS_BESIDE_EXCHANGE,
    )
    other = swap_cores(other)
    (first,) = call(
        functools.partial(merge_kernel, slice_width), [first], [own, other], FLOPS_BESIDE_EXCHANGE
    )
    first = lax.all_to_all(first, SAME_CORE, 0, 0, tiled=True)
    second, inputs, lows, stats = call(
        functools.partial(owner_kernel, groups),
        [
            array(low, rows, 2 * slice_width + 2 * rank),
            array(full, rows, slice_width),
            array(low, 2, rows, slice_width),
            array(full, rows, STATS),
        ],
        [first, in_left, out_right],
        4 * rows * owned * rank * slice_width,
    )
    second, second_other = to_group(second, groups)
    total_rows = groups * members
    third = array(low, ring // 2, rows, slice_width + 2 * rank)
    third, other, pair, hidden_ranks = call(
        functools.partial(hidden_kernel, groups),
        [
            third,
            third,
            array(full, 2, total_rows, hidden),
            array(full, 2, total_rows, rank),
        ],
        [second, second_other, base_in, base_out, in_right, out_left],
        6 * total_rows * hidden * (width + owned * rank),
    )
    (third,) = call(
        add_kernel,
        [array(third.dtype, *third.shape)],
        [third, swap_cores(other)],
        FLOPS_BESIDE_EXCHANGE,
    )
    third = lax.all_to_all(third, HALF_CORE, 0, 0, tiled=True)
    own, other = call(
        halves_kernel,
        [array(kind, rows, slice_width + 2 * rank) for kind in (full, low)],
        [third],
        0,
    )
    others = lax.all_gather(other, "half", axis=0)
    fourth, ranks = call(
        functools.partial(finish_kernel, groups),
        [array(low, devices // 2, owned, slice_width + STATS), array(full, 2, rows, rank)],
        [own, others, in_left, inputs, stats],
        2 * rows * owned * rank * slice_width,
    )
    fourth, combine, pair, hidden_ranks = lax.optimization_barrier(
        (fourth, combine, pair, hidden_ranks)
    )
    fourth = lax.all_to_all(fourth, SAME_CORE, 0, 0, tiled=True)
    grad_in_right, grad_out_left = call(
        functools.partial(outer_kernel, owned),
        [array(low, members, rank, hidden)] * 2,
        [hidden_ranks, pair],
        4 * members * rank * hidden * rows,
    )
    (mixing,) = call(
        mixing_kernel,
        [array(full, slots, count)],
        [cot_rows, saved, combine],
        2 * count * slots * width,
    )
    grad_in_left, grad_out_right = call(
        functools.partial(outer_kernel, owned),
        [array(low, owned, rank, slice_width)] * 2,
        [ranks, lows],
        4 * owned * rank * slice_width * rows,
    )
    parts = math.gcd(4, count // 16)
    (token_grad,) = call(
        functools.partial(tokens_kernel, groups),
        [array(low, count, width)],
        [fourth, swap_cores(fourth), image_rows, router, logits, mixing],
        6 * count * slots * width,
        pltpu.HBM,
        [pltpu.VMEM((count, width), low), pltpu.SemaphoreType.DMA((parts,))],
    )
    return (
        token_grad[None],
        grad_in_left.swapaxes(1, 2),
        grad_in_right,
        grad_out_left.swapaxes(1, 2),
        grad_out_right,
    )


def solution(mesh):
    groups, ring = mesh.shape["dp"], mesh.shape["seq"]
    cores = math.gcd(2, ring // groups)
    split = mesh.devices.reshape(groups, groups, ring // groups // cores, cores)
    mesh = jax.sharding.Mesh(split, BOTH)
    in_specs = (
        P("dp", SEQ, None),
        P("dp", SEQ, None),
        P(),
        P("dp", None, None),
        P(None, SEQ),
        P(SEQ, None),
        P(SEQ, "dp", None),
        P("dp", None, SEQ),
        P("dp", SEQ, None),
        P(SEQ, None, "dp"),
    )
    out_specs = (
        P("dp", SEQ, None),
        P(SEQ, "dp", None),
        P("dp", None, SEQ),
        P("dp", SEQ, None),
        P(SEQ, None, "dp"),
    )
    return jax.shard_map(local, mesh=mesh, in_specs=in_specs, out_specs=out_specs, check_vma=False)
```

```python
import functools
import math

import jax
import jax.numpy as jnp
from jax import lax
from jax.experimental import pallas as pl
from jax.experimental.pallas import tpu as pltpu
from jax.sharding import PartitionSpec as P

PLACE = ("chip", "core")
SEQ = ("half", *PLACE)
BOTH = ("dp", *SEQ)
HALF = ("dp", *PLACE)
HALF_CORE = ("dp", "chip")
SAME_CORE = ("dp", "half", "chip")
STATS = 128
FLOPS_BESIDE_EXCHANGE = 10**10


def gelu_backward(preact, upstream):
    return jax.vjp(jax.nn.gelu, preact)[1](upstream)[0]


def dot_first(left, right):
    return lax.dot_general(
        left, right, (((0,), (0,)), ((), ())), preferred_element_type=jnp.float32
    )


def dot_last(left, right):
    return lax.dot_general(
        left, right, (((1,), (1,)), ((), ())), preferred_element_type=jnp.float32
    )


def split(value):
    high = lax.reduce_precision(value, 8, 7)
    low = lax.reduce_precision(value - high, 8, 7)
    return high.astype(jnp.bfloat16), low.astype(jnp.bfloat16)


def joined(high, low):
    return high.astype(jnp.float32) + low.astype(jnp.float32)


def exchange(blocks):
    flat = blocks.reshape((-1,) + blocks.shape[2:])
    return lax.all_to_all(flat, BOTH, 0, 0, tiled=True).reshape(blocks.shape)


def local_plain(
    tokens,
    cotangent,
    router,
    slot_outputs,
    base_in,
    base_out,
    in_left,
    in_right,
    out_left,
    out_right,
):
    groups, ring = lax.axis_size("dp"), lax.axis_size(SEQ)
    image_rows = tokens[0]
    cot_rows = cotangent[0]
    saved_outputs = slot_outputs[0]
    width = image_rows.shape[1]
    slots = router.shape[1]
    owned, slice_width, rank = in_left.shape
    members = in_right.shape[0]
    places = members // owned
    group, place = lax.axis_index("dp"), lax.axis_index(SEQ)

    logits = jnp.dot(image_rows, router, preferred_element_type=jnp.float32)
    peak_high, peak_low = split(jnp.max(logits, axis=0))
    near = jnp.exp(logits - joined(peak_high, peak_low))
    total_high, total_low = split(jnp.sum(near, axis=0))
    combine = jax.nn.softmax(logits, axis=1)
    sums = jnp.stack(
        [
            dot_first(near.astype(jnp.bfloat16), image_rows),
            dot_first(combine.astype(jnp.bfloat16), cot_rows),
        ],
        axis=1,
    ).astype(jnp.bfloat16)
    sums = sums.reshape(ring, owned, 2, groups, slice_width).transpose(3, 0, 1, 2, 4)
    sums = sums.reshape(groups, ring, owned, 2 * slice_width)
    stats = jnp.stack([peak_high, peak_low, total_high, total_low], axis=1)
    stats = jnp.pad(stats, ((0, 0), (0, STATS - 4))).reshape(1, ring, owned, STATS)
    stats = jnp.broadcast_to(stats, (groups, ring, owned, STATS))
    first = exchange(jnp.concatenate([sums, stats], axis=3))

    tail = 2 * slice_width
    peaks = joined(first[..., tail], first[..., tail + 1])
    totals = joined(first[..., tail + 2], first[..., tail + 3])
    peak = jnp.max(peaks, axis=1)
    near_scale = jnp.exp(peaks - peak[:, None])
    total = jnp.sum(near_scale * totals, axis=1)
    near_scale = near_scale / total[:, None]
    parts = first[..., :tail].astype(jnp.float32)
    slot_inputs = jnp.sum(parts[..., :slice_width] * near_scale[..., None], axis=1)
    inputs_own = slot_inputs.astype(jnp.bfloat16)
    grads_own = jnp.sum(parts[..., slice_width:], axis=1).astype(jnp.bfloat16)
    up_part = jnp.einsum("gjd,jdr->gjr", inputs_own, in_left, preferred_element_type=jnp.float32)
    back_part = jnp.einsum("gjd,jrd->gjr", grads_own, out_right, preferred_element_type=jnp.float32)
    second = jnp.concatenate(
        [inputs_own, grads_own, *split(up_part), *split(back_part)], axis=2
    )
    second = exchange(jnp.broadcast_to(second, (groups, ring) + second.shape))
    second = lax.dynamic_slice_in_dim(second, group * places, places, 1)

    def gathered(start):
        piece = second[..., start : start + slice_width]
        return piece.transpose(2, 1, 3, 0, 4).reshape(groups * members, width)

    def ranks(start):
        piece = joined(
            second[..., start : start + rank], second[..., start + rank : start + 2 * rank]
        )
        piece = jnp.sum(piece, axis=0).transpose(1, 0, 2, 3)
        return piece.reshape(groups, members, rank).astype(jnp.bfloat16)

    inputs_low, grads_low = gathered(0), gathered(slice_width)
    up_low, back_low = ranks(tail), ranks(tail + 2 * rank)
    hidden = base_in.shape[1]
    preact = jnp.dot(inputs_low, base_in, preferred_element_type=jnp.float32).reshape(
        groups, members, hidden
    ) + jnp.einsum("gjr,jrf->gjf", up_low, in_right, preferred_element_type=jnp.float32)
    hidden_low = jax.nn.gelu(preact).astype(jnp.bfloat16)
    hidden_grad = dot_last(grads_low, base_out).reshape(groups, members, hidden) + jnp.einsum(
        "gjr,jfr->gjf", back_low, out_left, preferred_element_type=jnp.float32
    )
    preact_grad = gelu_backward(preact, hidden_grad).astype(jnp.bfloat16)
    slot_term = dot_last(preact_grad.reshape(groups * members, hidden), base_in)
    down_term = jnp.einsum(
        "gjf,jrf->gjr", preact_grad, in_right, preferred_element_type=jnp.float32
    )
    value_term = jnp.einsum(
        "gjf,jfr->gjr", hidden_low, out_left, preferred_element_type=jnp.float32
    )
    slot_term = slot_term.astype(jnp.bfloat16).reshape(groups, places, owned, groups, slice_width)
    slot_term = slot_term.transpose(3, 1, 0, 2, 4)
    rank_term = jnp.concatenate([down_term, value_term], axis=2).astype(jnp.bfloat16)
    rank_term = rank_term.reshape(groups, places, owned, 2 * rank).transpose(1, 0, 2, 3)
    rank_term = jnp.broadcast_to(rank_term, (groups,) + rank_term.shape)
    third = jnp.concatenate([slot_term, rank_term], axis=4)
    third = lax.dynamic_update_slice_in_dim(
        jnp.zeros((groups, ring) + third.shape[2:], jnp.bfloat16), third, group * places, 1
    )
    third = exchange(third)
    third = lax.dynamic_index_in_dim(third, place // places, 0, keepdims=False)
    third = jnp.sum(third.astype(jnp.float32), axis=0)
    down_own = third[..., slice_width : slice_width + rank].astype(jnp.bfloat16)
    value_own = third[..., slice_width + rank :].astype(jnp.bfloat16)
    slot_grads_own = (
        third[..., :slice_width]
        + jnp.einsum("gjr,jdr->gjd", down_own, in_left, preferred_element_type=jnp.float32)
    ).astype(jnp.bfloat16)
    shift_part = jnp.sum(slot_grads_own.astype(jnp.float32) * slot_inputs, axis=2)
    stats = jnp.stack([*split(peak), *split(total), *split(shift_part)], axis=2)
    stats = jnp.pad(stats, ((0, 0), (0, 0), (0, STATS - 6)))
    fourth = jnp.concatenate([slot_grads_own, stats], axis=2)[:, None]
    fourth = exchange(jnp.broadcast_to(fourth, (groups, ring) + fourth.shape[2:]))
    slot_grads = fourth[..., :slice_width].transpose(1, 2, 0, 3).reshape(slots, width)
    stats = fourth[..., slice_width:].astype(jnp.float32).reshape(groups, slots, STATS)
    slot_peak = stats[0, :, 0] + stats[0, :, 1]
    slot_total = stats[0, :, 2] + stats[0, :, 3]
    shift_back = jnp.sum(stats[:, :, 4] + stats[:, :, 5], axis=0)

    dispatch = jnp.exp(logits - slot_peak) / slot_total
    dispatch_low = dispatch.astype(jnp.bfloat16)
    weight_grad = dot_last(image_rows, slot_grads)
    dispatch_logit = dispatch * (weight_grad - shift_back)
    mixing_grad = dot_last(cot_rows, saved_outputs)
    combine_logit = combine * (mixing_grad - jnp.sum(combine * mixing_grad, axis=1, keepdims=True))
    logit_grad = (dispatch_logit + combine_logit).astype(jnp.bfloat16)
    token_grad = (
        jnp.dot(dispatch_low, slot_grads, preferred_element_type=jnp.float32)
        + dot_last(logit_grad, router)
    ).astype(jnp.bfloat16)
    grad_in_right = jnp.einsum(
        "gjr,gjf->jrf", up_low, preact_grad, preferred_element_type=jnp.float32
    ).astype(jnp.bfloat16)
    grad_out_left = jnp.einsum(
        "gjf,gjr->jfr", hidden_low, back_low, preferred_element_type=jnp.float32
    ).astype(jnp.bfloat16)
    grad_in_left = jnp.einsum(
        "gjd,gjr->jdr", inputs_own, down_own, preferred_element_type=jnp.float32
    ).astype(jnp.bfloat16)
    grad_out_right = jnp.einsum(
        "gjr,gjd->jrd", value_own, grads_own, preferred_element_type=jnp.float32
    ).astype(jnp.bfloat16)
    return (token_grad[None], grad_in_left, grad_in_right, grad_out_left, grad_out_right)


def dot_plain(left, right):
    return jnp.dot(left, right, preferred_element_type=jnp.float32)


def halves(value):
    high = value.astype(jnp.bfloat16).astype(jnp.float32)
    low = (value - high).astype(jnp.bfloat16).astype(jnp.float32)
    return high, low


def in_lanes(columns, shape):
    lane = lax.broadcasted_iota(jnp.int32, shape, len(shape) - 1)
    out = jnp.zeros(shape, jnp.float32)
    for number, column in enumerate(columns):
        out = jnp.where(lane == number, column, out)
    return out


def own_block(value, owned):
    rows, rank = value.shape
    wide = jnp.concatenate([value] * owned, axis=1)
    shape = (rows, owned * rank)
    block = lax.broadcasted_iota(jnp.int32, shape, 1) // rank
    expert = lax.broadcasted_iota(jnp.int32, shape, 0) % owned
    return jnp.where(block == expert, wide, 0.0).astype(jnp.bfloat16)


def from_own_block(value, owned):
    rows, wide = value.shape
    rank = wide // owned
    block = lax.broadcasted_iota(jnp.int32, value.shape, 1) // rank
    expert = lax.broadcasted_iota(jnp.int32, value.shape, 0) % owned
    kept = jnp.where(block == expert, value, 0.0)
    out = kept[:, :rank]
    for number in range(1, owned):
        out = out + kept[:, number * rank : (number + 1) * rank]
    return out


def early_kernel(out):
    out[...] = jnp.zeros(out.shape, out.dtype)


def sums_kernel(
    owned, groups, _, tokens, cotangent, router, own, other, logits_out, combine_out
):
    chips = own.shape[0] // groups
    core = lax.axis_index("core")
    image_rows = tokens[...]
    logits = dot_last(router[...], image_rows)
    high, low = halves(jnp.max(logits, axis=1, keepdims=True))
    near = jnp.exp(logits - (high + low))
    total_high, total_low = halves(jnp.sum(near, axis=1, keepdims=True))
    spread = jnp.exp(logits - jnp.max(logits, axis=0, keepdims=True))
    combine = spread / jnp.sum(spread, axis=0, keepdims=True)
    logits_out[...] = logits
    combine_out[...] = combine
    stats = in_lanes([high, low, total_high, total_low], (logits.shape[0], STATS))
    stats = stats.astype(jnp.bfloat16)
    inputs = dot_plain(near.astype(jnp.bfloat16), image_rows).astype(jnp.bfloat16)
    grads = dot_plain(combine.astype(jnp.bfloat16), cotangent[...]).astype(jnp.bfloat16)
    width = inputs.shape[1] // groups

    def block(rows, columns):
        return jnp.concatenate([inputs[rows, columns], grads[rows, columns], stats[rows]], axis=1)

    for group in range(groups):
        columns = slice(group * width, (group + 1) * width)
        for chip in range(chips):
            start = 2 * chip * owned
            even = block(slice(start, start + owned), columns)
            odd = block(slice(start + owned, start + 2 * owned), columns)
            own[group * chips + chip] = jnp.where(core == 0, even, odd)
            other[group * chips + chip] = jnp.where(core == 0, odd, even)


def merge_kernel(width, own, other, out):
    parts = []
    for part in (own, other):
        stats = part[:, :, 2 * width :].astype(jnp.float32)
        parts.append((stats[:, :, 0:1] + stats[:, :, 1:2], stats[:, :, 2:3] + stats[:, :, 3:4]))
    peak = jnp.maximum(parts[0][0], parts[1][0])
    scales = [jnp.exp(part[0] - peak) for part in parts]
    total = scales[0] * parts[0][1] + scales[1] * parts[1][1]
    stats = in_lanes([*halves(peak), *halves(total)], own.shape[:2] + (STATS,))
    inputs = [
        part[:, :, :width].astype(jnp.float32) * scale
        for part, scale in zip((own, other), scales, strict=True)
    ]
    grads = [part[:, :, width : 2 * width].astype(jnp.float32) for part in (own, other)]
    out[:, :, :width] = (inputs[0] + inputs[1]).astype(jnp.bfloat16)
    out[:, :, width : 2 * width] = (grads[0] + grads[1]).astype(jnp.bfloat16)
    out[:, :, 2 * width :] = stats.astype(jnp.bfloat16)


def mixing_kernel(cotangent, saved, combine, out):
    mixing = dot_last(saved[...], cotangent[...])
    weights = combine[...]
    out[...] = weights * (mixing - jnp.sum(weights * mixing, axis=0, keepdims=True))


def owner_kernel(groups, first, in_left, out_right, second, inputs_out, lows_out, stats_out):
    ring = first.shape[0] // groups
    owned, rank, width = in_left.shape
    inputs, grads, stats_rows = [], [], []
    for group in range(groups):
        rows = slice(group * ring, (group + 1) * ring)
        stats = first[rows, :, 2 * width :].astype(jnp.float32)
        peaks = stats[:, :, 0:1] + stats[:, :, 1:2]
        totals = stats[:, :, 2:3] + stats[:, :, 3:4]
        peak = jnp.max(peaks, axis=0)
        scale = jnp.exp(peaks - peak[None])
        total = jnp.sum(scale * totals, axis=0)
        scale = scale / total[None]
        inputs.append(jnp.sum(first[rows, :, :width].astype(jnp.float32) * scale, axis=0))
        grads.append(jnp.sum(first[rows, :, width : 2 * width].astype(jnp.float32), axis=0))
        stats_rows.append(in_lanes([*halves(peak), *halves(total)], (owned, STATS)))
    inputs, grads = jnp.concatenate(inputs, axis=0), jnp.concatenate(grads, axis=0)
    inputs_out[...] = inputs
    stats_out[...] = jnp.concatenate(stats_rows, axis=0)
    inputs_low, grads_low = inputs.astype(jnp.bfloat16), grads.astype(jnp.bfloat16)
    lows_out[0] = inputs_low
    lows_out[1] = grads_low
    up = dot_last(inputs_low, in_left[...].reshape(owned * rank, width))
    back = dot_last(grads_low, out_right[...].reshape(owned * rank, width))
    ranks = [from_own_block(up, owned), from_own_block(back, owned)]
    ranks = jnp.concatenate(ranks, axis=1).astype(jnp.bfloat16)
    block = jnp.concatenate([inputs_low, grads_low, ranks], axis=1)
    second[...] = block


def pack_kernel(own, beside, out):
    here = lax.axis_index("half")
    for group in range(out.shape[0]):
        block = jnp.where(here == group, own[...], beside[...])
        for place in range(out.shape[1]):
            out[group, place] = block


def hidden_kernel(
    groups,
    second,
    second_other,
    base_in,
    base_out,
    in_right,
    out_left,
    third,
    pair_out,
    ranks_out,
):
    first_core = lax.axis_index("core") == 0
    members, rank, hidden = in_right.shape
    rows = second.shape[1]
    owned = rows // groups
    places = members // owned
    width = base_in.shape[1] // groups

    def gathered(columns):
        parts = []
        for half in range(groups):
            taken = []
            for chip in range(places // 2):
                block = half * (places // 2) + chip
                own = second[block, :, columns].astype(jnp.float32)
                other = second_other[block, :, columns].astype(jnp.float32)
                taken.append(jnp.where(first_core, own, other))
                taken.append(jnp.where(first_core, other, own))
            parts.append(jnp.concatenate(taken, axis=0))
        return parts

    def low_rank(value, table):
        value = value.astype(jnp.float32)
        taken = []
        for place in range(places):
            own = own_block(value[place * rows : (place + 1) * rows], owned)
            part = table[place * owned : (place + 1) * owned].reshape(owned * rank, hidden)
            taken.append(dot_plain(own, part))
        return jnp.concatenate(taken, axis=0)

    def to_rank(value, table):
        taken = []
        for place in range(places):
            part = table[place * owned : (place + 1) * owned].reshape(owned * rank, hidden)
            wide = dot_last(value[place * rows : (place + 1) * rows].astype(jnp.bfloat16), part)
            taken.append(from_own_block(wide, owned))
        return jnp.concatenate(taken, axis=0)

    ranks = functools.reduce(jnp.add, gathered(slice(2 * width, 2 * width + 2 * rank)))
    up, back = ranks[:, :rank].astype(jnp.bfloat16), ranks[:, rank:].astype(jnp.bfloat16)
    preact = low_rank(up, in_right)
    for half, part in enumerate(gathered(slice(0, width))):
        columns = slice(half * width, (half + 1) * width)
        preact = preact + dot_last(part.astype(jnp.bfloat16), base_in[:, columns])
    hidden_grad = low_rank(back, out_left)
    for half, part in enumerate(gathered(slice(width, 2 * width))):
        columns = slice(half * width, (half + 1) * width)
        hidden_grad = hidden_grad + dot_last(part.astype(jnp.bfloat16), base_out[:, columns])
    root = 0.7978845608028654
    bent = jnp.tanh(root * (preact + 0.044715 * (preact * preact * preact)))
    hidden_value = 0.5 * preact * (1.0 + bent)
    slope = 0.5 * (1.0 + bent) + 0.5 * preact * (1.0 - bent * bent) * (
        root * (1.0 + 3.0 * 0.044715 * (preact * preact))
    )
    hidden_low = hidden_value.astype(jnp.bfloat16).astype(jnp.float32)
    preact_grad = (hidden_grad * slope).astype(jnp.bfloat16).astype(jnp.float32)
    pair_out[0] = preact_grad
    pair_out[1] = hidden_low
    ranks_out[0] = up.astype(jnp.float32)
    ranks_out[1] = back.astype(jnp.float32)
    slot_term = dot_plain(preact_grad.astype(jnp.bfloat16), base_in[...]).astype(jnp.bfloat16)
    down = to_rank(preact_grad, in_right)
    value = to_rank(hidden_low, out_left)
    ranks = jnp.concatenate([down, value], axis=1).astype(jnp.bfloat16)
    for half in range(groups):
        columns = slice(half * width, (half + 1) * width)
        for place in range(places):
            taken = slice(place * rows, (place + 1) * rows)
            block = half * places + place
            third[block, :, :width] = slot_term[taken, columns]
            third[block, :, width:] = ranks[taken]


def outer_kernel(owned, left_rows, right_rows, *outs):
    rows = left_rows.shape[1] // (outs[0].shape[0] // owned)
    for number, out in enumerate(outs):
        for place in range(out.shape[0] // owned):
            taken = slice(place * rows, (place + 1) * rows)
            own = own_block(left_rows[number, taken], owned)
            product = dot_first(own, right_rows[number, taken].astype(jnp.bfloat16))
            out[place * owned : (place + 1) * owned] = product.astype(jnp.bfloat16).reshape(
                (owned,) + out.shape[1:]
            )


def halves_kernel(third, own, other):
    places = third.shape[0] // 2
    here = lax.axis_index("half")
    for out, group in ((own, here), (other, 1 - here)):
        taken = third[pl.ds(group * places, places)].astype(jnp.float32)
        out[...] = jnp.sum(taken, axis=0).astype(out.dtype)


def finish_kernel(groups, own, other, in_left, inputs, stats, fourth, ranks_out):
    owned, rank, width = in_left.shape
    summed = own[...] + other[...].astype(jnp.float32)
    ranks = summed[:, width:].astype(jnp.bfloat16).astype(jnp.float32)
    ranks_out[0] = ranks[:, :rank]
    ranks_out[1] = ranks[:, rank:]
    down = own_block(ranks[:, :rank], owned)
    grads = summed[:, :width] + dot_plain(down, in_left[...].reshape(owned * rank, width))
    grads = grads.astype(jnp.bfloat16).astype(jnp.float32)
    high, low = halves(jnp.sum(grads * inputs[...], axis=1, keepdims=True))
    lane = lax.broadcasted_iota(jnp.int32, stats.shape, 1)
    tail = jnp.where(lane == 4, high, jnp.where(lane == 5, low, stats[...]))
    block = jnp.concatenate([grads, tail], axis=1).astype(jnp.bfloat16)
    for group in range(groups):
        rows = block[group * owned : (group + 1) * owned]
        for place in range(fourth.shape[0] // groups):
            fourth[group * (fourth.shape[0] // groups) + place] = rows


def tokens_kernel(groups, fourth, fourth_other, tokens, router, logits, mixing, out_far, out, sent):
    blocks, owned, _ = fourth.shape
    chips = blocks // groups
    width = tokens.shape[1] // groups
    first_core = lax.axis_index("core") == 0

    def rows(half, columns):
        taken = []
        for chip in range(chips):
            own = fourth[half * chips + chip, :, columns].astype(jnp.float32)
            other = fourth_other[half * chips + chip, :, columns].astype(jnp.float32)
            taken.append(jnp.where(first_core, own, other))
            taken.append(jnp.where(first_core, other, own))
        return jnp.concatenate(taken, axis=0)

    grads = jnp.concatenate([rows(half, slice(0, width)) for half in range(groups)], axis=1)
    grads = grads.astype(jnp.bfloat16)
    stats = [rows(half, slice(width, width + STATS)) for half in range(groups)]
    peak = stats[0][:, 0:1] + stats[0][:, 1:2]
    total = stats[0][:, 2:3] + stats[0][:, 3:4]
    shift = functools.reduce(jnp.add, [part[:, 4:5] + part[:, 5:6] for part in stats])
    dispatch = jnp.exp(logits[...] - peak) / total
    weight_grad = dot_last(grads, tokens[...])
    logit_grad = dispatch * (weight_grad - shift) + mixing[...]
    left = jnp.concatenate([dispatch, logit_grad], axis=0).astype(jnp.bfloat16)
    right = jnp.concatenate([grads, router[...]], axis=0)
    parts = sent.shape[0]
    size = out.shape[0] // parts
    copies = []
    for part in range(parts):
        rows = slice(part * size, (part + 1) * size)
        out[rows] = dot_first(left[:, rows], right).astype(jnp.bfloat16)
        copy = pltpu.make_async_copy(out.at[rows], out_far.at[rows], sent.at[part])
        copy.start()
        copies.append(copy)
    for copy in copies:
        copy.wait()


def swap(blocks, axis):
    return lax.ppermute(blocks, axis, [(0, 1), (1, 0)])


def to_group(block, groups):
    chips = lax.axis_size("chip")
    beside = swap(block, "half")
    (blocks,) = call(
        pack_kernel,
        [array(block.dtype, groups, chips, *block.shape)],
        [block, beside],
        FLOPS_BESIDE_EXCHANGE,
    )
    blocks = blocks.reshape(groups * chips, *block.shape)
    blocks = lax.all_to_all(blocks, HALF_CORE, 0, 0, tiled=True)
    return blocks, swap(blocks, "core")


def call(kernel, outs, args, flops, space=pltpu.VMEM, scratch=()):
    size = sum(array.size * array.dtype.itemsize for array in args)
    size += sum(out.size * out.dtype.itemsize for out in outs)
    return pl.pallas_call(
        kernel,
        out_shape=outs,
        in_specs=[pl.BlockSpec(memory_space=pltpu.VMEM) for _ in args],
        out_specs=[pl.BlockSpec(memory_space=space) for _ in outs],
        scratch_shapes=scratch,
        cost_estimate=pl.CostEstimate(flops=flops, bytes_accessed=size, transcendentals=0),
        compiler_params=pltpu.CompilerParams(vmem_limit_bytes=24 * 2**20),
    )(*args)


def array(dtype, *shape):
    return jax.ShapeDtypeStruct(shape, dtype)


def local(
    tokens,
    cotangent,
    router,
    slot_outputs,
    base_in,
    base_out,
    in_left,
    in_right,
    out_left,
    out_right,
):
    groups, ring = lax.axis_size("dp"), lax.axis_size(SEQ)
    devices = groups * ring
    _, count, width = tokens.shape
    slots = router.shape[1]
    owned, slice_width, rank = in_left.shape
    members, _, hidden = in_right.shape
    rows = groups * owned
    if groups != 2 or ring % 4 or slice_width % 128 or rows % 8 or members % owned:
        return local_plain(
            tokens,
            cotangent,
            router,
            slot_outputs,
            base_in,
            base_out,
            in_left,
            in_right,
            out_left,
            out_right,
        )
    low, full = jnp.bfloat16, jnp.float32
    image_rows, cot_rows, saved = tokens[0], cotangent[0], slot_outputs[0]
    router, base_in = router.T, base_in.T
    in_left, out_left = in_left.swapaxes(1, 2), out_left.swapaxes(1, 2)
    (early,) = call(early_kernel, [array(full, 8, 128)], [], FLOPS_BESIDE_EXCHANGE)
    first = array(low, devices // 2, owned, 2 * slice_width + STATS)
    own, other, logits, combine = call(
        functools.partial(sums_kernel, owned, groups),
        [first, first, array(full, slots, count), array(full, slots, count)],
        [early, image_rows, cot_rows, router],
        6 * count * slots * width + FLOPS_BESIDE_EXCHANGE,
    )
    other = swap(other, "core")
    (first,) = call(
        functools.partial(merge_kernel, slice_width), [first], [own, other], FLOPS_BESIDE_EXCHANGE
    )
    first = lax.all_to_all(first, SAME_CORE, 0, 0, tiled=True)
    second, inputs, lows, stats = call(
        functools.partial(owner_kernel, groups),
        [
            array(low, rows, 2 * slice_width + 2 * rank),
            array(full, rows, slice_width),
            array(low, 2, rows, slice_width),
            array(full, rows, STATS),
        ],
        [first, in_left, out_right],
        4 * rows * owned * rank * slice_width,
    )
    second, second_other = to_group(second, groups)
    total_rows = groups * members
    third, pair, hidden_ranks = call(
        functools.partial(hidden_kernel, groups),
        [
            array(low, ring, rows, slice_width + 2 * rank),
            array(full, 2, total_rows, hidden),
            array(full, 2, total_rows, rank),
        ],
        [second, second_other, base_in, base_out, in_right, out_left],
        6 * total_rows * hidden * (width + owned * rank),
    )
    third = lax.all_to_all(third, HALF, 0, 0, tiled=True)
    own, other = call(
        halves_kernel,
        [array(kind, rows, slice_width + 2 * rank) for kind in (full, low)],
        [third],
        0,
    )
    other = swap(other, "half")
    fourth, ranks = call(
        functools.partial(finish_kernel, groups),
        [array(low, devices // 2, owned, slice_width + STATS), array(full, 2, rows, rank)],
        [own, other, in_left, inputs, stats],
        2 * rows * owned * rank * slice_width,
    )
    fourth, combine, pair, hidden_ranks = lax.optimization_barrier(
        (fourth, combine, pair, hidden_ranks)
    )
    fourth = lax.all_to_all(fourth, SAME_CORE, 0, 0, tiled=True)
    grad_in_right, grad_out_left = call(
        functools.partial(outer_kernel, owned),
        [array(low, members, rank, hidden)] * 2,
        [hidden_ranks, pair],
        4 * members * rank * hidden * rows,
    )
    (mixing,) = call(
        mixing_kernel,
        [array(full, slots, count)],
        [cot_rows, saved, combine],
        2 * count * slots * width,
    )
    grad_in_left, grad_out_right = call(
        functools.partial(outer_kernel, owned),
        [array(low, owned, rank, slice_width)] * 2,
        [ranks, lows],
        4 * owned * rank * slice_width * rows,
    )
    outs = (grad_in_left, grad_in_right, grad_out_left, grad_out_right)
    fourth, mixing, outs = lax.optimization_barrier((fourth, mixing, outs))
    grad_in_left, grad_in_right, grad_out_left, grad_out_right = outs
    parts = math.gcd(4, count // 16)
    (token_grad,) = call(
        functools.partial(tokens_kernel, groups),
        [array(low, count, width)],
        [fourth, swap(fourth, "core"), image_rows, router, logits, mixing],
        6 * count * slots * width,
        pltpu.HBM,
        [pltpu.VMEM((count, width), low), pltpu.SemaphoreType.DMA((parts,))],
    )
    return (
        token_grad[None],
        grad_in_left.swapaxes(1, 2),
        grad_in_right,
        grad_out_left.swapaxes(1, 2),
        grad_out_right,
    )


def solution(mesh):
    groups, ring = mesh.shape["dp"], mesh.shape["seq"]
    cores = math.gcd(2, ring // groups)
    split = mesh.devices.reshape(groups, groups, ring // groups // cores, cores)
    mesh = jax.sharding.Mesh(split, BOTH)
    in_specs = (
        P("dp", SEQ, None),
        P("dp", SEQ, None),
        P(),
        P("dp", None, None),
        P(None, SEQ),
        P(SEQ, None),
        P(SEQ, "dp", None),
        P("dp", None, SEQ),
        P("dp", SEQ, None),
        P(SEQ, None, "dp"),
    )
    out_specs = (
        P("dp", SEQ, None),
        P(SEQ, "dp", None),
        P("dp", None, SEQ),
        P("dp", SEQ, None),
        P(SEQ, None, "dp"),
    )
    return jax.shard_map(local, mesh=mesh, in_specs=in_specs, out_specs=out_specs, check_vma=False)
```

```python
import functools
import math

import jax
import jax.numpy as jnp
from jax import lax
from jax.experimental import pallas as pl
from jax.experimental.pallas import tpu as pltpu
from jax.sharding import PartitionSpec as P

PLACE = ("chip", "core")
SEQ = ("half", *PLACE)
BOTH = ("dp", *SEQ)
HALF = ("dp", *PLACE)
HALF_CORE = ("dp", "chip")
SAME_CORE = ("dp", "half", "chip")
STATS = 128
FLOPS_BESIDE_EXCHANGE = 10**10


def gelu_backward(preact, upstream):
    return jax.vjp(jax.nn.gelu, preact)[1](upstream)[0]


def dot_first(left, right):
    return lax.dot_general(
        left, right, (((0,), (0,)), ((), ())), preferred_element_type=jnp.float32
    )


def dot_last(left, right):
    return lax.dot_general(
        left, right, (((1,), (1,)), ((), ())), preferred_element_type=jnp.float32
    )


def split(value):
    high = lax.reduce_precision(value, 8, 7)
    low = lax.reduce_precision(value - high, 8, 7)
    return high.astype(jnp.bfloat16), low.astype(jnp.bfloat16)


def joined(high, low):
    return high.astype(jnp.float32) + low.astype(jnp.float32)


def exchange(blocks):
    flat = blocks.reshape((-1,) + blocks.shape[2:])
    return lax.all_to_all(flat, BOTH, 0, 0, tiled=True).reshape(blocks.shape)


def local_plain(
    tokens,
    cotangent,
    router,
    slot_outputs,
    base_in,
    base_out,
    in_left,
    in_right,
    out_left,
    out_right,
):
    groups, ring = lax.axis_size("dp"), lax.axis_size(SEQ)
    image_rows = tokens[0]
    cot_rows = cotangent[0]
    saved_outputs = slot_outputs[0]
    width = image_rows.shape[1]
    slots = router.shape[1]
    owned, slice_width, rank = in_left.shape
    members = in_right.shape[0]
    places = members // owned
    group, place = lax.axis_index("dp"), lax.axis_index(SEQ)

    logits = jnp.dot(image_rows, router, preferred_element_type=jnp.float32)
    peak_high, peak_low = split(jnp.max(logits, axis=0))
    near = jnp.exp(logits - joined(peak_high, peak_low))
    total_high, total_low = split(jnp.sum(near, axis=0))
    combine = jax.nn.softmax(logits, axis=1)
    sums = jnp.stack(
        [
            dot_first(near.astype(jnp.bfloat16), image_rows),
            dot_first(combine.astype(jnp.bfloat16), cot_rows),
        ],
        axis=1,
    ).astype(jnp.bfloat16)
    sums = sums.reshape(ring, owned, 2, groups, slice_width).transpose(3, 0, 1, 2, 4)
    sums = sums.reshape(groups, ring, owned, 2 * slice_width)
    stats = jnp.stack([peak_high, peak_low, total_high, total_low], axis=1)
    stats = jnp.pad(stats, ((0, 0), (0, STATS - 4))).reshape(1, ring, owned, STATS)
    stats = jnp.broadcast_to(stats, (groups, ring, owned, STATS))
    first = exchange(jnp.concatenate([sums, stats], axis=3))

    tail = 2 * slice_width
    peaks = joined(first[..., tail], first[..., tail + 1])
    totals = joined(first[..., tail + 2], first[..., tail + 3])
    peak = jnp.max(peaks, axis=1)
    near_scale = jnp.exp(peaks - peak[:, None])
    total = jnp.sum(near_scale * totals, axis=1)
    near_scale = near_scale / total[:, None]
    parts = first[..., :tail].astype(jnp.float32)
    slot_inputs = jnp.sum(parts[..., :slice_width] * near_scale[..., None], axis=1)
    inputs_own = slot_inputs.astype(jnp.bfloat16)
    grads_own = jnp.sum(parts[..., slice_width:], axis=1).astype(jnp.bfloat16)
    up_part = jnp.einsum("gjd,jdr->gjr", inputs_own, in_left, preferred_element_type=jnp.float32)
    back_part = jnp.einsum("gjd,jrd->gjr", grads_own, out_right, preferred_element_type=jnp.float32)
    second = jnp.concatenate(
        [inputs_own, grads_own, *split(up_part), *split(back_part)], axis=2
    )
    second = exchange(jnp.broadcast_to(second, (groups, ring) + second.shape))
    second = lax.dynamic_slice_in_dim(second, group * places, places, 1)

    def gathered(start):
        piece = second[..., start : start + slice_width]
        return piece.transpose(2, 1, 3, 0, 4).reshape(groups * members, width)

    def ranks(start):
        piece = joined(
            second[..., start : start + rank], second[..., start + rank : start + 2 * rank]
        )
        piece = jnp.sum(piece, axis=0).transpose(1, 0, 2, 3)
        return piece.reshape(groups, members, rank).astype(jnp.bfloat16)

    inputs_low, grads_low = gathered(0), gathered(slice_width)
    up_low, back_low = ranks(tail), ranks(tail + 2 * rank)
    hidden = base_in.shape[1]
    preact = jnp.dot(inputs_low, base_in, preferred_element_type=jnp.float32).reshape(
        groups, members, hidden
    ) + jnp.einsum("gjr,jrf->gjf", up_low, in_right, preferred_element_type=jnp.float32)
    hidden_low = jax.nn.gelu(preact).astype(jnp.bfloat16)
    hidden_grad = dot_last(grads_low, base_out).reshape(groups, members, hidden) + jnp.einsum(
        "gjr,jfr->gjf", back_low, out_left, preferred_element_type=jnp.float32
    )
    preact_grad = gelu_backward(preact, hidden_grad).astype(jnp.bfloat16)
    slot_term = dot_last(preact_grad.reshape(groups * members, hidden), base_in)
    down_term = jnp.einsum(
        "gjf,jrf->gjr", preact_grad, in_right, preferred_element_type=jnp.float32
    )
    value_term = jnp.einsum(
        "gjf,jfr->gjr", hidden_low, out_left, preferred_element_type=jnp.float32
    )
    slot_term = slot_term.astype(jnp.bfloat16).reshape(groups, places, owned, groups, slice_width)
    slot_term = slot_term.transpose(3, 1, 0, 2, 4)
    rank_term = jnp.concatenate([down_term, value_term], axis=2).astype(jnp.bfloat16)
    rank_term = rank_term.reshape(groups, places, owned, 2 * rank).transpose(1, 0, 2, 3)
    rank_term = jnp.broadcast_to(rank_term, (groups,) + rank_term.shape)
    third = jnp.concatenate([slot_term, rank_term], axis=4)
    third = lax.dynamic_update_slice_in_dim(
        jnp.zeros((groups, ring) + third.shape[2:], jnp.bfloat16), third, group * places, 1
    )
    third = exchange(third)
    third = lax.dynamic_index_in_dim(third, place // places, 0, keepdims=False)
    third = jnp.sum(third.astype(jnp.float32), axis=0)
    down_own = third[..., slice_width : slice_width + rank].astype(jnp.bfloat16)
    value_own = third[..., slice_width + rank :].astype(jnp.bfloat16)
    slot_grads_own = (
        third[..., :slice_width]
        + jnp.einsum("gjr,jdr->gjd", down_own, in_left, preferred_element_type=jnp.float32)
    ).astype(jnp.bfloat16)
    shift_part = jnp.sum(slot_grads_own.astype(jnp.float32) * slot_inputs, axis=2)
    stats = jnp.stack([*split(peak), *split(total), *split(shift_part)], axis=2)
    stats = jnp.pad(stats, ((0, 0), (0, 0), (0, STATS - 6)))
    fourth = jnp.concatenate([slot_grads_own, stats], axis=2)[:, None]
    fourth = exchange(jnp.broadcast_to(fourth, (groups, ring) + fourth.shape[2:]))
    slot_grads = fourth[..., :slice_width].transpose(1, 2, 0, 3).reshape(slots, width)
    stats = fourth[..., slice_width:].astype(jnp.float32).reshape(groups, slots, STATS)
    slot_peak = stats[0, :, 0] + stats[0, :, 1]
    slot_total = stats[0, :, 2] + stats[0, :, 3]
    shift_back = jnp.sum(stats[:, :, 4] + stats[:, :, 5], axis=0)

    dispatch = jnp.exp(logits - slot_peak) / slot_total
    dispatch_low = dispatch.astype(jnp.bfloat16)
    weight_grad = dot_last(image_rows, slot_grads)
    dispatch_logit = dispatch * (weight_grad - shift_back)
    mixing_grad = dot_last(cot_rows, saved_outputs)
    combine_logit = combine * (mixing_grad - jnp.sum(combine * mixing_grad, axis=1, keepdims=True))
    logit_grad = (dispatch_logit + combine_logit).astype(jnp.bfloat16)
    token_grad = (
        jnp.dot(dispatch_low, slot_grads, preferred_element_type=jnp.float32)
        + dot_last(logit_grad, router)
    ).astype(jnp.bfloat16)
    grad_in_right = jnp.einsum(
        "gjr,gjf->jrf", up_low, preact_grad, preferred_element_type=jnp.float32
    ).astype(jnp.bfloat16)
    grad_out_left = jnp.einsum(
        "gjf,gjr->jfr", hidden_low, back_low, preferred_element_type=jnp.float32
    ).astype(jnp.bfloat16)
    grad_in_left = jnp.einsum(
        "gjd,gjr->jdr", inputs_own, down_own, preferred_element_type=jnp.float32
    ).astype(jnp.bfloat16)
    grad_out_right = jnp.einsum(
        "gjr,gjd->jrd", value_own, grads_own, preferred_element_type=jnp.float32
    ).astype(jnp.bfloat16)
    return (token_grad[None], grad_in_left, grad_in_right, grad_out_left, grad_out_right)


def dot_turned(left, right):
    return dot_last(right, left).T


def dot_plain(left, right):
    return jnp.dot(left, right, preferred_element_type=jnp.float32)


def halves(value):
    high = value.astype(jnp.bfloat16).astype(jnp.float32)
    low = (value - high).astype(jnp.bfloat16).astype(jnp.float32)
    return high, low


def in_lanes(columns, shape):
    lane = lax.broadcasted_iota(jnp.int32, shape, len(shape) - 1)
    out = jnp.zeros(shape, jnp.float32)
    for number, column in enumerate(columns):
        out = jnp.where(lane == number, column, out)
    return out


def own_block(value, owned):
    rows, rank = value.shape
    wide = jnp.concatenate([value] * owned, axis=1)
    shape = (rows, owned * rank)
    block = lax.broadcasted_iota(jnp.int32, shape, 1) // rank
    expert = lax.broadcasted_iota(jnp.int32, shape, 0) % owned
    return jnp.where(block == expert, wide, 0.0).astype(jnp.bfloat16)


def from_own_block(value, owned):
    rows, wide = value.shape
    rank = wide // owned
    block = lax.broadcasted_iota(jnp.int32, value.shape, 1) // rank
    expert = lax.broadcasted_iota(jnp.int32, value.shape, 0) % owned
    kept = jnp.where(block == expert, value, 0.0)
    out = kept[:, :rank]
    for number in range(1, owned):
        out = out + kept[:, number * rank : (number + 1) * rank]
    return out


def early_kernel(out):
    out[...] = jnp.zeros(out.shape, out.dtype)


def sums_kernel(
    owned, groups, _, tokens, cotangent, router, own, other, logits_out, combine_out
):
    chips = own.shape[0] // groups
    core = lax.axis_index("core")
    image_rows = tokens[...]
    logits = dot_last(router[...], image_rows)
    high, low = halves(jnp.max(logits, axis=1, keepdims=True))
    near = jnp.exp(logits - (high + low))
    total_high, total_low = halves(jnp.sum(near, axis=1, keepdims=True))
    spread = jnp.exp(logits - jnp.max(logits, axis=0, keepdims=True))
    combine = spread / jnp.sum(spread, axis=0, keepdims=True)
    logits_out[...] = logits
    combine_out[...] = combine
    stats = in_lanes([high, low, total_high, total_low], (logits.shape[0], STATS))
    stats = stats.astype(jnp.bfloat16)
    inputs = dot_plain(near.astype(jnp.bfloat16), image_rows).astype(jnp.bfloat16)
    grads = dot_plain(combine.astype(jnp.bfloat16), cotangent[...]).astype(jnp.bfloat16)
    width = inputs.shape[1] // groups

    def block(rows, columns):
        return jnp.concatenate([inputs[rows, columns], grads[rows, columns], stats[rows]], axis=1)

    for group in range(groups):
        columns = slice(group * width, (group + 1) * width)
        for chip in range(chips):
            start = 2 * chip * owned
            even = block(slice(start, start + owned), columns)
            odd = block(slice(start + owned, start + 2 * owned), columns)
            own[group * chips + chip] = jnp.where(core == 0, even, odd)
            other[group * chips + chip] = jnp.where(core == 0, odd, even)


def merge_kernel(width, own, other, out):
    parts = []
    for part in (own, other):
        stats = part[:, :, 2 * width :].astype(jnp.float32)
        parts.append((stats[:, :, 0:1] + stats[:, :, 1:2], stats[:, :, 2:3] + stats[:, :, 3:4]))
    peak = jnp.maximum(parts[0][0], parts[1][0])
    scales = [jnp.exp(part[0] - peak) for part in parts]
    total = scales[0] * parts[0][1] + scales[1] * parts[1][1]
    stats = in_lanes([*halves(peak), *halves(total)], own.shape[:2] + (STATS,))
    inputs = [
        part[:, :, :width].astype(jnp.float32) * scale
        for part, scale in zip((own, other), scales, strict=True)
    ]
    grads = [part[:, :, width : 2 * width].astype(jnp.float32) for part in (own, other)]
    out[:, :, :width] = (inputs[0] + inputs[1]).astype(jnp.bfloat16)
    out[:, :, width : 2 * width] = (grads[0] + grads[1]).astype(jnp.bfloat16)
    out[:, :, 2 * width :] = stats.astype(jnp.bfloat16)


def mixing_kernel(cotangent, saved, combine, out):
    mixing = dot_last(saved[...], cotangent[...])
    weights = combine[...]
    out[...] = weights * (mixing - jnp.sum(weights * mixing, axis=0, keepdims=True))


def owner_kernel(groups, first, in_left, out_right, second, inputs_out, lows_out, stats_out):
    ring = first.shape[0] // groups
    owned, rank, width = in_left.shape
    inputs, grads, stats_rows = [], [], []
    for group in range(groups):
        rows = slice(group * ring, (group + 1) * ring)
        stats = first[rows, :, 2 * width :].astype(jnp.float32)
        peaks = stats[:, :, 0:1] + stats[:, :, 1:2]
        totals = stats[:, :, 2:3] + stats[:, :, 3:4]
        peak = jnp.max(peaks, axis=0)
        scale = jnp.exp(peaks - peak[None])
        total = jnp.sum(scale * totals, axis=0)
        scale = scale / total[None]
        inputs.append(jnp.sum(first[rows, :, :width].astype(jnp.float32) * scale, axis=0))
        grads.append(jnp.sum(first[rows, :, width : 2 * width].astype(jnp.float32), axis=0))
        stats_rows.append(in_lanes([*halves(peak), *halves(total)], (owned, STATS)))
    inputs, grads = jnp.concatenate(inputs, axis=0), jnp.concatenate(grads, axis=0)
    inputs_out[...] = inputs
    stats_out[...] = jnp.concatenate(stats_rows, axis=0)
    inputs_low, grads_low = inputs.astype(jnp.bfloat16), grads.astype(jnp.bfloat16)
    lows_out[0] = inputs_low
    lows_out[1] = grads_low
    up = dot_last(inputs_low, in_left[...].reshape(owned * rank, width))
    back = dot_last(grads_low, out_right[...].reshape(owned * rank, width))
    ranks = [from_own_block(up, owned), from_own_block(back, owned)]
    ranks = jnp.concatenate(ranks, axis=1).astype(jnp.bfloat16)
    block = jnp.concatenate([inputs_low, grads_low, ranks], axis=1)
    second[...] = block


def pack_kernel(own, beside, out):
    here = lax.axis_index("half")
    for group in range(out.shape[0]):
        block = jnp.where(here == group, own[...], beside[...])
        for place in range(out.shape[1]):
            out[group, place] = block


def factor_products(blocks, in_right, out_left, core):
    members, rank, hidden = in_right.shape
    rows = blocks.shape[1]
    chips = blocks.shape[0] // 2
    owned = members // (2 * chips)
    start = blocks.shape[2] - 2 * rank
    ranks = jnp.zeros((chips * rows, 2 * rank), jnp.float32)
    for half in range(2):
        part = blocks[half * chips : (half + 1) * chips, :, start:].astype(jnp.float32)
        ranks = ranks + part.reshape(ranks.shape)
    out = []
    for number, table in enumerate((in_right, out_left)):
        value = ranks[:, number * rank : (number + 1) * rank]
        value = value.astype(jnp.bfloat16).astype(jnp.float32)
        taken = []
        for chip in range(chips):
            own = own_block(value[chip * rows : (chip + 1) * rows], owned)
            part = table[pl.ds((2 * chip + core) * owned, owned)].reshape(owned * rank, hidden)
            taken.append(dot_plain(own, part))
        out.append((value, jnp.concatenate(taken, axis=0)))
    return out


def near_kernel(second, in_right, out_left, ranks_out, products_out):
    found = factor_products(second, in_right, out_left, lax.axis_index("core"))
    for number, (value, product) in enumerate(found):
        ranks_out[number] = value
        products_out[number] = product


def hidden_kernel(
    groups,
    second,
    second_other,
    near_ranks,
    near_products,
    base_in,
    base_out,
    in_right,
    out_left,
    third,
    pair_out,
    ranks_out,
):
    first_core = lax.axis_index("core") == 0
    members, rank, hidden = in_right.shape
    rows = second.shape[1]
    owned = rows // groups
    places = members // owned
    width = base_in.shape[1] // groups

    def gathered(columns):
        parts = []
        for half in range(groups):
            taken = []
            for chip in range(places // 2):
                block = half * (places // 2) + chip
                own = second[block, :, columns].astype(jnp.float32)
                other = second_other[block, :, columns].astype(jnp.float32)
                taken.append(jnp.where(first_core, own, other))
                taken.append(jnp.where(first_core, other, own))
            parts.append(jnp.concatenate(taken, axis=0))
        return parts

    def in_order(near, far):
        taken = []
        for chip in range(places // 2):
            own = near[chip * rows : (chip + 1) * rows]
            other = far[chip * rows : (chip + 1) * rows]
            taken.append(jnp.where(first_core, own, other))
            taken.append(jnp.where(first_core, other, own))
        return jnp.concatenate(taken, axis=0)

    def to_rank(value, table):
        taken = []
        for place in range(places):
            part = table[place * owned : (place + 1) * owned].reshape(owned * rank, hidden)
            wide = dot_last(value[place * rows : (place + 1) * rows].astype(jnp.bfloat16), part)
            taken.append(from_own_block(wide, owned))
        return jnp.concatenate(taken, axis=0)

    far = factor_products(second_other, in_right, out_left, 1 - lax.axis_index("core"))
    up, back = [in_order(near_ranks[number], far[number][0]) for number in range(2)]
    preact, hidden_grad = [in_order(near_products[number], far[number][1]) for number in range(2)]
    for half, part in enumerate(gathered(slice(0, width))):
        columns = slice(half * width, (half + 1) * width)
        preact = preact + dot_turned(part.astype(jnp.bfloat16), base_in[:, columns])
    for half, part in enumerate(gathered(slice(width, 2 * width))):
        columns = slice(half * width, (half + 1) * width)
        hidden_grad = hidden_grad + dot_turned(part.astype(jnp.bfloat16), base_out[:, columns])
    root = 0.7978845608028654
    bent = jnp.tanh(root * (preact + 0.044715 * (preact * preact * preact)))
    hidden_value = 0.5 * preact * (1.0 + bent)
    slope = 0.5 * (1.0 + bent) + 0.5 * preact * (1.0 - bent * bent) * (
        root * (1.0 + 3.0 * 0.044715 * (preact * preact))
    )
    hidden_low = hidden_value.astype(jnp.bfloat16).astype(jnp.float32)
    preact_grad = (hidden_grad * slope).astype(jnp.bfloat16).astype(jnp.float32)
    pair_out[0] = preact_grad
    pair_out[1] = hidden_low
    ranks_out[0] = up
    ranks_out[1] = back
    slot_term = dot_plain(preact_grad.astype(jnp.bfloat16), base_in[...]).astype(jnp.bfloat16)
    down = to_rank(preact_grad, in_right)
    value = to_rank(hidden_low, out_left)
    ranks = jnp.concatenate([down, value], axis=1).astype(jnp.bfloat16)
    for half in range(groups):
        columns = slice(half * width, (half + 1) * width)
        for place in range(places):
            taken = slice(place * rows, (place + 1) * rows)
            block = half * places + place
            third[block, :, :width] = slot_term[taken, columns]
            third[block, :, width:] = ranks[taken]


def outer_kernel(owned, left_rows, right_rows, *outs):
    rows = left_rows.shape[1] // (outs[0].shape[0] // owned)
    for number, out in enumerate(outs):
        for place in range(out.shape[0] // owned):
            taken = slice(place * rows, (place + 1) * rows)
            own = own_block(left_rows[number, taken], owned)
            product = dot_first(own, right_rows[number, taken].astype(jnp.bfloat16))
            out[place * owned : (place + 1) * owned] = product.astype(jnp.bfloat16).reshape(
                (owned,) + out.shape[1:]
            )


def halves_kernel(third, own, other):
    places = third.shape[0] // 2
    here = lax.axis_index("half")
    for out, group in ((own, here), (other, 1 - here)):
        taken = third[pl.ds(group * places, places)].astype(jnp.float32)
        out[...] = jnp.sum(taken, axis=0).astype(out.dtype)


def finish_kernel(groups, own, other, in_left, inputs, stats, fourth, ranks_out):
    owned, rank, width = in_left.shape
    summed = own[...] + other[...].astype(jnp.float32)
    ranks = summed[:, width:].astype(jnp.bfloat16).astype(jnp.float32)
    ranks_out[0] = ranks[:, :rank]
    ranks_out[1] = ranks[:, rank:]
    down = own_block(ranks[:, :rank], owned)
    grads = summed[:, :width] + dot_plain(down, in_left[...].reshape(owned * rank, width))
    grads = grads.astype(jnp.bfloat16).astype(jnp.float32)
    high, low = halves(jnp.sum(grads * inputs[...], axis=1, keepdims=True))
    lane = lax.broadcasted_iota(jnp.int32, stats.shape, 1)
    tail = jnp.where(lane == 4, high, jnp.where(lane == 5, low, stats[...]))
    block = jnp.concatenate([grads, tail], axis=1).astype(jnp.bfloat16)
    for group in range(groups):
        rows = block[group * owned : (group + 1) * owned]
        for place in range(fourth.shape[0] // groups):
            fourth[group * (fourth.shape[0] // groups) + place] = rows


def tokens_kernel(
    groups,
    fourth,
    fourth_other,
    tokens,
    router,
    logits,
    mixing,
    grad_left,
    grad_right,
    out_far,
    grad_left_far,
    grad_right_far,
    out,
    sent,
    grads_sent,
):
    copies = [
        pltpu.make_async_copy(grad_left, grad_left_far, grads_sent.at[0]),
        pltpu.make_async_copy(grad_right, grad_right_far, grads_sent.at[1]),
    ]
    for copy in copies:
        copy.start()
    blocks, owned, _ = fourth.shape
    chips = blocks // groups
    width = tokens.shape[1] // groups
    first_core = lax.axis_index("core") == 0

    def rows(half, columns):
        taken = []
        for chip in range(chips):
            own = fourth[half * chips + chip, :, columns].astype(jnp.float32)
            other = fourth_other[half * chips + chip, :, columns].astype(jnp.float32)
            taken.append(jnp.where(first_core, own, other))
            taken.append(jnp.where(first_core, other, own))
        return jnp.concatenate(taken, axis=0)

    grads = jnp.concatenate([rows(half, slice(0, width)) for half in range(groups)], axis=1)
    grads = grads.astype(jnp.bfloat16)
    stats = [rows(half, slice(width, width + STATS)) for half in range(groups)]
    peak = stats[0][:, 0:1] + stats[0][:, 1:2]
    total = stats[0][:, 2:3] + stats[0][:, 3:4]
    shift = functools.reduce(jnp.add, [part[:, 4:5] + part[:, 5:6] for part in stats])
    dispatch = jnp.exp(logits[...] - peak) / total
    weight_grad = dot_last(grads, tokens[...])
    logit_grad = dispatch * (weight_grad - shift) + mixing[...]
    left = jnp.concatenate([dispatch, logit_grad], axis=0).T.astype(jnp.bfloat16)
    right = jnp.concatenate([grads, router[...]], axis=0)
    parts = sent.shape[0]
    size = out.shape[1] // parts
    for part in range(parts):
        columns = slice(part * size, (part + 1) * size)
        out[:, columns] = dot_plain(left, right[:, columns]).astype(jnp.bfloat16)
        copy = pltpu.make_async_copy(
            out.at[:, columns], out_far.at[:, columns], sent.at[part]
        )
        copy.start()
        copies.append(copy)
    for copy in copies:
        copy.wait()


def swap(blocks, axis):
    return lax.ppermute(blocks, axis, [(0, 1), (1, 0)])


def to_group(block, beside, groups):
    chips = lax.axis_size("chip")
    (blocks,) = call(
        pack_kernel,
        [array(block.dtype, groups, chips, *block.shape)],
        [block, beside],
        FLOPS_BESIDE_EXCHANGE,
    )
    blocks = blocks.reshape(groups * chips, *block.shape)
    blocks = lax.all_to_all(blocks, HALF_CORE, 0, 0, tiled=True)
    return blocks, swap(blocks, "core")


def call(kernel, outs, args, flops, space=pltpu.VMEM, scratch=(), size=None):
    if size is None:
        size = sum(array.size * array.dtype.itemsize for array in (*args, *outs))
    return pl.pallas_call(
        kernel,
        out_shape=outs,
        in_specs=[pl.BlockSpec(memory_space=pltpu.VMEM) for _ in args],
        out_specs=[pl.BlockSpec(memory_space=space) for _ in outs],
        scratch_shapes=scratch,
        cost_estimate=pl.CostEstimate(flops=flops, bytes_accessed=size, transcendentals=0),
        compiler_params=pltpu.CompilerParams(vmem_limit_bytes=24 * 2**20),
    )(*args)


def array(dtype, *shape):
    return jax.ShapeDtypeStruct(shape, dtype)


def local(
    tokens,
    cotangent,
    router,
    slot_outputs,
    base_in,
    base_out,
    in_left,
    in_right,
    out_left,
    out_right,
):
    groups, ring = lax.axis_size("dp"), lax.axis_size(SEQ)
    devices = groups * ring
    _, count, width = tokens.shape
    slots = router.shape[1]
    owned, slice_width, rank = in_left.shape
    members, _, hidden = in_right.shape
    rows = groups * owned
    if groups != 2 or ring % 4 or slice_width % 128 or rows % 8 or members % owned:
        return local_plain(
            tokens,
            cotangent,
            router,
            slot_outputs,
            base_in,
            base_out,
            in_left,
            in_right,
            out_left,
            out_right,
        )
    low, full = jnp.bfloat16, jnp.float32
    image_rows, cot_rows, saved = tokens[0], cotangent[0], slot_outputs[0]
    router, base_in = router.T, base_in.T
    in_left, out_left = in_left.swapaxes(1, 2), out_left.swapaxes(1, 2)
    (early,) = call(early_kernel, [array(full, 8, 128)], [], FLOPS_BESIDE_EXCHANGE)
    first = array(low, devices // 2, owned, 2 * slice_width + STATS)
    own, other, logits, combine = call(
        functools.partial(sums_kernel, owned, groups),
        [first, first, array(full, slots, count), array(full, slots, count)],
        [early, image_rows, cot_rows, router],
        6 * count * slots * width + FLOPS_BESIDE_EXCHANGE,
    )
    other = swap(other, "core")
    (first,) = call(
        functools.partial(merge_kernel, slice_width), [first], [own, other], FLOPS_BESIDE_EXCHANGE
    )
    first = lax.all_to_all(first, SAME_CORE, 0, 0, tiled=True)
    second, inputs, lows, stats = call(
        functools.partial(owner_kernel, groups),
        [
            array(low, rows, 2 * slice_width + 2 * rank),
            array(full, rows, slice_width),
            array(low, 2, rows, slice_width),
            array(full, rows, STATS),
        ],
        [first, in_left, out_right],
        4 * rows * owned * rank * slice_width,
    )
    second, combine = lax.optimization_barrier((second, combine))
    beside = swap(second, "half")
    (mixing,) = call(
        mixing_kernel,
        [array(full, slots, count)],
        [cot_rows, saved, combine],
        2 * count * slots * width,
    )
    beside, mixing = lax.optimization_barrier((beside, mixing))
    second, second_other = to_group(second, beside, groups)
    total_rows = groups * members
    near_ranks, near_products = call(
        near_kernel,
        [array(full, 2, total_rows // 2, rank), array(full, 2, total_rows // 2, hidden)],
        [second, in_right, out_left],
        2 * total_rows * owned * rank * hidden,
        size=0,
    )
    third, pair, hidden_ranks = call(
        functools.partial(hidden_kernel, groups),
        [
            array(low, ring, rows, slice_width + 2 * rank),
            array(full, 2, total_rows, hidden),
            array(full, 2, total_rows, rank),
        ],
        [
            second,
            second_other,
            near_ranks,
            near_products,
            base_in,
            base_out,
            in_right,
            out_left,
        ],
        6 * total_rows * hidden * (width + owned * rank),
    )
    third = lax.all_to_all(third, HALF, 0, 0, tiled=True)
    own, other = call(
        halves_kernel,
        [array(kind, rows, slice_width + 2 * rank) for kind in (full, low)],
        [third],
        0,
    )
    other, pair, hidden_ranks = lax.optimization_barrier((other, pair, hidden_ranks))
    other = swap(other, "half")
    grad_in_right, grad_out_left = call(
        functools.partial(outer_kernel, owned),
        [array(low, members, rank, hidden)] * 2,
        [hidden_ranks, pair],
        4 * members * rank * hidden * rows,
    )
    other, grad_in_right, grad_out_left = lax.optimization_barrier(
        (other, grad_in_right, grad_out_left)
    )
    fourth, ranks = call(
        functools.partial(finish_kernel, groups),
        [array(low, devices // 2, owned, slice_width + STATS), array(full, 2, rows, rank)],
        [own, other, in_left, inputs, stats],
        2 * rows * owned * rank * slice_width,
    )
    fourth = lax.all_to_all(fourth, SAME_CORE, 0, 0, tiled=True)
    fourth, ranks = lax.optimization_barrier((fourth, ranks))
    fourth_other = swap(fourth, "core")
    grad_in_left, grad_out_right = call(
        functools.partial(outer_kernel, owned),
        [array(low, owned, rank, slice_width)] * 2,
        [ranks, lows],
        4 * owned * rank * slice_width * rows,
    )
    fourth_other, grad_in_left, grad_out_right = lax.optimization_barrier(
        (fourth_other, grad_in_left, grad_out_right)
    )
    parts = width // 256 if width % 256 == 0 else 1
    token_grad, grad_in_left, grad_out_right = call(
        functools.partial(tokens_kernel, groups),
        [array(low, count, width)] + [array(low, owned, rank, slice_width)] * 2,
        [
            fourth,
            fourth_other,
            image_rows,
            router,
            logits,
            mixing,
            grad_in_left,
            grad_out_right,
        ],
        6 * count * slots * width,
        pltpu.HBM,
        [
            pltpu.VMEM((count, width), low),
            pltpu.SemaphoreType.DMA((parts,)),
            pltpu.SemaphoreType.DMA((2,)),
        ],
    )
    return (
        token_grad[None],
        grad_in_left.swapaxes(1, 2),
        grad_in_right,
        grad_out_left.swapaxes(1, 2),
        grad_out_right,
    )


def solution(mesh):
    groups, ring = mesh.shape["dp"], mesh.shape["seq"]
    cores = math.gcd(2, ring // groups)
    split = mesh.devices.reshape(groups, groups, ring // groups // cores, cores)
    mesh = jax.sharding.Mesh(split, BOTH)
    in_specs = (
        P("dp", SEQ, None),
        P("dp", SEQ, None),
        P(),
        P("dp", None, None),
        P(None, SEQ),
        P(SEQ, None),
        P(SEQ, "dp", None),
        P("dp", None, SEQ),
        P("dp", SEQ, None),
        P(SEQ, None, "dp"),
    )
    out_specs = (
        P("dp", SEQ, None),
        P(SEQ, "dp", None),
        P("dp", None, SEQ),
        P("dp", SEQ, None),
        P(SEQ, None, "dp"),
    )
    return jax.shard_map(local, mesh=mesh, in_specs=in_specs, out_specs=out_specs, check_vma=False)
```

```python
import functools
import math

import jax
import jax.numpy as jnp
from jax import lax
from jax.experimental import pallas as pl
from jax.experimental.pallas import tpu as pltpu
from jax.sharding import PartitionSpec as P

PLACE = ("chip", "core")
SEQ = ("half", *PLACE)
BOTH = ("dp", *SEQ)
HALF = ("dp", *PLACE)
HALF_CORE = ("dp", "chip")
SAME_CORE = ("dp", "half", "chip")
STATS = 128
FLOPS_BESIDE_EXCHANGE = 10**10


def gelu_backward(preact, upstream):
    return jax.vjp(jax.nn.gelu, preact)[1](upstream)[0]


def dot_first(left, right):
    return lax.dot_general(
        left, right, (((0,), (0,)), ((), ())), preferred_element_type=jnp.float32
    )


def dot_last(left, right):
    return lax.dot_general(
        left, right, (((1,), (1,)), ((), ())), preferred_element_type=jnp.float32
    )


def split(value):
    high = lax.reduce_precision(value, 8, 7)
    low = lax.reduce_precision(value - high, 8, 7)
    return high.astype(jnp.bfloat16), low.astype(jnp.bfloat16)


def joined(high, low):
    return high.astype(jnp.float32) + low.astype(jnp.float32)


def exchange(blocks):
    flat = blocks.reshape((-1,) + blocks.shape[2:])
    return lax.all_to_all(flat, BOTH, 0, 0, tiled=True).reshape(blocks.shape)


def local_plain(
    tokens,
    cotangent,
    router,
    slot_outputs,
    base_in,
    base_out,
    in_left,
    in_right,
    out_left,
    out_right,
):
    groups, ring = lax.axis_size("dp"), lax.axis_size(SEQ)
    image_rows = tokens[0]
    cot_rows = cotangent[0]
    saved_outputs = slot_outputs[0]
    width = image_rows.shape[1]
    slots = router.shape[1]
    owned, slice_width, rank = in_left.shape
    members = in_right.shape[0]
    places = members // owned
    group, place = lax.axis_index("dp"), lax.axis_index(SEQ)

    logits = jnp.dot(image_rows, router, preferred_element_type=jnp.float32)
    peak_high, peak_low = split(jnp.max(logits, axis=0))
    near = jnp.exp(logits - joined(peak_high, peak_low))
    total_high, total_low = split(jnp.sum(near, axis=0))
    combine = jax.nn.softmax(logits, axis=1)
    sums = jnp.stack(
        [
            dot_first(near.astype(jnp.bfloat16), image_rows),
            dot_first(combine.astype(jnp.bfloat16), cot_rows),
        ],
        axis=1,
    ).astype(jnp.bfloat16)
    sums = sums.reshape(ring, owned, 2, groups, slice_width).transpose(3, 0, 1, 2, 4)
    sums = sums.reshape(groups, ring, owned, 2 * slice_width)
    stats = jnp.stack([peak_high, peak_low, total_high, total_low], axis=1)
    stats = jnp.pad(stats, ((0, 0), (0, STATS - 4))).reshape(1, ring, owned, STATS)
    stats = jnp.broadcast_to(stats, (groups, ring, owned, STATS))
    first = exchange(jnp.concatenate([sums, stats], axis=3))

    tail = 2 * slice_width
    peaks = joined(first[..., tail], first[..., tail + 1])
    totals = joined(first[..., tail + 2], first[..., tail + 3])
    peak = jnp.max(peaks, axis=1)
    near_scale = jnp.exp(peaks - peak[:, None])
    total = jnp.sum(near_scale * totals, axis=1)
    near_scale = near_scale / total[:, None]
    parts = first[..., :tail].astype(jnp.float32)
    slot_inputs = jnp.sum(parts[..., :slice_width] * near_scale[..., None], axis=1)
    inputs_own = slot_inputs.astype(jnp.bfloat16)
    grads_own = jnp.sum(parts[..., slice_width:], axis=1).astype(jnp.bfloat16)
    up_part = jnp.einsum("gjd,jdr->gjr", inputs_own, in_left, preferred_element_type=jnp.float32)
    back_part = jnp.einsum("gjd,jrd->gjr", grads_own, out_right, preferred_element_type=jnp.float32)
    second = jnp.concatenate(
        [inputs_own, grads_own, *split(up_part), *split(back_part)], axis=2
    )
    second = exchange(jnp.broadcast_to(second, (groups, ring) + second.shape))
    second = lax.dynamic_slice_in_dim(second, group * places, places, 1)

    def gathered(start):
        piece = second[..., start : start + slice_width]
        return piece.transpose(2, 1, 3, 0, 4).reshape(groups * members, width)

    def ranks(start):
        piece = joined(
            second[..., start : start + rank], second[..., start + rank : start + 2 * rank]
        )
        piece = jnp.sum(piece, axis=0).transpose(1, 0, 2, 3)
        return piece.reshape(groups, members, rank).astype(jnp.bfloat16)

    inputs_low, grads_low = gathered(0), gathered(slice_width)
    up_low, back_low = ranks(tail), ranks(tail + 2 * rank)
    hidden = base_in.shape[1]
    preact = jnp.dot(inputs_low, base_in, preferred_element_type=jnp.float32).reshape(
        groups, members, hidden
    ) + jnp.einsum("gjr,jrf->gjf", up_low, in_right, preferred_element_type=jnp.float32)
    hidden_low = jax.nn.gelu(preact).astype(jnp.bfloat16)
    hidden_grad = dot_last(grads_low, base_out).reshape(groups, members, hidden) + jnp.einsum(
        "gjr,jfr->gjf", back_low, out_left, preferred_element_type=jnp.float32
    )
    preact_grad = gelu_backward(preact, hidden_grad).astype(jnp.bfloat16)
    slot_term = dot_last(preact_grad.reshape(groups * members, hidden), base_in)
    down_term = jnp.einsum(
        "gjf,jrf->gjr", preact_grad, in_right, preferred_element_type=jnp.float32
    )
    value_term = jnp.einsum(
        "gjf,jfr->gjr", hidden_low, out_left, preferred_element_type=jnp.float32
    )
    slot_term = slot_term.astype(jnp.bfloat16).reshape(groups, places, owned, groups, slice_width)
    slot_term = slot_term.transpose(3, 1, 0, 2, 4)
    rank_term = jnp.concatenate([down_term, value_term], axis=2).astype(jnp.bfloat16)
    rank_term = rank_term.reshape(groups, places, owned, 2 * rank).transpose(1, 0, 2, 3)
    rank_term = jnp.broadcast_to(rank_term, (groups,) + rank_term.shape)
    third = jnp.concatenate([slot_term, rank_term], axis=4)
    third = lax.dynamic_update_slice_in_dim(
        jnp.zeros((groups, ring) + third.shape[2:], jnp.bfloat16), third, group * places, 1
    )
    third = exchange(third)
    third = lax.dynamic_index_in_dim(third, place // places, 0, keepdims=False)
    third = jnp.sum(third.astype(jnp.float32), axis=0)
    down_own = third[..., slice_width : slice_width + rank].astype(jnp.bfloat16)
    value_own = third[..., slice_width + rank :].astype(jnp.bfloat16)
    slot_grads_own = (
        third[..., :slice_width]
        + jnp.einsum("gjr,jdr->gjd", down_own, in_left, preferred_element_type=jnp.float32)
    ).astype(jnp.bfloat16)
    shift_part = jnp.sum(slot_grads_own.astype(jnp.float32) * slot_inputs, axis=2)
    stats = jnp.stack([*split(peak), *split(total), *split(shift_part)], axis=2)
    stats = jnp.pad(stats, ((0, 0), (0, 0), (0, STATS - 6)))
    fourth = jnp.concatenate([slot_grads_own, stats], axis=2)[:, None]
    fourth = exchange(jnp.broadcast_to(fourth, (groups, ring) + fourth.shape[2:]))
    slot_grads = fourth[..., :slice_width].transpose(1, 2, 0, 3).reshape(slots, width)
    stats = fourth[..., slice_width:].astype(jnp.float32).reshape(groups, slots, STATS)
    slot_peak = stats[0, :, 0] + stats[0, :, 1]
    slot_total = stats[0, :, 2] + stats[0, :, 3]
    shift_back = jnp.sum(stats[:, :, 4] + stats[:, :, 5], axis=0)

    dispatch = jnp.exp(logits - slot_peak) / slot_total
    dispatch_low = dispatch.astype(jnp.bfloat16)
    weight_grad = dot_last(image_rows, slot_grads)
    dispatch_logit = dispatch * (weight_grad - shift_back)
    mixing_grad = dot_last(cot_rows, saved_outputs)
    combine_logit = combine * (mixing_grad - jnp.sum(combine * mixing_grad, axis=1, keepdims=True))
    logit_grad = (dispatch_logit + combine_logit).astype(jnp.bfloat16)
    token_grad = (
        jnp.dot(dispatch_low, slot_grads, preferred_element_type=jnp.float32)
        + dot_last(logit_grad, router)
    ).astype(jnp.bfloat16)
    grad_in_right = jnp.einsum(
        "gjr,gjf->jrf", up_low, preact_grad, preferred_element_type=jnp.float32
    ).astype(jnp.bfloat16)
    grad_out_left = jnp.einsum(
        "gjf,gjr->jfr", hidden_low, back_low, preferred_element_type=jnp.float32
    ).astype(jnp.bfloat16)
    grad_in_left = jnp.einsum(
        "gjd,gjr->jdr", inputs_own, down_own, preferred_element_type=jnp.float32
    ).astype(jnp.bfloat16)
    grad_out_right = jnp.einsum(
        "gjr,gjd->jrd", value_own, grads_own, preferred_element_type=jnp.float32
    ).astype(jnp.bfloat16)
    return (token_grad[None], grad_in_left, grad_in_right, grad_out_left, grad_out_right)


def dot_turned(left, right):
    return dot_last(right, left).T


def dot_plain(left, right):
    return jnp.dot(left, right, preferred_element_type=jnp.float32)


def halves(value):
    high = value.astype(jnp.bfloat16).astype(jnp.float32)
    low = (value - high).astype(jnp.bfloat16).astype(jnp.float32)
    return high, low


def in_lanes(columns, shape):
    lane = lax.broadcasted_iota(jnp.int32, shape, len(shape) - 1)
    out = jnp.zeros(shape, jnp.float32)
    for number, column in enumerate(columns):
        out = jnp.where(lane == number, column, out)
    return out


def own_block(value, owned):
    rows, rank = value.shape
    wide = jnp.concatenate([value] * owned, axis=1)
    shape = (rows, owned * rank)
    block = lax.broadcasted_iota(jnp.int32, shape, 1) // rank
    expert = lax.broadcasted_iota(jnp.int32, shape, 0) % owned
    return jnp.where(block == expert, wide, 0.0).astype(jnp.bfloat16)


def from_own_block(value, owned):
    rows, wide = value.shape
    rank = wide // owned
    block = lax.broadcasted_iota(jnp.int32, value.shape, 1) // rank
    expert = lax.broadcasted_iota(jnp.int32, value.shape, 0) % owned
    kept = jnp.where(block == expert, value, 0.0)
    out = kept[:, :rank]
    for number in range(1, owned):
        out = out + kept[:, number * rank : (number + 1) * rank]
    return out


def early_kernel(out):
    out[...] = jnp.zeros(out.shape, out.dtype)


def sums_kernel(
    owned, groups, _, tokens, cotangent, router, own, other, logits_out, combine_out
):
    chips = own.shape[0] // groups
    core = lax.axis_index("core")
    image_rows = tokens[...]
    logits = dot_last(router[...], image_rows)
    high, low = halves(jnp.max(logits, axis=1, keepdims=True))
    near = jnp.exp(logits - (high + low))
    total_high, total_low = halves(jnp.sum(near, axis=1, keepdims=True))
    spread = jnp.exp(logits - jnp.max(logits, axis=0, keepdims=True))
    combine = spread / jnp.sum(spread, axis=0, keepdims=True)
    logits_out[...] = logits
    combine_out[...] = combine
    stats = in_lanes([high, low, total_high, total_low], (logits.shape[0], STATS))
    stats = stats.astype(jnp.bfloat16)
    inputs = dot_plain(near.astype(jnp.bfloat16), image_rows).astype(jnp.bfloat16)
    grads = dot_plain(combine.astype(jnp.bfloat16), cotangent[...]).astype(jnp.bfloat16)
    width = inputs.shape[1] // groups

    def block(rows, columns):
        return jnp.concatenate([inputs[rows, columns], grads[rows, columns], stats[rows]], axis=1)

    for group in range(groups):
        columns = slice(group * width, (group + 1) * width)
        for chip in range(chips):
            start = 2 * chip * owned
            even = block(slice(start, start + owned), columns)
            odd = block(slice(start + owned, start + 2 * owned), columns)
            own[group * chips + chip] = jnp.where(core == 0, even, odd)
            other[group * chips + chip] = jnp.where(core == 0, odd, even)


def merge_kernel(width, own, other, out):
    parts = []
    for part in (own, other):
        stats = part[:, :, 2 * width :].astype(jnp.float32)
        parts.append((stats[:, :, 0:1] + stats[:, :, 1:2], stats[:, :, 2:3] + stats[:, :, 3:4]))
    peak = jnp.maximum(parts[0][0], parts[1][0])
    scales = [jnp.exp(part[0] - peak) for part in parts]
    total = scales[0] * parts[0][1] + scales[1] * parts[1][1]
    stats = in_lanes([*halves(peak), *halves(total)], own.shape[:2] + (STATS,))
    inputs = [
        part[:, :, :width].astype(jnp.float32) * scale
        for part, scale in zip((own, other), scales, strict=True)
    ]
    grads = [part[:, :, width : 2 * width].astype(jnp.float32) for part in (own, other)]
    out[:, :, :width] = (inputs[0] + inputs[1]).astype(jnp.bfloat16)
    out[:, :, width : 2 * width] = (grads[0] + grads[1]).astype(jnp.bfloat16)
    out[:, :, 2 * width :] = stats.astype(jnp.bfloat16)


def mixing_kernel(cotangent, saved, combine, out):
    mixing = dot_last(saved[...], cotangent[...])
    weights = combine[...]
    out[...] = weights * (mixing - jnp.sum(weights * mixing, axis=0, keepdims=True))


def owner_kernel(groups, first, in_left, out_right, second, inputs_out, lows_out, stats_out):
    ring = first.shape[0] // groups
    owned, rank, width = in_left.shape
    inputs, grads, stats_rows = [], [], []
    for group in range(groups):
        rows = slice(group * ring, (group + 1) * ring)
        stats = first[rows, :, 2 * width :].astype(jnp.float32)
        peaks = stats[:, :, 0:1] + stats[:, :, 1:2]
        totals = stats[:, :, 2:3] + stats[:, :, 3:4]
        peak = jnp.max(peaks, axis=0)
        scale = jnp.exp(peaks - peak[None])
        total = jnp.sum(scale * totals, axis=0)
        scale = scale / total[None]
        inputs.append(jnp.sum(first[rows, :, :width].astype(jnp.float32) * scale, axis=0))
        grads.append(jnp.sum(first[rows, :, width : 2 * width].astype(jnp.float32), axis=0))
        stats_rows.append(in_lanes([*halves(peak), *halves(total)], (owned, STATS)))
    inputs, grads = jnp.concatenate(inputs, axis=0), jnp.concatenate(grads, axis=0)
    inputs_out[...] = inputs
    stats_out[...] = jnp.concatenate(stats_rows, axis=0)
    inputs_low, grads_low = inputs.astype(jnp.bfloat16), grads.astype(jnp.bfloat16)
    lows_out[0] = inputs_low
    lows_out[1] = grads_low
    up = dot_last(inputs_low, in_left[...].reshape(owned * rank, width))
    back = dot_last(grads_low, out_right[...].reshape(owned * rank, width))
    ranks = [from_own_block(up, owned), from_own_block(back, owned)]
    ranks = jnp.concatenate(ranks, axis=1).astype(jnp.bfloat16)
    block = jnp.concatenate([inputs_low, grads_low, ranks], axis=1)
    second[...] = block


def pack_kernel(own, beside, out):
    here = lax.axis_index("half")
    for group in range(out.shape[0]):
        block = jnp.where(here == group, own[...], beside[...])
        for place in range(out.shape[1]):
            out[group, place] = block


def factor_products(blocks, in_right, out_left, core):
    members, rank, hidden = in_right.shape
    rows = blocks.shape[1]
    chips = blocks.shape[0] // 2
    owned = members // (2 * chips)
    start = blocks.shape[2] - 2 * rank
    ranks = jnp.zeros((chips * rows, 2 * rank), jnp.float32)
    for half in range(2):
        part = blocks[half * chips : (half + 1) * chips, :, start:].astype(jnp.float32)
        ranks = ranks + part.reshape(ranks.shape)
    out = []
    for number, table in enumerate((in_right, out_left)):
        value = ranks[:, number * rank : (number + 1) * rank]
        value = value.astype(jnp.bfloat16).astype(jnp.float32)
        taken = []
        for chip in range(chips):
            own = own_block(value[chip * rows : (chip + 1) * rows], owned)
            part = table[pl.ds((2 * chip + core) * owned, owned)].reshape(owned * rank, hidden)
            taken.append(dot_plain(own, part))
        out.append((value, jnp.concatenate(taken, axis=0)))
    return out


def near_kernel(second, in_right, out_left, _, __, ranks_out, products_out):
    found = factor_products(second, in_right, out_left, lax.axis_index("core"))
    for number, (value, product) in enumerate(found):
        ranks_out[number] = value
        products_out[number] = product


def hidden_kernel(
    groups,
    second,
    second_other,
    near_ranks,
    near_products,
    base_in,
    base_out,
    in_right,
    out_left,
    third,
    pair_out,
    ranks_out,
):
    first_core = lax.axis_index("core") == 0
    members, rank, hidden = in_right.shape
    rows = second.shape[1]
    owned = rows // groups
    places = members // owned
    width = base_in.shape[1] // groups

    def gathered(columns):
        parts = []
        for half in range(groups):
            taken = []
            for chip in range(places // 2):
                block = half * (places // 2) + chip
                own = second[block, :, columns].astype(jnp.float32)
                other = second_other[block, :, columns].astype(jnp.float32)
                taken.append(jnp.where(first_core, own, other))
                taken.append(jnp.where(first_core, other, own))
            parts.append(jnp.concatenate(taken, axis=0))
        return parts

    def in_order(near, far):
        taken = []
        for chip in range(places // 2):
            own = near[chip * rows : (chip + 1) * rows]
            other = far[chip * rows : (chip + 1) * rows]
            taken.append(jnp.where(first_core, own, other))
            taken.append(jnp.where(first_core, other, own))
        return jnp.concatenate(taken, axis=0)

    def to_rank(value, table):
        taken = []
        for place in range(places):
            part = table[place * owned : (place + 1) * owned].reshape(owned * rank, hidden)
            wide = dot_last(value[place * rows : (place + 1) * rows].astype(jnp.bfloat16), part)
            taken.append(from_own_block(wide, owned))
        return jnp.concatenate(taken, axis=0)

    far = factor_products(second_other, in_right, out_left, 1 - lax.axis_index("core"))
    up, back = [in_order(near_ranks[number], far[number][0]) for number in range(2)]
    preact, hidden_grad = [in_order(near_products[number], far[number][1]) for number in range(2)]
    for half, part in enumerate(gathered(slice(0, width))):
        columns = slice(half * width, (half + 1) * width)
        preact = preact + dot_turned(part.astype(jnp.bfloat16), base_in[:, columns])
    for half, part in enumerate(gathered(slice(width, 2 * width))):
        columns = slice(half * width, (half + 1) * width)
        hidden_grad = hidden_grad + dot_turned(part.astype(jnp.bfloat16), base_out[:, columns])
    root = 0.7978845608028654
    bent = jnp.tanh(root * (preact + 0.044715 * (preact * preact * preact)))
    hidden_value = 0.5 * preact * (1.0 + bent)
    slope = 0.5 * (1.0 + bent) + 0.5 * preact * (1.0 - bent * bent) * (
        root * (1.0 + 3.0 * 0.044715 * (preact * preact))
    )
    hidden_low = hidden_value.astype(jnp.bfloat16).astype(jnp.float32)
    preact_grad = (hidden_grad * slope).astype(jnp.bfloat16).astype(jnp.float32)
    pair_out[0] = preact_grad
    pair_out[1] = hidden_low
    ranks_out[0] = up
    ranks_out[1] = back
    slot_term = dot_plain(preact_grad.astype(jnp.bfloat16), base_in[...]).astype(jnp.bfloat16)
    down = to_rank(preact_grad, in_right)
    value = to_rank(hidden_low, out_left)
    ranks = jnp.concatenate([down, value], axis=1).astype(jnp.bfloat16)
    for half in range(groups):
        columns = slice(half * width, (half + 1) * width)
        for place in range(places):
            taken = slice(place * rows, (place + 1) * rows)
            block = half * places + place
            third[block, :, :width] = slot_term[taken, columns]
            third[block, :, width:] = ranks[taken]


def outer_kernel(owned, left_rows, right_rows, *outs):
    rows = left_rows.shape[1] // (outs[0].shape[0] // owned)
    for number, out in enumerate(outs):
        for place in range(out.shape[0] // owned):
            taken = slice(place * rows, (place + 1) * rows)
            own = own_block(left_rows[number, taken], owned)
            product = dot_first(own, right_rows[number, taken].astype(jnp.bfloat16))
            out[place * owned : (place + 1) * owned] = product.astype(jnp.bfloat16).reshape(
                (owned,) + out.shape[1:]
            )


def halves_kernel(third, own, other):
    places = third.shape[0] // 2
    here = lax.axis_index("half")
    for out, group in ((own, here), (other, 1 - here)):
        taken = third[pl.ds(group * places, places)].astype(jnp.float32)
        out[...] = jnp.sum(taken, axis=0).astype(out.dtype)


def finish_kernel(groups, own, other, in_left, inputs, stats, fourth, ranks_out):
    owned, rank, width = in_left.shape
    summed = own[...] + other[...].astype(jnp.float32)
    ranks = summed[:, width:].astype(jnp.bfloat16).astype(jnp.float32)
    ranks_out[0] = ranks[:, :rank]
    ranks_out[1] = ranks[:, rank:]
    down = own_block(ranks[:, :rank], owned)
    grads = summed[:, :width] + dot_plain(down, in_left[...].reshape(owned * rank, width))
    grads = grads.astype(jnp.bfloat16).astype(jnp.float32)
    high, low = halves(jnp.sum(grads * inputs[...], axis=1, keepdims=True))
    lane = lax.broadcasted_iota(jnp.int32, stats.shape, 1)
    tail = jnp.where(lane == 4, high, jnp.where(lane == 5, low, stats[...]))
    block = jnp.concatenate([grads, tail], axis=1).astype(jnp.bfloat16)
    for group in range(groups):
        rows = block[group * owned : (group + 1) * owned]
        for place in range(fourth.shape[0] // groups):
            fourth[group * (fourth.shape[0] // groups) + place] = rows


def tokens_kernel(
    groups,
    fourth,
    fourth_other,
    tokens,
    router,
    logits,
    mixing,
    grad_left,
    grad_right,
    out_far,
    grad_left_far,
    grad_right_far,
    out,
    sent,
    grads_sent,
):
    copies = [
        pltpu.make_async_copy(grad_left, grad_left_far, grads_sent.at[0]),
        pltpu.make_async_copy(grad_right, grad_right_far, grads_sent.at[1]),
    ]
    for copy in copies:
        copy.start()
    blocks, owned, _ = fourth.shape
    chips = blocks // groups
    width = tokens.shape[1] // groups
    first_core = lax.axis_index("core") == 0

    def rows(half, columns):
        taken = []
        for chip in range(chips):
            own = fourth[half * chips + chip, :, columns].astype(jnp.float32)
            other = fourth_other[half * chips + chip, :, columns].astype(jnp.float32)
            taken.append(jnp.where(first_core, own, other))
            taken.append(jnp.where(first_core, other, own))
        return jnp.concatenate(taken, axis=0)

    grads = jnp.concatenate([rows(half, slice(0, width)) for half in range(groups)], axis=1)
    grads = grads.astype(jnp.bfloat16)
    stats = [rows(half, slice(width, width + STATS)) for half in range(groups)]
    peak = stats[0][:, 0:1] + stats[0][:, 1:2]
    total = stats[0][:, 2:3] + stats[0][:, 3:4]
    shift = functools.reduce(jnp.add, [part[:, 4:5] + part[:, 5:6] for part in stats])
    dispatch = jnp.exp(logits[...] - peak) / total
    weight_grad = dot_last(grads, tokens[...])
    logit_grad = dispatch * (weight_grad - shift) + mixing[...]
    left = jnp.concatenate([dispatch, logit_grad], axis=0).T.astype(jnp.bfloat16)
    right = jnp.concatenate([grads, router[...]], axis=0)
    parts = sent.shape[0]
    size = out.shape[1] // parts
    for part in range(parts):
        columns = slice(part * size, (part + 1) * size)
        out[:, columns] = dot_plain(left, right[:, columns]).astype(jnp.bfloat16)
        copy = pltpu.make_async_copy(
            out.at[:, columns], out_far.at[:, columns], sent.at[part]
        )
        copy.start()
        copies.append(copy)
    for copy in copies:
        copy.wait()


def swap(blocks, axis):
    return lax.ppermute(blocks, axis, [(0, 1), (1, 0)])


def to_group(block, beside, groups):
    chips = lax.axis_size("chip")
    (blocks,) = call(
        pack_kernel,
        [array(block.dtype, groups, chips, *block.shape)],
        [block, beside],
        FLOPS_BESIDE_EXCHANGE,
    )
    blocks = blocks.reshape(groups * chips, *block.shape)
    blocks = lax.all_to_all(blocks, HALF_CORE, 0, 0, tiled=True)
    return blocks, swap(blocks, "core")


def call(kernel, outs, args, flops, space=pltpu.VMEM, scratch=(), size=None):
    if size is None:
        size = sum(array.size * array.dtype.itemsize for array in (*args, *outs))
    return pl.pallas_call(
        kernel,
        out_shape=outs,
        in_specs=[pl.BlockSpec(memory_space=pltpu.VMEM) for _ in args],
        out_specs=[pl.BlockSpec(memory_space=space) for _ in outs],
        scratch_shapes=scratch,
        cost_estimate=pl.CostEstimate(flops=flops, bytes_accessed=size, transcendentals=0),
        compiler_params=pltpu.CompilerParams(vmem_limit_bytes=24 * 2**20),
    )(*args)


def array(dtype, *shape):
    return jax.ShapeDtypeStruct(shape, dtype)


def local(
    tokens,
    cotangent,
    router,
    slot_outputs,
    base_in,
    base_out,
    in_left,
    in_right,
    out_left,
    out_right,
):
    groups, ring = lax.axis_size("dp"), lax.axis_size(SEQ)
    devices = groups * ring
    _, count, width = tokens.shape
    slots = router.shape[1]
    owned, slice_width, rank = in_left.shape
    members, _, hidden = in_right.shape
    rows = groups * owned
    if groups != 2 or ring % 4 or slice_width % 128 or rows % 8 or members % owned:
        return local_plain(
            tokens,
            cotangent,
            router,
            slot_outputs,
            base_in,
            base_out,
            in_left,
            in_right,
            out_left,
            out_right,
        )
    low, full = jnp.bfloat16, jnp.float32
    image_rows, cot_rows, saved = tokens[0], cotangent[0], slot_outputs[0]
    router, base_in = router.T, base_in.T
    in_left, out_left = in_left.swapaxes(1, 2), out_left.swapaxes(1, 2)
    (early,) = call(early_kernel, [array(full, 8, 128)], [], FLOPS_BESIDE_EXCHANGE)
    first = array(low, devices // 2, owned, 2 * slice_width + STATS)
    own, other, logits, combine = call(
        functools.partial(sums_kernel, owned, groups),
        [first, first, array(full, slots, count), array(full, slots, count)],
        [early, image_rows, cot_rows, router],
        6 * count * slots * width + FLOPS_BESIDE_EXCHANGE,
    )
    other = swap(other, "core")
    (first,) = call(
        functools.partial(merge_kernel, slice_width), [first], [own, other], FLOPS_BESIDE_EXCHANGE
    )
    first = lax.all_to_all(first, SAME_CORE, 0, 0, tiled=True)
    second, inputs, lows, stats = call(
        functools.partial(owner_kernel, groups),
        [
            array(low, rows, 2 * slice_width + 2 * rank),
            array(full, rows, slice_width),
            array(low, 2, rows, slice_width),
            array(full, rows, STATS),
        ],
        [first, in_left, out_right],
        4 * rows * owned * rank * slice_width,
    )
    second, combine = lax.optimization_barrier((second, combine))
    beside = swap(second, "half")
    (mixing,) = call(
        mixing_kernel,
        [array(full, slots, count)],
        [cot_rows, saved, combine],
        2 * count * slots * width,
    )
    beside, mixing = lax.optimization_barrier((beside, mixing))
    second, second_other = to_group(second, beside, groups)
    total_rows = groups * members
    near_ranks, near_products = call(
        near_kernel,
        [array(full, 2, total_rows // 2, rank), array(full, 2, total_rows // 2, hidden)],
        [second, in_right, out_left, base_in, base_out],
        2 * total_rows * owned * rank * hidden,
        size=0,
    )
    third, pair, hidden_ranks = call(
        functools.partial(hidden_kernel, groups),
        [
            array(low, ring, rows, slice_width + 2 * rank),
            array(full, 2, total_rows, hidden),
            array(full, 2, total_rows, rank),
        ],
        [
            second,
            second_other,
            near_ranks,
            near_products,
            base_in,
            base_out,
            in_right,
            out_left,
        ],
        6 * total_rows * hidden * (width + owned * rank),
    )
    third = lax.all_to_all(third, HALF, 0, 0, tiled=True)
    own, other = call(
        halves_kernel,
        [array(kind, rows, slice_width + 2 * rank) for kind in (full, low)],
        [third],
        0,
    )
    other, pair, hidden_ranks = lax.optimization_barrier((other, pair, hidden_ranks))
    other = swap(other, "half")
    grad_in_right, grad_out_left = call(
        functools.partial(outer_kernel, owned),
        [array(low, members, rank, hidden)] * 2,
        [hidden_ranks, pair],
        4 * members * rank * hidden * rows,
    )
    other, grad_in_right, grad_out_left = lax.optimization_barrier(
        (other, grad_in_right, grad_out_left)
    )
    fourth, ranks = call(
        functools.partial(finish_kernel, groups),
        [array(low, devices // 2, owned, slice_width + STATS), array(full, 2, rows, rank)],
        [own, other, in_left, inputs, stats],
        2 * rows * owned * rank * slice_width,
    )
    fourth = lax.all_to_all(fourth, SAME_CORE, 0, 0, tiled=True)
    fourth, ranks = lax.optimization_barrier((fourth, ranks))
    fourth_other = swap(fourth, "core")
    grad_in_left, grad_out_right = call(
        functools.partial(outer_kernel, owned),
        [array(low, owned, rank, slice_width)] * 2,
        [ranks, lows],
        4 * owned * rank * slice_width * rows,
    )
    fourth_other, grad_in_left, grad_out_right = lax.optimization_barrier(
        (fourth_other, grad_in_left, grad_out_right)
    )
    parts = width // 256 if width % 256 == 0 else 1
    token_grad, grad_in_left, grad_out_right = call(
        functools.partial(tokens_kernel, groups),
        [array(low, count, width)] + [array(low, owned, rank, slice_width)] * 2,
        [
            fourth,
            fourth_other,
            image_rows,
            router,
            logits,
            mixing,
            grad_in_left,
            grad_out_right,
        ],
        6 * count * slots * width,
        pltpu.HBM,
        [
            pltpu.VMEM((count, width), low),
            pltpu.SemaphoreType.DMA((parts,)),
            pltpu.SemaphoreType.DMA((2,)),
        ],
    )
    return (
        token_grad[None],
        grad_in_left.swapaxes(1, 2),
        grad_in_right,
        grad_out_left.swapaxes(1, 2),
        grad_out_right,
    )


def solution(mesh):
    groups, ring = mesh.shape["dp"], mesh.shape["seq"]
    cores = math.gcd(2, ring // groups)
    split = mesh.devices.reshape(groups, groups, ring // groups // cores, cores)
    mesh = jax.sharding.Mesh(split, BOTH)
    in_specs = (
        P("dp", SEQ, None),
        P("dp", SEQ, None),
        P(),
        P("dp", None, None),
        P(None, SEQ),
        P(SEQ, None),
        P(SEQ, "dp", None),
        P("dp", None, SEQ),
        P("dp", SEQ, None),
        P(SEQ, None, "dp"),
    )
    out_specs = (
        P("dp", SEQ, None),
        P(SEQ, "dp", None),
        P("dp", None, SEQ),
        P("dp", SEQ, None),
        P(SEQ, None, "dp"),
    )
    return jax.shard_map(local, mesh=mesh, in_specs=in_specs, out_specs=out_specs, check_vma=False)
```

```python
import functools
import math

import jax
import jax.numpy as jnp
from jax import lax
from jax.experimental import pallas as pl
from jax.experimental.pallas import tpu as pltpu
from jax.sharding import PartitionSpec as P

PLACE = ("chip", "core")
SEQ = ("half", *PLACE)
BOTH = ("dp", *SEQ)
HALF = ("dp", *PLACE)
HALF_CORE = ("dp", "chip")
SAME_CORE = ("dp", "half", "chip")
STATS = 128
FLOPS_BESIDE_EXCHANGE = 10**10


def gelu_backward(preact, upstream):
    return jax.vjp(jax.nn.gelu, preact)[1](upstream)[0]


def dot_first(left, right):
    return lax.dot_general(
        left, right, (((0,), (0,)), ((), ())), preferred_element_type=jnp.float32
    )


def dot_last(left, right):
    return lax.dot_general(
        left, right, (((1,), (1,)), ((), ())), preferred_element_type=jnp.float32
    )


def split(value):
    high = lax.reduce_precision(value, 8, 7)
    low = lax.reduce_precision(value - high, 8, 7)
    return high.astype(jnp.bfloat16), low.astype(jnp.bfloat16)


def joined(high, low):
    return high.astype(jnp.float32) + low.astype(jnp.float32)


def exchange(blocks):
    flat = blocks.reshape((-1,) + blocks.shape[2:])
    return lax.all_to_all(flat, BOTH, 0, 0, tiled=True).reshape(blocks.shape)


def local_plain(
    tokens,
    cotangent,
    router,
    slot_outputs,
    base_in,
    base_out,
    in_left,
    in_right,
    out_left,
    out_right,
):
    groups, ring = lax.axis_size("dp"), lax.axis_size(SEQ)
    image_rows = tokens[0]
    cot_rows = cotangent[0]
    saved_outputs = slot_outputs[0]
    width = image_rows.shape[1]
    slots = router.shape[1]
    owned, slice_width, rank = in_left.shape
    members = in_right.shape[0]
    places = members // owned
    group, place = lax.axis_index("dp"), lax.axis_index(SEQ)

    logits = jnp.dot(image_rows, router, preferred_element_type=jnp.float32)
    peak_high, peak_low = split(jnp.max(logits, axis=0))
    near = jnp.exp(logits - joined(peak_high, peak_low))
    total_high, total_low = split(jnp.sum(near, axis=0))
    combine = jax.nn.softmax(logits, axis=1)
    sums = jnp.stack(
        [
            dot_first(near.astype(jnp.bfloat16), image_rows),
            dot_first(combine.astype(jnp.bfloat16), cot_rows),
        ],
        axis=1,
    ).astype(jnp.bfloat16)
    sums = sums.reshape(ring, owned, 2, groups, slice_width).transpose(3, 0, 1, 2, 4)
    sums = sums.reshape(groups, ring, owned, 2 * slice_width)
    stats = jnp.stack([peak_high, peak_low, total_high, total_low], axis=1)
    stats = jnp.pad(stats, ((0, 0), (0, STATS - 4))).reshape(1, ring, owned, STATS)
    stats = jnp.broadcast_to(stats, (groups, ring, owned, STATS))
    first = exchange(jnp.concatenate([sums, stats], axis=3))

    tail = 2 * slice_width
    peaks = joined(first[..., tail], first[..., tail + 1])
    totals = joined(first[..., tail + 2], first[..., tail + 3])
    peak = jnp.max(peaks, axis=1)
    near_scale = jnp.exp(peaks - peak[:, None])
    total = jnp.sum(near_scale * totals, axis=1)
    near_scale = near_scale / total[:, None]
    parts = first[..., :tail].astype(jnp.float32)
    slot_inputs = jnp.sum(parts[..., :slice_width] * near_scale[..., None], axis=1)
    inputs_own = slot_inputs.astype(jnp.bfloat16)
    grads_own = jnp.sum(parts[..., slice_width:], axis=1).astype(jnp.bfloat16)
    up_part = jnp.einsum("gjd,jdr->gjr", inputs_own, in_left, preferred_element_type=jnp.float32)
    back_part = jnp.einsum("gjd,jrd->gjr", grads_own, out_right, preferred_element_type=jnp.float32)
    second = jnp.concatenate(
        [inputs_own, grads_own, *split(up_part), *split(back_part)], axis=2
    )
    second = exchange(jnp.broadcast_to(second, (groups, ring) + second.shape))
    second = lax.dynamic_slice_in_dim(second, group * places, places, 1)

    def gathered(start):
        piece = second[..., start : start + slice_width]
        return piece.transpose(2, 1, 3, 0, 4).reshape(groups * members, width)

    def ranks(start):
        piece = joined(
            second[..., start : start + rank], second[..., start + rank : start + 2 * rank]
        )
        piece = jnp.sum(piece, axis=0).transpose(1, 0, 2, 3)
        return piece.reshape(groups, members, rank).astype(jnp.bfloat16)

    inputs_low, grads_low = gathered(0), gathered(slice_width)
    up_low, back_low = ranks(tail), ranks(tail + 2 * rank)
    hidden = base_in.shape[1]
    preact = jnp.dot(inputs_low, base_in, preferred_element_type=jnp.float32).reshape(
        groups, members, hidden
    ) + jnp.einsum("gjr,jrf->gjf", up_low, in_right, preferred_element_type=jnp.float32)
    hidden_low = jax.nn.gelu(preact).astype(jnp.bfloat16)
    hidden_grad = dot_last(grads_low, base_out).reshape(groups, members, hidden) + jnp.einsum(
        "gjr,jfr->gjf", back_low, out_left, preferred_element_type=jnp.float32
    )
    preact_grad = gelu_backward(preact, hidden_grad).astype(jnp.bfloat16)
    slot_term = dot_last(preact_grad.reshape(groups * members, hidden), base_in)
    down_term = jnp.einsum(
        "gjf,jrf->gjr", preact_grad, in_right, preferred_element_type=jnp.float32
    )
    value_term = jnp.einsum(
        "gjf,jfr->gjr", hidden_low, out_left, preferred_element_type=jnp.float32
    )
    slot_term = slot_term.astype(jnp.bfloat16).reshape(groups, places, owned, groups, slice_width)
    slot_term = slot_term.transpose(3, 1, 0, 2, 4)
    rank_term = jnp.concatenate([down_term, value_term], axis=2).astype(jnp.bfloat16)
    rank_term = rank_term.reshape(groups, places, owned, 2 * rank).transpose(1, 0, 2, 3)
    rank_term = jnp.broadcast_to(rank_term, (groups,) + rank_term.shape)
    third = jnp.concatenate([slot_term, rank_term], axis=4)
    third = lax.dynamic_update_slice_in_dim(
        jnp.zeros((groups, ring) + third.shape[2:], jnp.bfloat16), third, group * places, 1
    )
    third = exchange(third)
    third = lax.dynamic_index_in_dim(third, place // places, 0, keepdims=False)
    third = jnp.sum(third.astype(jnp.float32), axis=0)
    down_own = third[..., slice_width : slice_width + rank].astype(jnp.bfloat16)
    value_own = third[..., slice_width + rank :].astype(jnp.bfloat16)
    slot_grads_own = (
        third[..., :slice_width]
        + jnp.einsum("gjr,jdr->gjd", down_own, in_left, preferred_element_type=jnp.float32)
    ).astype(jnp.bfloat16)
    shift_part = jnp.sum(slot_grads_own.astype(jnp.float32) * slot_inputs, axis=2)
    stats = jnp.stack([*split(peak), *split(total), *split(shift_part)], axis=2)
    stats = jnp.pad(stats, ((0, 0), (0, 0), (0, STATS - 6)))
    fourth = jnp.concatenate([slot_grads_own, stats], axis=2)[:, None]
    fourth = exchange(jnp.broadcast_to(fourth, (groups, ring) + fourth.shape[2:]))
    slot_grads = fourth[..., :slice_width].transpose(1, 2, 0, 3).reshape(slots, width)
    stats = fourth[..., slice_width:].astype(jnp.float32).reshape(groups, slots, STATS)
    slot_peak = stats[0, :, 0] + stats[0, :, 1]
    slot_total = stats[0, :, 2] + stats[0, :, 3]
    shift_back = jnp.sum(stats[:, :, 4] + stats[:, :, 5], axis=0)

    dispatch = jnp.exp(logits - slot_peak) / slot_total
    dispatch_low = dispatch.astype(jnp.bfloat16)
    weight_grad = dot_last(image_rows, slot_grads)
    dispatch_logit = dispatch * (weight_grad - shift_back)
    mixing_grad = dot_last(cot_rows, saved_outputs)
    combine_logit = combine * (mixing_grad - jnp.sum(combine * mixing_grad, axis=1, keepdims=True))
    logit_grad = (dispatch_logit + combine_logit).astype(jnp.bfloat16)
    token_grad = (
        jnp.dot(dispatch_low, slot_grads, preferred_element_type=jnp.float32)
        + dot_last(logit_grad, router)
    ).astype(jnp.bfloat16)
    grad_in_right = jnp.einsum(
        "gjr,gjf->jrf", up_low, preact_grad, preferred_element_type=jnp.float32
    ).astype(jnp.bfloat16)
    grad_out_left = jnp.einsum(
        "gjf,gjr->jfr", hidden_low, back_low, preferred_element_type=jnp.float32
    ).astype(jnp.bfloat16)
    grad_in_left = jnp.einsum(
        "gjd,gjr->jdr", inputs_own, down_own, preferred_element_type=jnp.float32
    ).astype(jnp.bfloat16)
    grad_out_right = jnp.einsum(
        "gjr,gjd->jrd", value_own, grads_own, preferred_element_type=jnp.float32
    ).astype(jnp.bfloat16)
    return (token_grad[None], grad_in_left, grad_in_right, grad_out_left, grad_out_right)


def dot_turned(left, right):
    return dot_last(right, left).T


def dot_plain(left, right):
    return jnp.dot(left, right, preferred_element_type=jnp.float32)


def halves(value):
    high = value.astype(jnp.bfloat16).astype(jnp.float32)
    low = (value - high).astype(jnp.bfloat16).astype(jnp.float32)
    return high, low


def in_lanes(columns, shape):
    lane = lax.broadcasted_iota(jnp.int32, shape, len(shape) - 1)
    out = jnp.zeros(shape, jnp.float32)
    for number, column in enumerate(columns):
        out = jnp.where(lane == number, column, out)
    return out


def own_block(value, owned):
    rows, rank = value.shape
    wide = jnp.concatenate([value] * owned, axis=1)
    shape = (rows, owned * rank)
    block = lax.broadcasted_iota(jnp.int32, shape, 1) // rank
    expert = lax.broadcasted_iota(jnp.int32, shape, 0) % owned
    return jnp.where(block == expert, wide, 0.0).astype(jnp.bfloat16)


def from_own_block(value, owned):
    rows, wide = value.shape
    rank = wide // owned
    block = lax.broadcasted_iota(jnp.int32, value.shape, 1) // rank
    expert = lax.broadcasted_iota(jnp.int32, value.shape, 0) % owned
    kept = jnp.where(block == expert, value, 0.0)
    out = kept[:, :rank]
    for number in range(1, owned):
        out = out + kept[:, number * rank : (number + 1) * rank]
    return out


def early_kernel(out):
    out[...] = jnp.zeros(out.shape, out.dtype)


def sums_kernel(
    owned, groups, _, tokens, cotangent, router, own, other, logits_out, combine_out
):
    chips = own.shape[0] // groups
    core = lax.axis_index("core")
    image_rows = tokens[...]
    logits = dot_last(router[...], image_rows)
    high, low = halves(jnp.max(logits, axis=1, keepdims=True))
    near = jnp.exp(logits - (high + low))
    total_high, total_low = halves(jnp.sum(near, axis=1, keepdims=True))
    spread = jnp.exp(logits - jnp.max(logits, axis=0, keepdims=True))
    combine = spread / jnp.sum(spread, axis=0, keepdims=True)
    logits_out[...] = logits
    combine_out[...] = combine
    stats = in_lanes([high, low, total_high, total_low], (logits.shape[0], STATS))
    stats = stats.astype(jnp.bfloat16)
    inputs = dot_plain(near.astype(jnp.bfloat16), image_rows).astype(jnp.bfloat16)
    grads = dot_plain(combine.astype(jnp.bfloat16), cotangent[...]).astype(jnp.bfloat16)
    width = inputs.shape[1] // groups

    def block(rows, columns):
        return jnp.concatenate([inputs[rows, columns], grads[rows, columns], stats[rows]], axis=1)

    for group in range(groups):
        columns = slice(group * width, (group + 1) * width)
        for chip in range(chips):
            start = 2 * chip * owned
            even = block(slice(start, start + owned), columns)
            odd = block(slice(start + owned, start + 2 * owned), columns)
            own[group * chips + chip] = jnp.where(core == 0, even, odd)
            other[group * chips + chip] = jnp.where(core == 0, odd, even)


def merge_kernel(width, own, other, out):
    parts = []
    for part in (own, other):
        stats = part[:, :, 2 * width :].astype(jnp.float32)
        parts.append((stats[:, :, 0:1] + stats[:, :, 1:2], stats[:, :, 2:3] + stats[:, :, 3:4]))
    peak = jnp.maximum(parts[0][0], parts[1][0])
    scales = [jnp.exp(part[0] - peak) for part in parts]
    total = scales[0] * parts[0][1] + scales[1] * parts[1][1]
    stats = in_lanes([*halves(peak), *halves(total)], own.shape[:2] + (STATS,))
    inputs = [
        part[:, :, :width].astype(jnp.float32) * scale
        for part, scale in zip((own, other), scales, strict=True)
    ]
    grads = [part[:, :, width : 2 * width].astype(jnp.float32) for part in (own, other)]
    out[:, :, :width] = (inputs[0] + inputs[1]).astype(jnp.bfloat16)
    out[:, :, width : 2 * width] = (grads[0] + grads[1]).astype(jnp.bfloat16)
    out[:, :, 2 * width :] = stats.astype(jnp.bfloat16)


def mixing_kernel(cotangent, saved, combine, out):
    mixing = dot_last(saved[...], cotangent[...])
    weights = combine[...]
    out[...] = weights * (mixing - jnp.sum(weights * mixing, axis=0, keepdims=True))


def owner_kernel(groups, first, in_left, out_right, second, inputs_out, lows_out, stats_out):
    ring = first.shape[0] // groups
    owned, rank, width = in_left.shape
    inputs, grads, stats_rows = [], [], []
    for group in range(groups):
        rows = slice(group * ring, (group + 1) * ring)
        stats = first[rows, :, 2 * width :].astype(jnp.float32)
        peaks = stats[:, :, 0:1] + stats[:, :, 1:2]
        totals = stats[:, :, 2:3] + stats[:, :, 3:4]
        peak = jnp.max(peaks, axis=0)
        scale = jnp.exp(peaks - peak[None])
        total = jnp.sum(scale * totals, axis=0)
        scale = scale / total[None]
        inputs.append(jnp.sum(first[rows, :, :width].astype(jnp.float32) * scale, axis=0))
        grads.append(jnp.sum(first[rows, :, width : 2 * width].astype(jnp.float32), axis=0))
        stats_rows.append(in_lanes([*halves(peak), *halves(total)], (owned, STATS)))
    inputs, grads = jnp.concatenate(inputs, axis=0), jnp.concatenate(grads, axis=0)
    inputs_out[...] = inputs
    stats_out[...] = jnp.concatenate(stats_rows, axis=0)
    inputs_low, grads_low = inputs.astype(jnp.bfloat16), grads.astype(jnp.bfloat16)
    lows_out[0] = inputs_low
    lows_out[1] = grads_low
    up = dot_last(inputs_low, in_left[...].reshape(owned * rank, width))
    back = dot_last(grads_low, out_right[...].reshape(owned * rank, width))
    ranks = [from_own_block(up, owned), from_own_block(back, owned)]
    ranks = jnp.concatenate(ranks, axis=1).astype(jnp.bfloat16)
    block = jnp.concatenate([inputs_low, grads_low, ranks], axis=1)
    second[...] = block


def pack_kernel(own, beside, out):
    here = lax.axis_index("half")
    for group in range(out.shape[0]):
        block = jnp.where(here == group, own[...], beside[...])
        for place in range(out.shape[1]):
            out[group, place] = block


def factor_products(blocks, in_right, out_left, core):
    members, rank, hidden = in_right.shape
    rows = blocks.shape[1]
    chips = blocks.shape[0] // 2
    owned = members // (2 * chips)
    start = blocks.shape[2] - 2 * rank
    ranks = jnp.zeros((chips * rows, 2 * rank), jnp.float32)
    for half in range(2):
        part = blocks[half * chips : (half + 1) * chips, :, start:].astype(jnp.float32)
        ranks = ranks + part.reshape(ranks.shape)
    out = []
    for number, table in enumerate((in_right, out_left)):
        value = ranks[:, number * rank : (number + 1) * rank]
        value = value.astype(jnp.bfloat16).astype(jnp.float32)
        taken = []
        for chip in range(chips):
            own = own_block(value[chip * rows : (chip + 1) * rows], owned)
            part = table[pl.ds((2 * chip + core) * owned, owned)].reshape(owned * rank, hidden)
            taken.append(dot_plain(own, part))
        out.append((value, jnp.concatenate(taken, axis=0)))
    return out


def near_kernel(second, in_right, out_left, _, __, ranks_out, products_out):
    found = factor_products(second, in_right, out_left, lax.axis_index("core"))
    for number, (value, product) in enumerate(found):
        ranks_out[number] = value
        products_out[number] = product


def hidden_kernel(
    groups,
    second,
    second_other,
    near_ranks,
    near_products,
    base_in,
    base_out,
    in_right,
    out_left,
    third,
    pair_out,
    ranks_out,
):
    first_core = lax.axis_index("core") == 0
    members, rank, hidden = in_right.shape
    rows = second.shape[1]
    owned = rows // groups
    places = members // owned
    width = base_in.shape[1] // groups

    def gathered(columns):
        parts = []
        for half in range(groups):
            taken = []
            for chip in range(places // 2):
                block = half * (places // 2) + chip
                own = second[block, :, columns].astype(jnp.float32)
                other = second_other[block, :, columns].astype(jnp.float32)
                taken.append(jnp.where(first_core, own, other))
                taken.append(jnp.where(first_core, other, own))
            parts.append(jnp.concatenate(taken, axis=0))
        return parts

    def in_order(near, far):
        taken = []
        for chip in range(places // 2):
            own = near[chip * rows : (chip + 1) * rows]
            other = far[chip * rows : (chip + 1) * rows]
            taken.append(jnp.where(first_core, own, other))
            taken.append(jnp.where(first_core, other, own))
        return jnp.concatenate(taken, axis=0)

    def to_rank(value, table):
        taken = []
        for place in range(places):
            part = table[place * owned : (place + 1) * owned].reshape(owned * rank, hidden)
            wide = dot_last(value[place * rows : (place + 1) * rows].astype(jnp.bfloat16), part)
            taken.append(from_own_block(wide, owned))
        return jnp.concatenate(taken, axis=0)

    far = factor_products(second_other, in_right, out_left, 1 - lax.axis_index("core"))
    up, back = [in_order(near_ranks[number], far[number][0]) for number in range(2)]
    preact, hidden_grad = [in_order(near_products[number], far[number][1]) for number in range(2)]
    for half, part in enumerate(gathered(slice(0, width))):
        columns = slice(half * width, (half + 1) * width)
        preact = preact + dot_turned(part.astype(jnp.bfloat16), base_in[:, columns])
    for half, part in enumerate(gathered(slice(width, 2 * width))):
        columns = slice(half * width, (half + 1) * width)
        hidden_grad = hidden_grad + dot_turned(part.astype(jnp.bfloat16), base_out[:, columns])
    root = 0.7978845608028654
    bent = jnp.tanh(root * (preact + 0.044715 * (preact * preact * preact)))
    hidden_value = 0.5 * preact * (1.0 + bent)
    slope = 0.5 * (1.0 + bent) + 0.5 * preact * (1.0 - bent * bent) * (
        root * (1.0 + 3.0 * 0.044715 * (preact * preact))
    )
    hidden_low = hidden_value.astype(jnp.bfloat16).astype(jnp.float32)
    preact_grad = (hidden_grad * slope).astype(jnp.bfloat16).astype(jnp.float32)
    pair_out[0] = preact_grad
    pair_out[1] = hidden_low
    ranks_out[0] = up
    ranks_out[1] = back
    slot_term = dot_plain(preact_grad.astype(jnp.bfloat16), base_in[...]).astype(jnp.bfloat16)
    down = to_rank(preact_grad, in_right)
    value = to_rank(hidden_low, out_left)
    ranks = jnp.concatenate([down, value], axis=1).astype(jnp.bfloat16)
    for half in range(groups):
        columns = slice(half * width, (half + 1) * width)
        for place in range(places):
            taken = slice(place * rows, (place + 1) * rows)
            block = half * places + place
            third[block, :, :width] = slot_term[taken, columns]
            third[block, :, width:] = ranks[taken]


def outer_kernel(owned, left_rows, right_rows, *outs):
    rows = left_rows.shape[1] // (outs[0].shape[0] // owned)
    for number, out in enumerate(outs):
        for place in range(out.shape[0] // owned):
            taken = slice(place * rows, (place + 1) * rows)
            own = own_block(left_rows[number, taken], owned)
            product = dot_first(own, right_rows[number, taken].astype(jnp.bfloat16))
            out[place * owned : (place + 1) * owned] = product.astype(jnp.bfloat16).reshape(
                (owned,) + out.shape[1:]
            )


def halves_kernel(third, own, other):
    places = third.shape[0] // 2
    here = lax.axis_index("half")
    for out, group in ((own, here), (other, 1 - here)):
        taken = third[pl.ds(group * places, places)].astype(jnp.float32)
        out[...] = jnp.sum(taken, axis=0).astype(out.dtype)


def finish_kernel(groups, own, other, in_left, inputs, stats, fourth, ranks_out):
    owned, rank, width = in_left.shape
    summed = own[...] + other[...].astype(jnp.float32)
    ranks = summed[:, width:].astype(jnp.bfloat16).astype(jnp.float32)
    ranks_out[0] = ranks[:, :rank]
    ranks_out[1] = ranks[:, rank:]
    down = own_block(ranks[:, :rank], owned)
    grads = summed[:, :width] + dot_plain(down, in_left[...].reshape(owned * rank, width))
    grads = grads.astype(jnp.bfloat16).astype(jnp.float32)
    high, low = halves(jnp.sum(grads * inputs[...], axis=1, keepdims=True))
    lane = lax.broadcasted_iota(jnp.int32, stats.shape, 1)
    tail = jnp.where(lane == 4, high, jnp.where(lane == 5, low, stats[...]))
    block = jnp.concatenate([grads, tail], axis=1).astype(jnp.bfloat16)
    for group in range(groups):
        rows = block[group * owned : (group + 1) * owned]
        for place in range(fourth.shape[0] // groups):
            fourth[group * (fourth.shape[0] // groups) + place] = rows


def half_tokens(blocks, tokens, logits, mixing, core):
    number, owned, _ = blocks.shape
    chips = number // 2
    width = tokens.shape[1] // 2

    def rows(half, columns):
        taken = [blocks[half * chips + chip, :, columns] for chip in range(chips)]
        return jnp.concatenate([part.astype(jnp.float32) for part in taken], axis=0)

    def chosen(values):
        taken = []
        for chip in range(chips):
            even = values[2 * chip * owned : (2 * chip + 1) * owned]
            odd = values[(2 * chip + 1) * owned : (2 * chip + 2) * owned]
            taken.append(jnp.where(core == 0, even, odd))
        return jnp.concatenate(taken, axis=0)

    grads = jnp.concatenate([rows(half, slice(0, width)) for half in range(2)], axis=1)
    grads = grads.astype(jnp.bfloat16)
    stats = [rows(half, slice(width, width + STATS)) for half in range(2)]
    peak = stats[0][:, 0:1] + stats[0][:, 1:2]
    total = stats[0][:, 2:3] + stats[0][:, 3:4]
    shift = functools.reduce(jnp.add, [part[:, 4:5] + part[:, 5:6] for part in stats])
    dispatch = jnp.exp(chosen(logits[...]) - peak) / total
    weight_grad = dot_last(grads, tokens[...])
    logit_grad = dispatch * (weight_grad - shift) + chosen(mixing[...])
    return grads, dispatch, logit_grad


def near_tokens_kernel(fourth, tokens, logits, mixing, grads, dispatch, logit_grad):
    found = half_tokens(fourth, tokens, logits, mixing, lax.axis_index("core"))
    grads[...], dispatch[...], logit_grad[...] = found


def tokens_kernel(
    fourth_other,
    near_grads,
    near_dispatch,
    near_logit_grad,
    tokens,
    router,
    logits,
    mixing,
    grad_left,
    grad_right,
    out_far,
    grad_left_far,
    grad_right_far,
    out,
    sent,
    grads_sent,
):
    copies = [
        pltpu.make_async_copy(grad_left, grad_left_far, grads_sent.at[0]),
        pltpu.make_async_copy(grad_right, grad_right_far, grads_sent.at[1]),
    ]
    for copy in copies:
        copy.start()
    core = lax.axis_index("core")
    far = half_tokens(fourth_other, tokens, logits, mixing, 1 - core)
    owned = fourth_other.shape[1]
    ordered = []
    for start in range(0, near_logit_grad.shape[0], owned):
        own, other = near_logit_grad[start : start + owned], far[2][start : start + owned]
        ordered.append(jnp.where(core == 0, own, other))
        ordered.append(jnp.where(core == 0, other, own))
    left = jnp.concatenate([near_dispatch[...], far[1], *ordered], axis=0).T.astype(jnp.bfloat16)
    right = jnp.concatenate([near_grads[...], far[0], router[...]], axis=0)
    parts = sent.shape[0]
    size = out.shape[1] // parts
    for part in range(parts):
        columns = slice(part * size, (part + 1) * size)
        out[:, columns] = dot_plain(left, right[:, columns]).astype(jnp.bfloat16)
        copy = pltpu.make_async_copy(
            out.at[:, columns], out_far.at[:, columns], sent.at[part]
        )
        copy.start()
        copies.append(copy)
    for copy in copies:
        copy.wait()


def swap(blocks, axis):
    return lax.ppermute(blocks, axis, [(0, 1), (1, 0)])


def to_group(block, beside, groups):
    chips = lax.axis_size("chip")
    (blocks,) = call(
        pack_kernel,
        [array(block.dtype, groups, chips, *block.shape)],
        [block, beside],
        FLOPS_BESIDE_EXCHANGE,
    )
    blocks = blocks.reshape(groups * chips, *block.shape)
    blocks = lax.all_to_all(blocks, HALF_CORE, 0, 0, tiled=True)
    return blocks, swap(blocks, "core")


def call(kernel, outs, args, flops, space=pltpu.VMEM, scratch=(), size=None):
    if size is None:
        size = sum(array.size * array.dtype.itemsize for array in (*args, *outs))
    return pl.pallas_call(
        kernel,
        out_shape=outs,
        in_specs=[pl.BlockSpec(memory_space=pltpu.VMEM) for _ in args],
        out_specs=[pl.BlockSpec(memory_space=space) for _ in outs],
        scratch_shapes=scratch,
        cost_estimate=pl.CostEstimate(flops=flops, bytes_accessed=size, transcendentals=0),
        compiler_params=pltpu.CompilerParams(vmem_limit_bytes=24 * 2**20),
    )(*args)


def array(dtype, *shape):
    return jax.ShapeDtypeStruct(shape, dtype)


def local(
    tokens,
    cotangent,
    router,
    slot_outputs,
    base_in,
    base_out,
    in_left,
    in_right,
    out_left,
    out_right,
):
    groups, ring = lax.axis_size("dp"), lax.axis_size(SEQ)
    devices = groups * ring
    _, count, width = tokens.shape
    slots = router.shape[1]
    owned, slice_width, rank = in_left.shape
    members, _, hidden = in_right.shape
    rows = groups * owned
    if groups != 2 or ring % 4 or slice_width % 128 or rows % 8 or members % owned:
        return local_plain(
            tokens,
            cotangent,
            router,
            slot_outputs,
            base_in,
            base_out,
            in_left,
            in_right,
            out_left,
            out_right,
        )
    low, full = jnp.bfloat16, jnp.float32
    image_rows, cot_rows, saved = tokens[0], cotangent[0], slot_outputs[0]
    router, base_in = router.T, base_in.T
    in_left, out_left = in_left.swapaxes(1, 2), out_left.swapaxes(1, 2)
    (early,) = call(early_kernel, [array(full, 8, 128)], [], FLOPS_BESIDE_EXCHANGE)
    first = array(low, devices // 2, owned, 2 * slice_width + STATS)
    own, other, logits, combine = call(
        functools.partial(sums_kernel, owned, groups),
        [first, first, array(full, slots, count), array(full, slots, count)],
        [early, image_rows, cot_rows, router],
        6 * count * slots * width + FLOPS_BESIDE_EXCHANGE,
    )
    other = swap(other, "core")
    (first,) = call(
        functools.partial(merge_kernel, slice_width), [first], [own, other], FLOPS_BESIDE_EXCHANGE
    )
    first = lax.all_to_all(first, SAME_CORE, 0, 0, tiled=True)
    second, inputs, lows, stats = call(
        functools.partial(owner_kernel, groups),
        [
            array(low, rows, 2 * slice_width + 2 * rank),
            array(full, rows, slice_width),
            array(low, 2, rows, slice_width),
            array(full, rows, STATS),
        ],
        [first, in_left, out_right],
        4 * rows * owned * rank * slice_width,
    )
    second, combine = lax.optimization_barrier((second, combine))
    beside = swap(second, "half")
    (mixing,) = call(
        mixing_kernel,
        [array(full, slots, count)],
        [cot_rows, saved, combine],
        2 * count * slots * width,
    )
    beside, mixing = lax.optimization_barrier((beside, mixing))
    second, second_other = to_group(second, beside, groups)
    total_rows = groups * members
    near_ranks, near_products = call(
        near_kernel,
        [array(full, 2, total_rows // 2, rank), array(full, 2, total_rows // 2, hidden)],
        [second, in_right, out_left, base_in, base_out],
        2 * total_rows * owned * rank * hidden,
        size=0,
    )
    third, pair, hidden_ranks = call(
        functools.partial(hidden_kernel, groups),
        [
            array(low, ring, rows, slice_width + 2 * rank),
            array(full, 2, total_rows, hidden),
            array(full, 2, total_rows, rank),
        ],
        [
            second,
            second_other,
            near_ranks,
            near_products,
            base_in,
            base_out,
            in_right,
            out_left,
        ],
        6 * total_rows * hidden * (width + owned * rank),
    )
    third = lax.all_to_all(third, HALF, 0, 0, tiled=True)
    own, other = call(
        halves_kernel,
        [array(kind, rows, slice_width + 2 * rank) for kind in (full, low)],
        [third],
        0,
    )
    other, pair, hidden_ranks = lax.optimization_barrier((other, pair, hidden_ranks))
    other = swap(other, "half")
    grad_in_right, grad_out_left = call(
        functools.partial(outer_kernel, owned),
        [array(low, members, rank, hidden)] * 2,
        [hidden_ranks, pair],
        4 * members * rank * hidden * rows,
    )
    other, grad_in_right, grad_out_left = lax.optimization_barrier(
        (other, grad_in_right, grad_out_left)
    )
    fourth, ranks = call(
        functools.partial(finish_kernel, groups),
        [array(low, devices // 2, owned, slice_width + STATS), array(full, 2, rows, rank)],
        [own, other, in_left, inputs, stats],
        2 * rows * owned * rank * slice_width,
    )
    fourth = lax.all_to_all(fourth, SAME_CORE, 0, 0, tiled=True)
    fourth, ranks = lax.optimization_barrier((fourth, ranks))
    fourth_other = swap(fourth, "core")
    grad_in_left, grad_out_right = call(
        functools.partial(outer_kernel, owned),
        [array(low, owned, rank, slice_width)] * 2,
        [ranks, lows],
        4 * owned * rank * slice_width * rows,
    )
    near = call(
        near_tokens_kernel,
        [
            array(low, slots // 2, width),
            array(full, slots // 2, count),
            array(full, slots // 2, count),
        ],
        [fourth, image_rows, logits, mixing],
        count * slots * width,
        size=0,
    )
    fourth_other, grad_in_left, grad_out_right, *near = lax.optimization_barrier(
        (fourth_other, grad_in_left, grad_out_right, *near)
    )
    parts = width // 256 if width % 256 == 0 else 1
    token_grad, grad_in_left, grad_out_right = call(
        tokens_kernel,
        [array(low, count, width)] + [array(low, owned, rank, slice_width)] * 2,
        [
            fourth_other,
            *near,
            image_rows,
            router,
            logits,
            mixing,
            grad_in_left,
            grad_out_right,
        ],
        6 * count * slots * width,
        pltpu.HBM,
        [
            pltpu.VMEM((count, width), low),
            pltpu.SemaphoreType.DMA((parts,)),
            pltpu.SemaphoreType.DMA((2,)),
        ],
    )
    return (
        token_grad[None],
        grad_in_left.swapaxes(1, 2),
        grad_in_right,
        grad_out_left.swapaxes(1, 2),
        grad_out_right,
    )


def solution(mesh):
    groups, ring = mesh.shape["dp"], mesh.shape["seq"]
    cores = math.gcd(2, ring // groups)
    split = mesh.devices.reshape(groups, groups, ring // groups // cores, cores)
    mesh = jax.sharding.Mesh(split, BOTH)
    in_specs = (
        P("dp", SEQ, None),
        P("dp", SEQ, None),
        P(),
        P("dp", None, None),
        P(None, SEQ),
        P(SEQ, None),
        P(SEQ, "dp", None),
        P("dp", None, SEQ),
        P("dp", SEQ, None),
        P(SEQ, None, "dp"),
    )
    out_specs = (
        P("dp", SEQ, None),
        P(SEQ, "dp", None),
        P("dp", None, SEQ),
        P("dp", SEQ, None),
        P(SEQ, None, "dp"),
    )
    return jax.shard_map(local, mesh=mesh, in_specs=in_specs, out_specs=out_specs, check_vma=False)
```

```python
import functools
import math

import jax
import jax.numpy as jnp
from jax import lax
from jax.experimental import pallas as pl
from jax.experimental.pallas import tpu as pltpu
from jax.sharding import PartitionSpec as P

PLACE = ("chip", "core")
SEQ = ("half", *PLACE)
BOTH = ("dp", *SEQ)
HALF = ("dp", *PLACE)
HALF_CORE = ("dp", "chip")
SAME_CORE = ("dp", "half", "chip")
STATS = 128
FLOPS_BESIDE_EXCHANGE = 10**10


def gelu_backward(preact, upstream):
    return jax.vjp(jax.nn.gelu, preact)[1](upstream)[0]


def dot_first(left, right):
    return lax.dot_general(
        left, right, (((0,), (0,)), ((), ())), preferred_element_type=jnp.float32
    )


def dot_last(left, right):
    return lax.dot_general(
        left, right, (((1,), (1,)), ((), ())), preferred_element_type=jnp.float32
    )


def split(value):
    high = lax.reduce_precision(value, 8, 7)
    low = lax.reduce_precision(value - high, 8, 7)
    return high.astype(jnp.bfloat16), low.astype(jnp.bfloat16)


def joined(high, low):
    return high.astype(jnp.float32) + low.astype(jnp.float32)


def exchange(blocks):
    flat = blocks.reshape((-1,) + blocks.shape[2:])
    return lax.all_to_all(flat, BOTH, 0, 0, tiled=True).reshape(blocks.shape)


def local_plain(
    tokens,
    cotangent,
    router,
    slot_outputs,
    base_in,
    base_out,
    in_left,
    in_right,
    out_left,
    out_right,
):
    groups, ring = lax.axis_size("dp"), lax.axis_size(SEQ)
    image_rows = tokens[0]
    cot_rows = cotangent[0]
    saved_outputs = slot_outputs[0]
    width = image_rows.shape[1]
    slots = router.shape[1]
    owned, slice_width, rank = in_left.shape
    members = in_right.shape[0]
    places = members // owned
    group, place = lax.axis_index("dp"), lax.axis_index(SEQ)

    logits = jnp.dot(image_rows, router, preferred_element_type=jnp.float32)
    peak_high, peak_low = split(jnp.max(logits, axis=0))
    near = jnp.exp(logits - joined(peak_high, peak_low))
    total_high, total_low = split(jnp.sum(near, axis=0))
    combine = jax.nn.softmax(logits, axis=1)
    sums = jnp.stack(
        [
            dot_first(near.astype(jnp.bfloat16), image_rows),
            dot_first(combine.astype(jnp.bfloat16), cot_rows),
        ],
        axis=1,
    ).astype(jnp.bfloat16)
    sums = sums.reshape(ring, owned, 2, groups, slice_width).transpose(3, 0, 1, 2, 4)
    sums = sums.reshape(groups, ring, owned, 2 * slice_width)
    stats = jnp.stack([peak_high, peak_low, total_high, total_low], axis=1)
    stats = jnp.pad(stats, ((0, 0), (0, STATS - 4))).reshape(1, ring, owned, STATS)
    stats = jnp.broadcast_to(stats, (groups, ring, owned, STATS))
    first = exchange(jnp.concatenate([sums, stats], axis=3))

    tail = 2 * slice_width
    peaks = joined(first[..., tail], first[..., tail + 1])
    totals = joined(first[..., tail + 2], first[..., tail + 3])
    peak = jnp.max(peaks, axis=1)
    near_scale = jnp.exp(peaks - peak[:, None])
    total = jnp.sum(near_scale * totals, axis=1)
    near_scale = near_scale / total[:, None]
    parts = first[..., :tail].astype(jnp.float32)
    slot_inputs = jnp.sum(parts[..., :slice_width] * near_scale[..., None], axis=1)
    inputs_own = slot_inputs.astype(jnp.bfloat16)
    grads_own = jnp.sum(parts[..., slice_width:], axis=1).astype(jnp.bfloat16)
    up_part = jnp.einsum("gjd,jdr->gjr", inputs_own, in_left, preferred_element_type=jnp.float32)
    back_part = jnp.einsum("gjd,jrd->gjr", grads_own, out_right, preferred_element_type=jnp.float32)
    second = jnp.concatenate(
        [inputs_own, grads_own, *split(up_part), *split(back_part)], axis=2
    )
    second = exchange(jnp.broadcast_to(second, (groups, ring) + second.shape))
    second = lax.dynamic_slice_in_dim(second, group * places, places, 1)

    def gathered(start):
        piece = second[..., start : start + slice_width]
        return piece.transpose(2, 1, 3, 0, 4).reshape(groups * members, width)

    def ranks(start):
        piece = joined(
            second[..., start : start + rank], second[..., start + rank : start + 2 * rank]
        )
        piece = jnp.sum(piece, axis=0).transpose(1, 0, 2, 3)
        return piece.reshape(groups, members, rank).astype(jnp.bfloat16)

    inputs_low, grads_low = gathered(0), gathered(slice_width)
    up_low, back_low = ranks(tail), ranks(tail + 2 * rank)
    hidden = base_in.shape[1]
    preact = jnp.dot(inputs_low, base_in, preferred_element_type=jnp.float32).reshape(
        groups, members, hidden
    ) + jnp.einsum("gjr,jrf->gjf", up_low, in_right, preferred_element_type=jnp.float32)
    hidden_low = jax.nn.gelu(preact).astype(jnp.bfloat16)
    hidden_grad = dot_last(grads_low, base_out).reshape(groups, members, hidden) + jnp.einsum(
        "gjr,jfr->gjf", back_low, out_left, preferred_element_type=jnp.float32
    )
    preact_grad = gelu_backward(preact, hidden_grad).astype(jnp.bfloat16)
    slot_term = dot_last(preact_grad.reshape(groups * members, hidden), base_in)
    down_term = jnp.einsum(
        "gjf,jrf->gjr", preact_grad, in_right, preferred_element_type=jnp.float32
    )
    value_term = jnp.einsum(
        "gjf,jfr->gjr", hidden_low, out_left, preferred_element_type=jnp.float32
    )
    slot_term = slot_term.astype(jnp.bfloat16).reshape(groups, places, owned, groups, slice_width)
    slot_term = slot_term.transpose(3, 1, 0, 2, 4)
    rank_term = jnp.concatenate([down_term, value_term], axis=2).astype(jnp.bfloat16)
    rank_term = rank_term.reshape(groups, places, owned, 2 * rank).transpose(1, 0, 2, 3)
    rank_term = jnp.broadcast_to(rank_term, (groups,) + rank_term.shape)
    third = jnp.concatenate([slot_term, rank_term], axis=4)
    third = lax.dynamic_update_slice_in_dim(
        jnp.zeros((groups, ring) + third.shape[2:], jnp.bfloat16), third, group * places, 1
    )
    third = exchange(third)
    third = lax.dynamic_index_in_dim(third, place // places, 0, keepdims=False)
    third = jnp.sum(third.astype(jnp.float32), axis=0)
    down_own = third[..., slice_width : slice_width + rank].astype(jnp.bfloat16)
    value_own = third[..., slice_width + rank :].astype(jnp.bfloat16)
    slot_grads_own = (
        third[..., :slice_width]
        + jnp.einsum("gjr,jdr->gjd", down_own, in_left, preferred_element_type=jnp.float32)
    ).astype(jnp.bfloat16)
    shift_part = jnp.sum(slot_grads_own.astype(jnp.float32) * slot_inputs, axis=2)
    stats = jnp.stack([*split(peak), *split(total), *split(shift_part)], axis=2)
    stats = jnp.pad(stats, ((0, 0), (0, 0), (0, STATS - 6)))
    fourth = jnp.concatenate([slot_grads_own, stats], axis=2)[:, None]
    fourth = exchange(jnp.broadcast_to(fourth, (groups, ring) + fourth.shape[2:]))
    slot_grads = fourth[..., :slice_width].transpose(1, 2, 0, 3).reshape(slots, width)
    stats = fourth[..., slice_width:].astype(jnp.float32).reshape(groups, slots, STATS)
    slot_peak = stats[0, :, 0] + stats[0, :, 1]
    slot_total = stats[0, :, 2] + stats[0, :, 3]
    shift_back = jnp.sum(stats[:, :, 4] + stats[:, :, 5], axis=0)

    dispatch = jnp.exp(logits - slot_peak) / slot_total
    dispatch_low = dispatch.astype(jnp.bfloat16)
    weight_grad = dot_last(image_rows, slot_grads)
    dispatch_logit = dispatch * (weight_grad - shift_back)
    mixing_grad = dot_last(cot_rows, saved_outputs)
    combine_logit = combine * (mixing_grad - jnp.sum(combine * mixing_grad, axis=1, keepdims=True))
    logit_grad = (dispatch_logit + combine_logit).astype(jnp.bfloat16)
    token_grad = (
        jnp.dot(dispatch_low, slot_grads, preferred_element_type=jnp.float32)
        + dot_last(logit_grad, router)
    ).astype(jnp.bfloat16)
    grad_in_right = jnp.einsum(
        "gjr,gjf->jrf", up_low, preact_grad, preferred_element_type=jnp.float32
    ).astype(jnp.bfloat16)
    grad_out_left = jnp.einsum(
        "gjf,gjr->jfr", hidden_low, back_low, preferred_element_type=jnp.float32
    ).astype(jnp.bfloat16)
    grad_in_left = jnp.einsum(
        "gjd,gjr->jdr", inputs_own, down_own, preferred_element_type=jnp.float32
    ).astype(jnp.bfloat16)
    grad_out_right = jnp.einsum(
        "gjr,gjd->jrd", value_own, grads_own, preferred_element_type=jnp.float32
    ).astype(jnp.bfloat16)
    return (token_grad[None], grad_in_left, grad_in_right, grad_out_left, grad_out_right)


def dot_turned(left, right):
    return dot_last(right, left).T


def dot_plain(left, right):
    return jnp.dot(left, right, preferred_element_type=jnp.float32)


def halves(value):
    high = value.astype(jnp.bfloat16).astype(jnp.float32)
    low = (value - high).astype(jnp.bfloat16).astype(jnp.float32)
    return high, low


def in_lanes(columns, shape):
    lane = lax.broadcasted_iota(jnp.int32, shape, len(shape) - 1)
    out = jnp.zeros(shape, jnp.float32)
    for number, column in enumerate(columns):
        out = jnp.where(lane == number, column, out)
    return out


def own_block(value, owned):
    rows, rank = value.shape
    wide = jnp.concatenate([value] * owned, axis=1)
    shape = (rows, owned * rank)
    block = lax.broadcasted_iota(jnp.int32, shape, 1) // rank
    expert = lax.broadcasted_iota(jnp.int32, shape, 0) % owned
    return jnp.where(block == expert, wide, 0.0).astype(jnp.bfloat16)


def from_own_block(value, owned):
    rows, wide = value.shape
    rank = wide // owned
    block = lax.broadcasted_iota(jnp.int32, value.shape, 1) // rank
    expert = lax.broadcasted_iota(jnp.int32, value.shape, 0) % owned
    kept = jnp.where(block == expert, value, 0.0)
    out = kept[:, :rank]
    for number in range(1, owned):
        out = out + kept[:, number * rank : (number + 1) * rank]
    return out


def early_kernel(out):
    out[...] = jnp.zeros(out.shape, out.dtype)


def sums_kernel(
    owned, groups, _, tokens, cotangent, router, own, other, logits_out, combine_out
):
    chips = own.shape[0] // groups
    core = lax.axis_index("core")
    image_rows = tokens[...]
    logits = dot_last(router[...], image_rows)
    high, low = halves(jnp.max(logits, axis=1, keepdims=True))
    near = jnp.exp(logits - (high + low))
    total_high, total_low = halves(jnp.sum(near, axis=1, keepdims=True))
    spread = jnp.exp(logits - jnp.max(logits, axis=0, keepdims=True))
    combine = spread / jnp.sum(spread, axis=0, keepdims=True)
    logits_out[...] = logits
    combine_out[...] = combine
    stats = in_lanes([high, low, total_high, total_low], (logits.shape[0], STATS))
    stats = stats.astype(jnp.bfloat16)
    inputs = dot_plain(near.astype(jnp.bfloat16), image_rows).astype(jnp.bfloat16)
    grads = dot_plain(combine.astype(jnp.bfloat16), cotangent[...]).astype(jnp.bfloat16)
    width = inputs.shape[1] // groups

    def block(rows, columns):
        return jnp.concatenate([inputs[rows, columns], grads[rows, columns], stats[rows]], axis=1)

    for group in range(groups):
        columns = slice(group * width, (group + 1) * width)
        for chip in range(chips):
            start = 2 * chip * owned
            even = block(slice(start, start + owned), columns)
            odd = block(slice(start + owned, start + 2 * owned), columns)
            own[group * chips + chip] = jnp.where(core == 0, even, odd)
            other[group * chips + chip] = jnp.where(core == 0, odd, even)


def merge_kernel(width, own, other, out):
    parts = []
    for part in (own, other):
        stats = part[:, :, 2 * width :].astype(jnp.float32)
        parts.append((stats[:, :, 0:1] + stats[:, :, 1:2], stats[:, :, 2:3] + stats[:, :, 3:4]))
    peak = jnp.maximum(parts[0][0], parts[1][0])
    scales = [jnp.exp(part[0] - peak) for part in parts]
    total = scales[0] * parts[0][1] + scales[1] * parts[1][1]
    stats = in_lanes([*halves(peak), *halves(total)], own.shape[:2] + (STATS,))
    inputs = [
        part[:, :, :width].astype(jnp.float32) * scale
        for part, scale in zip((own, other), scales, strict=True)
    ]
    grads = [part[:, :, width : 2 * width].astype(jnp.float32) for part in (own, other)]
    out[:, :, :width] = (inputs[0] + inputs[1]).astype(jnp.bfloat16)
    out[:, :, width : 2 * width] = (grads[0] + grads[1]).astype(jnp.bfloat16)
    out[:, :, 2 * width :] = stats.astype(jnp.bfloat16)


def mixing_kernel(cotangent, saved, combine, out):
    mixing = dot_last(saved[...], cotangent[...])
    weights = combine[...]
    out[...] = weights * (mixing - jnp.sum(weights * mixing, axis=0, keepdims=True))


def owner_kernel(groups, first, in_left, out_right, second, inputs_out, lows_out, stats_out):
    ring = first.shape[0] // groups
    owned, rank, width = in_left.shape
    inputs, grads, stats_rows = [], [], []
    for group in range(groups):
        rows = slice(group * ring, (group + 1) * ring)
        stats = first[rows, :, 2 * width :].astype(jnp.float32)
        peaks = stats[:, :, 0:1] + stats[:, :, 1:2]
        totals = stats[:, :, 2:3] + stats[:, :, 3:4]
        peak = jnp.max(peaks, axis=0)
        scale = jnp.exp(peaks - peak[None])
        total = jnp.sum(scale * totals, axis=0)
        scale = scale / total[None]
        inputs.append(jnp.sum(first[rows, :, :width].astype(jnp.float32) * scale, axis=0))
        grads.append(jnp.sum(first[rows, :, width : 2 * width].astype(jnp.float32), axis=0))
        stats_rows.append(in_lanes([*halves(peak), *halves(total)], (owned, STATS)))
    inputs, grads = jnp.concatenate(inputs, axis=0), jnp.concatenate(grads, axis=0)
    inputs_out[...] = inputs
    stats_out[...] = jnp.concatenate(stats_rows, axis=0)
    inputs_low, grads_low = inputs.astype(jnp.bfloat16), grads.astype(jnp.bfloat16)
    lows_out[0] = inputs_low
    lows_out[1] = grads_low
    up = dot_last(inputs_low, in_left[...].reshape(owned * rank, width))
    back = dot_last(grads_low, out_right[...].reshape(owned * rank, width))
    ranks = [from_own_block(up, owned), from_own_block(back, owned)]
    ranks = jnp.concatenate(ranks, axis=1).astype(jnp.bfloat16)
    block = jnp.concatenate([inputs_low, grads_low, ranks], axis=1)
    second[...] = block


def pack_kernel(own, beside, out):
    here = lax.axis_index("half")
    for group in range(out.shape[0]):
        block = jnp.where(here == group, own[...], beside[...])
        for place in range(out.shape[1]):
            out[group, place] = block


def factor_products(blocks, in_right, out_left, core):
    members, rank, hidden = in_right.shape
    rows = blocks.shape[1]
    chips = blocks.shape[0] // 2
    owned = members // (2 * chips)
    start = blocks.shape[2] - 2 * rank
    ranks = jnp.zeros((chips * rows, 2 * rank), jnp.float32)
    for half in range(2):
        part = blocks[half * chips : (half + 1) * chips, :, start:].astype(jnp.float32)
        ranks = ranks + part.reshape(ranks.shape)
    out = []
    for number, table in enumerate((in_right, out_left)):
        value = ranks[:, number * rank : (number + 1) * rank]
        value = value.astype(jnp.bfloat16).astype(jnp.float32)
        taken = []
        for chip in range(chips):
            own = own_block(value[chip * rows : (chip + 1) * rows], owned)
            part = table[pl.ds((2 * chip + core) * owned, owned)].reshape(owned * rank, hidden)
            taken.append(dot_plain(own, part))
        out.append((value, jnp.concatenate(taken, axis=0)))
    return out


def near_kernel(second, in_right, out_left, _, __, ranks_out, products_out):
    found = factor_products(second, in_right, out_left, lax.axis_index("core"))
    for number, (value, product) in enumerate(found):
        ranks_out[number] = value
        products_out[number] = product


def hidden_kernel(
    groups,
    second,
    second_other,
    near_ranks,
    near_products,
    base_in,
    base_out,
    in_right,
    out_left,
    third,
    pair_out,
    ranks_out,
):
    first_core = lax.axis_index("core") == 0
    members, rank, hidden = in_right.shape
    rows = second.shape[1]
    owned = rows // groups
    places = members // owned
    width = base_in.shape[1] // groups

    def gathered(columns):
        parts = []
        for half in range(groups):
            taken = []
            for chip in range(places // 2):
                block = half * (places // 2) + chip
                own = second[block, :, columns].astype(jnp.float32)
                other = second_other[block, :, columns].astype(jnp.float32)
                taken.append(jnp.where(first_core, own, other))
                taken.append(jnp.where(first_core, other, own))
            parts.append(jnp.concatenate(taken, axis=0))
        return parts

    def in_order(near, far):
        taken = []
        for chip in range(places // 2):
            own = near[chip * rows : (chip + 1) * rows]
            other = far[chip * rows : (chip + 1) * rows]
            taken.append(jnp.where(first_core, own, other))
            taken.append(jnp.where(first_core, other, own))
        return jnp.concatenate(taken, axis=0)

    def to_rank(value, table):
        taken = []
        for place in range(places):
            part = table[place * owned : (place + 1) * owned].reshape(owned * rank, hidden)
            wide = dot_last(value[place * rows : (place + 1) * rows].astype(jnp.bfloat16), part)
            taken.append(from_own_block(wide, owned))
        return jnp.concatenate(taken, axis=0)

    far = factor_products(second_other, in_right, out_left, 1 - lax.axis_index("core"))
    up, back = [in_order(near_ranks[number], far[number][0]) for number in range(2)]
    preact, hidden_grad = [in_order(near_products[number], far[number][1]) for number in range(2)]
    for half, part in enumerate(gathered(slice(0, width))):
        columns = slice(half * width, (half + 1) * width)
        preact = preact + dot_turned(part.astype(jnp.bfloat16), base_in[:, columns])
    for half, part in enumerate(gathered(slice(width, 2 * width))):
        columns = slice(half * width, (half + 1) * width)
        hidden_grad = hidden_grad + dot_turned(part.astype(jnp.bfloat16), base_out[:, columns])
    root = 0.7978845608028654
    bent = jnp.tanh(root * (preact + 0.044715 * (preact * preact * preact)))
    hidden_value = 0.5 * preact * (1.0 + bent)
    slope = 0.5 * (1.0 + bent) + 0.5 * preact * (1.0 - bent * bent) * (
        root * (1.0 + 3.0 * 0.044715 * (preact * preact))
    )
    hidden_low = hidden_value.astype(jnp.bfloat16).astype(jnp.float32)
    preact_grad = (hidden_grad * slope).astype(jnp.bfloat16).astype(jnp.float32)
    pair_out[0] = preact_grad
    pair_out[1] = hidden_low
    ranks_out[0] = up
    ranks_out[1] = back
    slot_term = dot_plain(preact_grad.astype(jnp.bfloat16), base_in[...]).astype(jnp.bfloat16)
    down = to_rank(preact_grad, in_right)
    value = to_rank(hidden_low, out_left)
    ranks = jnp.concatenate([down, value], axis=1).astype(jnp.bfloat16)
    for half in range(groups):
        columns = slice(half * width, (half + 1) * width)
        for place in range(places):
            taken = slice(place * rows, (place + 1) * rows)
            block = half * places + place
            third[block, :, :width] = slot_term[taken, columns]
            third[block, :, width:] = ranks[taken]


def outer_kernel(owned, left_rows, right_rows, *outs):
    rows = left_rows.shape[1] // (outs[0].shape[0] // owned)
    for number, out in enumerate(outs):
        for place in range(out.shape[0] // owned):
            taken = slice(place * rows, (place + 1) * rows)
            own = own_block(left_rows[number, taken], owned)
            product = dot_first(own, right_rows[number, taken].astype(jnp.bfloat16))
            out[place * owned : (place + 1) * owned] = product.astype(jnp.bfloat16).reshape(
                (owned,) + out.shape[1:]
            )


def halves_kernel(third, own, other):
    places = third.shape[0] // 2
    here = lax.axis_index("half")
    for out, group in ((own, here), (other, 1 - here)):
        taken = third[pl.ds(group * places, places)].astype(jnp.float32)
        out[...] = jnp.sum(taken, axis=0).astype(out.dtype)


def finish_kernel(groups, own, other, in_left, inputs, stats, fourth, ranks_out):
    owned, rank, width = in_left.shape
    summed = own[...] + other[...].astype(jnp.float32)
    ranks = summed[:, width:].astype(jnp.bfloat16).astype(jnp.float32)
    ranks_out[0] = ranks[:, :rank]
    ranks_out[1] = ranks[:, rank:]
    down = own_block(ranks[:, :rank], owned)
    grads = summed[:, :width] + dot_plain(down, in_left[...].reshape(owned * rank, width))
    grads = grads.astype(jnp.bfloat16).astype(jnp.float32)
    high, low = halves(jnp.sum(grads * inputs[...], axis=1, keepdims=True))
    lane = lax.broadcasted_iota(jnp.int32, stats.shape, 1)
    tail = jnp.where(lane == 4, high, jnp.where(lane == 5, low, stats[...]))
    block = jnp.concatenate([grads, tail], axis=1).astype(jnp.bfloat16)
    for group in range(groups):
        rows = block[group * owned : (group + 1) * owned]
        for place in range(fourth.shape[0] // groups):
            fourth[group * (fourth.shape[0] // groups) + place] = rows


def tokens_kernel(
    groups,
    fourth,
    fourth_other,
    tokens,
    router,
    logits,
    mixing,
    grad_left,
    grad_right,
    out_far,
    grad_left_far,
    grad_right_far,
    out,
    sent,
    grads_sent,
):
    copies = [
        pltpu.make_async_copy(grad_left, grad_left_far, grads_sent.at[0]),
        pltpu.make_async_copy(grad_right, grad_right_far, grads_sent.at[1]),
    ]
    for copy in copies:
        copy.start()
    blocks, owned, _ = fourth.shape
    chips = blocks // groups
    width = tokens.shape[1] // groups
    first_core = lax.axis_index("core") == 0

    def rows(half, columns):
        taken = []
        for chip in range(chips):
            own = fourth[half * chips + chip, :, columns].astype(jnp.float32)
            other = fourth_other[half * chips + chip, :, columns].astype(jnp.float32)
            taken.append(jnp.where(first_core, own, other))
            taken.append(jnp.where(first_core, other, own))
        return jnp.concatenate(taken, axis=0)

    grads = jnp.concatenate([rows(half, slice(0, width)) for half in range(groups)], axis=1)
    grads = grads.astype(jnp.bfloat16)
    stats = [rows(half, slice(width, width + STATS)) for half in range(groups)]
    peak = stats[0][:, 0:1] + stats[0][:, 1:2]
    total = stats[0][:, 2:3] + stats[0][:, 3:4]
    shift = functools.reduce(jnp.add, [part[:, 4:5] + part[:, 5:6] for part in stats])
    dispatch = jnp.exp(logits[...] - peak) / total
    weight_grad = dot_last(grads, tokens[...])
    logit_grad = dispatch * (weight_grad - shift) + mixing[...]
    left = jnp.concatenate([dispatch, logit_grad], axis=0).T.astype(jnp.bfloat16)
    right = jnp.concatenate([grads, router[...]], axis=0)
    parts = sent.shape[0]
    size = out.shape[1] // parts
    for part in range(parts):
        columns = slice(part * size, (part + 1) * size)
        out[:, columns] = dot_plain(left, right[:, columns]).astype(jnp.bfloat16)
        copy = pltpu.make_async_copy(
            out.at[:, columns], out_far.at[:, columns], sent.at[part]
        )
        copy.start()
        copies.append(copy)
    for copy in copies:
        copy.wait()


def swap(blocks, axis):
    return lax.ppermute(blocks, axis, [(0, 1), (1, 0)])


def to_group(block, beside, groups):
    chips = lax.axis_size("chip")
    (blocks,) = call(
        pack_kernel,
        [array(block.dtype, groups, chips, *block.shape)],
        [block, beside],
        FLOPS_BESIDE_EXCHANGE,
    )
    blocks = blocks.reshape(groups * chips, *block.shape)
    blocks = lax.all_to_all(blocks, HALF_CORE, 0, 0, tiled=True)
    return blocks, swap(blocks, "core")


def call(kernel, outs, args, flops, space=pltpu.VMEM, scratch=(), size=None):
    if size is None:
        size = sum(array.size * array.dtype.itemsize for array in (*args, *outs))
    return pl.pallas_call(
        kernel,
        out_shape=outs,
        in_specs=[pl.BlockSpec(memory_space=pltpu.VMEM) for _ in args],
        out_specs=[pl.BlockSpec(memory_space=space) for _ in outs],
        scratch_shapes=scratch,
        cost_estimate=pl.CostEstimate(flops=flops, bytes_accessed=size, transcendentals=0),
        compiler_params=pltpu.CompilerParams(vmem_limit_bytes=24 * 2**20),
    )(*args)


def array(dtype, *shape):
    return jax.ShapeDtypeStruct(shape, dtype)


def local(
    tokens,
    cotangent,
    router,
    slot_outputs,
    base_in,
    base_out,
    in_left,
    in_right,
    out_left,
    out_right,
):
    groups, ring = lax.axis_size("dp"), lax.axis_size(SEQ)
    devices = groups * ring
    _, count, width = tokens.shape
    slots = router.shape[1]
    owned, slice_width, rank = in_left.shape
    members, _, hidden = in_right.shape
    rows = groups * owned
    if groups != 2 or ring % 4 or slice_width % 128 or rows % 8 or members % owned:
        return local_plain(
            tokens,
            cotangent,
            router,
            slot_outputs,
            base_in,
            base_out,
            in_left,
            in_right,
            out_left,
            out_right,
        )
    low, full = jnp.bfloat16, jnp.float32
    image_rows, cot_rows, saved = tokens[0], cotangent[0], slot_outputs[0]
    router, base_in = router.T, base_in.T
    in_left, out_left = in_left.swapaxes(1, 2), out_left.swapaxes(1, 2)
    (early,) = call(early_kernel, [array(full, 8, 128)], [], FLOPS_BESIDE_EXCHANGE)
    first = array(low, devices // 2, owned, 2 * slice_width + STATS)
    own, other, logits, combine = call(
        functools.partial(sums_kernel, owned, groups),
        [first, first, array(full, slots, count), array(full, slots, count)],
        [early, image_rows, cot_rows, router],
        6 * count * slots * width + FLOPS_BESIDE_EXCHANGE,
    )
    other = swap(other, "core")
    (first,) = call(
        functools.partial(merge_kernel, slice_width), [first], [own, other], FLOPS_BESIDE_EXCHANGE
    )
    first = lax.all_to_all(first, SAME_CORE, 0, 0, tiled=True)
    second, inputs, lows, stats = call(
        functools.partial(owner_kernel, groups),
        [
            array(low, rows, 2 * slice_width + 2 * rank),
            array(full, rows, slice_width),
            array(low, 2, rows, slice_width),
            array(full, rows, STATS),
        ],
        [first, in_left, out_right],
        4 * rows * owned * rank * slice_width,
    )
    second, combine = lax.optimization_barrier((second, combine))
    beside = swap(second, "half")
    (mixing,) = call(
        mixing_kernel,
        [array(full, slots, count)],
        [cot_rows, saved, combine],
        2 * count * slots * width,
    )
    beside, mixing = lax.optimization_barrier((beside, mixing))
    second, second_other = to_group(second, beside, groups)
    total_rows = groups * members
    near_ranks, near_products = call(
        near_kernel,
        [array(full, 2, total_rows // 2, rank), array(full, 2, total_rows // 2, hidden)],
        [second, in_right, out_left, base_in, base_out],
        2 * total_rows * owned * rank * hidden,
        size=0,
    )
    third, pair, hidden_ranks = call(
        functools.partial(hidden_kernel, groups),
        [
            array(low, ring, rows, slice_width + 2 * rank),
            array(full, 2, total_rows, hidden),
            array(full, 2, total_rows, rank),
        ],
        [
            second,
            second_other,
            near_ranks,
            near_products,
            base_in,
            base_out,
            in_right,
            out_left,
        ],
        6 * total_rows * hidden * (width + owned * rank),
    )
    third = lax.all_to_all(third, HALF, 0, 0, tiled=True)
    own, other = call(
        halves_kernel,
        [array(kind, rows, slice_width + 2 * rank) for kind in (full, low)],
        [third],
        0,
    )
    other, pair, hidden_ranks = lax.optimization_barrier((other, pair, hidden_ranks))
    other = swap(other, "half")
    grad_in_right, grad_out_left = call(
        functools.partial(outer_kernel, owned),
        [array(low, members, rank, hidden)] * 2,
        [hidden_ranks, pair],
        4 * members * rank * hidden * rows,
    )
    other, grad_in_right, grad_out_left = lax.optimization_barrier(
        (other, grad_in_right, grad_out_left)
    )
    fourth, ranks = call(
        functools.partial(finish_kernel, groups),
        [array(low, devices // 2, owned, slice_width + STATS), array(full, 2, rows, rank)],
        [own, other, in_left, inputs, stats],
        2 * rows * owned * rank * slice_width,
    )
    fourth = lax.all_to_all(fourth, SAME_CORE, 0, 0, tiled=True)
    fourth, ranks = lax.optimization_barrier((fourth, ranks))
    fourth_other = swap(fourth, "core")
    grad_in_left, grad_out_right = call(
        functools.partial(outer_kernel, owned),
        [array(low, owned, rank, slice_width)] * 2,
        [ranks, lows],
        4 * owned * rank * slice_width * rows,
    )
    fourth_other, grad_in_left, grad_out_right = lax.optimization_barrier(
        (fourth_other, grad_in_left, grad_out_right)
    )
    parts = 2 if width % 256 == 0 else 1
    token_grad, grad_in_left, grad_out_right = call(
        functools.partial(tokens_kernel, groups),
        [array(low, count, width)] + [array(low, owned, rank, slice_width)] * 2,
        [
            fourth,
            fourth_other,
            image_rows,
            router,
            logits,
            mixing,
            grad_in_left,
            grad_out_right,
        ],
        6 * count * slots * width,
        pltpu.HBM,
        [
            pltpu.VMEM((count, width), low),
            pltpu.SemaphoreType.DMA((parts,)),
            pltpu.SemaphoreType.DMA((2,)),
        ],
    )
    return (
        token_grad[None],
        grad_in_left.swapaxes(1, 2),
        grad_in_right,
        grad_out_left.swapaxes(1, 2),
        grad_out_right,
    )


def solution(mesh):
    groups, ring = mesh.shape["dp"], mesh.shape["seq"]
    cores = math.gcd(2, ring // groups)
    split = mesh.devices.reshape(groups, groups, ring // groups // cores, cores)
    mesh = jax.sharding.Mesh(split, BOTH)
    in_specs = (
        P("dp", SEQ, None),
        P("dp", SEQ, None),
        P(),
        P("dp", None, None),
        P(None, SEQ),
        P(SEQ, None),
        P(SEQ, "dp", None),
        P("dp", None, SEQ),
        P("dp", SEQ, None),
        P(SEQ, None, "dp"),
    )
    out_specs = (
        P("dp", SEQ, None),
        P(SEQ, "dp", None),
        P("dp", None, SEQ),
        P("dp", SEQ, None),
        P(SEQ, None, "dp"),
    )
    return jax.shard_map(local, mesh=mesh, in_specs=in_specs, out_specs=out_specs, check_vma=False)
```
